32 devices in a mesh: section: 2 (over x), replica: 4 (over z), shard: 4 (over y, core).
Axes of the slice: x: 2, y: 2, z: 4, core: 2. Of those that a mesh axis runs over, the one named last changes fastest.
Arguments:
- tokens_in: bfloat16 [2048, 2048], P(('replica', 'shard')), may hold values from -6 to 6
- positions: int32 [2048], P(('replica', 'shard')), may hold values from 0 to 63, as said below
- attn_gain: float32 [2, 2048], P('section'), may hold values from 0.25 to 1.75
- qkv_weight: bfloat16 [2, 2048, 3072], P('section', 'shard'), may hold values from -0.125 to 0.125
- out_weight: bfloat16 [2, 2048, 2048], P('section', 'shard'), may hold values from -0.375 to 0.375
- mlp_gain: float32 [2, 2048], P('section'), may hold values from 0.25 to 1.75
- gate_up_weight: bfloat16 [2, 2048, 16384], P('section', 'shard'), may hold values from -0.125 to 0.125
- down_weight: bfloat16 [2, 8192, 2048], P('section', 'shard'), may hold values from -0.0625 to 0.0625
- cotangent: bfloat16 [2048, 2048], P(('replica', 'shard')), may hold values from -6 to 6
Outputs:
- block_out: bfloat16 [2, 2048, 2048], P('section', ('replica', 'shard'))
- grad_in: float32 [2, 2048, 2048], P('section', ('replica', 'shard'))
- attn_gain_grad: float32 [2, 2048], P('section')
- qkv_grad: float32 [2, 2048, 3072], P('section', ('replica', 'shard'))
- out_grad: float32 [2, 2048, 2048], P('section', ('replica', 'shard'))
- mlp_gain_grad: float32 [2, 2048], P('section')
- gate_up_grad: float32 [2, 2048, 16384], P('section', ('replica', 'shard'))
- down_grad: float32 [2, 8192, 2048], P('section', ('replica', 'shard'))
The draws below stay inside these ranges and needn't reach their ends.
Inputs may be any that keep to these rules, and one draw needn't show every extreme that they name: `positions`: within each sequence of 64 tokens the first position is 0 and every later one is the previous plus 1 or is 0; a token sees the earlier tokens back to the last position 0.
All inputs are finite; a program needn't handle non-finite values.
Results may differ from the reference program's by a relative error of at most 0.023.
Values may be sent and summed in bfloat16 or wider, within the bound.
A program may use at most 640 MiB of HBM per device.

```python
import jax
import jax.numpy as jnp
from jax import lax

D = 2048
HEADS = 32
KV_HEADS = 8
HEAD = 64
FF = 8192
SEQ = 64
MICRO = 2
QKV = 3072
TOKENS = 2048
N_SECTION = 2
N_REPLICA = 4
N_SHARD = 4


def draw_positions(key, part):
    key = jax.random.fold_in(key, 7)
    seq_count = TOKENS // SEQ
    pick_key, break_key = jax.random.split(key)
    rolled = jax.random.randint(break_key, (seq_count, SEQ), 0, SEQ)
    chosen = jax.random.randint(pick_key, (), 0, seq_count)
    offsets = jnp.arange(SEQ, dtype=jnp.int32)
    at_start = offsets[None, :] == 0
    break_flags = (rolled < 3) | at_start
    break_flags = break_flags & ((jnp.arange(seq_count)[:, None] != chosen) | at_start)
    starts = lax.cummax(jnp.where(break_flags, offsets[None, :], 0), axis=1)
    return (offsets[None, :] - starts).reshape(seq_count * SEQ).astype(jnp.int32)


def block_levels(rng, extent, cuts, smallest, largest):
    def one(dim, parts):
        heights = jax.random.uniform(jax.random.fold_in(jax.random.fold_in(rng, 6), dim), (parts,), jnp.float32, smallest / len(cuts), largest / len(cuts))
        return jnp.repeat(jnp.exp(heights), extent[dim] // parts).reshape((-1,) + (1,) * (len(extent) - dim - 1))

    level = one(*cuts[0])
    for cut in cuts[1:]:
        level = level * one(*cut)
    return level


def noise(rng, extent, deviation, limit, cuts=(), held_as=jnp.bfloat16):
    factor_of = block_levels(rng, extent, cuts, -0.22, 0.18) if cuts else 1.0
    values = jax.random.normal(rng, extent, jnp.float32) * deviation * factor_of
    return jnp.minimum(jnp.maximum(values, -limit), limit).astype(held_as)


def setup_inputs(seed: int = 0) -> dict:
    streams_of = jax.random.split(jax.random.key(seed), 10)
    return {
        "tokens_in": noise(streams_of[0], (TOKENS, D), 1.0, 6.0, ((0, 16),)),
        "positions": draw_positions(jax.random.fold_in(streams_of[9], 71), 0),
        "attn_gain": jnp.clip(1.0 + 0.15 * jax.random.normal(streams_of[2], (N_SECTION, D), jnp.float32), 0.25, 1.75),
        "qkv_weight": noise(streams_of[3], (N_SECTION, D, QKV), D ** -0.5, 0.125, ((0, 2), (1, 4))),
        "out_weight": noise(streams_of[4], (N_SECTION, D, D), (D // 8) ** -0.5, 0.375, ((0, 2), (1, 4))),
        "mlp_gain": jnp.clip(1.0 + 0.15 * jax.random.normal(streams_of[5], (N_SECTION, D), jnp.float32), 0.25, 1.75),
        "gate_up_weight": noise(streams_of[6], (N_SECTION, D, 2 * FF), D ** -0.5, 0.125, ((0, 2), (1, 4))),
        "down_weight": noise(streams_of[7], (N_SECTION, FF, D), FF ** -0.5, 0.0625, ((0, 2), (1, 4))),
        "cotangent": noise(streams_of[8], (TOKENS, D), 1.0, 6.0, ((0, 16),)),
    }


EPSILON = 1e-05
ROPE_BASE = 500000.0
HIGHEST = lax.Precision.HIGHEST

@jax.custom_vjp
def low(v):
    return lax.optimization_barrier(v.astype(jnp.bfloat16)).astype(jnp.float32)

@jax.custom_vjp
def low_back(v):
    return v

def low_keep(v):
    return (low(v), None)

def low_pass(kept, grad):
    return (grad,)

def back_keep(v):
    return (v, None)

def back_low(kept, grad):
    return (low(grad),)
low.defvjp(low_keep, low_pass)
low_back.defvjp(back_keep, back_low)

def rope_tables(seq_pos):
    half_index = jnp.arange(HEAD // 2, dtype=jnp.float32)
    frequency = jnp.power(ROPE_BASE, -2.0 * half_index / HEAD)
    angles = seq_pos.astype(jnp.float32)[:, None] * frequency[None, :]
    return (jnp.cos(angles)[:, None, :], jnp.sin(angles)[:, None, :])

def rotate(vectors, cosine, sine):
    first_half = vectors[..., :HEAD // 2]
    second_half = vectors[..., HEAD // 2:]
    return jnp.concatenate([first_half * cosine - second_half * sine, second_half * cosine + first_half * sine], -1)

def visible(seq_pos):
    row_index = jnp.arange(SEQ)[:, None]
    col_index = jnp.arange(SEQ)[None, :]
    return (col_index <= row_index) & (row_index - col_index <= seq_pos[:, None])

def attend(inputs_seq):
    queries, keys_in, values_in, seq_pos = inputs_seq
    grouped = queries.reshape(SEQ, KV_HEADS, HEADS // KV_HEADS, HEAD)
    scores = jnp.einsum('qgrd,kgd->grqk', grouped, keys_in, precision=HIGHEST) * HEAD ** (-0.5)
    scores = low_back(scores)
    masked = jnp.where(visible(seq_pos), scores, -1e+30)
    top_score = lax.optimization_barrier(jnp.max(masked, -1, keepdims=True))
    expon = jnp.exp(masked - top_score)
    probs = expon / lax.optimization_barrier(jnp.sum(expon, -1, keepdims=True))
    output = jnp.einsum('grqk,kgd->qgrd', low(probs), values_in, precision=HIGHEST)
    return output.reshape(SEQ, D)

def rms_norm(values):
    return values * lax.rsqrt(lax.optimization_barrier(jnp.mean(values * values, -1, keepdims=True)) + EPSILON)

def layer(state, seq_pos, gain_one, qkv_full, out_full, gain_two, gate_up_full, down_full):
    rows_now = state.shape[0]
    seq_count = rows_now // SEQ
    normed = low(rms_norm(state) * gain_one)
    projected = low_back(jnp.dot(normed, qkv_full, precision=HIGHEST))
    cosine, sine = rope_tables(seq_pos.reshape(rows_now))
    kv_cols = KV_HEADS * HEAD
    queries = low(rotate(projected[:, :D].reshape(rows_now, HEADS, HEAD), cosine, sine))
    keys_in = low(rotate(projected[:, D:D + kv_cols].reshape(rows_now, KV_HEADS, HEAD), cosine, sine))
    values_in = low(projected[:, D + kv_cols:].reshape(rows_now, KV_HEADS, HEAD))
    outputs = lax.map(jax.checkpoint(attend), (queries.reshape(seq_count, SEQ, HEADS, HEAD), keys_in.reshape(seq_count, SEQ, KV_HEADS, HEAD), values_in.reshape(seq_count, SEQ, KV_HEADS, HEAD), seq_pos))
    attended = low(low_back(outputs.reshape(rows_now, D)))
    branch = low_back(jnp.dot(attended, out_full, precision=HIGHEST))
    middle = state + branch
    normed_two = low(rms_norm(middle) * gain_two)
    gate_up = low_back(jnp.dot(normed_two, gate_up_full, precision=HIGHEST))
    hidden_act = low(jax.nn.silu(gate_up[:, :FF]) * gate_up[:, FF:])
    return middle + jnp.dot(hidden_act, down_full, precision=HIGHEST)

def reference(tokens_in, positions, attn_gain, qkv_weight, out_weight, mlp_gain, gate_up_weight, down_weight, cotangent):
    params = (attn_gain.astype(jnp.float32), qkv_weight.astype(jnp.float32), out_weight.astype(jnp.float32), mlp_gain.astype(jnp.float32), gate_up_weight.astype(jnp.float32), down_weight.astype(jnp.float32))
    group_seqs = MICRO * N_SHARD
    group_rows = group_seqs * SEQ

    def forward(state, weights, bumps, seq_pos):
        results = []
        current = state
        for section_at in range(N_SECTION):
            result = layer(current, seq_pos, *[member[section_at] for member in weights])
            if section_at < N_SECTION - 1:
                current = low(low_back(result)) + bumps[section_at]
                results.append(current)
            else:
                results.append(result)
        return jnp.stack(results)

    def one_group(carry, span):
        tokens_group, pos_group, cot_group = span
        bumps = jnp.zeros((N_SECTION - 1, group_rows, D), jnp.float32)
        outputs, pullback = jax.vjp(lambda state, weights, extra: forward(state, weights, extra, pos_group), tokens_group.astype(jnp.float32), params, bumps)
        cot_full = jnp.concatenate([jnp.zeros((N_SECTION - 1, group_rows, D), jnp.float32), cot_group.astype(jnp.float32)[None]], 0)
        grad_state, grad_weights, grad_bumps = pullback(cot_full)
        grad_stack = jnp.concatenate([grad_state[None], low(grad_bumps)], 0)
        new_carry = jax.tree.map(lambda total, term: total + term, carry, grad_weights)
        return (new_carry, (outputs.astype(jnp.bfloat16), grad_stack))
    zero_grads = jax.tree.map(lambda member: jnp.zeros(member.shape, jnp.float32), params)
    spans = (tokens_in.reshape(N_REPLICA, group_rows, D), positions.reshape(N_REPLICA, group_seqs, SEQ), cotangent.reshape(N_REPLICA, group_rows, D))
    grads, (outs_all, grads_in) = lax.scan(one_group, zero_grads, spans)
    block_out = jnp.transpose(outs_all, (1, 0, 2, 3)).reshape(N_SECTION, TOKENS, D)
    grad_in = jnp.transpose(grads_in, (1, 0, 2, 3)).reshape(N_SECTION, TOKENS, D)
    return (block_out, grad_in, grads[0], grads[1], grads[2], grads[3], grads[4], grads[5])
```

```python
import jax
import jax.numpy as jnp
from jax import lax
from jax.sharding import PartitionSpec as P

HEADS = 32
KV_HEADS = 8
HEAD = 64
SEQ = 64
EPSILON = 1e-05
ROPE_BASE = 500000.0
BF = jnp.bfloat16
F32 = jnp.float32
CONTRACT_LAST = (((1,), (1,)), ((), ()))
CONTRACT_FIRST = (((0,), (0,)), ((), ()))


def dot(left, right):
    return jnp.dot(left, right, preferred_element_type=F32)


def dot_rows(left, right):
    return lax.dot_general(left, right, CONTRACT_LAST, preferred_element_type=F32)


def dot_tokens(left, right):
    return lax.dot_general(left, right, CONTRACT_FIRST, preferred_element_type=F32)


def rope_tables(seq_pos):
    half_index = jnp.arange(HEAD // 2, dtype=F32)
    frequency = jnp.power(ROPE_BASE, -2.0 * half_index / HEAD)
    angles = seq_pos.astype(F32)[:, None] * frequency[None, :]
    return (jnp.cos(angles)[:, None, :], jnp.sin(angles)[:, None, :])


def rotate(vectors, cosine, sine):
    first_half = vectors[..., : HEAD // 2]
    second_half = vectors[..., HEAD // 2 :]
    return jnp.concatenate(
        [first_half * cosine - second_half * sine, second_half * cosine + first_half * sine], -1
    )


def visible(seq_pos):
    row_index = jnp.arange(SEQ)[None, :, None]
    col_index = jnp.arange(SEQ)[None, None, :]
    return (col_index <= row_index) & (row_index - col_index <= seq_pos[:, :, None])


def rms_parts(values):
    inverse = lax.rsqrt(jnp.mean(values * values, -1, keepdims=True) + EPSILON)
    return (values * inverse, inverse)


def norm_back(grad_normed, normal_rows, inverse, gain_row):
    scaled = grad_normed * gain_row
    gain_term = jnp.sum(grad_normed * normal_rows, 0)
    grad_rows = inverse * (scaled - normal_rows * jnp.mean(scaled * normal_rows, -1, keepdims=True))
    return (grad_rows, gain_term)


def attention_forward(state, tables, allowed, gain, qkv_full, out_full):
    rows = state.shape[0]
    seqs = rows // SEQ
    width = HEADS * HEAD
    kv_cols = KV_HEADS * HEAD
    normal_one, scale_one = rms_parts(state)
    normed = (normal_one * gain).astype(BF)
    projected = dot(normed, qkv_full)
    cosine, sine = tables
    queries = rotate(projected[:, :width].reshape(rows, HEADS, HEAD), cosine, sine).astype(BF)
    keys_in = rotate(
        projected[:, width : width + kv_cols].reshape(rows, KV_HEADS, HEAD), cosine, sine
    ).astype(BF)
    values_in = projected[:, width + kv_cols :].reshape(rows, KV_HEADS, HEAD).astype(BF)
    grouped = queries.reshape(seqs, SEQ, KV_HEADS, HEADS // KV_HEADS, HEAD)
    keys_in = keys_in.reshape(seqs, SEQ, KV_HEADS, HEAD)
    values_in = values_in.reshape(seqs, SEQ, KV_HEADS, HEAD)
    scores = jnp.einsum(
        "sqgrd,skgd->sgrqk", grouped, keys_in, preferred_element_type=F32
    ) * HEAD ** (-0.5)
    masked = jnp.where(allowed[:, None, None], scores, -1e30)
    top_score = jnp.max(masked, -1, keepdims=True)
    expon = jnp.exp(masked - top_score)
    probs = expon / jnp.sum(expon, -1, keepdims=True)
    attended = (
        jnp.einsum("sgrqk,skgd->sqgrd", probs.astype(BF), values_in, preferred_element_type=F32)
        .reshape(rows, width)
        .astype(BF)
    )
    middle = state + dot(attended, out_full)
    return middle, (normal_one, scale_one, normed, grouped, keys_in, values_in, probs, attended)


def attention_backward(grad_out, grouped, keys_in, values_in, probs, tables):
    rows = grad_out.shape[0]
    seqs = rows // SEQ
    scale_factor = HEAD ** (-0.5)
    grad_grouped = grad_out.reshape(seqs, SEQ, KV_HEADS, HEADS // KV_HEADS, HEAD)
    grad_probs = jnp.einsum("sqgrd,skgd->sgrqk", grad_grouped, values_in, preferred_element_type=F32)
    grad_values = jnp.einsum(
        "sgrqk,sqgrd->skgd", probs.astype(BF), grad_grouped, preferred_element_type=F32
    )
    row_dot = jnp.sum(probs * grad_probs, -1, keepdims=True)
    grad_scores = (probs * (grad_probs - row_dot)).astype(BF)
    grad_queries = (
        jnp.einsum("sgrqk,skgd->sqgrd", grad_scores, keys_in, preferred_element_type=F32)
        * scale_factor
    )
    grad_keys = (
        jnp.einsum("sgrqk,sqgrd->skgd", grad_scores, grouped, preferred_element_type=F32)
        * scale_factor
    )
    cosine, sine = tables
    return jnp.concatenate(
        [
            rotate(grad_queries.reshape(rows, HEADS, HEAD), cosine, -sine).reshape(rows, -1),
            rotate(grad_keys.reshape(rows, KV_HEADS, HEAD), cosine, -sine).reshape(rows, -1),
            grad_values.reshape(rows, -1),
        ],
        1,
    ).astype(BF)


def gather_slice(rows):
    return lax.all_gather(rows, "shard", axis=0, tiled=True)


def gather_section(rows):
    return lax.all_gather(rows, ("replica", "shard"), axis=0, tiled=True)


def scatter_slice(partial):
    return lax.psum_scatter(partial, "shard", scatter_dimension=0, tiled=True)


def feed_forward(normed_rows, gate_up_part):
    gate_up = dot(normed_rows, gate_up_part)
    half = gate_up.shape[1] // 2
    gate = gate_up[:, :half]
    hidden = (gate * jax.nn.sigmoid(gate) * gate_up[:, half:]).astype(BF)
    return gate_up, hidden


def feed_backward(upstream, gate_up, down_part):
    half = gate_up.shape[1] // 2
    gate, up = gate_up[:, :half], gate_up[:, half:]
    grad_hidden = dot_rows(upstream, down_part)
    sigmoid = jax.nn.sigmoid(gate)
    grad_gate = grad_hidden * up * sigmoid * (1.0 + gate * (1.0 - sigmoid))
    grad_up = grad_hidden * gate * sigmoid
    return jnp.concatenate([grad_gate, grad_up], 1).astype(BF)


def on_device(
    tokens_in,
    positions,
    attn_gain,
    qkv_weight,
    out_weight,
    mlp_gain,
    gate_up_weight,
    down_weight,
    cotangent,
):
    sections = lax.axis_size("section")
    replicas = lax.axis_size("replica")
    shards = lax.axis_size("shard")
    section_at = lax.axis_index("section")
    replica_at = lax.axis_index("replica")
    shard_at = lax.axis_index("shard")
    is_first = section_at == 0
    is_last = section_at == sections - 1
    rows, width = tokens_in.shape
    seqs = rows // SEQ
    up_steps = [(at, at + 1) for at in range(sections - 1)]
    down_steps = [(at + 1, at) for at in range(sections - 1)]

    tables = rope_tables(positions)
    allowed = visible(positions.reshape(seqs, SEQ))
    gain_one, gain_two = attn_gain[0], mlp_gain[0]

    qkv_full = lax.all_gather(qkv_weight[0], "shard", axis=0, tiled=True)
    out_full = lax.all_gather(out_weight[0], "shard", axis=0, tiled=True)
    gate_up_local = gate_up_weight[0]
    ff = gate_up_local.shape[1] // 2
    ff_part = ff // shards
    gate_up_part = lax.all_to_all(
        gate_up_local.reshape(-1, 2, shards, ff_part), "shard", 2, 0, tiled=True
    ).reshape(width, 2 * ff_part)
    down_part = down_weight[0]

    received = jnp.zeros((rows, width), BF)
    for tick_at in range(sections):
        state = jnp.where(is_first, tokens_in, received).astype(F32)
        middle, kept = attention_forward(state, tables, allowed, gain_one, qkv_full, out_full)
        normal_two, scale_two = rms_parts(middle)
        normed_two = (normal_two * gain_two).astype(BF)
        gate_up, hidden = feed_forward(gather_slice(normed_two), gate_up_part)
        result = middle + scatter_slice(dot(hidden, down_part).astype(BF)).astype(F32)
        block_out = result.astype(BF)
        if tick_at + 1 < sections:
            received = lax.ppermute(block_out, "section", up_steps)
    normal_one, scale_one, normed, grouped, keys_in, values_in, probs, attended = kept

    received_grad = jnp.zeros((rows, width), BF)
    for tick_at in range(sections):
        upstream = jnp.where(is_last, cotangent, received_grad)
        grad_gate_up = feed_backward(gather_slice(upstream), gate_up, down_part)
        grad_normed_two = scatter_slice(dot_rows(grad_gate_up, gate_up_part).astype(BF)).astype(F32)
        grad_rows, gain_term_two = norm_back(grad_normed_two, normal_two, scale_two, gain_two)
        grad_middle = upstream.astype(F32) + grad_rows
        grad_branch = grad_middle.astype(BF)
        grad_attended = dot_rows(grad_branch, out_full).astype(BF)
        grad_projected = attention_backward(
            grad_attended, grouped, keys_in, values_in, probs, tables
        )
        grad_normed = dot_rows(grad_projected, qkv_full)
        grad_rows, gain_term_one = norm_back(grad_normed, normal_one, scale_one, gain_one)
        grad_state = grad_middle + grad_rows
        grad_low = grad_state.astype(BF)
        if tick_at + 1 < sections:
            received_grad = lax.ppermute(grad_low, "section", down_steps)
    grad_in = jnp.where(is_first, grad_state, grad_low.astype(F32))

    both = ("replica", "shard")
    normed_two_all = gather_section(normed_two)
    upstream_all = gather_section(upstream)
    gate_up_all, hidden_all = feed_forward(normed_two_all, gate_up_part)
    grad_gate_up_all = feed_backward(upstream_all, gate_up_all, down_part)

    slice_rows = width // replicas
    left_rows = lax.dynamic_slice_in_dim(normed_two_all, replica_at * slice_rows, slice_rows, 1)
    gate_up_grad = dot_tokens(left_rows, grad_gate_up_all).astype(BF)
    gate_up_grad = lax.all_to_all(
        gate_up_grad.reshape(slice_rows, 2, 1, ff_part), "shard", 0, 2, tiled=True
    ).reshape(slice_rows // shards, 2 * ff).astype(F32)

    ff_rows = ff // (replicas * shards)
    owner = (replica_at * shards) // replicas
    first_col = (replica_at * shards) % replicas * ff_rows
    hidden_rows = lax.dynamic_slice_in_dim(hidden_all, first_col + shard_at * ff_rows, ff_rows, 1)
    for step in range(1, shards):
        target = lax.rem(shard_at + step, shards)
        part = lax.dynamic_slice_in_dim(hidden_all, first_col + target * ff_rows, ff_rows, 1)
        pairs = []
        for at in range(replicas):
            source = at * shards // replicas
            pairs.append((at * shards + source, at * shards + (source + step) % shards))
        sent = lax.ppermute(part, both, pairs)
        hidden_rows = jnp.where(lax.rem(owner + step, shards) == shard_at, sent, hidden_rows)
    down_grad = dot_tokens(hidden_rows, upstream_all)

    attended_rows = lax.all_to_all(attended, both, 1, 0, tiled=True)
    normed_rows = lax.all_to_all(normed, both, 1, 0, tiled=True)
    out_grad = dot_tokens(attended_rows, gather_section(grad_branch))
    qkv_grad = dot_tokens(normed_rows, gather_section(grad_projected))

    gains = jnp.stack([gain_term_one, gain_term_two])
    gains = jnp.sum(lax.all_gather(gains, both, axis=0), 0)
    return (
        block_out[None],
        grad_in[None],
        gains[0][None],
        qkv_grad[None],
        out_grad[None],
        gains[1][None],
        gate_up_grad[None],
        down_grad[None],
    )


def solution(mesh):
    both = ("replica", "shard")
    return jax.shard_map(
        on_device,
        mesh=mesh,
        in_specs=(
            P(both, None),
            P(both),
            P("section", None),
            P("section", "shard", None),
            P("section", "shard", None),
            P("section", None),
            P("section", "shard", None),
            P("section", "shard", None),
            P(both, None),
        ),
        out_specs=(
            P("section", both, None),
            P("section", both, None),
            P("section", None),
            P("section", both, None),
            P("section", both, None),
            P("section", None),
            P("section", both, None),
            P("section", both, None),
        ),
        check_vma=False,
    )
```

```python
import functools

import jax
import jax.numpy as jnp
from jax import lax
from jax.experimental import pallas as pl
from jax.experimental.pallas import tpu as pltpu
from jax.sharding import PartitionSpec as P

HEADS = 32
KV_HEADS = 8
HEAD = 64
SEQ = 64
EPSILON = 1e-05
ROPE_BASE = 500000.0
BF = jnp.bfloat16
F32 = jnp.float32
CONTRACT_LAST = (((1,), (1,)), ((), ()))
CONTRACT_FIRST = (((0,), (0,)), ((), ()))


MESH = pl.DeviceIdType.MESH
VMEM_LIMIT = 60 * 2**20
TILE = 128


def dot(left, right):
    return jnp.dot(left, right, preferred_element_type=F32)


def dot_rows(left, right):
    return lax.dot_general(left, right, CONTRACT_LAST, preferred_element_type=F32)


def dot_tokens(left, right):
    return lax.dot_general(left, right, CONTRACT_FIRST, preferred_element_type=F32)


def rope_tables(seq_pos):
    half_index = jnp.arange(HEAD // 2, dtype=F32)
    frequency = jnp.power(ROPE_BASE, -2.0 * half_index / HEAD)
    angles = seq_pos.astype(F32)[:, None] * frequency[None, :]
    cosine, sine = jnp.cos(angles), jnp.sin(angles)
    return (
        jnp.concatenate([cosine] * 4, 1),
        jnp.concatenate([-sine, sine, -sine, sine], 1),
    )


def visible(seq_pos):
    rows = seq_pos.shape[0]
    row_index = jnp.arange(rows)[:, None]
    col_index = jnp.arange(rows)[None, :]
    same = row_index // SEQ == col_index // SEQ
    seen = (col_index <= row_index) & (row_index - col_index <= seq_pos[:, None])
    return jnp.where(same & seen, 1.0, 0.0).astype(F32)


def lanes(rows):
    return lax.broadcasted_iota(jnp.int32, (rows, TILE), 1)


def swap_halves(tile, lane):
    return jnp.where(lane % HEAD < HEAD // 2, pltpu.roll(tile, TILE - HEAD // 2, 1), pltpu.roll(tile, HEAD // 2, 1))


def spread(tile, odd, lane):
    turned = pltpu.roll(tile, HEAD, 1)
    lower, upper = (turned, tile) if odd else (tile, turned)
    return jnp.concatenate(
        [jnp.where(lane < HEAD, lower, 0.0), jnp.where(lane < HEAD, 0.0, upper)], 0
    ).astype(BF)


def softmax_pair(queries, spread_keys, allowed):
    scores = dot_rows(queries, spread_keys) * HEAD ** (-0.5)
    halves = []
    for side in range(2):
        masked = jnp.where(allowed > 0.5, scores[:, side * TILE : (side + 1) * TILE], -1e30)
        expon = jnp.exp(masked - jnp.max(masked, -1, keepdims=True))
        halves.append(expon / jnp.sum(expon, -1, keepdims=True))
    return halves


def attend_forward(
    tokens_ref, received_ref, gain_one_ref, gain_two_ref, cos_ref, sin_ref, allowed_ref, qkv_hbm, out_hbm,
    middle_ref, normed_two_ref, normed_ref, rotated_ref, attended_ref,
    qkv_ref, out_ref, sems,
):
    rows, width = tokens_ref.shape
    cols = qkv_hbm.shape[1]
    step = 512
    copies = [
        pltpu.make_async_copy(
            qkv_hbm.at[:, pl.ds(at, step)], qkv_ref.at[:, pl.ds(at, step)], sems.at[at // step]
        )
        for at in range(0, cols, step)
    ]
    out_copies = [
        pltpu.make_async_copy(
            out_hbm.at[:, pl.ds(at, step)], out_ref.at[:, pl.ds(at, step)], sems.at[(cols + at) // step]
        )
        for at in range(0, width, step)
    ]
    for copy in copies + out_copies:
        copy.start()
    first = lax.axis_index("section") == 0
    state = jnp.where(first, tokens_ref[...], received_ref[...]).astype(F32)
    inverse = lax.rsqrt(jnp.mean(state * state, -1, keepdims=True) + EPSILON)
    normed_ref[...] = (state * inverse * gain_one_ref[...]).astype(BF)
    lane = lanes(rows)
    cosine, sine, allowed = cos_ref[...], sin_ref[...], allowed_ref[...]
    rope_cols = (HEADS + KV_HEADS) * HEAD
    for at in range(0, cols, step):
        copies[at // step].wait()
        projected = dot(normed_ref[...], qkv_ref[:, at : at + step])
        for tile_at in range(0, step, TILE):
            tile = projected[:, tile_at : tile_at + TILE]
            if at + tile_at < rope_cols:
                tile = tile * cosine + swap_halves(tile, lane) * sine
            rotated_ref[:, at + tile_at : at + tile_at + TILE] = tile.astype(BF)
    for group in range(KV_HEADS):
        key_at = width + group // 2 * TILE
        value_at = rope_cols + group // 2 * TILE
        keys = spread(rotated_ref[:, key_at : key_at + TILE].astype(F32), group % 2, lane)
        values = spread(rotated_ref[:, value_at : value_at + TILE].astype(F32), group % 2, lane)
        for pair in range(2):
            at = (group * 2 + pair) * TILE
            halves = softmax_pair(rotated_ref[:, at : at + TILE], keys, allowed)
            probs = jnp.concatenate([half.astype(BF) for half in halves], 1)
            attended_ref[:, at : at + TILE] = dot(probs, values).astype(BF)
    total = jnp.zeros((rows, 1), F32)
    for at in range(0, width, step):
        out_copies[at // step].wait()
        state = jnp.where(first, tokens_ref[:, at : at + step], received_ref[:, at : at + step]).astype(F32)
        middle = state + dot(attended_ref[...], out_ref[:, at : at + step])
        middle_ref[:, at : at + step] = middle
        total += jnp.sum(middle * middle, -1, keepdims=True)
    inverse = lax.rsqrt(total / width + EPSILON)
    normed_two_ref[...] = (middle_ref[...] * inverse * gain_two_ref[...]).astype(BF)


def attend_backward(
    grad_ref, cotangent_ref, received_ref, middle_ref, tokens_ref, state_ref, rotated_ref,
    gain_one_ref, gain_two_ref, cos_ref, sin_ref, allowed_ref, qkv_hbm, out_hbm,
    grad_state_ref, grad_low_ref, grad_branch_ref, grad_projected_ref, gain_terms_ref,
    qkv_ref, out_ref, grad_out_ref, middle_grad_ref, sems,
):
    rows, width = middle_ref.shape
    cols = qkv_hbm.shape[1]
    step = 512
    steps = width // step
    out_copies = [
        pltpu.make_async_copy(out_hbm.at[pl.ds(at * step, step)], out_ref.at[pl.ds(at * step, step)], sems.at[at])
        for at in range(steps)
    ]
    copies = [
        pltpu.make_async_copy(
            qkv_hbm.at[pl.ds(at * step, step)], qkv_ref.at[pl.ds(at * step, step)], sems.at[steps + at]
        )
        for at in range(steps)
    ]
    for copy in out_copies + copies:
        copy.start()
    first = lax.axis_index("section") == 0
    last = lax.axis_index("section") == lax.axis_size("section") - 1

    def norm_back(grad, values, gain):
        inverse = lax.rsqrt(jnp.mean(values * values, -1, keepdims=True) + EPSILON)
        normal = values * inverse
        term = jnp.sum(grad * normal, 0, keepdims=True)
        scaled = grad * gain
        return inverse * (scaled - normal * jnp.mean(scaled * normal, -1, keepdims=True)), term

    upstream = jnp.where(last, cotangent_ref[...], received_ref[...]).astype(F32)
    back, term = norm_back(grad_ref[...], middle_ref[...], gain_two_ref[...])
    gain_terms_ref[1:2, :] = term
    middle_grad_ref[...] = upstream + back
    grad_branch_ref[...] = middle_grad_ref[...].astype(BF)
    for at in range(steps):
        out_copies[at].wait()
        grad_out_ref[:, at * step : (at + 1) * step] = dot_rows(
            grad_branch_ref[...], out_ref[at * step : (at + 1) * step, :]
        ).astype(BF)
    lane = lanes(rows)
    cosine, sine, allowed = cos_ref[...], sin_ref[...], allowed_ref[...]
    rope_cols = (HEADS + KV_HEADS) * HEAD
    scale = HEAD ** (-0.5)

    def unrotate(tile):
        return tile * cosine - swap_halves(tile, lane) * sine

    for group_pair in range(KV_HEADS // 2):
        key_at = width + group_pair * TILE
        value_at = rope_cols + group_pair * TILE
        sums = []
        for odd in range(2):
            keys = spread(rotated_ref[:, key_at : key_at + TILE].astype(F32), odd, lane)
            values = spread(rotated_ref[:, value_at : value_at + TILE].astype(F32), odd, lane)
            key_sum = jnp.zeros((rows, TILE), F32)
            value_sum = jnp.zeros((rows, TILE), F32)
            for pair in range(2):
                at = ((group_pair * 2 + odd) * 2 + pair) * TILE
                queries = rotated_ref[:, at : at + TILE]
                grad_out = grad_out_ref[:, at : at + TILE]
                halves = softmax_pair(queries, keys, allowed)
                grad_probs = dot_rows(grad_out, values)
                grad_halves = []
                for side in range(2):
                    grad = grad_probs[:, side * TILE : (side + 1) * TILE]
                    row_dot = jnp.sum(halves[side] * grad, -1, keepdims=True)
                    grad_halves.append((halves[side] * (grad - row_dot)).astype(BF))
                grad_scores = jnp.concatenate(grad_halves, 1)
                probs = jnp.concatenate([half.astype(BF) for half in halves], 1)
                grad_projected_ref[:, at : at + TILE] = unrotate(dot(grad_scores, keys) * scale).astype(BF)
                key_terms = dot_tokens(grad_scores, queries)
                value_terms = dot_tokens(probs, grad_out)
                key_sum += jnp.where(lane < HEAD, key_terms[:rows], key_terms[rows:])
                value_sum += jnp.where(lane < HEAD, value_terms[:rows], value_terms[rows:])
            sums.append((key_sum + pltpu.roll(key_sum, HEAD, 1), value_sum + pltpu.roll(value_sum, HEAD, 1)))
        keys_grad = jnp.where(lane < HEAD, sums[0][0], sums[1][0]) * scale
        grad_projected_ref[:, key_at : key_at + TILE] = unrotate(keys_grad).astype(BF)
        grad_projected_ref[:, value_at : value_at + TILE] = jnp.where(
            lane < HEAD, sums[0][1], sums[1][1]
        ).astype(BF)
    for at in range(steps):
        copies[at].wait()
        grad_state_ref[:, at * step : (at + 1) * step] = dot_rows(
            grad_projected_ref[...], qkv_ref[at * step : (at + 1) * step, :]
        )
    state = jnp.where(first, tokens_ref[...], state_ref[...]).astype(F32)
    back, term = norm_back(grad_state_ref[...], state, gain_one_ref[...])
    gain_terms_ref[0:1, :] = term
    grad_state = middle_grad_ref[...] + back
    grad_low = grad_state.astype(BF)
    grad_low_ref[...] = grad_low
    grad_state_ref[...] = jnp.where(first, grad_state, grad_low.astype(F32))


def call_attend_forward(*operands):
    rows, width = operands[0].shape
    cols = operands[7].shape[1]
    specs = [pl.BlockSpec(memory_space=pltpu.VMEM)] * 7 + [pl.BlockSpec(memory_space=pl.ANY)] * 2
    return pl.pallas_call(
        attend_forward,
        out_shape=(
            jax.ShapeDtypeStruct((rows, width), F32),
            jax.ShapeDtypeStruct((rows, width), BF),
            jax.ShapeDtypeStruct((rows, width), BF),
            jax.ShapeDtypeStruct((rows, cols), BF),
            jax.ShapeDtypeStruct((rows, width), BF),
        ),
        in_specs=specs,
        out_specs=[pl.BlockSpec(memory_space=pltpu.VMEM)] * 5,
        scratch_shapes=[
            pltpu.VMEM((width, cols), BF),
            pltpu.VMEM((width, width), BF),
            pltpu.SemaphoreType.DMA(((cols + width) // 512,)),
        ],
        compiler_params=pltpu.CompilerParams(vmem_limit_bytes=VMEM_LIMIT),
        name="attend_forward",
    )(*operands)


def call_attend_backward(*operands):
    rows, width = operands[3].shape
    cols = operands[12].shape[1]
    specs = [pl.BlockSpec(memory_space=pltpu.VMEM)] * 12 + [pl.BlockSpec(memory_space=pl.ANY)] * 2
    return pl.pallas_call(
        attend_backward,
        out_shape=(
            jax.ShapeDtypeStruct((rows, width), F32),
            jax.ShapeDtypeStruct((rows, width), BF),
            jax.ShapeDtypeStruct((rows, width), BF),
            jax.ShapeDtypeStruct((rows, cols), BF),
            jax.ShapeDtypeStruct((2, width), F32),
        ),
        in_specs=specs,
        out_specs=[pl.BlockSpec(memory_space=pltpu.VMEM)] * 5,
        scratch_shapes=[
            pltpu.VMEM((width, cols), BF),
            pltpu.VMEM((width, width), BF),
            pltpu.VMEM((rows, width), BF),
            pltpu.VMEM((rows, width), F32),
            pltpu.SemaphoreType.DMA((2 * width // 512,)),
        ],
        compiler_params=pltpu.CompilerParams(vmem_limit_bytes=VMEM_LIMIT),
        name="attend_backward",
    )(*operands)


CHUNK = 512


def feed_kernel(backward, rows, *refs):
    if backward:
        (cotangent_ref, received_ref, gate_up_ref, first_hbm, second_hbm, result_ref, all_ref, mid_ref,
         first_ref, second_ref, part_ref, take_ref, sent_ref, land_ref, own_ref, own_take_ref,
         load_sems, send_sems, recv_sems) = refs
    else:
        (mine_ref, middle_ref, first_hbm, second_hbm, result_ref, all_ref, gate_up_ref,
         mid_ref, first_ref, second_ref, part_ref, take_ref, sent_ref, land_ref, own_ref, own_take_ref,
         load_sems, send_sems, recv_sems) = refs
    shard = lax.axis_index("shard")
    chip, core = shard // 2, shard % 2
    beside = chip * 2 + (1 - core)
    across = (1 - chip) * 2 + core
    half = rows // 2
    width = all_ref.shape[1]
    ff = second_ref.shape[0] if not backward else first_ref.shape[0]
    first_steps = ff // CHUNK
    second_steps = width // CHUNK

    def load_first(at):
        if backward:
            place = (pl.ds(pl.multiple_of(at * CHUNK, CHUNK), CHUNK), slice(None))
            return [pltpu.make_async_copy(first_hbm.at[place], first_ref.at[place], load_sems.at[0, at])]
        places = [
            (slice(None), pl.ds(pl.multiple_of(side * ff + at * CHUNK, CHUNK), CHUNK)) for side in range(2)
        ]
        return [
            pltpu.make_async_copy(first_hbm.at[place], first_ref.at[place], load_sems.at[side, at])
            for side, place in enumerate(places)
        ]

    def load_second(at):
        span = pl.ds(pl.multiple_of(at * CHUNK, CHUNK), CHUNK)
        place = (span, slice(None)) if backward else (slice(None), span)
        return pltpu.make_async_copy(second_hbm.at[place], second_ref.at[place], load_sems.at[2, at])

    for at in range(first_steps):
        for copy in load_first(at):
            copy.start()
    for at in range(second_steps):
        load_second(at).start()

    def remote(source, target, at, device):
        return pltpu.make_async_remote_copy(
            source, target, send_sems.at[at], recv_sems.at[at], device_id={"shard": device}, device_id_type=MESH
        )

    def owned(owner, offset, count):
        return all_ref.at[pl.ds(pl.multiple_of(owner * rows + offset, half), count)]

    barrier = pltpu.get_barrier_semaphore()
    for device in (beside, across):
        pl.semaphore_signal(barrier, inc=1, device_id={"shard": device}, device_id_type=MESH)
    pl.semaphore_wait(barrier, 2)

    place = pl.ds(pl.multiple_of(shard * rows, rows), rows)
    if backward:
        last = lax.axis_index("section") == lax.axis_size("section") - 1
        all_ref[place, :] = jnp.where(last, cotangent_ref[...], received_ref[...])
    else:
        all_ref[place, :] = mine_ref[...]
    across_copies = [remote(owned(shard, at * half, half), owned(shard, at * half, half), 1 + at, across) for at in range(2)]
    beside_copy = remote(owned(shard, 0, rows), owned(shard, 0, rows), 0, beside)
    relays = [remote(owned(across, at * half, half), owned(across, at * half, half), 3 + at, beside) for at in range(2)]
    for copy in across_copies:
        copy.start()
    beside_copy.start()

    def first_product(block, waits):
        span = pl.ds(pl.multiple_of(block * 2 * rows, 2 * rows), 2 * rows)

        def step(at, carry):
            cols = pl.ds(pl.multiple_of(at * CHUNK, CHUNK), CHUNK)
            high = pl.ds(pl.multiple_of(ff + at * CHUNK, CHUNK), CHUNK)
            if waits:
                for copy in load_first(at):
                    copy.wait()
            if backward:
                grad_hidden = dot_rows(all_ref[span, :], first_ref[cols, :])
                gate = gate_up_ref[span, cols].astype(F32)
                up = gate_up_ref[span, high].astype(F32)
                sigmoid = jax.nn.sigmoid(gate)
                mid_ref[span, cols] = (grad_hidden * up * sigmoid * (1.0 + gate * (1.0 - sigmoid))).astype(BF)
                mid_ref[span, high] = (grad_hidden * gate * sigmoid).astype(BF)
            else:
                gate = dot(all_ref[span, :], first_ref[:, cols])
                up = dot(all_ref[span, :], first_ref[:, high])
                gate_up_ref[span, cols] = gate.astype(BF)
                gate_up_ref[span, high] = up.astype(BF)
                mid_ref[span, cols] = (gate * jax.nn.sigmoid(gate) * up).astype(BF)
            return carry

        lax.fori_loop(0, first_steps, step, 0)

    def second_product(block, at, target_ref):
        span = pl.ds(pl.multiple_of(block * 2 * rows, 2 * rows), 2 * rows)
        cols = pl.ds(pl.multiple_of(at * CHUNK, CHUNK), CHUNK)
        if backward:
            partial = dot_rows(mid_ref[span, :], second_ref[cols, :])
        else:
            partial = dot(mid_ref[span, :], second_ref[:, cols])
        target_ref[at, 0] = partial[:rows].astype(BF)
        target_ref[at, 1] = partial[rows:].astype(BF)

    def give(at):
        return remote(part_ref.at[at, 1 - core], take_ref.at[at], 5 + at, beside)

    def cross(at):
        return remote(sent_ref.at[at], land_ref.at[at], 5 + second_steps + at, across)

    def give_own(at):
        return remote(own_ref.at[at, 1 - core], own_take_ref.at[at], 5 + 2 * second_steps + at, beside)

    def pass_on(at):
        give(at).wait_recv()
        sent_ref[at] = (part_ref[at, core].astype(F32) + take_ref[at].astype(F32)).astype(BF)
        cross(at).start()

    beside_copy.wait_recv()
    first_product(chip, True)
    for at in range(2):
        across_copies[at].wait_recv()
        relays[at].start()
    for at in range(2):
        relays[at].wait_recv()
    first_product(1 - chip, False)

    def other_step(at, carry):
        load_second(at).wait()
        second_product(1 - chip, at, part_ref)
        give(at).start()

        @pl.when(at > 0)
        def _():
            pass_on(at - 1)

        return carry

    lax.fori_loop(0, second_steps, other_step, 0)

    def own_step(at, carry):
        @pl.when(at == 0)
        def _():
            pass_on(second_steps - 1)

        second_product(chip, at, own_ref)
        give_own(at).start()
        return carry

    lax.fori_loop(0, second_steps, own_step, 0)
    for at in range(second_steps):
        give_own(at).wait_recv()
        cross(at).wait_recv()
        cols = slice(at * CHUNK, (at + 1) * CHUNK)
        total = own_ref[at, core].astype(F32) + own_take_ref[at].astype(F32) + land_ref[at].astype(F32)
        if backward:
            result_ref[:, cols] = total
        else:
            result_ref[:, cols] = (middle_ref[:, cols] + total).astype(BF)
    for copy in [beside_copy] + across_copies + relays:
        copy.wait_send()
    for at in range(second_steps):
        give(at).wait_send()
        cross(at).wait_send()
        give_own(at).wait_send()


def call_feed(backward, operands, collective):
    first, second = operands[-2], operands[-1]
    rows, width = operands[0].shape
    shards = lax.axis_size("shard")
    ff = first.shape[0] if backward else second.shape[0]
    every = shards * rows
    steps = width // CHUNK
    out_shape = [
        jax.ShapeDtypeStruct((rows, width), F32 if backward else BF),
        jax.ShapeDtypeStruct((every, width), BF),
        jax.ShapeDtypeStruct((every, 2 * ff), BF),
    ]
    copies = 5 + 3 * steps
    piece = pltpu.VMEM((steps, rows, CHUNK), BF)
    pair = pltpu.VMEM((steps, 2, rows, CHUNK), BF)
    scratch = [pltpu.VMEM(first.shape, BF), pltpu.VMEM(second.shape, BF), pair, piece, piece, piece, pair, piece]
    if not backward:
        scratch.insert(0, pltpu.VMEM((every, ff), BF))
    scratch += [
        pltpu.SemaphoreType.DMA((3, max(ff // CHUNK, steps))),
        pltpu.SemaphoreType.DMA((copies,)),
        pltpu.SemaphoreType.DMA((copies,)),
    ]
    return pl.pallas_call(
        functools.partial(feed_kernel, backward, rows),
        out_shape=out_shape,
        in_specs=[pl.BlockSpec(memory_space=pltpu.VMEM)] * (len(operands) - 2)
        + [pl.BlockSpec(memory_space=pl.ANY)] * 2,
        out_specs=[pl.BlockSpec(memory_space=pltpu.VMEM)] * 3,
        scratch_shapes=scratch,
        compiler_params=pltpu.CompilerParams(
            collective_id=collective, has_side_effects=True, vmem_limit_bytes=VMEM_LIMIT
        ),
        name="feed_backward" if backward else "feed_forward",
    )(*operands)


def gather_section(rows):
    return lax.all_gather(rows, ("replica", "shard"), axis=0, tiled=True)


def on_device(
    tokens_in,
    positions,
    attn_gain,
    qkv_weight,
    out_weight,
    mlp_gain,
    gate_up_weight,
    down_weight,
    cotangent,
):
    sections = lax.axis_size("section")
    replicas = lax.axis_size("replica")
    shards = lax.axis_size("shard")
    replica_at = lax.axis_index("replica")
    shard_at = lax.axis_index("shard")
    rows, width = tokens_in.shape
    up_steps = [(at, at + 1) for at in range(sections - 1)]
    down_steps = [(at + 1, at) for at in range(sections - 1)]

    cosine, sine = rope_tables(positions)
    allowed = visible(positions)

    qkv_full = lax.all_gather(qkv_weight[0], "shard", axis=0, tiled=True)
    out_full = lax.all_gather(out_weight[0], "shard", axis=0, tiled=True)
    gate_up_local = gate_up_weight[0]
    ff = gate_up_local.shape[1] // 2
    ff_part = ff // shards
    gate_up_part = lax.all_to_all(
        gate_up_local.reshape(-1, 2, shards, ff_part), "shard", 2, 0, tiled=True
    ).reshape(width, 2 * ff_part)
    down_part = down_weight[0]

    received = jnp.zeros((rows, width), BF)
    for tick_at in range(sections):
        state = received
        middle, normed_two, normed, rotated, attended = call_attend_forward(
            tokens_in, state, attn_gain, mlp_gain, cosine, sine, allowed, qkv_full, out_full
        )
        block_out, normed_two_slice, gate_up = call_feed(
            False, (normed_two, middle, gate_up_part, down_part), 1
        )
        if tick_at + 1 < sections:
            received = lax.ppermute(block_out, "section", up_steps)

    received_grad = jnp.zeros((rows, width), BF)
    for tick_at in range(sections):
        grad_normed_two, upstream_slice, grad_gate_up = call_feed(
            True, (cotangent, received_grad, gate_up, down_part, gate_up_part), 2
        )
        grad_in, grad_low, grad_branch, grad_projected, gains = call_attend_backward(
            grad_normed_two, cotangent, received_grad, middle, tokens_in, state, rotated,
            attn_gain, mlp_gain, cosine, sine, allowed, qkv_full, out_full,
        )
        upstream = jnp.where(lax.axis_index("section") == sections - 1, cotangent, received_grad)
        if tick_at + 1 < sections:
            received_grad = lax.ppermute(grad_low, "section", down_steps)

    both = ("replica", "shard")
    normed_two_all = gather_section(normed_two)
    upstream_all = gather_section(upstream)
    gate_up_all = dot(normed_two_all, gate_up_part)
    gate_all, up_all = gate_up_all[:, :ff_part], gate_up_all[:, ff_part:]
    sigmoid = jax.nn.sigmoid(gate_all)
    hidden_all = (gate_all * sigmoid * up_all).astype(BF)
    grad_hidden = dot_rows(upstream_all, down_part)
    grad_gate = grad_hidden * up_all * sigmoid * (1.0 + gate_all * (1.0 - sigmoid))
    grad_up = grad_hidden * gate_all * sigmoid
    grad_gate_up_all = jnp.concatenate([grad_gate, grad_up], 1).astype(BF)

    slice_rows = width // replicas
    left_rows = lax.dynamic_slice_in_dim(normed_two_all, replica_at * slice_rows, slice_rows, 1)
    gate_up_grad = dot_tokens(left_rows, grad_gate_up_all).astype(BF)
    gate_up_grad = lax.all_to_all(
        gate_up_grad.reshape(slice_rows, 2, 1, ff_part), "shard", 0, 2, tiled=True
    ).reshape(slice_rows // shards, 2 * ff).astype(F32)

    ff_rows = ff // (replicas * shards)
    owner = (replica_at * shards) // replicas
    first_col = (replica_at * shards) % replicas * ff_rows
    hidden_rows = lax.dynamic_slice_in_dim(hidden_all, first_col + shard_at * ff_rows, ff_rows, 1)
    for step in range(1, shards):
        target = lax.rem(shard_at + step, shards)
        part = lax.dynamic_slice_in_dim(hidden_all, first_col + target * ff_rows, ff_rows, 1)
        pairs = []
        for at in range(replicas):
            source = at * shards // replicas
            pairs.append((at * shards + source, at * shards + (source + step) % shards))
        sent = lax.ppermute(part, both, pairs)
        hidden_rows = jnp.where(lax.rem(owner + step, shards) == shard_at, sent, hidden_rows)
    down_grad = dot_tokens(hidden_rows, upstream_all)

    attended_rows = lax.all_to_all(attended, both, 1, 0, tiled=True)
    normed_rows = lax.all_to_all(normed, both, 1, 0, tiled=True)
    out_grad = dot_tokens(attended_rows, gather_section(grad_branch))
    qkv_grad = dot_tokens(normed_rows, gather_section(grad_projected))

    gains = jnp.sum(lax.all_gather(gains, both, axis=0), 0)
    return (
        block_out[None],
        grad_in[None],
        gains[0][None],
        qkv_grad[None],
        out_grad[None],
        gains[1][None],
        gate_up_grad[None],
        down_grad[None],
    )


def solution(mesh):
    both = ("replica", "shard")
    return jax.shard_map(
        on_device,
        mesh=mesh,
        in_specs=(
            P(both, None),
            P(both),
            P("section", None),
            P("section", "shard", None),
            P("section", "shard", None),
            P("section", None),
            P("section", "shard", None),
            P("section", "shard", None),
            P(both, None),
        ),
        out_specs=(
            P("section", both, None),
            P("section", both, None),
            P("section", None),
            P("section", both, None),
            P("section", both, None),
            P("section", None),
            P("section", both, None),
            P("section", both, None),
        ),
        check_vma=False,
    )
```

```python
import functools

import jax
import jax.numpy as jnp
from jax import lax
from jax.experimental import pallas as pl
from jax.experimental.pallas import tpu as pltpu
from jax.sharding import PartitionSpec as P

HEADS = 32
KV_HEADS = 8
HEAD = 64
SEQ = 64
EPSILON = 1e-05
ROPE_BASE = 500000.0
BF = jnp.bfloat16
F32 = jnp.float32
CONTRACT_LAST = (((1,), (1,)), ((), ()))
CONTRACT_FIRST = (((0,), (0,)), ((), ()))


MESH = pl.DeviceIdType.MESH
VMEM_LIMIT = 60 * 2**20
TILE = 128


def dot(left, right):
    return jnp.dot(left, right, preferred_element_type=F32)


def dot_rows(left, right):
    return lax.dot_general(left, right, CONTRACT_LAST, preferred_element_type=F32)


def dot_tokens(left, right):
    return lax.dot_general(left, right, CONTRACT_FIRST, preferred_element_type=F32)


def rope_tables(seq_pos):
    half_index = jnp.arange(HEAD // 2, dtype=F32)
    frequency = jnp.power(ROPE_BASE, -2.0 * half_index / HEAD)
    angles = seq_pos.astype(F32)[:, None] * frequency[None, :]
    cosine, sine = jnp.cos(angles), jnp.sin(angles)
    return (
        jnp.concatenate([cosine] * 4, 1),
        jnp.concatenate([-sine, sine, -sine, sine], 1),
    )


def visible(seq_pos):
    rows = seq_pos.shape[0]
    row_index = jnp.arange(rows)[:, None]
    col_index = jnp.arange(rows)[None, :]
    same = row_index // SEQ == col_index // SEQ
    seen = (col_index <= row_index) & (row_index - col_index <= seq_pos[:, None])
    return jnp.where(same & seen, 1.0, 0.0).astype(F32)


def lanes(rows):
    return lax.broadcasted_iota(jnp.int32, (rows, TILE), 1)


def swap_halves(tile, lane):
    return jnp.where(lane % HEAD < HEAD // 2, pltpu.roll(tile, TILE - HEAD // 2, 1), pltpu.roll(tile, HEAD // 2, 1))


def spread(tile, odd, lane):
    turned = pltpu.roll(tile, HEAD, 1)
    lower, upper = (turned, tile) if odd else (tile, turned)
    return jnp.concatenate(
        [jnp.where(lane < HEAD, lower, 0.0), jnp.where(lane < HEAD, 0.0, upper)], 0
    ).astype(BF)


def softmax_pair(queries, spread_keys, allowed):
    scores = dot_rows(queries, spread_keys) * HEAD ** (-0.5)
    halves = []
    for side in range(2):
        masked = jnp.where(allowed > 0.5, scores[:, side * TILE : (side + 1) * TILE], -1e30)
        expon = jnp.exp(masked - jnp.max(masked, -1, keepdims=True))
        halves.append(expon / jnp.sum(expon, -1, keepdims=True))
    return halves


def attend_forward(
    state_ref, gain_one_ref, gain_two_ref, cos_ref, sin_ref, allowed_ref, qkv_hbm, out_hbm,
    middle_ref, normed_two_ref, normed_ref, rotated_ref, attended_ref,
    qkv_ref, out_ref, sems,
):
    rows, width = state_ref.shape
    cols = qkv_hbm.shape[1]
    step = 512
    copies = [
        pltpu.make_async_copy(
            qkv_hbm.at[:, pl.ds(at, step)], qkv_ref.at[:, pl.ds(at, step)], sems.at[at // step]
        )
        for at in range(0, cols, step)
    ]
    out_copies = [
        pltpu.make_async_copy(
            out_hbm.at[:, pl.ds(at, step)], out_ref.at[:, pl.ds(at, step)], sems.at[(cols + at) // step]
        )
        for at in range(0, width, step)
    ]
    for copy in copies + out_copies:
        copy.start()
    state = state_ref[...].astype(F32)
    inverse = lax.rsqrt(jnp.mean(state * state, -1, keepdims=True) + EPSILON)
    normed_ref[...] = (state * inverse * gain_one_ref[...]).astype(BF)
    lane = lanes(rows)
    cosine, sine, allowed = cos_ref[...], sin_ref[...], allowed_ref[...]
    rope_cols = (HEADS + KV_HEADS) * HEAD
    for at in range(0, cols, step):
        copies[at // step].wait()
        projected = dot(normed_ref[...], qkv_ref[:, at : at + step])
        for tile_at in range(0, step, TILE):
            tile = projected[:, tile_at : tile_at + TILE]
            if at + tile_at < rope_cols:
                tile = tile * cosine + swap_halves(tile, lane) * sine
            rotated_ref[:, at + tile_at : at + tile_at + TILE] = tile.astype(BF)
    for group in range(KV_HEADS):
        key_at = width + group // 2 * TILE
        value_at = rope_cols + group // 2 * TILE
        keys = spread(rotated_ref[:, key_at : key_at + TILE].astype(F32), group % 2, lane)
        values = spread(rotated_ref[:, value_at : value_at + TILE].astype(F32), group % 2, lane)
        for pair in range(2):
            at = (group * 2 + pair) * TILE
            halves = softmax_pair(rotated_ref[:, at : at + TILE], keys, allowed)
            probs = jnp.concatenate([half.astype(BF) for half in halves], 1)
            attended_ref[:, at : at + TILE] = dot(probs, values).astype(BF)
    total = jnp.zeros((rows, 1), F32)
    for at in range(0, width, step):
        out_copies[at // step].wait()
        middle = state_ref[:, at : at + step].astype(F32) + dot(attended_ref[...], out_ref[:, at : at + step])
        middle_ref[:, at : at + step] = middle
        total += jnp.sum(middle * middle, -1, keepdims=True)
    inverse = lax.rsqrt(total / width + EPSILON)
    normed_two_ref[...] = (middle_ref[...] * inverse * gain_two_ref[...]).astype(BF)


def attend_backward(
    rounds, grad_ref, upstream_ref, middle_ref, state_ref, rotated_ref,
    gain_one_ref, gain_two_ref, cos_ref, sin_ref, allowed_ref, qkv_hbm, out_hbm,
    grad_state_ref, grad_low_ref, grad_branch_ref, grad_projected_ref, gain_terms_ref,
    qkv_ref, out_ref, grad_out_ref, middle_grad_ref, sems,
):
    rows, width = middle_ref.shape
    cols = qkv_hbm.shape[1]
    step = 512
    steps = width // step
    out_copies = [
        pltpu.make_async_copy(out_hbm.at[pl.ds(at * step, step)], out_ref.at[pl.ds(at * step, step)], sems.at[at])
        for at in range(steps)
    ]
    copies = [
        pltpu.make_async_copy(
            qkv_hbm.at[pl.ds(at * step, step)], qkv_ref.at[pl.ds(at * step, step)], sems.at[steps + at]
        )
        for at in range(steps)
    ]
    for copy in out_copies + copies:
        copy.start()

    def norm_back(grad, values, gain):
        inverse = lax.rsqrt(jnp.mean(values * values, -1, keepdims=True) + EPSILON)
        normal = values * inverse
        term = jnp.sum(grad * normal, 0, keepdims=True)
        scaled = grad * gain
        return inverse * (scaled - normal * jnp.mean(scaled * normal, -1, keepdims=True)), term

    upstream = upstream_ref[...].astype(F32)
    back, term = norm_back(grad_ref[...], middle_ref[...], gain_two_ref[...])
    gain_terms_ref[1:2, :] = term
    middle_grad_ref[...] = upstream + back
    grad_branch_ref[...] = middle_grad_ref[...].astype(BF)
    for at in range(steps):
        out_copies[at].wait()
        grad_out_ref[:, at * step : (at + 1) * step] = dot_rows(
            grad_branch_ref[...], out_ref[at * step : (at + 1) * step, :]
        ).astype(BF)
    lane = lanes(rows)
    cosine, sine, allowed = cos_ref[...], sin_ref[...], allowed_ref[...]
    rope_cols = (HEADS + KV_HEADS) * HEAD
    scale = HEAD ** (-0.5)

    def unrotate(tile):
        return tile * cosine - swap_halves(tile, lane) * sine

    for group_pair in range(KV_HEADS // 2):
        key_at = width + group_pair * TILE
        value_at = rope_cols + group_pair * TILE
        sums = []
        for odd in range(2):
            keys = spread(rotated_ref[:, key_at : key_at + TILE].astype(F32), odd, lane)
            values = spread(rotated_ref[:, value_at : value_at + TILE].astype(F32), odd, lane)
            key_sum = jnp.zeros((rows, TILE), F32)
            value_sum = jnp.zeros((rows, TILE), F32)
            for pair in range(2):
                at = ((group_pair * 2 + odd) * 2 + pair) * TILE
                queries = rotated_ref[:, at : at + TILE]
                grad_out = grad_out_ref[:, at : at + TILE]
                halves = softmax_pair(queries, keys, allowed)
                grad_probs = dot_rows(grad_out, values)
                grad_halves = []
                for side in range(2):
                    grad = grad_probs[:, side * TILE : (side + 1) * TILE]
                    row_dot = jnp.sum(halves[side] * grad, -1, keepdims=True)
                    grad_halves.append((halves[side] * (grad - row_dot)).astype(BF))
                grad_scores = jnp.concatenate(grad_halves, 1)
                probs = jnp.concatenate([half.astype(BF) for half in halves], 1)
                grad_projected_ref[:, at : at + TILE] = unrotate(dot(grad_scores, keys) * scale).astype(BF)
                key_terms = dot_tokens(grad_scores, queries)
                value_terms = dot_tokens(probs, grad_out)
                key_sum += jnp.where(lane < HEAD, key_terms[:rows], key_terms[rows:])
                value_sum += jnp.where(lane < HEAD, value_terms[:rows], value_terms[rows:])
            sums.append((key_sum + pltpu.roll(key_sum, HEAD, 1), value_sum + pltpu.roll(value_sum, HEAD, 1)))
        keys_grad = jnp.where(lane < HEAD, sums[0][0], sums[1][0]) * scale
        grad_projected_ref[:, key_at : key_at + TILE] = unrotate(keys_grad).astype(BF)
        grad_projected_ref[:, value_at : value_at + TILE] = jnp.where(
            lane < HEAD, sums[0][1], sums[1][1]
        ).astype(BF)
    for at in range(steps):
        copies[at].wait()
        grad_state_ref[:, at * step : (at + 1) * step] = dot_rows(
            grad_projected_ref[...], qkv_ref[at * step : (at + 1) * step, :]
        )
    state = state_ref[...].astype(F32)
    back, term = norm_back(grad_state_ref[...], state, gain_one_ref[...])
    gain_terms_ref[0:1, :] = term
    grad_state = middle_grad_ref[...] + back
    grad_low = grad_state.astype(BF)
    grad_low_ref[...] = grad_low
    grad_state_ref[...] = grad_low.astype(F32) if rounds else grad_state


def gated(section, body):
    def kernel(*refs):
        @pl.when(lax.axis_index("section") == section)
        def _():
            body(*refs)

    return kernel


def call_attend_forward(section, *operands):
    rows, width = operands[0].shape
    cols = operands[6].shape[1]
    specs = [pl.BlockSpec(memory_space=pltpu.VMEM)] * 6 + [pl.BlockSpec(memory_space=pl.ANY)] * 2
    return pl.pallas_call(
        gated(section, attend_forward),
        out_shape=(
            jax.ShapeDtypeStruct((rows, width), F32),
            jax.ShapeDtypeStruct((rows, width), BF),
            jax.ShapeDtypeStruct((rows, width), BF),
            jax.ShapeDtypeStruct((rows, cols), BF),
            jax.ShapeDtypeStruct((rows, width), BF),
        ),
        in_specs=specs,
        out_specs=[pl.BlockSpec(memory_space=pltpu.VMEM)] * 5,
        scratch_shapes=[
            pltpu.VMEM((width, cols), BF),
            pltpu.VMEM((width, width), BF),
            pltpu.SemaphoreType.DMA(((cols + width) // 512,)),
        ],
        compiler_params=pltpu.CompilerParams(vmem_limit_bytes=VMEM_LIMIT),
        name="attend_forward",
    )(*operands)


def call_attend_backward(section, *operands):
    rows, width = operands[2].shape
    cols = operands[10].shape[1]
    specs = [pl.BlockSpec(memory_space=pltpu.VMEM)] * 10 + [pl.BlockSpec(memory_space=pl.ANY)] * 2
    return pl.pallas_call(
        gated(section, functools.partial(attend_backward, section > 0)),
        out_shape=(
            jax.ShapeDtypeStruct((rows, width), F32),
            jax.ShapeDtypeStruct((rows, width), BF),
            jax.ShapeDtypeStruct((rows, width), BF),
            jax.ShapeDtypeStruct((rows, cols), BF),
            jax.ShapeDtypeStruct((2, width), F32),
        ),
        in_specs=specs,
        out_specs=[pl.BlockSpec(memory_space=pltpu.VMEM)] * 5,
        scratch_shapes=[
            pltpu.VMEM((width, cols), BF),
            pltpu.VMEM((width, width), BF),
            pltpu.VMEM((rows, width), BF),
            pltpu.VMEM((rows, width), F32),
            pltpu.SemaphoreType.DMA((2 * width // 512,)),
        ],
        compiler_params=pltpu.CompilerParams(vmem_limit_bytes=VMEM_LIMIT),
        name="attend_backward",
    )(*operands)


CHUNK = 512


def feed_kernel(backward, rows, *refs):
    if backward:
        (mine_ref, gate_up_ref, first_hbm, second_hbm, result_ref, all_ref, mid_ref,
         first_ref, second_ref, part_ref, take_ref, sent_ref, land_ref, own_ref, own_take_ref,
         load_sems, send_sems, recv_sems) = refs
    else:
        (mine_ref, middle_ref, first_hbm, second_hbm, result_ref, all_ref, gate_up_ref,
         mid_ref, first_ref, second_ref, part_ref, take_ref, sent_ref, land_ref, own_ref, own_take_ref,
         load_sems, send_sems, recv_sems) = refs
    shard = lax.axis_index("shard")
    chip, core = shard // 2, shard % 2
    beside = chip * 2 + (1 - core)
    across = (1 - chip) * 2 + core
    half = rows // 2
    width = all_ref.shape[1]
    ff = second_ref.shape[0] if not backward else first_ref.shape[0]
    first_steps = ff // CHUNK
    second_steps = width // CHUNK

    def load_first(at):
        if backward:
            place = (pl.ds(pl.multiple_of(at * CHUNK, CHUNK), CHUNK), slice(None))
            return [pltpu.make_async_copy(first_hbm.at[place], first_ref.at[place], load_sems.at[0, at])]
        places = [
            (slice(None), pl.ds(pl.multiple_of(side * ff + at * CHUNK, CHUNK), CHUNK)) for side in range(2)
        ]
        return [
            pltpu.make_async_copy(first_hbm.at[place], first_ref.at[place], load_sems.at[side, at])
            for side, place in enumerate(places)
        ]

    def load_second(at):
        span = pl.ds(pl.multiple_of(at * CHUNK, CHUNK), CHUNK)
        place = (span, slice(None)) if backward else (slice(None), span)
        return pltpu.make_async_copy(second_hbm.at[place], second_ref.at[place], load_sems.at[2, at])

    for at in range(first_steps):
        for copy in load_first(at):
            copy.start()
    for at in range(second_steps):
        load_second(at).start()

    def remote(source, target, at, device):
        return pltpu.make_async_remote_copy(
            source, target, send_sems.at[at], recv_sems.at[at], device_id={"shard": device}, device_id_type=MESH
        )

    def owned(owner, offset, count):
        return all_ref.at[pl.ds(pl.multiple_of(owner * rows + offset, half), count)]

    barrier = pltpu.get_barrier_semaphore()
    for device in (beside, across):
        pl.semaphore_signal(barrier, inc=1, device_id={"shard": device}, device_id_type=MESH)
    pl.semaphore_wait(barrier, 2)

    place = pl.ds(pl.multiple_of(shard * rows, rows), rows)
    all_ref[place, :] = mine_ref[...]
    across_copies = [remote(owned(shard, at * half, half), owned(shard, at * half, half), 1 + at, across) for at in range(2)]
    beside_copy = remote(owned(shard, 0, rows), owned(shard, 0, rows), 0, beside)
    relays = [remote(owned(across, at * half, half), owned(across, at * half, half), 3 + at, beside) for at in range(2)]
    for copy in across_copies:
        copy.start()
    beside_copy.start()

    def first_product(block, waits):
        span = pl.ds(pl.multiple_of(block * 2 * rows, 2 * rows), 2 * rows)

        def step(at, carry):
            cols = pl.ds(pl.multiple_of(at * CHUNK, CHUNK), CHUNK)
            high = pl.ds(pl.multiple_of(ff + at * CHUNK, CHUNK), CHUNK)
            if waits:
                for copy in load_first(at):
                    copy.wait()
            if backward:
                grad_hidden = dot_rows(all_ref[span, :], first_ref[cols, :])
                gate = gate_up_ref[span, cols].astype(F32)
                up = gate_up_ref[span, high].astype(F32)
                sigmoid = jax.nn.sigmoid(gate)
                mid_ref[span, cols] = (grad_hidden * up * sigmoid * (1.0 + gate * (1.0 - sigmoid))).astype(BF)
                mid_ref[span, high] = (grad_hidden * gate * sigmoid).astype(BF)
            else:
                gate = dot(all_ref[span, :], first_ref[:, cols])
                up = dot(all_ref[span, :], first_ref[:, high])
                gate_up_ref[span, cols] = gate.astype(BF)
                gate_up_ref[span, high] = up.astype(BF)
                mid_ref[span, cols] = (gate * jax.nn.sigmoid(gate) * up).astype(BF)
            return carry

        lax.fori_loop(0, first_steps, step, 0)

    def second_product(block, at, target_ref):
        span = pl.ds(pl.multiple_of(block * 2 * rows, 2 * rows), 2 * rows)
        cols = pl.ds(pl.multiple_of(at * CHUNK, CHUNK), CHUNK)
        if backward:
            partial = dot_rows(mid_ref[span, :], second_ref[cols, :])
        else:
            partial = dot(mid_ref[span, :], second_ref[:, cols])
        target_ref[at, 0] = partial[:rows].astype(BF)
        target_ref[at, 1] = partial[rows:].astype(BF)

    def give(at):
        return remote(part_ref.at[at, 1 - core], take_ref.at[at], 5 + at, beside)

    def cross(at):
        return remote(sent_ref.at[at], land_ref.at[at], 5 + second_steps + at, across)

    def give_own(at):
        return remote(own_ref.at[at, 1 - core], own_take_ref.at[at], 5 + 2 * second_steps + at, beside)

    def pass_on(at):
        give(at).wait_recv()
        sent_ref[at] = (part_ref[at, core].astype(F32) + take_ref[at].astype(F32)).astype(BF)
        cross(at).start()

    beside_copy.wait_recv()
    first_product(chip, True)
    for at in range(2):
        across_copies[at].wait_recv()
        relays[at].start()
    for at in range(2):
        relays[at].wait_recv()
    first_product(1 - chip, False)

    def other_step(at, carry):
        load_second(at).wait()
        second_product(1 - chip, at, part_ref)
        give(at).start()

        @pl.when(at > 0)
        def _():
            pass_on(at - 1)

        return carry

    lax.fori_loop(0, second_steps, other_step, 0)

    def own_step(at, carry):
        @pl.when(at == 0)
        def _():
            pass_on(second_steps - 1)

        second_product(chip, at, own_ref)
        give_own(at).start()
        return carry

    lax.fori_loop(0, second_steps, own_step, 0)
    for at in range(second_steps):
        give_own(at).wait_recv()
        cross(at).wait_recv()
        cols = slice(at * CHUNK, (at + 1) * CHUNK)
        total = own_ref[at, core].astype(F32) + own_take_ref[at].astype(F32) + land_ref[at].astype(F32)
        if backward:
            result_ref[:, cols] = total
        else:
            result_ref[:, cols] = (middle_ref[:, cols] + total).astype(BF)
    for copy in [beside_copy] + across_copies + relays:
        copy.wait_send()
    for at in range(second_steps):
        give(at).wait_send()
        cross(at).wait_send()
        give_own(at).wait_send()


def call_feed(section, backward, operands, collective):
    first, second = operands[-2], operands[-1]
    rows, width = operands[0].shape
    shards = lax.axis_size("shard")
    ff = first.shape[0] if backward else second.shape[0]
    every = shards * rows
    steps = width // CHUNK
    out_shape = [
        jax.ShapeDtypeStruct((rows, width), F32 if backward else BF),
        jax.ShapeDtypeStruct((every, width), BF),
        jax.ShapeDtypeStruct((every, 2 * ff), BF),
    ]
    copies = 5 + 3 * steps
    piece = pltpu.VMEM((steps, rows, CHUNK), BF)
    pair = pltpu.VMEM((steps, 2, rows, CHUNK), BF)
    scratch = [pltpu.VMEM(first.shape, BF), pltpu.VMEM(second.shape, BF), pair, piece, piece, piece, pair, piece]
    if not backward:
        scratch.insert(0, pltpu.VMEM((every, ff), BF))
    scratch += [
        pltpu.SemaphoreType.DMA((3, max(ff // CHUNK, steps))),
        pltpu.SemaphoreType.DMA((copies,)),
        pltpu.SemaphoreType.DMA((copies,)),
    ]
    return pl.pallas_call(
        gated(section, functools.partial(feed_kernel, backward, rows)),
        out_shape=out_shape,
        in_specs=[pl.BlockSpec(memory_space=pltpu.VMEM)] * (len(operands) - 2)
        + [pl.BlockSpec(memory_space=pl.ANY)] * 2,
        out_specs=[pl.BlockSpec(memory_space=pltpu.VMEM)] * 3,
        scratch_shapes=scratch,
        compiler_params=pltpu.CompilerParams(
            collective_id=collective, has_side_effects=True, vmem_limit_bytes=VMEM_LIMIT
        ),
        name="feed_backward" if backward else "feed_forward",
    )(*operands)


def weights_kernel(
    qkv_ref, out_ref, gate_up_ref, qkv_full, out_full, gate_up_part, qkv_hold, out_hold, gate_up_hold, local_sems, send_sems,
    recv_sems,
):
    shard, replica = lax.axis_index("shard"), lax.axis_index("replica")
    chip, core = shard // 2, shard % 2
    beside = {"shard": chip * 2 + (1 - core)}
    across = {"shard": (1 - chip) * 2 + core}
    diagonal = {"shard": (1 - chip) * 2 + (1 - core)}
    mine = replica % 2
    partner = {"replica": replica + 1 - 2 * mine}
    rows = qkv_ref.shape[0]
    half = rows // 2
    ff = gate_up_ref.shape[1] // 2
    part = gate_up_part.shape[1] // 2

    def remote(source, target, at, device):
        return pltpu.make_async_remote_copy(
            source, target, send_sems.at[at], recv_sems.at[at], device_id=device, device_id_type=MESH
        )

    def span(start, count):
        return pl.ds(pl.multiple_of(start, count), count)

    sides = [pl.ds(side * part, part) for side in range(2)]
    loads = [
        pltpu.make_async_copy(qkv_ref, qkv_hold, local_sems.at[0]),
        pltpu.make_async_copy(out_ref, out_hold, local_sems.at[1]),
    ] + [
        pltpu.make_async_copy(
            gate_up_ref.at[:, span(side * ff + shard * part, part)], gate_up_hold.at[side], local_sems.at[2 + side]
        )
        for side in range(2)
    ]
    own_rows = span(shard * rows, rows)
    stores = [
        pltpu.make_async_copy(qkv_hold, qkv_full.at[own_rows], local_sems.at[4]),
        pltpu.make_async_copy(out_hold, out_full.at[own_rows], local_sems.at[5]),
    ] + [
        pltpu.make_async_copy(gate_up_hold.at[side], gate_up_part.at[own_rows, sides[side]], local_sems.at[6 + side])
        for side in range(2)
    ]
    for copy in loads:
        copy.start()

    pieces = []
    for source, whole, count in ((qkv_ref, qkv_full, 64), (out_ref, out_full, 128)):
        for offset in range(0, half, count):

            def place(owner, part_of, whole=whole, offset=offset, count=count):
                return whole.at[span(owner["shard"] * rows + part_of * half + offset, count)]

            own = source.at[span(mine * half + offset, count)]
            pieces.append((own, place, across, True))
    for offset in range(0, half, 128):
        for side in range(2):
            for device in (across, diagonal):

                def place(owner, part_of, offset=offset, side=side):
                    return gate_up_part.at[
                        span(owner["shard"] * rows + part_of * half + offset, 128), pl.ds(side * part, part)
                    ]

                own = gate_up_ref.at[
                    span(mine * half + offset, 128), span(side * ff + device["shard"] * part, part)
                ]
                pieces.append((own, place, device, False))
    count = len(pieces)
    me = {"shard": shard}
    over = [remote(own, place(me, mine), at, device) for at, (own, place, device, _) in enumerate(pieces)]
    passed = [
        remote(place(device, mine), place(device, mine), count + at, partner)
        for at, (_, place, device, _) in enumerate(pieces)
    ]
    relays = [
        [
            remote(place(across, which), place(across, which), (2 + turn) * count + at, beside)
            if relayed
            else None
            for at, (_, place, _, relayed) in enumerate(pieces)
        ]
        for turn, which in enumerate((mine, 1 - mine))
    ]
    direct = [
        remote(qkv_ref, qkv_full.at[span(shard * rows, rows)], 4 * count, beside),
        remote(out_ref, out_full.at[span(shard * rows, rows)], 4 * count + 1, beside),
    ]
    for side in range(2):
        direct.append(
            remote(
                gate_up_ref.at[:, span(side * ff + beside["shard"] * part, part)],
                gate_up_part.at[span(shard * rows, rows), pl.ds(side * part, part)],
                4 * count + 2 + side,
                beside,
            )
        )

    barrier = pltpu.get_barrier_semaphore()
    for device in (beside, across, diagonal, partner):
        pl.semaphore_signal(barrier, inc=1, device_id=device, device_id_type=MESH)
    pl.semaphore_wait(barrier, 4)

    started = []

    def start(copy):
        copy.start()
        started.append(copy)

    ahead = 3
    for copy in over[:ahead]:
        start(copy)
    for copy in direct:
        start(copy)
    for load, store in zip(loads, stores):
        load.wait()
        store.start()
    for at in range(count + 1):
        if at < count:
            over[at].wait_recv()
            start(passed[at])
            if relays[0][at] is not None:
                start(relays[0][at])
            if at + ahead < count:
                over[at].wait_send()
                started[:] = [copy for copy in started if copy is not over[at]]
                start(over[at + ahead])
        if at > 0:
            passed[at - 1].wait_recv()
            if relays[1][at - 1] is not None:
                start(relays[1][at - 1])
    for copies in relays:
        for copy in copies:
            if copy is not None:
                copy.wait_recv()
    for copy in direct:
        copy.wait_recv()
    for copy in stores:
        copy.wait()
    for copy in started:
        copy.wait_send()


def call_weights(qkv_weight, out_weight, gate_up_weight, collective):
    shards = lax.axis_size("shard")
    rows = qkv_weight.shape[0]
    count = 4 + 2 + 8
    anywhere = pl.BlockSpec(memory_space=pl.ANY)
    return pl.pallas_call(
        weights_kernel,
        out_shape=[
            jax.ShapeDtypeStruct((shards * rows, qkv_weight.shape[1]), BF),
            jax.ShapeDtypeStruct((shards * rows, out_weight.shape[1]), BF),
            jax.ShapeDtypeStruct((shards * rows, gate_up_weight.shape[1] // shards), BF),
        ],
        in_specs=[anywhere] * 3,
        out_specs=[anywhere] * 3,
        scratch_shapes=[
            pltpu.VMEM(qkv_weight.shape, BF),
            pltpu.VMEM(out_weight.shape, BF),
            pltpu.VMEM((2, rows, gate_up_weight.shape[1] // (2 * shards)), BF),
            pltpu.SemaphoreType.DMA((8,)),
            pltpu.SemaphoreType.DMA((4 * count + 4,)),
            pltpu.SemaphoreType.DMA((4 * count + 4,)),
        ],
        compiler_params=pltpu.CompilerParams(
            collective_id=collective, has_side_effects=True, vmem_limit_bytes=VMEM_LIMIT
        ),
        name="weights",
    )(qkv_weight, out_weight, gate_up_weight)


def slice_peers():
    shard = lax.axis_index("shard")
    chip, core = shard // 2, shard % 2
    return shard, chip * 2 + (1 - core), (1 - chip) * 2 + core, (1 - chip) * 2 + (1 - core)


def slice_barrier(devices, replicas=1):
    barrier = pltpu.get_barrier_semaphore()
    for device in devices:
        pl.semaphore_signal(barrier, inc=1, device_id={"shard": device}, device_id_type=MESH)
    for turn in range(1, replicas):
        target = lax.rem(lax.axis_index("replica") + turn, replicas)
        pl.semaphore_signal(barrier, inc=1, device_id={"replica": target}, device_id_type=MESH)
    pl.semaphore_wait(barrier, len(devices) + replicas - 1)


def replica_copy(source, target, turn, send_sems, recv_sems, base):
    replicas = lax.axis_size("replica")
    device = lax.rem(lax.axis_index("replica") + replicas - turn, replicas)
    return pltpu.make_async_remote_copy(
        source, target, send_sems.at[base + turn], recv_sems.at[base + turn],
        device_id={"replica": device}, device_id_type=MESH,
    )


def attend_grads_kernel(
    projected_ref, branch_ref, left_qkv_ref, left_out_ref, upstream_ref, qkv_part_ref, out_part_ref, others_hbm,
    all_ref, send_sems, recv_sems,
):
    shard, beside, across, _ = slice_peers()
    replica, replicas = lax.axis_index("replica"), lax.axis_size("replica")
    rows, cols = projected_ref.shape
    pieces = all_ref.shape[0]
    step = all_ref.shape[2]
    slice_barrier((beside, across), replicas)
    spread_copies = [
        replica_copy(upstream_ref, others_hbm.at[replica], turn, send_sems, recv_sems, 3 * pieces)
        for turn in range(1, replicas)
    ]

    def remote(owner, piece, at, device):
        place = all_ref.at[piece, pl.ds(pl.multiple_of(owner * rows, rows), rows)]
        return pltpu.make_async_remote_copy(
            place, place, send_sems.at[at], recv_sems.at[at], device_id={"shard": device}, device_id_type=MESH
        )

    own = pl.ds(pl.multiple_of(shard * rows, rows), rows)
    over = [remote(shard, piece, piece, across) for piece in range(pieces)]
    direct = [remote(shard, piece, pieces + piece, beside) for piece in range(pieces)]
    relays = [remote(across, piece, 2 * pieces + piece, beside) for piece in range(pieces)]
    for piece in range(pieces):
        at = piece * step
        all_ref[piece, own, :] = (
            projected_ref[:, at : at + step] if at < cols else branch_ref[:, at - cols : at - cols + step]
        )
        over[piece].start()
        direct[piece].start()
    for copy in spread_copies:
        copy.start()
    for piece in range(pieces):
        over[piece].wait_recv()
        relays[piece].start()
    for piece in range(pieces):
        direct[piece].wait_recv()
        relays[piece].wait_recv()
        at = piece * step
        if at < cols:
            qkv_part_ref[:, at : at + step] = dot(left_qkv_ref[...], all_ref[piece]).astype(BF)
        else:
            out_part_ref[:, at - cols : at - cols + step] = dot(left_out_ref[...], all_ref[piece]).astype(BF)
    for copy in over + direct + relays:
        copy.wait_send()
    for copy in spread_copies:
        copy.wait()


def call_attend_grads(projected, branch, left_qkv, left_out, upstream, collective):
    replicas = lax.axis_size("replica")
    rows, cols = projected.shape
    width = branch.shape[1]
    every, tokens = left_qkv.shape
    pieces = (cols + width) // CHUNK
    return pl.pallas_call(
        attend_grads_kernel,
        out_shape=[
            jax.ShapeDtypeStruct((every, cols), BF),
            jax.ShapeDtypeStruct((every, width), BF),
            jax.ShapeDtypeStruct((replicas,) + upstream.shape, BF),
        ],
        in_specs=[pl.BlockSpec(memory_space=pltpu.VMEM)] * 5,
        out_specs=[pl.BlockSpec(memory_space=pltpu.VMEM)] * 2 + [pl.BlockSpec(memory_space=pl.ANY)],
        scratch_shapes=[
            pltpu.VMEM((pieces, tokens, CHUNK), BF),
            pltpu.SemaphoreType.DMA((3 * pieces + replicas,)),
            pltpu.SemaphoreType.DMA((3 * pieces + replicas,)),
        ],
        compiler_params=pltpu.CompilerParams(
            collective_id=collective, has_side_effects=True, vmem_limit_bytes=VMEM_LIMIT
        ),
        name="attend_grads",
    )(projected, branch, left_qkv, left_out, upstream)


def feed_grads_kernel(
    upstream_ref, left_ref, hidden_ref, others_hbm, gate_up_hbm, down_hbm,
    gate_up_grad_ref, down_grad_ref, gathered_hbm,
    down_ref, block_ref, gate_up_ref, mid_ref, sum_ref, stage_ref,
    load_sems, block_sems, send_sems, recv_sems,
):
    shard, beside, across, diagonal = slice_peers()
    replica, replicas = lax.axis_index("replica"), lax.axis_size("replica")
    rows = others_hbm.shape[1]
    every, width = upstream_ref.shape
    part = down_ref.shape[0]
    ff = gate_up_grad_ref.shape[1] // 2
    steps = part // CHUNK
    wide = width // CHUNK
    out_rows = gate_up_grad_ref.shape[0]

    load_down = pltpu.make_async_copy(down_hbm, down_ref, load_sems.at[0])
    load_down.start()

    def block_at(turn):
        return lax.rem(replica + turn, replicas)

    def load_gate_up(turn):
        source = gate_up_hbm.at[pl.ds(pl.multiple_of(block_at(turn) * every, every), every)]
        return pltpu.make_async_copy(source, gate_up_ref.at[turn % 2], block_sems.at[0, turn % 2])

    def load_block(turn):
        return pltpu.make_async_copy(gathered_hbm.at[turn], block_ref.at[turn % 2], block_sems.at[1, turn % 2])

    load_gate_up(0).start()

    def remote(source, target, at, device):
        return pltpu.make_async_remote_copy(
            source, target, send_sems.at[at], recv_sems.at[at], device_id={"shard": device}, device_id_type=MESH
        )

    def landing(turn, owner):
        return gathered_hbm.at[turn, pl.ds(pl.multiple_of(owner * rows, rows), rows)]

    def over(turn):
        return remote(others_hbm.at[block_at(turn)], landing(turn, shard), 3 * turn, across)

    def direct(turn):
        return remote(others_hbm.at[block_at(turn)], landing(turn, shard), 3 * turn + 1, beside)

    def relay(turn):
        return remote(landing(turn, across), landing(turn, across), 3 * turn + 2, beside)

    def keep(turn):
        return pltpu.make_async_copy(others_hbm.at[block_at(turn)], landing(turn, shard), load_sems.at[turn])

    slice_barrier((beside, across, diagonal))
    for turn in range(1, replicas):
        keep(turn).start()
    for turn in range(1, min(3, replicas)):
        over(turn).start()
        direct(turn).start()
    sum_ref[...] = jnp.zeros_like(sum_ref)
    down_grad_ref[...] = jnp.zeros_like(down_grad_ref)
    load_down.wait()

    def send_grad(at, peer, device):
        cols = pl.ds(pl.multiple_of(at * CHUNK, CHUNK), CHUNK)
        side, offset = at // steps, at % steps
        target = pl.ds(pl.multiple_of(side * ff + shard * part + offset * CHUNK, CHUNK), CHUNK)
        return remote(
            stage_ref.at[pl.ds(pl.multiple_of(device * out_rows, out_rows), out_rows), cols],
            gate_up_grad_ref.at[:, target],
            3 * replicas + peer * 2 * steps + at,
            device,
        )

    def work(turn, grad_rows):
        slot = turn % 2
        load_gate_up(turn).wait()
        tokens = pl.ds(pl.multiple_of(block_at(turn) * every, every), every)

        def products(at, carry):
            cols = pl.ds(pl.multiple_of(at * CHUNK, CHUNK), CHUNK)
            high = pl.ds(pl.multiple_of(part + at * CHUNK, CHUNK), CHUNK)
            grad_hidden = dot_rows(grad_rows[...], down_ref[cols, :])
            gate = gate_up_ref[slot, :, cols].astype(F32)
            up = gate_up_ref[slot, :, high].astype(F32)
            sigmoid = jax.nn.sigmoid(gate)
            mid_ref[:, cols] = (grad_hidden * up * sigmoid * (1.0 + gate * (1.0 - sigmoid))).astype(BF)
            mid_ref[:, high] = (grad_hidden * gate * sigmoid).astype(BF)
            return carry

        lax.fori_loop(0, steps, products, 0)

        def sums(at, carry):
            cols = pl.ds(pl.multiple_of(at * CHUNK, CHUNK), CHUNK)
            total = sum_ref[:, cols] + dot(left_ref[:, tokens], mid_ref[:, cols])
            if turn < replicas - 1:
                sum_ref[:, cols] = total
            else:
                stage_ref[:, cols] = total.astype(BF)
                for peer, device in enumerate((across, diagonal, beside)):
                    send_grad(at, peer, device).start()
            return carry

        lax.fori_loop(0, 2 * steps, sums, 0)

        def down_sums(at, carry):
            cols = pl.ds(pl.multiple_of(at * CHUNK, CHUNK), CHUNK)
            down_grad_ref[:, cols] += dot(hidden_ref[:, tokens], grad_rows[:, cols])
            return carry

        lax.fori_loop(0, wide, down_sums, 0)

    for turn in range(replicas):
        if turn + 1 < replicas:
            load_gate_up(turn + 1).start()
        if turn == 0:
            work(0, upstream_ref)
        else:
            work(turn, block_ref.at[turn % 2])
        after = turn + 1
        if after < replicas:
            over(after).wait_recv()
            relay(after).start()
            direct(after).wait_recv()
            keep(after).wait()
            relay(after).wait_recv()
            load_block(after).start()
            if after + 2 < replicas:
                over(after).wait_send()
                direct(after).wait_send()
                over(after + 2).start()
                direct(after + 2).start()
            load_block(after).wait()
    own = pl.ds(pl.multiple_of(shard * out_rows, out_rows), out_rows)

    def store_own(at, carry):
        cols = pl.ds(pl.multiple_of(at * CHUNK, CHUNK), CHUNK)
        target = pl.ds(
            pl.multiple_of((at // steps) * ff + shard * part + (at % steps) * CHUNK, CHUNK), CHUNK
        )
        gate_up_grad_ref[:, target] = stage_ref[own, cols]
        return carry

    lax.fori_loop(0, 2 * steps, store_own, 0)

    def finish(at, carry):
        for peer, device in enumerate((across, diagonal, beside)):
            send_grad(at, peer, device).wait_recv()
            send_grad(at, peer, device).wait_send()
        return carry

    lax.fori_loop(0, 2 * steps, finish, 0)
    for turn in range(1, replicas):
        relay(turn).wait_send()
        if turn + 2 >= replicas:
            over(turn).wait_send()
            direct(turn).wait_send()


def call_feed_grads(upstream, left, hidden, others, gate_up, down, collective):
    every, width = upstream.shape
    replicas, rows, _ = others.shape
    shards = lax.axis_size("shard")
    part = down.shape[0]
    out_rows = left.shape[0] // shards
    vmem, anywhere = pl.BlockSpec(memory_space=pltpu.VMEM), pl.BlockSpec(memory_space=pl.ANY)
    copies = 3 * replicas + 3 * 2 * (part // CHUNK)
    return pl.pallas_call(
        feed_grads_kernel,
        out_shape=[
            jax.ShapeDtypeStruct((out_rows, 2 * part * shards), BF),
            jax.ShapeDtypeStruct((hidden.shape[0], width), F32),
            jax.ShapeDtypeStruct((replicas, every, width), BF),
        ],
        in_specs=[vmem] * 3 + [anywhere] * 3,
        out_specs=[vmem, vmem, anywhere],
        scratch_shapes=[
            pltpu.VMEM(down.shape, BF),
            pltpu.VMEM((2, every, width), BF),
            pltpu.VMEM((2, every, 2 * part), BF),
            pltpu.VMEM((every, 2 * part), BF),
            pltpu.VMEM((left.shape[0], 2 * part), F32),
            pltpu.VMEM((left.shape[0], 2 * part), BF),
            pltpu.SemaphoreType.DMA((max(replicas, 2),)),
            pltpu.SemaphoreType.DMA((2, 2)),
            pltpu.SemaphoreType.DMA((copies,)),
            pltpu.SemaphoreType.DMA((copies,)),
        ],
        compiler_params=pltpu.CompilerParams(
            collective_id=collective, has_side_effects=True, vmem_limit_bytes=VMEM_LIMIT
        ),
        name="feed_grads",
    )(upstream, left, hidden, others, gate_up, down)


def prepare_kernel(
    normed_two_ref, lefts_ref, gate_up_hbm, gathered_hbm, gate_up_all_hbm, hidden_hbm, left_hbm,
    weight_ref, block_ref, gate_up_ref, hidden_ref,
    load_sems, store_sems, keep_sems, send_sems, recv_sems,
):
    shard, beside, across, diagonal = slice_peers()
    peers = (across, diagonal, beside)
    replica, replicas = lax.axis_index("replica"), lax.axis_size("replica")
    shards = lax.axis_size("shard")
    rows, width = normed_two_ref.shape
    every = rows * shards
    part = hidden_ref.shape[2]
    ff_rows = hidden_hbm.shape[1]
    steps = part // CHUNK
    kinds, groups, _, _, sub_rows = lefts_ref.shape
    owner = (replica * shards) // replicas
    first_col = lax.rem(replica * shards, replicas) * ff_rows

    def load_weight(side, at):
        place = (slice(None), pl.ds(pl.multiple_of(side * part + at * CHUNK, CHUNK), CHUNK))
        return pltpu.make_async_copy(gate_up_hbm.at[place], weight_ref.at[place], load_sems.at[side, at])

    for at in range(steps):
        for side in range(2):
            load_weight(side, at).start()

    def remote(source, target, at, device):
        return pltpu.make_async_remote_copy(
            source, target, send_sems.at[at], recv_sems.at[at], device_id={"shard": device}, device_id_type=MESH
        )

    def block_at(turn):
        return lax.rem(replica + turn, replicas)

    def landing(turn, who):
        return gathered_hbm.at[block_at(turn), pl.ds(pl.multiple_of(who * rows, rows), rows)]

    def over(turn):
        return remote(landing(turn, shard) if turn else normed_two_ref, landing(turn, shard), 3 * turn, across)

    def direct(turn):
        return remote(landing(turn, shard) if turn else normed_two_ref, landing(turn, shard), 3 * turn + 1, beside)

    def relay(turn):
        return remote(landing(turn, across), landing(turn, across), 3 * turn + 2, beside)

    def from_replica(turn):
        return replica_copy(normed_two_ref, landing(0, shard), turn, send_sems, recv_sems, 3 * replicas)

    def tokens(turn):
        return pl.ds(pl.multiple_of(block_at(turn) * every, every), every)

    def load_block(turn):
        return pltpu.make_async_copy(gathered_hbm.at[block_at(turn)], block_ref.at[turn % 2], store_sems.at[0, turn % 2])

    def store_block(turn):
        return pltpu.make_async_copy(gate_up_ref.at[turn % 2], gate_up_all_hbm.at[tokens(turn)], store_sems.at[1, turn % 2])

    def hidden_cols(turn, device):
        return hidden_ref.at[turn % 2, :, pl.ds(pl.multiple_of(first_col + device * ff_rows, ff_rows), ff_rows)]

    def hand_hidden(turn, peer):
        device = peers[peer]
        return remote(hidden_cols(turn, device), hidden_hbm.at[tokens(turn)], 4 * replicas + 3 * turn + peer, device)

    def keep_hidden(turn):
        return pltpu.make_async_copy(hidden_cols(turn, shard), hidden_hbm.at[tokens(turn)], store_sems.at[2, turn % 2])

    own_rows = pl.ds(pl.multiple_of(shard * rows, rows), rows)

    def hand_left(kind, group, peer):
        device = peers[peer]
        return remote(
            lefts_ref.at[kind, group, device],
            left_hbm.at[kind, group, own_rows],
            7 * replicas + (kind * groups + group) * 3 + peer,
            device,
        )

    def keep_left(kind, group):
        return pltpu.make_async_copy(
            lefts_ref.at[kind, group, shard], left_hbm.at[kind, group, own_rows], keep_sems.at[1 + kind * groups + group]
        )

    keep_own = pltpu.make_async_copy(normed_two_ref, landing(0, shard), keep_sems.at[0])
    slice_barrier(peers, replicas)
    over(0).start()
    direct(0).start()
    for turn in range(1, replicas):
        from_replica(turn).start()
    keep_own.start()
    for kind in range(kinds):
        for group in range(groups):
            keep_left(kind, group).start()
            for peer in range(3):
                hand_left(kind, group, peer).start()

    for turn in range(replicas):
        over(turn).wait_recv()
        relay(turn).start()
        if turn + 1 < replicas:
            from_replica(turn + 1).wait_recv()
            over(turn + 1).start()
            direct(turn + 1).start()
        direct(turn).wait_recv()
        if turn == 0:
            keep_own.wait()
        relay(turn).wait_recv()
        load_block(turn).start()
        load_block(turn).wait()
        if turn > 1:
            store_block(turn - 2).wait()

            @pl.when(shard == owner)
            def _(turn=turn):
                keep_hidden(turn - 2).wait()
                for peer in range(3):
                    hand_hidden(turn - 2, peer).wait_send()

        def products(at, carry, turn=turn):
            slot = turn % 2
            cols = pl.ds(pl.multiple_of(at * CHUNK, CHUNK), CHUNK)
            high = pl.ds(pl.multiple_of(part + at * CHUNK, CHUNK), CHUNK)
            if turn == 0:
                load_weight(0, at).wait()
                load_weight(1, at).wait()
            gate = dot(block_ref[slot], weight_ref[:, cols])
            up = dot(block_ref[slot], weight_ref[:, high])
            gate_up_ref[slot, :, cols] = gate.astype(BF)
            gate_up_ref[slot, :, high] = up.astype(BF)
            hidden_ref[slot, :, cols] = (gate * jax.nn.sigmoid(gate) * up).astype(BF)
            return carry

        lax.fori_loop(0, steps, products, 0)
        store_block(turn).start()

        @pl.when(shard == owner)
        def _(turn=turn):
            keep_hidden(turn).start()
            for peer in range(3):
                hand_hidden(turn, peer).start()

    for turn in range(max(0, replicas - 2), replicas):
        store_block(turn).wait()

        @pl.when(shard == owner)
        def _(turn=turn):
            keep_hidden(turn).wait()
            for peer in range(3):
                hand_hidden(turn, peer).wait_send()

    for turn in range(replicas):
        for peer in range(3):

            @pl.when(peers[peer] == owner)
            def _(turn=turn, peer=peer):
                hand_hidden(turn, peer).wait_recv()

        over(turn).wait_send()
        direct(turn).wait_send()
        relay(turn).wait_send()
        if turn:
            from_replica(turn).wait_send()
    for kind in range(kinds):
        for group in range(groups):
            keep_left(kind, group).wait()
            for peer in range(3):
                hand_left(kind, group, peer).wait()


def call_prepare(normed_two, normed, attended, gate_up_part, collective):
    rows, width = normed_two.shape
    shards, replicas = lax.axis_size("shard"), lax.axis_size("replica")
    part = gate_up_part.shape[1] // 2
    every = rows * shards
    sub_rows = width // (replicas * shards)
    ff_rows = part // replicas
    lefts = jnp.stack([normed, attended]).reshape(2, rows, replicas, shards, sub_rows).transpose(0, 2, 3, 1, 4)
    vmem, anywhere = pl.BlockSpec(memory_space=pltpu.VMEM), pl.BlockSpec(memory_space=pl.ANY)
    copies = 7 * replicas + 2 * replicas * 3
    return pl.pallas_call(
        prepare_kernel,
        out_shape=[
            jax.ShapeDtypeStruct((replicas, every, width), BF),
            jax.ShapeDtypeStruct((replicas * every, 2 * part), BF),
            jax.ShapeDtypeStruct((replicas * every, ff_rows), BF),
            jax.ShapeDtypeStruct((2, replicas, every, sub_rows), BF),
        ],
        in_specs=[vmem, vmem, anywhere],
        out_specs=[anywhere] * 4,
        scratch_shapes=[
            pltpu.VMEM(gate_up_part.shape, BF),
            pltpu.VMEM((2, every, width), BF),
            pltpu.VMEM((2, every, 2 * part), BF),
            pltpu.VMEM((2, every, part), BF),
            pltpu.SemaphoreType.DMA((2, part // CHUNK)),
            pltpu.SemaphoreType.DMA((3, 2)),
            pltpu.SemaphoreType.DMA((1 + 2 * replicas,)),
            pltpu.SemaphoreType.DMA((copies,)),
            pltpu.SemaphoreType.DMA((copies,)),
        ],
        compiler_params=pltpu.CompilerParams(
            collective_id=collective, has_side_effects=True, vmem_limit_bytes=VMEM_LIMIT
        ),
        name="prepare",
    )(normed_two, lefts, gate_up_part)


def on_device(
    tokens_in,
    positions,
    attn_gain,
    qkv_weight,
    out_weight,
    mlp_gain,
    gate_up_weight,
    down_weight,
    cotangent,
):
    sections = lax.axis_size("section")
    replicas = lax.axis_size("replica")
    shards = lax.axis_size("shard")
    replica_at = lax.axis_index("replica")
    rows, width = tokens_in.shape
    up_steps = [(at, at + 1) for at in range(sections - 1)]
    down_steps = [(at + 1, at) for at in range(sections - 1)]

    cosine, sine = rope_tables(positions)
    allowed = visible(positions)

    qkv_full, out_full, gate_up_part = call_weights(qkv_weight[0], out_weight[0], gate_up_weight[0], 3)
    down_part = down_weight[0]

    forward = []
    state = tokens_in
    for section in range(sections):
        middle, normed_two, normed, rotated, attended = call_attend_forward(
            section, state, attn_gain, mlp_gain, cosine, sine, allowed, qkv_full, out_full
        )
        block_out, _, gate_up = call_feed(
            section, False, (normed_two, middle, gate_up_part, down_part), 8 + section
        )
        forward.append((state, middle, rotated, gate_up, normed_two, normed, attended, block_out))
        if section + 1 < sections:
            state = lax.ppermute(block_out, "section", up_steps)

    def pick(values):
        chosen = values[-1]
        for section in range(sections - 1):
            chosen = jnp.where(lax.axis_index("section") == section, values[section], chosen)
        return chosen

    normed_two, normed, attended, block_out = [pick(values) for values in list(zip(*forward))[4:]]
    both = ("replica", "shard")
    slice_rows = width // replicas

    backward = []
    upstream = cotangent
    for section in reversed(range(sections)):
        state, middle, rotated, gate_up = forward[section][:4]
        grad_normed_two, upstream_slice, _ = call_feed(
            section, True, (upstream, gate_up, down_part, gate_up_part), 8 + sections + section
        )
        grad_in, grad_low, grad_branch, grad_projected, gains = call_attend_backward(
            section, grad_normed_two, upstream, middle, state, rotated,
            attn_gain, mlp_gain, cosine, sine, allowed, qkv_full, out_full,
        )
        backward.insert(0, (upstream, upstream_slice, grad_in, grad_branch, grad_projected, gains))
        if section == sections - 1:
            normed_two, normed, attended, grad_low = lax.optimization_barrier(
                (normed_two, normed, attended, grad_low)
            )
        if section > 0:
            upstream = lax.ppermute(grad_low, "section", down_steps)
        if section == sections - 1:
            normed_two_all, gate_up_all, hidden_rows, lefts = call_prepare(
                normed_two, normed, attended, gate_up_part, 6
            )
            left_rows = lax.dynamic_slice_in_dim(normed_two_all, replica_at * slice_rows, slice_rows, 2)
            left_rows = left_rows.reshape(-1, slice_rows).T
            hidden_rows = hidden_rows.T
            lefts = jnp.swapaxes(lefts, 2, 3).reshape(2, width // shards, shards * rows)
            upstream, gate_up_all, left_rows, hidden_rows, lefts = lax.optimization_barrier(
                (upstream, gate_up_all, left_rows, hidden_rows, lefts)
            )

    upstream, upstream_slice, grad_in, grad_branch, grad_projected, gains = [
        pick(values) for values in zip(*backward)
    ]
    qkv_grad, out_grad, upstream_all = call_attend_grads(
        grad_projected, grad_branch, lefts[0], lefts[1], upstream, 4
    )
    qkv_grad = lax.psum_scatter(qkv_grad, "replica", scatter_dimension=0, tiled=True).astype(F32)
    out_grad = lax.psum_scatter(out_grad, "replica", scatter_dimension=0, tiled=True).astype(F32)
    gate_up_grad, down_grad, _ = call_feed_grads(
        upstream_slice, left_rows, hidden_rows, upstream_all, gate_up_all, down_part, 5
    )
    gate_up_grad = gate_up_grad.astype(F32)
    gains = jnp.sum(lax.all_gather(gains, both, axis=0), 0)
    return (
        block_out[None],
        grad_in[None],
        gains[0][None],
        qkv_grad[None],
        out_grad[None],
        gains[1][None],
        gate_up_grad[None],
        down_grad[None],
    )


def solution(mesh):
    both = ("replica", "shard")
    return jax.shard_map(
        on_device,
        mesh=mesh,
        in_specs=(
            P(both, None),
            P(both),
            P("section", None),
            P("section", "shard", None),
            P("section", "shard", None),
            P("section", None),
            P("section", "shard", None),
            P("section", "shard", None),
            P(both, None),
        ),
        out_specs=(
            P("section", both, None),
            P("section", both, None),
            P("section", None),
            P("section", both, None),
            P("section", both, None),
            P("section", None),
            P("section", both, None),
            P("section", both, None),
        ),
        check_vma=False,
    )
```

```python
import functools

import jax
import jax.numpy as jnp
from jax import lax
from jax.experimental import pallas as pl
from jax.experimental.pallas import tpu as pltpu
from jax.sharding import PartitionSpec as P

HEADS = 32
KV_HEADS = 8
HEAD = 64
SEQ = 64
EPSILON = 1e-05
ROPE_BASE = 500000.0
BF = jnp.bfloat16
F32 = jnp.float32
CONTRACT_LAST = (((1,), (1,)), ((), ()))
CONTRACT_FIRST = (((0,), (0,)), ((), ()))


MESH = pl.DeviceIdType.MESH
VMEM_LIMIT = 60 * 2**20
TILE = 128


def dot(left, right):
    return jnp.dot(left, right, preferred_element_type=F32)


def dot_rows(left, right):
    return lax.dot_general(left, right, CONTRACT_LAST, preferred_element_type=F32)


def dot_tokens(left, right):
    return lax.dot_general(left, right, CONTRACT_FIRST, preferred_element_type=F32)


def rope_tables(seq_pos):
    half_index = jnp.arange(HEAD // 2, dtype=F32)
    frequency = jnp.power(ROPE_BASE, -2.0 * half_index / HEAD)
    angles = seq_pos.astype(F32)[:, None] * frequency[None, :]
    cosine, sine = jnp.cos(angles), jnp.sin(angles)
    return (
        jnp.concatenate([cosine] * 4, 1),
        jnp.concatenate([-sine, sine, -sine, sine], 1),
    )


def visible(seq_pos):
    rows = seq_pos.shape[0]
    row_index = jnp.arange(rows)[:, None]
    col_index = jnp.arange(rows)[None, :]
    same = row_index // SEQ == col_index // SEQ
    seen = (col_index <= row_index) & (row_index - col_index <= seq_pos[:, None])
    return jnp.where(same & seen, 1.0, 0.0).astype(F32)


def lanes(rows):
    return lax.broadcasted_iota(jnp.int32, (rows, TILE), 1)


def swap_halves(tile, lane):
    return jnp.where(lane % HEAD < HEAD // 2, pltpu.roll(tile, TILE - HEAD // 2, 1), pltpu.roll(tile, HEAD // 2, 1))


def spread(tile, odd, lane):
    turned = pltpu.roll(tile, HEAD, 1)
    lower, upper = (turned, tile) if odd else (tile, turned)
    return jnp.concatenate(
        [jnp.where(lane < HEAD, lower, 0.0), jnp.where(lane < HEAD, 0.0, upper)], 0
    ).astype(BF)


def softmax_pair(queries, spread_keys, allowed):
    scores = dot_rows(queries, spread_keys) * HEAD ** (-0.5)
    halves = []
    for side in range(2):
        masked = jnp.where(allowed > 0.5, scores[:, side * TILE : (side + 1) * TILE], -1e30)
        expon = jnp.exp(masked - jnp.max(masked, -1, keepdims=True))
        halves.append(expon / jnp.sum(expon, -1, keepdims=True))
    return halves


def attend_forward(
    state_ref, gain_one_ref, gain_two_ref, cos_ref, sin_ref, allowed_ref, qkv_hbm, out_hbm,
    middle_ref, normed_two_ref, normed_ref, rotated_ref, attended_ref,
    qkv_ref, out_ref, sems,
):
    rows, width = state_ref.shape
    cols = qkv_hbm.shape[1]
    step = 512
    copies = [
        pltpu.make_async_copy(
            qkv_hbm.at[:, pl.ds(at, step)], qkv_ref.at[:, pl.ds(at, step)], sems.at[at // step]
        )
        for at in range(0, cols, step)
    ]
    out_copies = [
        pltpu.make_async_copy(
            out_hbm.at[:, pl.ds(at, step)], out_ref.at[:, pl.ds(at, step)], sems.at[(cols + at) // step]
        )
        for at in range(0, width, step)
    ]
    for copy in copies + out_copies:
        copy.start()
    state = state_ref[...].astype(F32)
    inverse = lax.rsqrt(jnp.mean(state * state, -1, keepdims=True) + EPSILON)
    normed_ref[...] = (state * inverse * gain_one_ref[...]).astype(BF)
    lane = lanes(rows)
    cosine, sine, allowed = cos_ref[...], sin_ref[...], allowed_ref[...]
    rope_cols = (HEADS + KV_HEADS) * HEAD
    for at in range(0, cols, step):
        copies[at // step].wait()
        projected = dot(normed_ref[...], qkv_ref[:, at : at + step])
        for tile_at in range(0, step, TILE):
            tile = projected[:, tile_at : tile_at + TILE]
            if at + tile_at < rope_cols:
                tile = tile * cosine + swap_halves(tile, lane) * sine
            rotated_ref[:, at + tile_at : at + tile_at + TILE] = tile.astype(BF)
    for group in range(KV_HEADS):
        key_at = width + group // 2 * TILE
        value_at = rope_cols + group // 2 * TILE
        keys = spread(rotated_ref[:, key_at : key_at + TILE].astype(F32), group % 2, lane)
        values = spread(rotated_ref[:, value_at : value_at + TILE].astype(F32), group % 2, lane)
        for pair in range(2):
            at = (group * 2 + pair) * TILE
            halves = softmax_pair(rotated_ref[:, at : at + TILE], keys, allowed)
            probs = jnp.concatenate([half.astype(BF) for half in halves], 1)
            attended_ref[:, at : at + TILE] = dot(probs, values).astype(BF)
    total = jnp.zeros((rows, 1), F32)
    for at in range(0, width, step):
        out_copies[at // step].wait()
        middle = state_ref[:, at : at + step].astype(F32) + dot(attended_ref[...], out_ref[:, at : at + step])
        middle_ref[:, at : at + step] = middle
        total += jnp.sum(middle * middle, -1, keepdims=True)
    inverse = lax.rsqrt(total / width + EPSILON)
    normed_two_ref[...] = (middle_ref[...] * inverse * gain_two_ref[...]).astype(BF)


def attend_backward(
    rounds, grad_ref, upstream_ref, middle_ref, state_ref, rotated_ref,
    gain_one_ref, gain_two_ref, cos_ref, sin_ref, allowed_ref, qkv_hbm, out_hbm,
    grad_state_ref, grad_low_ref, grad_branch_ref, grad_projected_ref, gain_terms_ref,
    qkv_ref, out_ref, grad_out_ref, middle_grad_ref, sems,
):
    rows, width = middle_ref.shape
    cols = qkv_hbm.shape[1]
    step = 512
    steps = width // step
    out_copies = [
        pltpu.make_async_copy(out_hbm.at[pl.ds(at * step, step)], out_ref.at[pl.ds(at * step, step)], sems.at[at])
        for at in range(steps)
    ]
    copies = [
        pltpu.make_async_copy(
            qkv_hbm.at[pl.ds(at * step, step)], qkv_ref.at[pl.ds(at * step, step)], sems.at[steps + at]
        )
        for at in range(steps)
    ]
    for copy in out_copies + copies:
        copy.start()

    def norm_back(grad, values, gain):
        inverse = lax.rsqrt(jnp.mean(values * values, -1, keepdims=True) + EPSILON)
        normal = values * inverse
        term = jnp.sum(grad * normal, 0, keepdims=True)
        scaled = grad * gain
        return inverse * (scaled - normal * jnp.mean(scaled * normal, -1, keepdims=True)), term

    upstream = upstream_ref[...].astype(F32)
    back, term = norm_back(grad_ref[...], middle_ref[...], gain_two_ref[...])
    gain_terms_ref[1:2, :] = term
    middle_grad_ref[...] = upstream + back
    grad_branch_ref[...] = middle_grad_ref[...].astype(BF)
    for at in range(steps):
        out_copies[at].wait()
        grad_out_ref[:, at * step : (at + 1) * step] = dot_rows(
            grad_branch_ref[...], out_ref[at * step : (at + 1) * step, :]
        ).astype(BF)
    lane = lanes(rows)
    cosine, sine, allowed = cos_ref[...], sin_ref[...], allowed_ref[...]
    rope_cols = (HEADS + KV_HEADS) * HEAD
    scale = HEAD ** (-0.5)

    def unrotate(tile):
        return tile * cosine - swap_halves(tile, lane) * sine

    def group_step(group_pair, carry):
        key_at = pl.multiple_of(width + group_pair * TILE, TILE)
        value_at = pl.multiple_of(rope_cols + group_pair * TILE, TILE)
        sums = []
        for odd in range(2):
            keys = spread(rotated_ref[:, pl.ds(key_at, TILE)].astype(F32), odd, lane)
            values = spread(rotated_ref[:, pl.ds(value_at, TILE)].astype(F32), odd, lane)
            key_sum = jnp.zeros((rows, TILE), F32)
            value_sum = jnp.zeros((rows, TILE), F32)
            for pair in range(2):
                at = pl.multiple_of(((group_pair * 2 + odd) * 2 + pair) * TILE, TILE)
                queries = rotated_ref[:, pl.ds(at, TILE)]
                grad_out = grad_out_ref[:, pl.ds(at, TILE)]
                halves = softmax_pair(queries, keys, allowed)
                grad_probs = dot_rows(grad_out, values)
                grad_halves = []
                for side in range(2):
                    grad = grad_probs[:, side * TILE : (side + 1) * TILE]
                    row_dot = jnp.sum(halves[side] * grad, -1, keepdims=True)
                    grad_halves.append((halves[side] * (grad - row_dot)).astype(BF))
                grad_scores = jnp.concatenate(grad_halves, 1)
                probs = jnp.concatenate([half.astype(BF) for half in halves], 1)
                grad_projected_ref[:, pl.ds(at, TILE)] = unrotate(dot(grad_scores, keys) * scale).astype(BF)
                key_terms = dot_tokens(grad_scores, queries)
                value_terms = dot_tokens(probs, grad_out)
                key_sum += jnp.where(lane < HEAD, key_terms[:rows], key_terms[rows:])
                value_sum += jnp.where(lane < HEAD, value_terms[:rows], value_terms[rows:])
            sums.append((key_sum + pltpu.roll(key_sum, HEAD, 1), value_sum + pltpu.roll(value_sum, HEAD, 1)))
        keys_grad = jnp.where(lane < HEAD, sums[0][0], sums[1][0]) * scale
        grad_projected_ref[:, pl.ds(key_at, TILE)] = unrotate(keys_grad).astype(BF)
        grad_projected_ref[:, pl.ds(value_at, TILE)] = jnp.where(
            lane < HEAD, sums[0][1], sums[1][1]
        ).astype(BF)
        return carry

    lax.fori_loop(0, KV_HEADS // 2, group_step, 0)
    for at in range(steps):
        copies[at].wait()
        grad_state_ref[:, at * step : (at + 1) * step] = dot_rows(
            grad_projected_ref[...], qkv_ref[at * step : (at + 1) * step, :]
        )
    state = state_ref[...].astype(F32)
    back, term = norm_back(grad_state_ref[...], state, gain_one_ref[...])
    gain_terms_ref[0:1, :] = term
    grad_state = middle_grad_ref[...] + back
    grad_low = grad_state.astype(BF)
    grad_low_ref[...] = grad_low
    grad_state_ref[...] = grad_low.astype(F32) if rounds else grad_state


def gated(section, body):
    def kernel(*refs):
        @pl.when(lax.axis_index("section") == section)
        def _():
            body(*refs)

    return kernel


def call_attend_forward(section, *operands):
    rows, width = operands[0].shape
    cols = operands[6].shape[1]
    specs = [pl.BlockSpec(memory_space=pltpu.VMEM)] * 6 + [pl.BlockSpec(memory_space=pl.ANY)] * 2
    return pl.pallas_call(
        gated(section, attend_forward),
        out_shape=(
            jax.ShapeDtypeStruct((rows, width), F32),
            jax.ShapeDtypeStruct((rows, width), BF),
            jax.ShapeDtypeStruct((rows, width), BF),
            jax.ShapeDtypeStruct((rows, cols), BF),
            jax.ShapeDtypeStruct((rows, width), BF),
        ),
        in_specs=specs,
        out_specs=[pl.BlockSpec(memory_space=pltpu.VMEM)] * 5,
        scratch_shapes=[
            pltpu.VMEM((width, cols), BF),
            pltpu.VMEM((width, width), BF),
            pltpu.SemaphoreType.DMA(((cols + width) // 512,)),
        ],
        compiler_params=pltpu.CompilerParams(vmem_limit_bytes=VMEM_LIMIT),
        name="attend_forward",
    )(*operands)


def call_attend_backward(section, *operands):
    rows, width = operands[2].shape
    cols = operands[10].shape[1]
    specs = [pl.BlockSpec(memory_space=pltpu.VMEM)] * 10 + [pl.BlockSpec(memory_space=pl.ANY)] * 2
    return pl.pallas_call(
        gated(section, functools.partial(attend_backward, section > 0)),
        out_shape=(
            jax.ShapeDtypeStruct((rows, width), F32),
            jax.ShapeDtypeStruct((rows, width), BF),
            jax.ShapeDtypeStruct((rows, width), BF),
            jax.ShapeDtypeStruct((rows, cols), BF),
            jax.ShapeDtypeStruct((2, width), F32),
        ),
        in_specs=specs,
        out_specs=[pl.BlockSpec(memory_space=pltpu.VMEM)] * 5,
        scratch_shapes=[
            pltpu.VMEM((width, cols), BF),
            pltpu.VMEM((width, width), BF),
            pltpu.VMEM((rows, width), BF),
            pltpu.VMEM((rows, width), F32),
            pltpu.SemaphoreType.DMA((2 * width // 512,)),
        ],
        compiler_params=pltpu.CompilerParams(vmem_limit_bytes=VMEM_LIMIT),
        name="attend_backward",
    )(*operands)


def slice_peers():
    shard = lax.axis_index("shard")
    chip, core = shard // 2, shard % 2
    return shard, chip * 2 + (1 - core), (1 - chip) * 2 + core, (1 - chip) * 2 + (1 - core)


def slice_barrier(devices, turns=()):
    barrier = pltpu.get_barrier_semaphore()
    replicas = lax.axis_size("replica")
    for device in devices:
        pl.semaphore_signal(barrier, inc=1, device_id={"shard": device}, device_id_type=MESH)
    for turn in turns:
        target = lax.rem(lax.axis_index("replica") + turn, replicas)
        pl.semaphore_signal(barrier, inc=1, device_id={"replica": target}, device_id_type=MESH)
    pl.semaphore_wait(barrier, len(devices) + len(turns))


def replica_copy(source, target, turn, send_sems, recv_sems, base):
    replicas = lax.axis_size("replica")
    device = lax.rem(lax.axis_index("replica") + replicas - turn, replicas)
    return pltpu.make_async_remote_copy(
        source, target, send_sems.at[base + turn], recv_sems.at[base + turn],
        device_id={"replica": device}, device_id_type=MESH,
    )


CHUNK = 512


def feed_kernel(backward, rows, *refs):
    if backward:
        (mine_ref, gate_up_ref, first_hbm, second_hbm, result_ref, all_ref, mid_ref, others_hbm,
         first_ref, second_ref, part_ref, take_ref, sent_ref, land_ref, own_ref, own_take_ref,
         load_sems, send_sems, recv_sems) = refs
    else:
        (mine_ref, middle_ref, first_hbm, second_hbm, result_ref, all_ref, gate_up_ref,
         mid_ref, first_ref, second_ref, part_ref, take_ref, sent_ref, land_ref, own_ref, own_take_ref,
         load_sems, send_sems, recv_sems) = refs
    shard = lax.axis_index("shard")
    chip, core = shard // 2, shard % 2
    beside = chip * 2 + (1 - core)
    across = (1 - chip) * 2 + core
    half = rows // 2
    width = all_ref.shape[1]
    ff = second_ref.shape[0] if not backward else first_ref.shape[0]
    first_steps = ff // CHUNK
    second_steps = width // CHUNK

    def load_first(at):
        if backward:
            place = (pl.ds(pl.multiple_of(at * CHUNK, CHUNK), CHUNK), slice(None))
            return [pltpu.make_async_copy(first_hbm.at[place], first_ref.at[place], load_sems.at[0, at])]
        places = [
            (slice(None), pl.ds(pl.multiple_of(side * ff + at * CHUNK, CHUNK), CHUNK)) for side in range(2)
        ]
        return [
            pltpu.make_async_copy(first_hbm.at[place], first_ref.at[place], load_sems.at[side, at])
            for side, place in enumerate(places)
        ]

    def load_second(at):
        span = pl.ds(pl.multiple_of(at * CHUNK, CHUNK), CHUNK)
        place = (span, slice(None)) if backward else (slice(None), span)
        return pltpu.make_async_copy(second_hbm.at[place], second_ref.at[place], load_sems.at[2, at])

    for at in range(first_steps):
        for copy in load_first(at):
            copy.start()
    for at in range(second_steps):
        load_second(at).start()

    def remote(source, target, at, device):
        return pltpu.make_async_remote_copy(
            source, target, send_sems.at[at], recv_sems.at[at], device_id={"shard": device}, device_id_type=MESH
        )

    def owned(owner, offset, count):
        return all_ref.at[pl.ds(pl.multiple_of(owner * rows + offset, half), count)]

    turns = range(1, lax.axis_size("replica"), 2) if backward else ()
    slice_barrier((beside, across), turns)
    place = pl.ds(pl.multiple_of(shard * rows, rows), rows)
    all_ref[place, :] = mine_ref[...]
    across_copies = [remote(owned(shard, at * half, half), owned(shard, at * half, half), 1 + at, across) for at in range(2)]
    beside_copy = remote(owned(shard, 0, rows), owned(shard, 0, rows), 0, beside)
    relays = [remote(owned(across, at * half, half), owned(across, at * half, half), 3 + at, beside) for at in range(2)]
    for copy in across_copies:
        copy.start()
    beside_copy.start()
    spread_copies = [
        replica_copy(mine_ref, others_hbm.at[lax.axis_index("replica")], turn, send_sems, recv_sems, 5 + 3 * second_steps)
        for turn in turns
    ]
    for copy in spread_copies:
        copy.start()

    def first_product(block, waits):
        span = pl.ds(pl.multiple_of(block * 2 * rows, 2 * rows), 2 * rows)

        def step(at, carry):
            cols = pl.ds(pl.multiple_of(at * CHUNK, CHUNK), CHUNK)
            high = pl.ds(pl.multiple_of(ff + at * CHUNK, CHUNK), CHUNK)
            if waits:
                for copy in load_first(at):
                    copy.wait()
            if backward:
                grad_hidden = dot_rows(all_ref[span, :], first_ref[cols, :])
                gate = gate_up_ref[span, cols].astype(F32)
                up = gate_up_ref[span, high].astype(F32)
                sigmoid = jax.nn.sigmoid(gate)
                mid_ref[span, cols] = (grad_hidden * up * sigmoid * (1.0 + gate * (1.0 - sigmoid))).astype(BF)
                mid_ref[span, high] = (grad_hidden * gate * sigmoid).astype(BF)
            else:
                gate = dot(all_ref[span, :], first_ref[:, cols])
                up = dot(all_ref[span, :], first_ref[:, high])
                gate_up_ref[span, cols] = gate.astype(BF)
                gate_up_ref[span, high] = up.astype(BF)
                mid_ref[span, cols] = (gate * jax.nn.sigmoid(gate) * up).astype(BF)
            return carry

        lax.fori_loop(0, first_steps, step, 0)

    def second_product(block, at, target_ref):
        span = pl.ds(pl.multiple_of(block * 2 * rows, 2 * rows), 2 * rows)
        cols = pl.ds(pl.multiple_of(at * CHUNK, CHUNK), CHUNK)
        if backward:
            partial = dot_rows(mid_ref[span, :], second_ref[cols, :])
        else:
            partial = dot(mid_ref[span, :], second_ref[:, cols])
        target_ref[at, 0] = partial[:rows].astype(BF)
        target_ref[at, 1] = partial[rows:].astype(BF)

    def give(at):
        return remote(part_ref.at[at, 1 - core], take_ref.at[at], 5 + at, beside)

    def cross(at):
        return remote(sent_ref.at[at], land_ref.at[at], 5 + second_steps + at, across)

    def give_own(at):
        return remote(own_ref.at[at, 1 - core], own_take_ref.at[at], 5 + 2 * second_steps + at, beside)

    def pass_on(at):
        give(at).wait_recv()
        sent_ref[at] = (part_ref[at, core].astype(F32) + take_ref[at].astype(F32)).astype(BF)
        cross(at).start()

    beside_copy.wait_recv()
    first_product(chip, True)
    for at in range(2):
        across_copies[at].wait_recv()
        relays[at].start()
    for at in range(2):
        relays[at].wait_recv()
    first_product(1 - chip, False)

    def other_step(at, carry):
        load_second(at).wait()
        second_product(1 - chip, at, part_ref)
        give(at).start()

        @pl.when(at > 0)
        def _():
            pass_on(at - 1)

        return carry

    lax.fori_loop(0, second_steps, other_step, 0)

    def own_step(at, carry):
        @pl.when(at == 0)
        def _():
            pass_on(second_steps - 1)

        second_product(chip, at, own_ref)
        give_own(at).start()
        return carry

    lax.fori_loop(0, second_steps, own_step, 0)
    for at in range(second_steps):
        give_own(at).wait_recv()
        cross(at).wait_recv()
        cols = slice(at * CHUNK, (at + 1) * CHUNK)
        total = own_ref[at, core].astype(F32) + own_take_ref[at].astype(F32) + land_ref[at].astype(F32)
        if backward:
            result_ref[:, cols] = total
        else:
            result_ref[:, cols] = (middle_ref[:, cols] + total).astype(BF)
    for copy in [beside_copy] + across_copies + relays:
        copy.wait_send()
    for copy in spread_copies:
        copy.wait()
    for at in range(second_steps):
        give(at).wait_send()
        cross(at).wait_send()
        give_own(at).wait_send()


def call_feed(section, backward, operands, collective):
    first, second = operands[-2], operands[-1]
    rows, width = operands[0].shape
    shards = lax.axis_size("shard")
    ff = first.shape[0] if backward else second.shape[0]
    every = shards * rows
    steps = width // CHUNK
    out_shape = [
        jax.ShapeDtypeStruct((rows, width), F32 if backward else BF),
        jax.ShapeDtypeStruct((every, width), BF),
        jax.ShapeDtypeStruct((every, 2 * ff), BF),
    ]
    copies = 5 + 3 * steps
    if backward:
        replicas = lax.axis_size("replica")
        out_shape.append(jax.ShapeDtypeStruct((replicas, rows, width), BF))
        copies += replicas
    piece = pltpu.VMEM((steps, rows, CHUNK), BF)
    pair = pltpu.VMEM((steps, 2, rows, CHUNK), BF)
    scratch = [pltpu.VMEM(first.shape, BF), pltpu.VMEM(second.shape, BF), pair, piece, piece, piece, pair, piece]
    if not backward:
        scratch.insert(0, pltpu.VMEM((every, ff), BF))
    scratch += [
        pltpu.SemaphoreType.DMA((3, max(ff // CHUNK, steps))),
        pltpu.SemaphoreType.DMA((copies,)),
        pltpu.SemaphoreType.DMA((copies,)),
    ]
    return pl.pallas_call(
        gated(section, functools.partial(feed_kernel, backward, rows)),
        out_shape=out_shape,
        in_specs=[pl.BlockSpec(memory_space=pltpu.VMEM)] * (len(operands) - 2)
        + [pl.BlockSpec(memory_space=pl.ANY)] * 2,
        out_specs=[pl.BlockSpec(memory_space=pltpu.VMEM)] * 3 + [pl.BlockSpec(memory_space=pl.ANY)] * backward,
        scratch_shapes=scratch,
        compiler_params=pltpu.CompilerParams(
            collective_id=collective, has_side_effects=True, vmem_limit_bytes=VMEM_LIMIT
        ),
        name="feed_backward" if backward else "feed_forward",
    )(*operands)


def weights_kernel(
    qkv_ref, out_ref, gate_up_ref, qkv_full, out_full, gate_up_part, qkv_hold, out_hold, gate_up_hold, local_sems, send_sems,
    recv_sems,
):
    shard, replica = lax.axis_index("shard"), lax.axis_index("replica")
    chip, core = shard // 2, shard % 2
    beside = {"shard": chip * 2 + (1 - core)}
    across = {"shard": (1 - chip) * 2 + core}
    diagonal = {"shard": (1 - chip) * 2 + (1 - core)}
    mine = replica % 2
    partner = {"replica": replica + 1 - 2 * mine}
    rows = qkv_ref.shape[0]
    half = rows // 2
    ff = gate_up_ref.shape[1] // 2
    part = gate_up_part.shape[1] // 2

    def remote(source, target, at, device):
        return pltpu.make_async_remote_copy(
            source, target, send_sems.at[at], recv_sems.at[at], device_id=device, device_id_type=MESH
        )

    def span(start, count):
        return pl.ds(pl.multiple_of(start, count), count)

    sides = [pl.ds(side * part, part) for side in range(2)]
    loads = [
        pltpu.make_async_copy(qkv_ref, qkv_hold, local_sems.at[0]),
        pltpu.make_async_copy(out_ref, out_hold, local_sems.at[1]),
    ] + [
        pltpu.make_async_copy(
            gate_up_ref.at[:, span(side * ff + shard * part, part)], gate_up_hold.at[side], local_sems.at[2 + side]
        )
        for side in range(2)
    ]
    own_rows = span(shard * rows, rows)
    stores = [
        pltpu.make_async_copy(qkv_hold, qkv_full.at[own_rows], local_sems.at[4]),
        pltpu.make_async_copy(out_hold, out_full.at[own_rows], local_sems.at[5]),
    ] + [
        pltpu.make_async_copy(gate_up_hold.at[side], gate_up_part.at[own_rows, sides[side]], local_sems.at[6 + side])
        for side in range(2)
    ]
    for copy in loads:
        copy.start()

    pieces = []
    for source, whole, count in ((qkv_ref, qkv_full, 64), (out_ref, out_full, 128)):
        for offset in range(0, half, count):

            def place(owner, part_of, whole=whole, offset=offset, count=count):
                return whole.at[span(owner["shard"] * rows + part_of * half + offset, count)]

            own = source.at[span(mine * half + offset, count)]
            pieces.append((own, place, across, True))
    for offset in range(0, half, 128):
        for side in range(2):
            for device in (across, diagonal):

                def place(owner, part_of, offset=offset, side=side):
                    return gate_up_part.at[
                        span(owner["shard"] * rows + part_of * half + offset, 128), pl.ds(side * part, part)
                    ]

                own = gate_up_ref.at[
                    span(mine * half + offset, 128), span(side * ff + device["shard"] * part, part)
                ]
                pieces.append((own, place, device, False))
    count = len(pieces)
    me = {"shard": shard}
    over = [remote(own, place(me, mine), at, device) for at, (own, place, device, _) in enumerate(pieces)]
    passed = [
        remote(place(device, mine), place(device, mine), count + at, partner)
        for at, (_, place, device, _) in enumerate(pieces)
    ]
    relays = [
        [
            remote(place(across, which), place(across, which), (2 + turn) * count + at, beside)
            if relayed
            else None
            for at, (_, place, _, relayed) in enumerate(pieces)
        ]
        for turn, which in enumerate((mine, 1 - mine))
    ]
    direct = [
        remote(qkv_ref, qkv_full.at[span(shard * rows, rows)], 4 * count, beside),
        remote(out_ref, out_full.at[span(shard * rows, rows)], 4 * count + 1, beside),
    ]
    for side in range(2):
        direct.append(
            remote(
                gate_up_ref.at[:, span(side * ff + beside["shard"] * part, part)],
                gate_up_part.at[span(shard * rows, rows), pl.ds(side * part, part)],
                4 * count + 2 + side,
                beside,
            )
        )

    barrier = pltpu.get_barrier_semaphore()
    for device in (beside, across, diagonal, partner):
        pl.semaphore_signal(barrier, inc=1, device_id=device, device_id_type=MESH)
    pl.semaphore_wait(barrier, 4)

    started = []

    def start(copy):
        copy.start()
        started.append(copy)

    ahead = 3
    for copy in over[:ahead]:
        start(copy)
    for copy in direct:
        start(copy)
    for load, store in zip(loads, stores):
        load.wait()
        store.start()
    for at in range(count + 1):
        if at < count:
            over[at].wait_recv()
            start(passed[at])
            if relays[0][at] is not None:
                start(relays[0][at])
            if at + ahead < count:
                over[at].wait_send()
                started[:] = [copy for copy in started if copy is not over[at]]
                start(over[at + ahead])
        if at > 0:
            passed[at - 1].wait_recv()
            if relays[1][at - 1] is not None:
                start(relays[1][at - 1])
    for copies in relays:
        for copy in copies:
            if copy is not None:
                copy.wait_recv()
    for copy in direct:
        copy.wait_recv()
    for copy in stores:
        copy.wait()
    for copy in started:
        copy.wait_send()


def call_weights(qkv_weight, out_weight, gate_up_weight, collective):
    shards = lax.axis_size("shard")
    rows = qkv_weight.shape[0]
    count = 4 + 2 + 8
    anywhere = pl.BlockSpec(memory_space=pl.ANY)
    return pl.pallas_call(
        weights_kernel,
        out_shape=[
            jax.ShapeDtypeStruct((shards * rows, qkv_weight.shape[1]), BF),
            jax.ShapeDtypeStruct((shards * rows, out_weight.shape[1]), BF),
            jax.ShapeDtypeStruct((shards * rows, gate_up_weight.shape[1] // shards), BF),
        ],
        in_specs=[anywhere] * 3,
        out_specs=[anywhere] * 3,
        scratch_shapes=[
            pltpu.VMEM(qkv_weight.shape, BF),
            pltpu.VMEM(out_weight.shape, BF),
            pltpu.VMEM((2, rows, gate_up_weight.shape[1] // (2 * shards)), BF),
            pltpu.SemaphoreType.DMA((8,)),
            pltpu.SemaphoreType.DMA((4 * count + 4,)),
            pltpu.SemaphoreType.DMA((4 * count + 4,)),
        ],
        compiler_params=pltpu.CompilerParams(
            collective_id=collective, has_side_effects=True, vmem_limit_bytes=VMEM_LIMIT
        ),
        name="weights",
    )(qkv_weight, out_weight, gate_up_weight)


def attend_grads_kernel(
    projected_ref, branch_ref, left_ref, upstream_ref, gains_ref, terms_ref, gain_sum_ref, others_hbm,
    all_ref, gains_land_ref, send_sems, recv_sems,
):
    shard, beside, across, _ = slice_peers()
    replica, replicas = lax.axis_index("replica"), lax.axis_size("replica")
    rows, cols = projected_ref.shape
    pieces = all_ref.shape[0]
    step = all_ref.shape[2]
    sub_rows = terms_ref.shape[1]
    slice_barrier((beside, across), range(1, replicas))
    spread_copies = [
        replica_copy(upstream_ref, others_hbm.at[replica], turn, send_sems, recv_sems, 3 * pieces)
        for turn in range(2, replicas, 2)
    ]
    gain_copies = [
        replica_copy(gains_ref, gains_land_ref.at[replica], turn, send_sems, recv_sems, 3 * pieces + replicas)
        for turn in range(1, replicas)
    ]

    def remote(owner, piece, at, device):
        place = all_ref.at[piece, pl.ds(pl.multiple_of(owner * rows, rows), rows)]
        return pltpu.make_async_remote_copy(
            place, place, send_sems.at[at], recv_sems.at[at], device_id={"shard": device}, device_id_type=MESH
        )

    own = pl.ds(pl.multiple_of(shard * rows, rows), rows)
    over = [remote(shard, piece, piece, across) for piece in range(pieces)]
    direct = [remote(shard, piece, pieces + piece, beside) for piece in range(pieces)]
    relays = [remote(across, piece, 2 * pieces + piece, beside) for piece in range(pieces)]
    for piece in range(pieces):
        at = piece * step
        all_ref[piece, own, :] = (
            projected_ref[:, at : at + step] if at < cols else branch_ref[:, at - cols : at - cols + step]
        )
        over[piece].start()
        direct[piece].start()
    gains_land_ref[replica] = gains_ref[...]
    for copy in gain_copies + spread_copies:
        copy.start()

    def product(piece):
        direct[piece].wait_recv()
        relays[piece].wait_recv()
        at = piece * step
        total = dot(left_ref[0 if at < cols else 1], all_ref[piece]).astype(BF)
        for group in range(replicas):
            terms_ref[group, :, at : at + step] = total[group * sub_rows : (group + 1) * sub_rows]

    for piece in range(pieces):
        over[piece].wait_recv()
        relays[piece].start()
        if piece:
            product(piece - 1)
    product(pieces - 1)
    for copy in gain_copies:
        copy.wait()
    gain_sum_ref[...] = jnp.sum(gains_land_ref[...], 0)
    for copy in over + direct + relays:
        copy.wait_send()
    for copy in spread_copies:
        copy.wait()


def call_attend_grads(projected, branch, left, upstream, gains, collective):
    replicas = lax.axis_size("replica")
    rows, cols = projected.shape
    width = branch.shape[1]
    _, every, tokens = left.shape
    pieces = (cols + width) // CHUNK
    copies = 3 * pieces + 2 * replicas
    vmem = pl.BlockSpec(memory_space=pltpu.VMEM)
    return pl.pallas_call(
        attend_grads_kernel,
        out_shape=[
            jax.ShapeDtypeStruct((replicas, every // replicas, cols + width), BF),
            jax.ShapeDtypeStruct(gains.shape, F32),
            jax.ShapeDtypeStruct((replicas,) + upstream.shape, BF),
        ],
        in_specs=[vmem] * 5,
        out_specs=[vmem] * 2 + [pl.BlockSpec(memory_space=pl.ANY)],
        scratch_shapes=[
            pltpu.VMEM((pieces, tokens, CHUNK), BF),
            pltpu.VMEM((replicas,) + gains.shape, F32),
            pltpu.SemaphoreType.DMA((copies,)),
            pltpu.SemaphoreType.DMA((copies,)),
        ],
        compiler_params=pltpu.CompilerParams(
            collective_id=collective, has_side_effects=True, vmem_limit_bytes=VMEM_LIMIT
        ),
        name="attend_grads",
    )(projected, branch, left, upstream, gains)


def feed_grads_kernel(
    left_ref, hidden_ref, terms_ref, gains_ref, upstream_hbm, odd_hbm, even_hbm, early_hbm, gate_up_hbm, down_hbm,
    gate_up_grad_ref, down_grad_ref, attend_grad_ref, gain_sum_ref, gathered_hbm,
    down_ref, block_ref, gate_up_ref, mid_ref, sum_ref, stage_ref, chain_ref, gains_land_ref,
    load_sems, block_sems, keep_sem, send_sems, recv_sems,
):
    shard, beside, across, diagonal = slice_peers()
    peers = (across, diagonal, beside)
    replica, replicas = lax.axis_index("replica"), lax.axis_size("replica")
    early = lax.axis_index("section") == lax.axis_size("section") - 1
    late = lax.axis_index("section") < lax.axis_size("section") - 1
    rows = odd_hbm.shape[1]
    every, width = upstream_hbm.shape
    part = down_ref.shape[0]
    half_part = part // 2
    ff = gate_up_grad_ref.shape[1] // 2
    steps = half_part // CHUNK
    wide = width // CHUNK
    out_rows = gate_up_grad_ref.shape[0]
    grad_base = 3 * replicas
    chain_base = grad_base + 2 * 2 * steps * 3
    gain_base = chain_base + 2 * replicas

    load_down = pltpu.make_async_copy(down_hbm, down_ref, load_sems.at[3, 0])
    load_down.start()

    def block_at(turn):
        return lax.rem(replica + turn, replicas)

    def tokens(turn):
        return pl.ds(pl.multiple_of(block_at(turn) * every, every), every)

    def load_gate_up(half, turn, side):
        cols = pl.ds(side * part + half * half_part, half_part)
        slot = lax.rem(turn, 2)
        return pltpu.make_async_copy(
            gate_up_hbm.at[tokens(turn), cols], gate_up_ref.at[slot, side], load_sems.at[side, slot]
        )

    def block_copies(turn, source):
        slot = lax.rem(turn, 2)
        copies = []
        for at, owner in enumerate(peers + (shard,)):
            place = pl.ds(pl.multiple_of(owner * rows, rows), rows)
            if source is early_hbm:
                own = early_hbm.at[turn, place]
            else:
                own = gathered_hbm.at[turn, place] if source is None or at < 3 else source.at[block_at(turn)]
            copies.append(pltpu.make_async_copy(own, block_ref.at[slot, place], block_sems.at[slot, at]))
        return copies

    def load_block(turn):
        @pl.when(early & (turn > 0))
        def _():
            for copy in block_copies(turn, early_hbm):
                copy.start()

        @pl.when(late | (turn == 0))
        def _():
            for copy in block_copies(turn, None)[:3]:
                copy.start()

        cases = ((turn == 0, None), (late & (turn > 0) & (turn % 2 == 0), even_hbm), (late & (turn % 2 == 1), odd_hbm))
        for case, source in cases:

            @pl.when(case)
            def _(source=source):
                block_copies(turn, source)[3].start()

    def wait_block(turn):
        for copy in block_copies(turn, None):
            copy.wait()

    def remote(source, target, at, device):
        return pltpu.make_async_remote_copy(
            source, target, send_sems.at[at], recv_sems.at[at], device_id={"shard": device}, device_id_type=MESH
        )

    def landing(turn, owner):
        return gathered_hbm.at[turn, pl.ds(pl.multiple_of(owner * rows, rows), rows)]

    def over(turn, source):
        return remote(source.at[block_at(turn)], landing(turn, shard), 3 * turn, across)

    def direct(turn, source):
        return remote(source.at[block_at(turn)], landing(turn, shard), 3 * turn + 1, beside)

    def relay(turn):
        return remote(landing(turn, across), landing(turn, across), 3 * turn + 2, beside)

    def send_block(turn):
        for parity, source in ((0, even_hbm), (1, odd_hbm)):

            @pl.when(lax.rem(turn, 2) == parity)
            def _(source=source):
                over(turn, source).start()
                direct(turn, source).start()

    def chain_slot(block, at):
        return replicas - (replicas - block) * ((at - block + replicas - 1) // replicas)

    def chain_up(block):
        return pltpu.make_async_remote_copy(
            chain_ref.at[block], chain_ref.at[block], send_sems.at[chain_base + block],
            recv_sems.at[chain_base + block], device_id={"replica": replica + 1}, device_id_type=MESH,
        )

    def chain_down(block):
        return pltpu.make_async_remote_copy(
            chain_ref.at[block], chain_ref.at[chain_slot(block, replica - 1)],
            send_sems.at[chain_base + replicas + block],
            recv_sems.at[chain_base + replicas + block], device_id={"replica": replica - 1}, device_id_type=MESH,
        )

    def add_terms(block):
        chain_ref[block] = (chain_ref[block].astype(F32) + terms_ref[block].astype(F32)).astype(BF)

    def chain_step(step):
        high = replicas - 1 - step + replica

        @pl.when((replica > 0) & (step >= replica))
        def _():
            chain_up(high).wait_recv()

            @pl.when(step < replicas - 1)
            def _():
                add_terms(high)
                chain_up(high).start()

        low = step - (replicas - 1 - replica)

        @pl.when((replica < replicas - 1) & (step >= replicas - 1 - replica))
        def _():
            chain_down(low).wait_recv()

            @pl.when(step < replicas - 1)
            def _():
                add_terms(low)
                chain_down(low).start()

    def gain_copy(peer):
        return remote(
            gains_ref, gains_land_ref.at[shard], gain_base + peer, peers[peer]
        )

    barrier = pltpu.get_barrier_semaphore()
    for device in peers:
        pl.semaphore_signal(barrier, inc=1, device_id={"shard": device}, device_id_type=MESH)

    @pl.when(replica > 0)
    def _():
        pl.semaphore_signal(barrier, inc=1, device_id={"replica": replica - 1}, device_id_type=MESH)

    @pl.when(replica < replicas - 1)
    def _():
        pl.semaphore_signal(barrier, inc=1, device_id={"replica": replica + 1}, device_id_type=MESH)

    below = (replica + replicas - 1) // replicas
    above = (2 * replicas - 2 - replica) // replicas
    pl.semaphore_wait(barrier, 3 + below + above)

    @pl.when(late)
    def _():
        for turn in range(1, min(3, replicas)):
            send_block(turn)

    for block in reversed(range(1, replicas)):

        @pl.when(replica == 0)
        def _(block=block):
            chain_ref[block] = terms_ref[block]
            chain_up(block).start()

    for block in range(replicas - 1):

        @pl.when(replica == replicas - 1)
        def _(block=block):
            chain_ref[block] = terms_ref[block]
            chain_down(block).start()

    for peer in range(3):
        gain_copy(peer).start()
    gains_land_ref[shard] = gains_ref[...]
    load_own = pltpu.make_async_copy(upstream_hbm, block_ref.at[0], load_sems.at[2, 0])
    load_own.start()
    load_own.wait()
    keep_own = pltpu.make_async_copy(block_ref.at[0], gathered_hbm.at[0], keep_sem)
    keep_own.start()
    load_down.wait()
    keep_own.wait()

    def send_grad(half, at, peer):
        device = peers[peer]
        cols = pl.ds(pl.multiple_of(at * CHUNK, CHUNK), CHUNK)
        target = pl.ds(
            pl.multiple_of(
                (at // steps) * ff + shard * part + half * half_part + (at % steps) * CHUNK, CHUNK
            ),
            CHUNK,
        )
        return remote(
            stage_ref.at[half, pl.ds(pl.multiple_of(device * out_rows, out_rows), out_rows), cols],
            gate_up_grad_ref.at[:, target],
            grad_base + (half * 2 * steps + at) * 3 + peer,
            device,
        )

    def half_pass(half):
        for side in range(2):
            load_gate_up(half, 0, side).start()
        sum_ref[...] = jnp.zeros_like(sum_ref)

        def work(turn, carry):
            slot = lax.rem(turn, 2)
            later = lax.rem(turn + 1, replicas)
            for side in range(2):
                load_gate_up(half, turn, side).wait()

            @pl.when(turn + 1 < replicas)
            def _():
                for side in range(2):
                    load_gate_up(half, later, side).start()

            if half:

                @pl.when(turn + 1 < replicas)
                def _():
                    load_block(later)

            def products(at, inner):
                cols = pl.ds(pl.multiple_of(at * CHUNK, CHUNK), CHUNK)
                high = pl.ds(pl.multiple_of(half_part + at * CHUNK, CHUNK), CHUNK)
                down_rows = pl.ds(pl.multiple_of(half * half_part + at * CHUNK, CHUNK), CHUNK)
                grad_hidden = dot_rows(block_ref[slot], down_ref[down_rows, :])
                gate = gate_up_ref[slot, 0, :, cols].astype(F32)
                up = gate_up_ref[slot, 1, :, cols].astype(F32)
                sigmoid = jax.nn.sigmoid(gate)
                mid_ref[:, cols] = (grad_hidden * up * sigmoid * (1.0 + gate * (1.0 - sigmoid))).astype(BF)
                mid_ref[:, high] = (grad_hidden * gate * sigmoid).astype(BF)
                return inner

            lax.fori_loop(0, steps, products, 0)

            def sums(at, inner):
                cols = pl.ds(pl.multiple_of(at * CHUNK, CHUNK), CHUNK)
                total = sum_ref[:, cols] + dot(left_ref[:, tokens(turn)], mid_ref[:, cols])

                @pl.when(turn < replicas - 1)
                def _():
                    sum_ref[:, cols] = total

                @pl.when(turn == replicas - 1)
                def _():
                    stage_ref[half, :, cols] = total.astype(BF)
                    for peer in range(3):
                        send_grad(half, at, peer).start()

                return inner

            lax.fori_loop(0, 2 * steps, sums, 0)

            @pl.when(turn + 1 < replicas)
            def _():
                if half:
                    wait_block(later)
                else:

                    @pl.when(late)
                    def _():
                        over(later, even_hbm).wait_recv()
                        relay(later).start()
                        direct(later, even_hbm).wait_recv()
                        relay(later).wait_recv()

                    load_block(later)

                    @pl.when(late & (turn + 3 < replicas))
                    def _():
                        send_block(turn + 3)

                    wait_block(later)

            return carry

        return work

    first = half_pass(0)
    lax.fori_loop(0, replicas - 1, first, 0)
    chain_step(1)
    first(replicas - 1, 0)
    load_block(0)
    wait_block(0)
    second = half_pass(1)
    lax.fori_loop(0, replicas - 1, second, 0)
    if replicas > 2:
        chain_step(2)
    second(replicas - 1, 0)
    load_block(0)
    wait_block(0)
    down_grad_ref[...] = jnp.zeros_like(down_grad_ref)

    def down_work(turn, carry):
        slot = lax.rem(turn, 2)
        later = lax.rem(turn + 1, replicas)

        @pl.when(turn + 1 < replicas)
        def _():
            load_block(later)

        def down_sums(at, inner):
            cols = pl.ds(pl.multiple_of(at * CHUNK, CHUNK), CHUNK)
            down_grad_ref[:, cols] += dot(hidden_ref[:, tokens(turn)], block_ref[slot, :, cols])
            return inner

        lax.fori_loop(0, wide, down_sums, 0)

        @pl.when(turn + 1 < replicas)
        def _():
            wait_block(later)

        return carry

    lax.fori_loop(0, replicas, down_work, 0)
    for peer in range(3):
        gain_copy(peer).wait()
    gain_sum_ref[...] = jnp.sum(gains_land_ref[...], 0)
    own = pl.ds(pl.multiple_of(shard * out_rows, out_rows), out_rows)
    for half in range(2):

        def store_own(at, carry, half=half):
            cols = pl.ds(pl.multiple_of(at * CHUNK, CHUNK), CHUNK)
            target = pl.ds(
                pl.multiple_of(
                    (at // steps) * ff + shard * part + half * half_part + (at % steps) * CHUNK, CHUNK
                ),
                CHUNK,
            )
            gate_up_grad_ref[:, target] = stage_ref[half, own, cols]
            return carry

        lax.fori_loop(0, 2 * steps, store_own, 0)
    for step in range(3, replicas):
        chain_step(step)
    attend_grad_ref[...] = terms_ref[replica].astype(F32)

    @pl.when(replica > 0)
    def _():
        attend_grad_ref[...] += chain_ref[replica].astype(F32)

    @pl.when(replica < replicas - 1)
    def _():
        attend_grad_ref[...] += chain_ref[replicas].astype(F32)

    for half in range(2):

        def finish(at, carry, half=half):
            for peer in range(3):
                send_grad(half, at, peer).wait()
            return carry

        lax.fori_loop(0, 2 * steps, finish, 0)
    @pl.when(late)
    def _():
        for turn in range(1, replicas):
            over(turn, even_hbm).wait_send()
            direct(turn, even_hbm).wait_send()
            relay(turn).wait_send()

    for block in range(1, replicas):

        @pl.when(replica < block)
        def _(block=block):
            chain_up(block).wait_send()

    for block in range(replicas - 1):

        @pl.when(replica > block)
        def _(block=block):
            chain_down(block).wait_send()


def call_feed_grads(left, hidden, terms, gains, upstream, odd, even, early, gate_up, down, collective):
    every, width = upstream.shape
    replicas = odd.shape[0]
    shards = lax.axis_size("shard")
    part = down.shape[0]
    out_rows = left.shape[0] // shards
    vmem, anywhere = pl.BlockSpec(memory_space=pltpu.VMEM), pl.BlockSpec(memory_space=pl.ANY)
    copies = 5 * replicas + 3 * 2 * (part // CHUNK) + 3
    return pl.pallas_call(
        feed_grads_kernel,
        out_shape=[
            jax.ShapeDtypeStruct((out_rows, 2 * part * shards), BF),
            jax.ShapeDtypeStruct((hidden.shape[0], width), F32),
            jax.ShapeDtypeStruct(terms.shape[1:], F32),
            jax.ShapeDtypeStruct(gains.shape, F32),
            jax.ShapeDtypeStruct((replicas, every, width), BF),
        ],
        in_specs=[vmem] * 4 + [anywhere] * 6,
        out_specs=[vmem] * 4 + [anywhere],
        scratch_shapes=[
            pltpu.VMEM(down.shape, BF),
            pltpu.VMEM((2, every, width), BF),
            pltpu.VMEM((2, 2, every, part // 2), BF),
            pltpu.VMEM((every, part), BF),
            pltpu.VMEM((left.shape[0], part), F32),
            pltpu.VMEM((2, left.shape[0], part), BF),
            pltpu.VMEM((replicas + 1,) + terms.shape[1:], BF),
            pltpu.VMEM((shards,) + gains.shape, F32),
            pltpu.SemaphoreType.DMA((4, 2)),
            pltpu.SemaphoreType.DMA((2, 4)),
            pltpu.SemaphoreType.DMA,
            pltpu.SemaphoreType.DMA((copies,)),
            pltpu.SemaphoreType.DMA((copies,)),
        ],
        compiler_params=pltpu.CompilerParams(
            collective_id=collective, has_side_effects=True, vmem_limit_bytes=VMEM_LIMIT
        ),
        name="feed_grads",
    )(left, hidden, terms, gains, upstream, odd, even, early, gate_up, down)


def turn_order(replicas):
    return [0] + list(range(1, replicas, 2)) + list(range(2, replicas, 2))


def prepare_kernel(
    sections, normed_two_ref, lefts_ref, gate_up_hbm, *refs
):
    slices = refs[:sections]
    (gathered_hbm, gate_up_all_hbm, hidden_hbm, left_hbm, left_rows_ref,
     weight_ref, block_ref, gate_up_ref, hidden_ref, turned_ref,
     load_sems, store_sems, keep_sems, send_sems, recv_sems) = refs[sections:]
    shard, beside, across, diagonal = slice_peers()
    peers = (across, diagonal, beside)
    replica, replicas = lax.axis_index("replica"), lax.axis_size("replica")
    shards = lax.axis_size("shard")
    rows, width = normed_two_ref.shape
    every = rows * shards
    part = hidden_ref.shape[1]
    ff_rows = hidden_hbm.shape[0]
    steps = part // CHUNK
    slice_rows = left_rows_ref.shape[0]
    kinds, groups = lefts_ref.shape[:2]
    owner = (replica * shards) // replicas
    first_col = lax.rem(replica * shards, replicas) * ff_rows

    def load_weight(side, at):
        place = (slice(None), pl.ds(pl.multiple_of(side * part + at * CHUNK, CHUNK), CHUNK))
        return pltpu.make_async_copy(gate_up_hbm.at[place], weight_ref.at[place], load_sems.at[side, at])

    for at in range(steps):
        for side in range(2):
            load_weight(side, at).start()

    def remote(source, target, at, device):
        return pltpu.make_async_remote_copy(
            source, target, send_sems.at[at], recv_sems.at[at], device_id={"shard": device}, device_id_type=MESH
        )

    def landing(turn, who):
        return gathered_hbm.at[turn, pl.ds(pl.multiple_of(who * rows, rows), rows)]

    def over(turn):
        return remote(landing(turn, shard), landing(turn, shard), 3 * turn, across)

    def direct(turn):
        return remote(landing(turn, shard), landing(turn, shard), 3 * turn + 1, beside)

    def relay(turn):
        return remote(landing(turn, across), landing(turn, across), 3 * turn + 2, beside)

    def from_replica(turn):
        return replica_copy(normed_two_ref, landing(turn, shard), turn, send_sems, recv_sems, 3 * replicas)

    def tokens(turn):
        return pl.ds(pl.multiple_of(lax.rem(replica + turn, replicas) * every, every), every)

    def load_block(turn, slot):
        return pltpu.make_async_copy(gathered_hbm.at[turn], block_ref.at[slot], store_sems.at[0, slot])

    def store_block(turn, slot):
        return pltpu.make_async_copy(gate_up_ref.at[slot], gate_up_all_hbm.at[tokens(turn)], store_sems.at[1, slot])

    def hand_hidden(turn, slot, peer):
        device = peers[peer]
        return remote(
            turned_ref.at[slot, device], hidden_hbm.at[:, tokens(turn)], 4 * replicas + 3 * turn + peer, device
        )

    def keep_hidden(turn, slot):
        return pltpu.make_async_copy(
            turned_ref.at[slot, shard], hidden_hbm.at[:, tokens(turn)], store_sems.at[2, slot]
        )

    own_rows = pl.ds(pl.multiple_of(shard * rows, rows), rows)

    def hand_left(kind, group, peer):
        device = peers[peer]
        return remote(
            lefts_ref.at[kind, group, device],
            left_hbm.at[kind, group, :, own_rows],
            7 * replicas + (kind * groups + group) * 3 + peer,
            device,
        )

    def keep_left(kind, group):
        return pltpu.make_async_copy(
            lefts_ref.at[kind, group, shard], left_hbm.at[kind, group, :, own_rows],
            keep_sems.at[kind * groups + group],
        )

    for section in range(sections):

        @pl.when(lax.axis_index("section") == section)
        def _(section=section):
            pltpu.make_async_copy(slices[section], block_ref.at[0], store_sems.at[0, 0]).start()

    slice_barrier(peers, range(1, replicas))
    order = turn_order(replicas)
    if replicas > 1:
        from_replica(order[1]).start()
    for kind in range(kinds):
        for group in range(groups):
            keep_left(kind, group).start()
            for peer in range(3):
                hand_left(kind, group, peer).start()

    for at, turn in enumerate(order):
        later = order[at + 1] if at + 1 < replicas else None
        slot = at % 2
        if later is not None:
            from_replica(later).wait_recv()
            over(later).start()
            direct(later).start()
            if at + 2 < replicas:
                from_replica(later).wait_send()
                from_replica(order[at + 2]).start()
        load_block(turn, slot).wait()
        if at > 1:
            store_block(order[at - 2], slot).wait()

        def products(step, carry, at=at, slot=slot):
            cols = pl.ds(pl.multiple_of(step * CHUNK, CHUNK), CHUNK)
            high = pl.ds(pl.multiple_of(part + step * CHUNK, CHUNK), CHUNK)
            if at == 0:
                load_weight(0, step).wait()
                load_weight(1, step).wait()
            gate = dot(block_ref[slot], weight_ref[:, cols])
            up = dot(block_ref[slot], weight_ref[:, high])
            gate_up_ref[slot, :, cols] = gate.astype(BF)
            gate_up_ref[slot, :, high] = up.astype(BF)
            hidden_ref[:, cols] = (gate * jax.nn.sigmoid(gate) * up).astype(BF)
            return carry

        lax.fori_loop(0, steps, products, 0)
        store_block(turn, slot).start()
        if later is not None:
            over(later).wait_recv()
            relay(later).start()

        @pl.when(shard == owner)
        def _(at=at, turn=turn, slot=slot):
            if at > 1:
                keep_hidden(order[at - 2], slot).wait()
                for peer in range(3):
                    hand_hidden(order[at - 2], slot, peer).wait_send()

            def turn_over(device, carry):
                cols = pl.ds(pl.multiple_of(first_col + device * ff_rows, ff_rows), ff_rows)
                turned_ref[slot, device] = hidden_ref[:, cols].T
                return carry

            lax.fori_loop(0, shards, turn_over, 0)
            keep_hidden(turn, slot).start()
            for peer in range(3):
                hand_hidden(turn, slot, peer).start()

        slice_cols = pl.ds(pl.multiple_of(replica * slice_rows, slice_rows), slice_rows)
        left_rows_ref[:, tokens(turn)] = block_ref[slot, :, slice_cols].T
        if later is not None:
            direct(later).wait_recv()
            relay(later).wait_recv()
            load_block(later, 1 - slot).start()

    for at in range(max(0, replicas - 2), replicas):
        store_block(order[at], at % 2).wait()

        @pl.when(shard == owner)
        def _(at=at):
            keep_hidden(order[at], at % 2).wait()
            for peer in range(3):
                hand_hidden(order[at], at % 2, peer).wait_send()

    for turn in range(replicas):
        for peer in range(3):

            @pl.when(peers[peer] == owner)
            def _(turn=turn, peer=peer):
                hand_hidden(turn, 0, peer).wait_recv()

        if turn:
            over(turn).wait_send()
            direct(turn).wait_send()
            relay(turn).wait_send()
        if turn and turn == order[-1]:
            from_replica(turn).wait_send()
    for kind in range(kinds):
        for group in range(groups):
            keep_left(kind, group).wait()
            for peer in range(3):
                hand_left(kind, group, peer).wait()


def call_prepare(normed_two, normed, attended, gate_up_part, slices, collective):
    rows, width = normed_two.shape
    shards, replicas = lax.axis_size("shard"), lax.axis_size("replica")
    part = gate_up_part.shape[1] // 2
    every = rows * shards
    slice_rows = width // replicas
    sub_rows = slice_rows // shards
    ff_rows = part // replicas
    lefts = jnp.stack([normed.T, attended.T]).reshape(2, replicas, shards, sub_rows, rows)
    vmem, anywhere = pl.BlockSpec(memory_space=pltpu.VMEM), pl.BlockSpec(memory_space=pl.ANY)
    copies = 7 * replicas + 2 * replicas * 3
    outs = pl.pallas_call(
        functools.partial(prepare_kernel, len(slices)),
        out_shape=[
            jax.ShapeDtypeStruct((replicas, every, width), BF),
            jax.ShapeDtypeStruct((replicas * every, 2 * part), BF),
            jax.ShapeDtypeStruct((ff_rows, replicas * every), BF),
            jax.ShapeDtypeStruct((2, replicas, sub_rows, every), BF),
            jax.ShapeDtypeStruct((slice_rows, replicas * every), BF),
        ],
        in_specs=[vmem, vmem, anywhere] + [anywhere] * len(slices),
        out_specs=[anywhere] * 4 + [vmem],
        scratch_shapes=[
            pltpu.VMEM(gate_up_part.shape, BF),
            pltpu.VMEM((2, every, width), BF),
            pltpu.VMEM((2, every, 2 * part), BF),
            pltpu.VMEM((every, part), BF),
            pltpu.VMEM((2, shards, ff_rows, every), BF),
            pltpu.SemaphoreType.DMA((2, part // CHUNK)),
            pltpu.SemaphoreType.DMA((3, 2)),
            pltpu.SemaphoreType.DMA((2 * replicas,)),
            pltpu.SemaphoreType.DMA((copies,)),
            pltpu.SemaphoreType.DMA((copies,)),
        ],
        compiler_params=pltpu.CompilerParams(
            collective_id=collective, has_side_effects=True, vmem_limit_bytes=VMEM_LIMIT
        ),
        name="prepare",
    )(normed_two, lefts, gate_up_part, *slices)
    _, gate_up_all, hidden_rows, lefts, left_rows = outs
    return gate_up_all, hidden_rows, lefts.reshape(2, replicas * sub_rows, every), left_rows


def gather_kernel(mine_ref, gathered_hbm, send_sems, recv_sems):
    shard, beside, across, _ = slice_peers()
    replicas = lax.axis_size("replica")
    rows = mine_ref.shape[0]

    def remote(owner, turn, at, device):
        place = gathered_hbm.at[turn, pl.ds(pl.multiple_of(owner * rows, rows), rows)]
        return pltpu.make_async_remote_copy(
            place, place, send_sems.at[at], recv_sems.at[at], device_id={"shard": device}, device_id_type=MESH
        )

    own_rows = pl.ds(pl.multiple_of(shard * rows, rows), rows)
    slice_barrier((beside, across), range(1, replicas))
    order = turn_order(replicas)[1:]
    spread_copies = [
        replica_copy(mine_ref, gathered_hbm.at[turn, own_rows], turn, send_sems, recv_sems, 3 * replicas)
        for turn in order
    ]
    over = [remote(shard, turn, 3 * turn, across) for turn in order]
    direct = [remote(shard, turn, 3 * turn + 1, beside) for turn in order]
    relays = [remote(across, turn, 3 * turn + 2, beside) for turn in order]
    spread_copies[0].start()
    for at in range(replicas - 1):
        spread_copies[at].wait_recv()
        over[at].start()
        direct[at].start()
        spread_copies[at].wait_send()
        if at + 2 < replicas:
            spread_copies[at + 1].start()
        if at:
            over[at - 1].wait_recv()
            relays[at - 1].start()
    over[-1].wait_recv()
    relays[-1].start()
    for copy in direct + relays:
        copy.wait_recv()
    for copy in over + direct + relays:
        copy.wait_send()


def call_gather(section, mine, collective):
    replicas, shards = lax.axis_size("replica"), lax.axis_size("shard")
    rows, width = mine.shape
    return pl.pallas_call(
        gated(section, gather_kernel),
        out_shape=jax.ShapeDtypeStruct((replicas, shards * rows, width), BF),
        in_specs=[pl.BlockSpec(memory_space=pltpu.VMEM)],
        out_specs=pl.BlockSpec(memory_space=pl.ANY),
        scratch_shapes=[
            pltpu.SemaphoreType.DMA((4 * replicas,)),
            pltpu.SemaphoreType.DMA((4 * replicas,)),
        ],
        compiler_params=pltpu.CompilerParams(
            collective_id=collective, has_side_effects=True, vmem_limit_bytes=VMEM_LIMIT
        ),
        name="gather",
    )(mine)


def on_device(
    tokens_in,
    positions,
    attn_gain,
    qkv_weight,
    out_weight,
    mlp_gain,
    gate_up_weight,
    down_weight,
    cotangent,
):
    sections = lax.axis_size("section")
    rows, width = tokens_in.shape
    up_steps = [(at, at + 1) for at in range(sections - 1)]
    down_steps = [(at + 1, at) for at in range(sections - 1)]

    cosine, sine = rope_tables(positions)
    allowed = visible(positions)

    qkv_full, out_full, gate_up_part = call_weights(qkv_weight[0], out_weight[0], gate_up_weight[0], 3)
    down_part = down_weight[0]

    forward = []
    state = tokens_in
    for section in range(sections):
        middle, normed_two, normed, rotated, attended = call_attend_forward(
            section, state, attn_gain, mlp_gain, cosine, sine, allowed, qkv_full, out_full
        )
        block_out, normed_two_slice, gate_up = call_feed(
            section, False, (normed_two, middle, gate_up_part, down_part), 8 + section
        )
        forward.append((state, middle, rotated, gate_up, normed_two_slice, normed_two, normed, attended, block_out))
        if section + 1 < sections:
            state = lax.ppermute(block_out, "section", up_steps)
        if section + 2 == sections:
            held, _ = lax.optimization_barrier((cotangent, block_out))
            early = call_gather(sections - 1, held, 7)
            state, early = lax.optimization_barrier((state, early))

    def pick(values):
        chosen = values[-1]
        for section in range(sections - 1):
            chosen = jnp.where(lax.axis_index("section") == section, values[section], chosen)
        return chosen

    normed_two, normed, attended, block_out = [pick(values) for values in list(zip(*forward))[5:]]
    backward = []
    upstream = cotangent
    for section in reversed(range(sections)):
        state, middle, rotated, gate_up = forward[section][:4]
        grad_normed_two, upstream_slice, _, odd = call_feed(
            section, True, (upstream, gate_up, down_part, gate_up_part), 8 + sections + section
        )
        grad_in, grad_low, grad_branch, grad_projected, gains = call_attend_backward(
            section, grad_normed_two, upstream, middle, state, rotated,
            attn_gain, mlp_gain, cosine, sine, allowed, qkv_full, out_full,
        )
        backward.insert(0, (upstream, upstream_slice, odd, grad_in, grad_branch, grad_projected, gains))
        if section == sections - 1:
            normed_two, normed, attended, grad_low = lax.optimization_barrier(
                (normed_two, normed, attended, grad_low)
            )
        if section > 0:
            upstream = lax.ppermute(grad_low, "section", down_steps)
        if section == sections - 1:
            gate_up_all, hidden_rows, lefts, left_rows = call_prepare(
                normed_two, normed, attended, gate_up_part, [values[4] for values in forward], 6
            )
            upstream, gate_up_all, left_rows, hidden_rows, lefts = lax.optimization_barrier(
                (upstream, gate_up_all, left_rows, hidden_rows, lefts)
            )

    upstream, upstream_slice, odd, grad_in, grad_branch, grad_projected, gains = [
        pick(values) for values in zip(*backward)
    ]
    terms, gains, even = call_attend_grads(grad_projected, grad_branch, lefts, upstream, gains, 4)
    gate_up_grad, down_grad, attend_grad, gains, _ = call_feed_grads(
        left_rows, hidden_rows, terms, gains, upstream_slice, odd, even, early, gate_up_all, down_part, 5
    )
    gate_up_grad = gate_up_grad.astype(F32)
    qkv_cols = grad_projected.shape[1]
    qkv_grad, out_grad = attend_grad[:, :qkv_cols], attend_grad[:, qkv_cols:]
    return (
        block_out[None],
        grad_in[None],
        gains[0][None],
        qkv_grad[None],
        out_grad[None],
        gains[1][None],
        gate_up_grad[None],
        down_grad[None],
    )


def solution(mesh):
    both = ("replica", "shard")
    return jax.shard_map(
        on_device,
        mesh=mesh,
        in_specs=(
            P(both, None),
            P(both),
            P("section", None),
            P("section", "shard", None),
            P("section", "shard", None),
            P("section", None),
            P("section", "shard", None),
            P("section", "shard", None),
            P(both, None),
        ),
        out_specs=(
            P("section", both, None),
            P("section", both, None),
            P("section", None),
            P("section", both, None),
            P("section", both, None),
            P("section", None),
            P("section", both, None),
            P("section", both, None),
        ),
        check_vma=False,
    )
```

```python
import functools

import jax
import jax.numpy as jnp
from jax import lax
from jax.experimental import pallas as pl
from jax.experimental.pallas import tpu as pltpu
from jax.sharding import PartitionSpec as P

HEADS = 32
KV_HEADS = 8
HEAD = 64
SEQ = 64
EPSILON = 1e-05
ROPE_BASE = 500000.0
BF = jnp.bfloat16
F32 = jnp.float32
CONTRACT_LAST = (((1,), (1,)), ((), ()))
CONTRACT_FIRST = (((0,), (0,)), ((), ()))


MESH = pl.DeviceIdType.MESH
VMEM_LIMIT = 60 * 2**20
TILE = 128


def dot(left, right):
    return jnp.dot(left, right, preferred_element_type=F32)


def dot_rows(left, right):
    return lax.dot_general(left, right, CONTRACT_LAST, preferred_element_type=F32)


def dot_tokens(left, right):
    return lax.dot_general(left, right, CONTRACT_FIRST, preferred_element_type=F32)


def rope_tables(seq_pos):
    half_index = jnp.arange(HEAD // 2, dtype=F32)
    frequency = jnp.power(ROPE_BASE, -2.0 * half_index / HEAD)
    angles = seq_pos.astype(F32)[:, None] * frequency[None, :]
    cosine, sine = jnp.cos(angles), jnp.sin(angles)
    return (
        jnp.concatenate([cosine] * 4, 1),
        jnp.concatenate([-sine, sine, -sine, sine], 1),
    )


def visible(seq_pos):
    rows = seq_pos.shape[0]
    row_index = jnp.arange(rows)[:, None]
    col_index = jnp.arange(rows)[None, :]
    same = row_index // SEQ == col_index // SEQ
    seen = (col_index <= row_index) & (row_index - col_index <= seq_pos[:, None])
    return jnp.where(same & seen, 1.0, 0.0).astype(F32)


def lanes(rows):
    return lax.broadcasted_iota(jnp.int32, (rows, TILE), 1)


def swap_halves(tile, lane):
    return jnp.where(lane % HEAD < HEAD // 2, pltpu.roll(tile, TILE - HEAD // 2, 1), pltpu.roll(tile, HEAD // 2, 1))


def spread(tile, odd, lane):
    turned = pltpu.roll(tile, HEAD, 1)
    lower, upper = (turned, tile) if odd else (tile, turned)
    return jnp.concatenate(
        [jnp.where(lane < HEAD, lower, 0.0), jnp.where(lane < HEAD, 0.0, upper)], 0
    ).astype(BF)


def softmax_pair(queries, spread_keys, allowed):
    scores = dot_rows(queries, spread_keys) * HEAD ** (-0.5)
    halves = []
    for side in range(2):
        masked = jnp.where(allowed > 0.5, scores[:, side * TILE : (side + 1) * TILE], -1e30)
        expon = jnp.exp(masked - jnp.max(masked, -1, keepdims=True))
        halves.append(expon / jnp.sum(expon, -1, keepdims=True))
    return halves


def attend_parts(
    state_ref, gain_one_ref, gain_two_ref, cos_ref, sin_ref, allowed_ref, qkv_hbm, out_hbm,
    middle_ref, normed_two_ref, rotated_ref, lefts_ref,
    qkv_ref, out_ref, normed_ref, attended_ref, sems,
):
    rows, width = state_ref.shape
    cols = qkv_hbm.shape[1]
    step = 512
    rope_cols = (HEADS + KV_HEADS) * HEAD

    def qkv_copy(at):
        return pltpu.make_async_copy(qkv_hbm.at[:, pl.ds(at, step)], qkv_ref.at[:, pl.ds(at, step)], sems.at[at // step])

    def out_copy(at):
        return pltpu.make_async_copy(
            out_hbm.at[:, pl.ds(at, step)], out_ref.at[:, pl.ds(at, step)], sems.at[(cols + at) // step]
        )

    def begin():
        for at in range(0, cols, step):
            qkv_copy(at).start()
        state = state_ref[...].astype(F32)
        inverse = lax.rsqrt(jnp.mean(state * state, -1, keepdims=True) + EPSILON)
        normed_ref[...] = (state * inverse * gain_one_ref[...]).astype(BF)

    def project(at):
        qkv_copy(at).wait()
        lane = lanes(rows)
        projected = dot(normed_ref[...], qkv_ref[:, at : at + step])
        for tile_at in range(0, step, TILE):
            tile = projected[:, tile_at : tile_at + TILE]
            if at + tile_at < rope_cols:
                tile = tile * cos_ref[...] + swap_halves(tile, lane) * sin_ref[...]
            rotated_ref[:, at + tile_at : at + tile_at + TILE] = tile.astype(BF)

    def attend(group):
        lane = lanes(rows)
        key_at = width + group // 2 * TILE
        value_at = rope_cols + group // 2 * TILE
        keys = spread(rotated_ref[:, key_at : key_at + TILE].astype(F32), group % 2, lane)
        values = spread(rotated_ref[:, value_at : value_at + TILE].astype(F32), group % 2, lane)
        for pair in range(2):
            at = (group * 2 + pair) * TILE
            halves = softmax_pair(rotated_ref[:, at : at + TILE], keys, allowed_ref[...])
            probs = jnp.concatenate([half.astype(BF) for half in halves], 1)
            attended_ref[:, at : at + TILE] = dot(probs, values).astype(BF)

    def load_out():
        for at in range(0, width, step):
            out_copy(at).start()

    def leave(at):
        out_copy(at).wait()
        middle = state_ref[:, at : at + step].astype(F32) + dot(attended_ref[...], out_ref[:, at : at + step])
        middle_ref[:, at : at + step] = middle

    def finish():
        middle = middle_ref[...]
        inverse = lax.rsqrt(jnp.mean(middle * middle, -1, keepdims=True) + EPSILON)
        normed_two_ref[...] = (middle * inverse * gain_two_ref[...]).astype(BF)
        lefts_ref[0] = normed_ref[...].T
        lefts_ref[1] = attended_ref[...].T

    first = [begin] + [functools.partial(project, at) for at in range(0, cols, step)]
    first += [functools.partial(attend, group) for group in range(KV_HEADS)]
    second = [functools.partial(leave, at) for at in range(0, width, step)] + [finish]
    return first, load_out, second


def attend_forward(*refs):
    first, load_out, second = attend_parts(*refs)
    first[0]()
    load_out()
    for part in first[1:] + second:
        part()


def attend_backward(
    rounds, grad_ref, upstream_ref, middle_ref, state_ref, rotated_ref,
    gain_one_ref, gain_two_ref, cos_ref, sin_ref, allowed_ref, qkv_hbm, out_hbm,
    grad_state_ref, grad_low_ref, grad_projected_ref, gain_terms_ref, branch_hbm,
    qkv_ref, out_ref, grad_branch_ref, grad_out_ref, middle_grad_ref, sems, keep_sems, send_sems, recv_sems,
):
    rows, width = middle_ref.shape
    cols = qkv_hbm.shape[1]
    step = 512
    steps = width // step
    out_copies = [
        pltpu.make_async_copy(out_hbm.at[pl.ds(at * step, step)], out_ref.at[pl.ds(at * step, step)], sems.at[at])
        for at in range(steps)
    ]
    copies = [
        pltpu.make_async_copy(
            qkv_hbm.at[pl.ds(at * step, step)], qkv_ref.at[pl.ds(at * step, step)], sems.at[steps + at]
        )
        for at in range(steps)
    ]
    for copy in out_copies + copies:
        copy.start()
    shard, beside, across, _ = slice_peers()
    slice_barrier((beside, across))

    def branch_rows(owner, at):
        return branch_hbm.at[at, pl.ds(pl.multiple_of(owner * rows, rows), rows)]

    def remote(source, owner, at, kind, device):
        return pltpu.make_async_remote_copy(
            source, branch_rows(owner, at), send_sems.at[kind, at], recv_sems.at[kind, at],
            device_id={"shard": device}, device_id_type=MESH,
        )

    branch = [grad_branch_ref.at[:, pl.ds(at * step, step)] for at in range(steps)]
    over = [remote(branch[at], shard, at, 0, across) for at in range(steps)]
    direct = [remote(branch[at], shard, at, 1, beside) for at in range(steps)]
    relays = [remote(branch_rows(across, at), across, at, 2, beside) for at in range(steps)]
    keeps = [pltpu.make_async_copy(branch[at], branch_rows(shard, at), keep_sems.at[at]) for at in range(steps)]

    def norm_back(grad, values, gain):
        inverse = lax.rsqrt(jnp.mean(values * values, -1, keepdims=True) + EPSILON)
        normal = values * inverse
        term = jnp.sum(grad * normal, 0, keepdims=True)
        scaled = grad * gain
        return inverse * (scaled - normal * jnp.mean(scaled * normal, -1, keepdims=True)), term

    upstream = upstream_ref[...].astype(F32)
    back, term = norm_back(grad_ref[...], middle_ref[...], gain_two_ref[...])
    gain_terms_ref[1:2, :] = term
    middle_grad_ref[...] = upstream + back
    grad_branch_ref[...] = middle_grad_ref[...].astype(BF)
    for copy in over + direct + keeps:
        copy.start()
    for at in range(steps):
        out_copies[at].wait()
        grad_out_ref[:, at * step : (at + 1) * step] = dot_rows(
            grad_branch_ref[...], out_ref[at * step : (at + 1) * step, :]
        ).astype(BF)
    lane = lanes(rows)
    cosine, sine, allowed = cos_ref[...], sin_ref[...], allowed_ref[...]
    rope_cols = (HEADS + KV_HEADS) * HEAD
    scale = HEAD ** (-0.5)

    def unrotate(tile):
        return tile * cosine - swap_halves(tile, lane) * sine

    def group_step(group_pair, carry):
        key_at = pl.multiple_of(width + group_pair * TILE, TILE)
        value_at = pl.multiple_of(rope_cols + group_pair * TILE, TILE)
        sums = []
        for odd in range(2):
            keys = spread(rotated_ref[:, pl.ds(key_at, TILE)].astype(F32), odd, lane)
            values = spread(rotated_ref[:, pl.ds(value_at, TILE)].astype(F32), odd, lane)
            key_sum = jnp.zeros((rows, TILE), F32)
            value_sum = jnp.zeros((rows, TILE), F32)
            for pair in range(2):
                at = pl.multiple_of(((group_pair * 2 + odd) * 2 + pair) * TILE, TILE)
                queries = rotated_ref[:, pl.ds(at, TILE)]
                grad_out = grad_out_ref[:, pl.ds(at, TILE)]
                halves = softmax_pair(queries, keys, allowed)
                grad_probs = dot_rows(grad_out, values)
                grad_halves = []
                for side in range(2):
                    grad = grad_probs[:, side * TILE : (side + 1) * TILE]
                    row_dot = jnp.sum(halves[side] * grad, -1, keepdims=True)
                    grad_halves.append((halves[side] * (grad - row_dot)).astype(BF))
                grad_scores = jnp.concatenate(grad_halves, 1)
                probs = jnp.concatenate([half.astype(BF) for half in halves], 1)
                grad_projected_ref[:, pl.ds(at, TILE)] = unrotate(dot(grad_scores, keys) * scale).astype(BF)
                key_terms = dot_tokens(grad_scores, queries)
                value_terms = dot_tokens(probs, grad_out)
                key_sum += jnp.where(lane < HEAD, key_terms[:rows], key_terms[rows:])
                value_sum += jnp.where(lane < HEAD, value_terms[:rows], value_terms[rows:])
            sums.append((key_sum + pltpu.roll(key_sum, HEAD, 1), value_sum + pltpu.roll(value_sum, HEAD, 1)))
        keys_grad = jnp.where(lane < HEAD, sums[0][0], sums[1][0]) * scale
        grad_projected_ref[:, pl.ds(key_at, TILE)] = unrotate(keys_grad).astype(BF)
        grad_projected_ref[:, pl.ds(value_at, TILE)] = jnp.where(
            lane < HEAD, sums[0][1], sums[1][1]
        ).astype(BF)
        return carry

    lax.fori_loop(0, KV_HEADS // 2, group_step, 0)
    for at in range(steps):
        over[at].wait_recv()
        relays[at].start()
    for at in range(steps):
        copies[at].wait()
        grad_state_ref[:, at * step : (at + 1) * step] = dot_rows(
            grad_projected_ref[...], qkv_ref[at * step : (at + 1) * step, :]
        )
    state = state_ref[...].astype(F32)
    back, term = norm_back(grad_state_ref[...], state, gain_one_ref[...])
    gain_terms_ref[0:1, :] = term
    grad_state = middle_grad_ref[...] + back
    grad_low = grad_state.astype(BF)
    grad_low_ref[...] = grad_low
    grad_state_ref[...] = grad_low.astype(F32) if rounds else grad_state
    for copy in direct + relays:
        copy.wait()
    for copy in over:
        copy.wait_send()
    for copy in keeps:
        copy.wait()


def gated(section, body):
    def kernel(*refs):
        @pl.when(lax.axis_index("section") == section)
        def _():
            body(*refs)

    return kernel


def attend_shapes(rows, width, cols):
    return [
        jax.ShapeDtypeStruct((rows, width), F32),
        jax.ShapeDtypeStruct((rows, width), BF),
        jax.ShapeDtypeStruct((rows, cols), BF),
        jax.ShapeDtypeStruct((2, width, rows), BF),
    ], [
        pltpu.VMEM((width, cols), BF),
        pltpu.VMEM((width, width), BF),
        pltpu.VMEM((rows, width), BF),
        pltpu.VMEM((rows, width), BF),
        pltpu.SemaphoreType.DMA(((cols + width) // 512,)),
    ]


def call_attend_forward(section, *operands):
    rows, width = operands[0].shape
    out_shape, scratch = attend_shapes(rows, width, operands[6].shape[1])
    specs = [pl.BlockSpec(memory_space=pltpu.VMEM)] * 6 + [pl.BlockSpec(memory_space=pl.ANY)] * 2
    return pl.pallas_call(
        gated(section, attend_forward),
        out_shape=out_shape,
        in_specs=specs,
        out_specs=[pl.BlockSpec(memory_space=pltpu.VMEM)] * 4,
        scratch_shapes=scratch,
        compiler_params=pltpu.CompilerParams(vmem_limit_bytes=VMEM_LIMIT),
        name="attend_forward",
    )(*operands)


def call_attend_backward(section, collective, *operands):
    rows, width = operands[2].shape
    cols = operands[10].shape[1]
    steps = width // 512
    every = lax.axis_size("shard") * rows
    vmem, anywhere = pl.BlockSpec(memory_space=pltpu.VMEM), pl.BlockSpec(memory_space=pl.ANY)
    return pl.pallas_call(
        gated(section, functools.partial(attend_backward, section > 0)),
        out_shape=(
            jax.ShapeDtypeStruct((rows, width), F32),
            jax.ShapeDtypeStruct((rows, width), BF),
            jax.ShapeDtypeStruct((rows, cols), BF),
            jax.ShapeDtypeStruct((2, width), F32),
            jax.ShapeDtypeStruct((steps, every, 512), BF),
        ),
        in_specs=[vmem] * 10 + [anywhere] * 2,
        out_specs=[vmem] * 4 + [anywhere],
        scratch_shapes=[
            pltpu.VMEM((width, cols), BF),
            pltpu.VMEM((width, width), BF),
            pltpu.VMEM((rows, width), BF),
            pltpu.VMEM((rows, width), BF),
            pltpu.VMEM((rows, width), F32),
            pltpu.SemaphoreType.DMA((2 * steps,)),
            pltpu.SemaphoreType.DMA((steps,)),
            pltpu.SemaphoreType.DMA((3, steps)),
            pltpu.SemaphoreType.DMA((3, steps)),
        ],
        compiler_params=pltpu.CompilerParams(
            collective_id=collective, has_side_effects=True, vmem_limit_bytes=VMEM_LIMIT
        ),
        name="attend_backward",
    )(*operands)


def start_own(copies):
    for section, copy in enumerate(copies):

        @pl.when(lax.axis_index("section") == section)
        def _(copy=copy):
            copy.start()


def slice_peers():
    shard = lax.axis_index("shard")
    chip, core = shard // 2, shard % 2
    return shard, chip * 2 + (1 - core), (1 - chip) * 2 + core, (1 - chip) * 2 + (1 - core)


def slice_barrier(devices, turns=()):
    barrier = pltpu.get_barrier_semaphore()
    replicas = lax.axis_size("replica")
    for device in devices:
        pl.semaphore_signal(barrier, inc=1, device_id={"shard": device}, device_id_type=MESH)
    for turn in turns:
        target = lax.rem(lax.axis_index("replica") + turn, replicas)
        pl.semaphore_signal(barrier, inc=1, device_id={"replica": target}, device_id_type=MESH)
    pl.semaphore_wait(barrier, len(devices) + len(turns))


def replica_copy(source, target, turn, send_sems, recv_sems, base):
    replicas = lax.axis_size("replica")
    device = lax.rem(lax.axis_index("replica") + replicas - turn, replicas)
    return pltpu.make_async_remote_copy(
        source, target, send_sems.at[base + turn], recv_sems.at[base + turn],
        device_id={"replica": device}, device_id_type=MESH,
    )


CHUNK = 512


def feed_kernel(backward, rows, *refs):
    if backward:
        (mine_ref, gate_up_hbm, first_hbm, second_hbm, result_ref, all_hbm, others_hbm,
         mid_ref, all_ref, gate_up_ref, first_ref, second_ref, part_ref, take_ref, sent_ref, land_ref, own_ref,
         own_take_ref, load_sems, keep_sems, hold_sems, send_sems, recv_sems) = refs
    else:
        (mine_ref, middle_hbm, first_hbm, second_hbm, result_ref, all_hbm, gate_up_hbm,
         mid_ref, all_ref, gate_up_ref, first_ref, second_ref, part_ref, take_ref, sent_ref, land_ref, own_ref,
         own_take_ref, middle_ref, load_sems, keep_sems, hold_sems, send_sems, recv_sems) = refs
    shard, beside, across, _ = slice_peers()
    chip, core = shard // 2, shard % 2
    half = rows // 2
    parts, spans, _, piece, span_cols = part_ref.shape
    block = 2 * piece
    width = all_ref.shape[1]
    ff = first_ref.shape[0] if backward else second_ref.shape[0]
    first_steps = ff // CHUNK

    def load_first(at):
        if backward:
            place = (pl.ds(pl.multiple_of(at * CHUNK, CHUNK), CHUNK), slice(None))
            return [pltpu.make_async_copy(first_hbm.at[place], first_ref.at[place], load_sems.at[0, at])]
        places = [
            (slice(None), pl.ds(pl.multiple_of(side * ff + at * CHUNK, CHUNK), CHUNK)) for side in range(2)
        ]
        return [
            pltpu.make_async_copy(first_hbm.at[place], first_ref.at[place], load_sems.at[side, at])
            for side, place in enumerate(places)
        ]

    def load_second(at):
        span = pl.ds(pl.multiple_of(at * span_cols, span_cols), span_cols)
        place = (span, slice(None)) if backward else (slice(None), span)
        return pltpu.make_async_copy(second_hbm.at[place], second_ref.at[place], load_sems.at[2, at])

    load_extra = []
    if backward:
        for at in range(2 * lax.axis_size("shard")):
            group, part, owner = at // 4, at // 2 % 2, at % 2
            source = pl.ds(at * half, half)
            target = pl.ds(group * 2 * rows + owner * rows + part * half, half)
            load_extra.append(pltpu.make_async_copy(gate_up_hbm.at[source], gate_up_ref.at[target], hold_sems.at[at]))
    else:
        load_extra.append(pltpu.make_async_copy(middle_hbm, middle_ref, hold_sems.at[0]))
    if backward:
        for copy in load_extra:
            copy.start()
    for at in range(first_steps):
        for copy in load_first(at):
            copy.start()
    for at in range(spans):
        load_second(at).start()
    if not backward:
        load_extra[0].start()

    def remote(source, target, at, device):
        return pltpu.make_async_remote_copy(
            source, target, send_sems.at[at], recv_sems.at[at], device_id={"shard": device}, device_id_type=MESH
        )

    def place_of(owner, part):
        start = part * block + (owner % 2) * piece if parts == 2 else (owner % 2) * piece + part * half
        return pl.ds(pl.multiple_of((owner // 2) * 2 * rows + start, half), half)

    def owned(owner, part):
        return all_ref.at[place_of(owner, part)]

    turns = range(1, lax.axis_size("replica"), 2) if backward else ()
    slice_barrier((beside, across), turns)

    def across_copy(part):
        return remote(owned(shard, part), owned(shard, part), part, across)

    def relay(part):
        return remote(owned(across, part), owned(across, part), 4 + part, beside)

    beside_copies = [remote(owned(shard, part), owned(shard, part), 2 + part, beside) for part in range(2)]
    for part in range(2):
        all_ref[place_of(shard, part), :] = mine_ref[part * half : (part + 1) * half, :]
        across_copy(part).start()
    for copy in beside_copies:
        copy.start()
    base = 6 + (2 * parts + 1) * spans
    spread_copies = [
        replica_copy(mine_ref, others_hbm.at[lax.axis_index("replica")], turn, send_sems, recv_sems, base)
        for turn in turns
    ]
    for copy in spread_copies:
        copy.start()

    def first_product(start, count, waits):
        span = pl.ds(pl.multiple_of(start, count), count)

        def step(at, carry):
            cols = pl.ds(pl.multiple_of(at * CHUNK, CHUNK), CHUNK)
            high = pl.ds(pl.multiple_of(ff + at * CHUNK, CHUNK), CHUNK)
            if waits:
                for copy in load_first(at):
                    copy.wait()
            if backward:
                grad_hidden = dot_rows(all_ref[span, :], first_ref[cols, :])
                gate = gate_up_ref[span, cols].astype(F32)
                up = gate_up_ref[span, high].astype(F32)
                sigmoid = jax.nn.sigmoid(gate)
                mid_ref[span, cols] = (grad_hidden * up * sigmoid * (1.0 + gate * (1.0 - sigmoid))).astype(BF)
                mid_ref[span, high] = (grad_hidden * gate * sigmoid).astype(BF)
            else:
                gate = dot(all_ref[span, :], first_ref[:, cols])
                up = dot(all_ref[span, :], first_ref[:, high])
                gate_up_ref[span, cols] = gate.astype(BF)
                gate_up_ref[span, high] = up.astype(BF)
                mid_ref[span, cols] = (gate * jax.nn.sigmoid(gate) * up).astype(BF)
            return carry

        lax.fori_loop(0, first_steps, step, 0)

    def second_product(start, count, at, store):
        span = pl.ds(pl.multiple_of(start, count), count)

        def step(inner, carry):
            cols = pl.ds(pl.multiple_of(at * span_cols + inner * CHUNK, CHUNK), CHUNK)
            if backward:
                partial = dot_rows(mid_ref[span, :], second_ref[cols, :])
            else:
                partial = dot(mid_ref[span, :], second_ref[:, cols])
            store(pl.ds(pl.multiple_of(inner * CHUNK, CHUNK), CHUNK), partial.astype(BF))
            return carry

        lax.fori_loop(0, span_cols // CHUNK, step, 0)

    def give(part, at):
        return remote(part_ref.at[part, at, 1 - core], take_ref.at[part, at], 6 + part * spans + at, beside)

    def cross(part, at):
        return remote(sent_ref.at[part, at], land_ref.at[part, at], 6 + (parts + part) * spans + at, across)

    def give_own(at):
        return remote(own_ref.at[at, 1 - core], own_take_ref.at[at], 6 + 2 * parts * spans + at, beside)

    def pass_on(part, at):
        give(part, at).wait_recv()
        sent_ref[part, at] = (part_ref[part, at, core].astype(F32) + take_ref[part, at].astype(F32)).astype(BF)
        cross(part, at).start()

    own_start = chip * 2 * rows
    other_start = (1 - chip) * 2 * rows
    stores = []
    for copy in beside_copies:
        copy.wait_recv()
    if backward:
        for copy in load_extra:
            copy.wait()
    first_product(own_start, 2 * rows, True)
    if not backward:
        own_place = pl.ds(pl.multiple_of(own_start, 2 * rows), 2 * rows)
        stores.append(pltpu.make_async_copy(gate_up_ref.at[own_place], gate_up_hbm.at[own_place], keep_sems.at[1]))
        stores[-1].start()

    def store_part(part):
        place = pl.ds(pl.multiple_of(other_start + part * block, block), block)
        return pltpu.make_async_copy(gate_up_ref.at[place], gate_up_hbm.at[place], keep_sems.at[2 + part])

    def arrive(part):
        across_copy(part).wait_recv()
        relay(part).start()

    if parts == 1:
        for part in range(2):
            arrive(part)

    def other_part(part, carry):
        if parts == 1:
            for late in range(2):
                relay(late).wait_recv()
        else:
            arrive(part)
            relay(part).wait_recv()
        start = other_start + part * block
        first_product(start, block, False)
        if not backward:
            store_part(part).start()

        def span_step(at, inner):
            @pl.when(part == 0)
            def _():
                load_second(at).wait()

            def store(cols, partial):
                part_ref[part, at, 0, :, cols] = partial[:piece]
                part_ref[part, at, 1, :, cols] = partial[piece:]

            second_product(start, block, at, store)
            give(part, at).start()

            @pl.when(at > 0)
            def _():
                pass_on(part, at - 1)

            return inner

        lax.fori_loop(0, spans, span_step, 0)
        pass_on(part, spans - 1)
        return carry

    lax.fori_loop(0, parts, other_part, 0)
    if not backward:
        stores += [store_part(part) for part in range(parts)]
    for owner in range(lax.axis_size("shard")):
        for part in range(2):
            at = owner * 2 + part
            copy = pltpu.make_async_copy(
                all_ref.at[place_of(owner, part)], all_hbm.at[pl.ds(owner * rows + part * half, half)],
                keep_sems.at[4 + at],
            )
            copy.start()
            stores.append(copy)

    def own_step(at, carry):
        def store(cols, partial):
            for part in range(parts):
                for owner in range(2):
                    first_row = part * block + owner * piece
                    own_ref[at, owner, part * piece : (part + 1) * piece, cols] = partial[first_row : first_row + piece]

        second_product(own_start, 2 * rows, at, store)
        give_own(at).start()
        return carry

    lax.fori_loop(0, spans, own_step, 0)
    if not backward:
        load_extra[0].wait()
    for at in range(spans):
        give_own(at).wait_recv()
        cols = slice(at * span_cols, (at + 1) * span_cols)
        for part in range(parts):
            cross(part, at).wait_recv()
            place = slice(part * piece, (part + 1) * piece)
            total = (
                own_ref[at, core, place].astype(F32)
                + own_take_ref[at, place].astype(F32)
                + land_ref[part, at].astype(F32)
            )
            if backward:
                result_ref[place, cols] = total
            else:
                result_ref[place, cols] = (middle_ref[place, cols] + total).astype(BF)
    for part in range(2):
        beside_copies[part].wait_send()
        across_copy(part).wait_send()
        relay(part).wait_send()
    for copy in spread_copies + stores:
        copy.wait()
    for at in range(spans):
        give_own(at).wait_send()
        for part in range(parts):
            give(part, at).wait_send()
            cross(part, at).wait_send()


def call_feed(section, backward, operands, collective):
    first, second = operands[-2], operands[-1]
    rows, width = operands[0].shape
    shards, replicas = lax.axis_size("shard"), lax.axis_size("replica")
    ff = first.shape[0] if backward else second.shape[0]
    every = shards * rows
    parts, span_cols = (1, CHUNK) if backward else (2, 2 * CHUNK)
    spans, piece_rows = width // span_cols, rows // parts
    vmem, anywhere = pl.BlockSpec(memory_space=pltpu.VMEM), pl.BlockSpec(memory_space=pl.ANY)
    out_shape = [
        jax.ShapeDtypeStruct((rows, width), F32 if backward else BF),
        jax.ShapeDtypeStruct((every, width), BF),
        jax.ShapeDtypeStruct((replicas, rows, width) if backward else (every, 2 * ff), BF),
    ]
    copies = 6 + (2 * parts + 1) * spans + (replicas if backward else 0)
    piece = pltpu.VMEM((parts, spans, piece_rows, span_cols), BF)
    scratch = [
        pltpu.VMEM((every, 2 * ff if backward else ff), BF),
        pltpu.VMEM((every, width), BF),
        pltpu.VMEM((every, 2 * ff), BF),
        pltpu.VMEM(first.shape, BF),
        pltpu.VMEM(second.shape, BF),
        pltpu.VMEM((parts, spans, 2, piece_rows, span_cols), BF),
        piece,
        piece,
        piece,
        pltpu.VMEM((spans, 2, rows, span_cols), BF),
        pltpu.VMEM((spans, rows, span_cols), BF),
    ]
    if not backward:
        scratch.append(pltpu.VMEM((rows, width), F32))
    scratch += [
        pltpu.SemaphoreType.DMA((3, max(ff // CHUNK, spans))),
        pltpu.SemaphoreType.DMA((4 + 2 * shards,)),
        pltpu.SemaphoreType.DMA((2 * shards,)),
        pltpu.SemaphoreType.DMA((copies,)),
        pltpu.SemaphoreType.DMA((copies,)),
    ]
    return pl.pallas_call(
        gated(section, functools.partial(feed_kernel, backward, rows)),
        out_shape=out_shape,
        in_specs=[vmem] + [anywhere] * 3,
        out_specs=[vmem] + [anywhere] * 2,
        scratch_shapes=scratch,
        compiler_params=pltpu.CompilerParams(
            collective_id=collective, has_side_effects=True, vmem_limit_bytes=VMEM_LIMIT
        ),
        name="feed_backward" if backward else "feed_forward",
    )(*operands)


def weights_kernel(
    qkv_ref, out_ref, gate_up_ref, state_ref, gain_one_ref, gain_two_ref, cos_ref, sin_ref, allowed_ref,
    qkv_full, out_full, gate_up_part, middle_ref, normed_two_ref, rotated_ref, lefts_ref,
    qkv_hold, out_hold, gate_up_hold, qkv_work, out_work, normed_ref, attended_ref, work_sems,
    local_sems, send_sems, recv_sems,
):
    shard, replica = lax.axis_index("shard"), lax.axis_index("replica")
    chip, core = shard // 2, shard % 2
    beside = {"shard": chip * 2 + (1 - core)}
    across = {"shard": (1 - chip) * 2 + core}
    diagonal = {"shard": (1 - chip) * 2 + (1 - core)}
    mine = replica % 2
    partner = {"replica": replica + 1 - 2 * mine}
    rows = qkv_ref.shape[0]
    half = rows // 2
    ff = gate_up_ref.shape[1] // 2
    part = gate_up_part.shape[1] // 2

    def remote(source, target, at, device):
        return pltpu.make_async_remote_copy(
            source, target, send_sems.at[at], recv_sems.at[at], device_id=device, device_id_type=MESH
        )

    def span(start, count):
        return pl.ds(pl.multiple_of(start, count), count)

    sides = [pl.ds(side * part, part) for side in range(2)]
    loads = [
        pltpu.make_async_copy(qkv_ref, qkv_hold, local_sems.at[0]),
        pltpu.make_async_copy(out_ref, out_hold, local_sems.at[1]),
    ] + [
        pltpu.make_async_copy(
            gate_up_ref.at[:, span(side * ff + shard * part, part)], gate_up_hold.at[side], local_sems.at[2 + side]
        )
        for side in range(2)
    ]
    own_rows = span(shard * rows, rows)
    stores = [
        pltpu.make_async_copy(qkv_hold, qkv_full.at[own_rows], local_sems.at[4]),
        pltpu.make_async_copy(out_hold, out_full.at[own_rows], local_sems.at[5]),
    ] + [
        pltpu.make_async_copy(gate_up_hold.at[side], gate_up_part.at[own_rows, sides[side]], local_sems.at[6 + side])
        for side in range(2)
    ]
    for copy in loads:
        copy.start()

    pieces = []
    for source, whole, count in ((qkv_ref, qkv_full, 64), (out_ref, out_full, 64)):
        for offset in range(0, half, count):

            def place(owner, part_of, whole=whole, offset=offset, count=count):
                return whole.at[span(owner["shard"] * rows + part_of * half + offset, count)]

            own = source.at[span(mine * half + offset, count)]
            pieces.append((own, place, across, True))
    for offset in range(0, half, 128):
        for side in range(2):
            for device in (across, diagonal):

                def place(owner, part_of, offset=offset, side=side):
                    return gate_up_part.at[
                        span(owner["shard"] * rows + part_of * half + offset, 128), pl.ds(side * part, part)
                    ]

                own = gate_up_ref.at[
                    span(mine * half + offset, 128), span(side * ff + device["shard"] * part, part)
                ]
                pieces.append((own, place, device, False))
    count = len(pieces)
    me = {"shard": shard}
    over = [remote(own, place(me, mine), at, device) for at, (own, place, device, _) in enumerate(pieces)]
    passed = [
        remote(place(device, mine), place(device, mine), count + at, partner)
        for at, (_, place, device, _) in enumerate(pieces)
    ]
    relays = [
        [
            remote(place(across, which), place(across, which), (2 + turn) * count + at, beside)
            if relayed
            else None
            for at, (_, place, _, relayed) in enumerate(pieces)
        ]
        for turn, which in enumerate((mine, 1 - mine))
    ]
    direct = [
        remote(qkv_ref, qkv_full.at[span(shard * rows, rows)], 4 * count, beside),
        remote(out_ref, out_full.at[span(shard * rows, rows)], 4 * count + 1, beside),
    ]
    for side in range(2):
        direct.append(
            remote(
                gate_up_ref.at[:, span(side * ff + beside["shard"] * part, part)],
                gate_up_part.at[span(shard * rows, rows), pl.ds(side * part, part)],
                4 * count + 2 + side,
                beside,
            )
        )

    barrier = pltpu.get_barrier_semaphore()
    for device in (beside, across, diagonal, partner):
        pl.semaphore_signal(barrier, inc=1, device_id=device, device_id_type=MESH)
    pl.semaphore_wait(barrier, 4)

    started = []

    def start(copy):
        copy.start()
        started.append(copy)

    ahead = 3
    for copy in over[:ahead]:
        start(copy)
    for copy in direct:
        start(copy)
    for load, store in zip(loads, stores):
        load.wait()
        store.start()
    first, load_out, second = attend_parts(
        state_ref, gain_one_ref, gain_two_ref, cos_ref, sin_ref, allowed_ref, qkv_full, out_full,
        middle_ref, normed_two_ref, rotated_ref, lefts_ref,
        qkv_work, out_work, normed_ref, attended_ref, work_sems,
    )
    qkv_last = half // 64 - 1
    out_last = qkv_last + half // 64
    arrived = [0]

    def wait_relays(last):
        for at in range(arrived[0], last + 1):
            for copies in relays:
                copies[at].wait_recv()
        arrived[0] = last + 1

    def work(parts):
        @pl.when(lax.axis_index("section") == 0)
        def _():
            for part in parts:
                part()

    ready = list(first)
    for at in range(count + 1):
        if at < count:
            over[at].wait_recv()
            start(passed[at])
            if relays[0][at] is not None:
                start(relays[0][at])
            if at + ahead < count:
                over[at].wait_send()
                started[:] = [copy for copy in started if copy is not over[at]]
                start(over[at + ahead])
        if at > 0:
            passed[at - 1].wait_recv()
            if relays[1][at - 1] is not None:
                start(relays[1][at - 1])
        if at == qkv_last + 2:
            wait_relays(qkv_last)
            direct[0].wait_recv()
            stores[0].wait()
        if at == out_last + 2:
            wait_relays(out_last)
            direct[1].wait_recv()
            stores[1].wait()
            work([load_out])
            ready += second
        if at >= qkv_last + 2:
            work(ready[:3])
            ready = ready[3:]
    work(ready)
    for copy in direct[2:]:
        copy.wait_recv()
    for copy in stores[2:]:
        copy.wait()
    for copy in started:
        copy.wait_send()


def call_weights(qkv_weight, out_weight, gate_up_weight, operands, collective):
    shards = lax.axis_size("shard")
    rows = qkv_weight.shape[0]
    count = 2 * (rows // 128) + rows // 64
    out_shape, scratch = attend_shapes(*operands[0].shape, qkv_weight.shape[1])
    vmem = pl.BlockSpec(memory_space=pltpu.VMEM)
    anywhere = pl.BlockSpec(memory_space=pl.ANY)
    return pl.pallas_call(
        weights_kernel,
        out_shape=[
            jax.ShapeDtypeStruct((shards * rows, qkv_weight.shape[1]), BF),
            jax.ShapeDtypeStruct((shards * rows, out_weight.shape[1]), BF),
            jax.ShapeDtypeStruct((shards * rows, gate_up_weight.shape[1] // shards), BF),
        ] + out_shape,
        in_specs=[anywhere] * 3 + [vmem] * len(operands),
        out_specs=[anywhere] * 3 + [vmem] * len(out_shape),
        scratch_shapes=[
            pltpu.VMEM(qkv_weight.shape, BF),
            pltpu.VMEM(out_weight.shape, BF),
            pltpu.VMEM((2, rows, gate_up_weight.shape[1] // (2 * shards)), BF),
            *scratch,
            pltpu.SemaphoreType.DMA((8,)),
            pltpu.SemaphoreType.DMA((4 * count + 4,)),
            pltpu.SemaphoreType.DMA((4 * count + 4,)),
        ],
        compiler_params=pltpu.CompilerParams(
            collective_id=collective, has_side_effects=True, vmem_limit_bytes=VMEM_LIMIT
        ),
        name="weights",
    )(qkv_weight, out_weight, gate_up_weight, *operands)


def attend_grads_kernel(sections, *refs):
    sources = [refs[at * sections : (at + 1) * sections] for at in range(5)]
    (terms_ref, gain_sum_ref, others_hbm, all_ref, projected_ref, upstream_ref, gains_ref, gains_land_ref,
     lefts_ref, left_ref, load_sems, send_sems, recv_sems) = refs[5 * sections :]
    shard, beside, across, diagonal = slice_peers()
    peers = (across, diagonal, beside)
    replica, replicas = lax.axis_index("replica"), lax.axis_size("replica")
    rows, cols = projected_ref.shape
    every, step = all_ref.shape[1:]
    pieces = cols // step
    sub_rows = terms_ref.shape[1]
    loads = []
    for at, target in enumerate((projected_ref, gains_ref, upstream_ref)):
        loads.append([pltpu.make_async_copy(source, target, load_sems.at[at]) for source in sources[at]])
    loads.append(
        [
            pltpu.make_async_copy(source, all_ref.at[pl.ds(pieces, all_ref.shape[0] - pieces)], load_sems.at[3])
            for source in sources[3]
        ]
    )
    loads.append([pltpu.make_async_copy(source, lefts_ref, load_sems.at[4]) for source in sources[4]])
    for copies in loads:
        start_own(copies)
    slice_barrier(peers, range(1, replicas))
    kinds, groups = lefts_ref.shape[:2]
    left_base = 3 * pieces + 2 * replicas

    def hand_left(kind, group, peer):
        own_cols = pl.ds(pl.multiple_of(shard * rows, rows), rows)
        return pltpu.make_async_remote_copy(
            lefts_ref.at[kind, group, peers[peer]], left_ref.at[kind, group, :, own_cols],
            send_sems.at[left_base + (kind * groups + group) * 3 + peer],
            recv_sems.at[left_base + (kind * groups + group) * 3 + peer],
            device_id={"shard": peers[peer]}, device_id_type=MESH,
        )

    spread_copies = [
        replica_copy(upstream_ref, others_hbm.at[replica], turn, send_sems, recv_sems, 3 * pieces)
        for turn in range(2, replicas, 2)
    ]
    gain_copies = [
        replica_copy(gains_ref, gains_land_ref.at[replica], turn, send_sems, recv_sems, 3 * pieces + replicas)
        for turn in range(1, replicas)
    ]

    def remote(owner, piece, at, device):
        place = all_ref.at[piece, pl.ds(pl.multiple_of(owner * rows, rows), rows)]
        return pltpu.make_async_remote_copy(
            place, place, send_sems.at[at], recv_sems.at[at], device_id={"shard": device}, device_id_type=MESH
        )

    own = pl.ds(pl.multiple_of(shard * rows, rows), rows)
    over = [remote(shard, piece, piece, across) for piece in range(pieces)]
    direct = [remote(shard, piece, pieces + piece, beside) for piece in range(pieces)]
    relays = [remote(across, piece, 2 * pieces + piece, beside) for piece in range(pieces)]
    lefts = [(kind, group, peer) for kind in reversed(range(kinds)) for group in range(groups) for peer in range(3)]
    loads[4][0].wait()
    for place in lefts:
        hand_left(*place).start()
    for kind in range(kinds):
        for group in range(groups):
            left_ref[kind, group, :, own] = lefts_ref[kind, group, shard]
    loads[0][0].wait()
    for piece in range(pieces):
        all_ref[piece, own, :] = projected_ref[:, piece * step : (piece + 1) * step]
        over[piece].start()
        direct[piece].start()
    loads[1][0].wait()
    gains_land_ref[replica] = gains_ref[...]
    loads[2][0].wait()
    for copy in gain_copies + spread_copies:
        copy.start()

    def product(piece):
        at = piece * step
        kind = 0 if at < cols else 1
        left = jnp.concatenate([left_ref[kind, group] for group in range(groups)], 0)
        total = dot(left, all_ref[piece]).astype(BF)
        for group in range(groups):
            terms_ref[group, :, at : at + step] = total[group * sub_rows : (group + 1) * sub_rows]

    loads[3][0].wait()
    for place in lefts:
        hand_left(*place).wait_recv()
    for piece in range(pieces, all_ref.shape[0]):
        product(piece)
    for piece in range(pieces):
        over[piece].wait_recv()
        relays[piece].start()
        if piece:
            direct[piece - 1].wait_recv()
            relays[piece - 1].wait_recv()
            product(piece - 1)
    direct[pieces - 1].wait_recv()
    relays[pieces - 1].wait_recv()
    product(pieces - 1)
    for copy in gain_copies:
        copy.wait()
    gain_sum_ref[...] = jnp.sum(gains_land_ref[...], 0)
    for copy in over + direct + relays:
        copy.wait_send()
    for place in lefts:
        hand_left(*place).wait_send()
    for copy in spread_copies:
        copy.wait()


def call_attend_grads(lefts, projected, gains, upstream, branch, collective):
    replicas, sections = lax.axis_size("replica"), len(projected)
    rows, cols = projected[0].shape
    width = upstream[0].shape[1]
    shards = lax.axis_size("shard")
    every, tokens = width // shards, shards * rows
    sub_rows = every // replicas
    lefts = [values.reshape(2, replicas, shards, sub_rows, rows) for values in lefts]
    pieces = cols // CHUNK
    copies = 3 * pieces + 2 * replicas + 2 * replicas * 3
    vmem, anywhere = pl.BlockSpec(memory_space=pltpu.VMEM), pl.BlockSpec(memory_space=pl.ANY)
    return pl.pallas_call(
        functools.partial(attend_grads_kernel, sections),
        out_shape=[
            jax.ShapeDtypeStruct((replicas, every // replicas, cols + width), BF),
            jax.ShapeDtypeStruct(gains[0].shape, F32),
            jax.ShapeDtypeStruct((replicas, rows, width), BF),
        ],
        in_specs=[anywhere] * 5 * sections,
        out_specs=[vmem] * 2 + [anywhere],
        scratch_shapes=[
            pltpu.VMEM(((cols + width) // CHUNK, tokens, CHUNK), BF),
            pltpu.VMEM((rows, cols), BF),
            pltpu.VMEM((rows, width), BF),
            pltpu.VMEM(gains[0].shape, F32),
            pltpu.VMEM((replicas,) + gains[0].shape, F32),
            pltpu.VMEM(lefts[0].shape, BF),
            pltpu.VMEM((2, replicas, sub_rows, tokens), BF),
            pltpu.SemaphoreType.DMA((5,)),
            pltpu.SemaphoreType.DMA((copies,)),
            pltpu.SemaphoreType.DMA((copies,)),
        ],
        compiler_params=pltpu.CompilerParams(
            collective_id=collective, has_side_effects=True, vmem_limit_bytes=VMEM_LIMIT
        ),
        name="attend_grads",
    )(*projected, *gains, *upstream, *branch, *lefts)


def feed_grads_kernel(sections, left_ref, hidden_ref, terms_ref, gains_ref, *refs):
    upstream = refs[:sections]
    (odd_hbm, even_hbm, early_hbm, gate_up_hbm, down_hbm,
     gate_up_grad_ref, down_grad_ref, qkv_grad_ref, out_grad_ref, gain_sum_ref, gathered_hbm,
     down_ref, block_ref, gate_up_ref, mid_ref, sum_ref, stage_ref, chain_ref, gains_land_ref,
     load_sems, block_sems, keep_sem, send_sems, recv_sems) = refs[sections:]
    shard, beside, across, diagonal = slice_peers()
    peers = (across, diagonal, beside)
    replica, replicas = lax.axis_index("replica"), lax.axis_size("replica")
    early = lax.axis_index("section") == lax.axis_size("section") - 1
    late = lax.axis_index("section") < lax.axis_size("section") - 1
    rows = odd_hbm.shape[1]
    every, width = upstream[0].shape
    part = down_ref.shape[0]
    half_part = part // 2
    ff = gate_up_grad_ref.shape[1] // 2
    steps = half_part // CHUNK
    wide = width // CHUNK
    out_rows = gate_up_grad_ref.shape[0]
    grad_base = 3 * replicas
    chain_base = grad_base + 2 * 2 * steps * 3
    gain_base = chain_base + 2 * replicas

    load_down = pltpu.make_async_copy(down_hbm, down_ref, load_sems.at[3, 0])
    load_down.start()

    def block_at(turn):
        return lax.rem(replica + turn, replicas)

    def tokens(turn):
        return pl.ds(pl.multiple_of(block_at(turn) * every, every), every)

    def load_gate_up(half, turn, side):
        cols = pl.ds(side * part + half * half_part, half_part)
        slot = lax.rem(turn, 2)
        return pltpu.make_async_copy(
            gate_up_hbm.at[tokens(turn), cols], gate_up_ref.at[slot, side], load_sems.at[side, slot]
        )

    def block_copies(turn, source):
        slot = lax.rem(turn, 2)
        copies = []
        for at, owner in enumerate(peers + (shard,)):
            place = pl.ds(pl.multiple_of(owner * rows, rows), rows)
            if source is early_hbm:
                own = early_hbm.at[turn, place]
            else:
                own = gathered_hbm.at[turn, place] if source is None or at < 3 else source.at[block_at(turn)]
            copies.append(pltpu.make_async_copy(own, block_ref.at[slot, place], block_sems.at[slot, at]))
        return copies

    def load_block(turn):
        @pl.when(early & (turn % 2 == 1))
        def _():
            for copy in block_copies(turn, early_hbm):
                copy.start()

        @pl.when(late | (turn % 2 == 0))
        def _():
            for copy in block_copies(turn, None)[:3]:
                copy.start()

        cases = ((turn == 0, None), ((turn > 0) & (turn % 2 == 0), even_hbm), (late & (turn % 2 == 1), odd_hbm))
        for case, source in cases:

            @pl.when(case)
            def _(source=source):
                block_copies(turn, source)[3].start()

    def wait_block(turn):
        for copy in block_copies(turn, None):
            copy.wait()

    def remote(source, target, at, device):
        return pltpu.make_async_remote_copy(
            source, target, send_sems.at[at], recv_sems.at[at], device_id={"shard": device}, device_id_type=MESH
        )

    def landing(turn, owner):
        return gathered_hbm.at[turn, pl.ds(pl.multiple_of(owner * rows, rows), rows)]

    def over(turn, source):
        return remote(source.at[block_at(turn)], landing(turn, shard), 3 * turn, across)

    def direct(turn, source):
        return remote(source.at[block_at(turn)], landing(turn, shard), 3 * turn + 1, beside)

    def relay(turn):
        return remote(landing(turn, across), landing(turn, across), 3 * turn + 2, beside)

    def send_block(turn):
        for parity, source in ((0, even_hbm), (1, odd_hbm)):

            @pl.when((lax.rem(turn, 2) == 1) & late if parity else lax.rem(turn, 2) == 0)
            def _(source=source):
                over(turn, source).start()
                direct(turn, source).start()

    def chain_slot(block, at):
        return replicas - (replicas - block) * ((at - block + replicas - 1) // replicas)

    def chain_up(block):
        return pltpu.make_async_remote_copy(
            chain_ref.at[block], chain_ref.at[block], send_sems.at[chain_base + block],
            recv_sems.at[chain_base + block], device_id={"replica": replica + 1}, device_id_type=MESH,
        )

    def chain_down(block):
        return pltpu.make_async_remote_copy(
            chain_ref.at[block], chain_ref.at[chain_slot(block, replica - 1)],
            send_sems.at[chain_base + replicas + block],
            recv_sems.at[chain_base + replicas + block], device_id={"replica": replica - 1}, device_id_type=MESH,
        )

    def add_terms(block):
        chain_ref[block] = (chain_ref[block].astype(F32) + terms_ref[block].astype(F32)).astype(BF)

    def chain_step(step):
        high = replicas - 1 - step + replica

        @pl.when((replica > 0) & (step >= replica))
        def _():
            chain_up(high).wait_recv()

            @pl.when(step < replicas - 1)
            def _():
                add_terms(high)
                chain_up(high).start()

        low = step - (replicas - 1 - replica)

        @pl.when((replica < replicas - 1) & (step >= replicas - 1 - replica))
        def _():
            chain_down(low).wait_recv()

            @pl.when(step < replicas - 1)
            def _():
                add_terms(low)
                chain_down(low).start()

    def gain_copy(peer):
        return remote(
            gains_ref, gains_land_ref.at[shard], gain_base + peer, peers[peer]
        )

    barrier = pltpu.get_barrier_semaphore()
    for device in peers:
        pl.semaphore_signal(barrier, inc=1, device_id={"shard": device}, device_id_type=MESH)

    @pl.when(replica > 0)
    def _():
        pl.semaphore_signal(barrier, inc=1, device_id={"replica": replica - 1}, device_id_type=MESH)

    @pl.when(replica < replicas - 1)
    def _():
        pl.semaphore_signal(barrier, inc=1, device_id={"replica": replica + 1}, device_id_type=MESH)

    below = (replica + replicas - 1) // replicas
    above = (2 * replicas - 2 - replica) // replicas
    pl.semaphore_wait(barrier, 3 + below + above)

    for turn in range(1, min(3, replicas)):
        send_block(turn)

    for block in reversed(range(1, replicas)):

        @pl.when(replica == 0)
        def _(block=block):
            chain_ref[block] = terms_ref[block]
            chain_up(block).start()

    for block in range(replicas - 1):

        @pl.when(replica == replicas - 1)
        def _(block=block):
            chain_ref[block] = terms_ref[block]
            chain_down(block).start()

    for peer in range(3):
        gain_copy(peer).start()
    gains_land_ref[shard] = gains_ref[...]
    load_own = [pltpu.make_async_copy(source, block_ref.at[0], load_sems.at[2, 0]) for source in upstream]
    start_own(load_own)
    load_own[0].wait()
    keep_own = pltpu.make_async_copy(block_ref.at[0], gathered_hbm.at[0], keep_sem)
    keep_own.start()
    load_down.wait()
    keep_own.wait()

    def send_grad(half, at, peer):
        device = peers[peer]
        cols = pl.ds(pl.multiple_of(at * CHUNK, CHUNK), CHUNK)
        target = pl.ds(
            pl.multiple_of(
                (at // steps) * ff + shard * part + half * half_part + (at % steps) * CHUNK, CHUNK
            ),
            CHUNK,
        )
        return remote(
            stage_ref.at[half, pl.ds(pl.multiple_of(device * out_rows, out_rows), out_rows), cols],
            gate_up_grad_ref.at[:, target],
            grad_base + (half * 2 * steps + at) * 3 + peer,
            device,
        )

    def half_pass(half):
        for side in range(2):
            load_gate_up(half, 0, side).start()
        sum_ref[...] = jnp.zeros_like(sum_ref)

        def work(turn, carry):
            slot = lax.rem(turn, 2)
            later = lax.rem(turn + 1, replicas)
            for side in range(2):
                load_gate_up(half, turn, side).wait()

            @pl.when(turn + 1 < replicas)
            def _():
                for side in range(2):
                    load_gate_up(half, later, side).start()

            if half:

                @pl.when(turn + 1 < replicas)
                def _():
                    load_block(later)

            def products(at, inner):
                cols = pl.ds(pl.multiple_of(at * CHUNK, CHUNK), CHUNK)
                high = pl.ds(pl.multiple_of(half_part + at * CHUNK, CHUNK), CHUNK)
                down_rows = pl.ds(pl.multiple_of(half * half_part + at * CHUNK, CHUNK), CHUNK)
                grad_hidden = dot_rows(block_ref[slot], down_ref[down_rows, :])
                gate = gate_up_ref[slot, 0, :, cols].astype(F32)
                up = gate_up_ref[slot, 1, :, cols].astype(F32)
                sigmoid = jax.nn.sigmoid(gate)
                mid_ref[:, cols] = (grad_hidden * up * sigmoid * (1.0 + gate * (1.0 - sigmoid))).astype(BF)
                mid_ref[:, high] = (grad_hidden * gate * sigmoid).astype(BF)
                return inner

            lax.fori_loop(0, steps, products, 0)

            def sums(at, inner):
                cols = pl.ds(pl.multiple_of(at * CHUNK, CHUNK), CHUNK)
                total = sum_ref[:, cols] + dot(left_ref[:, tokens(turn)], mid_ref[:, cols])

                @pl.when(turn < replicas - 1)
                def _():
                    sum_ref[:, cols] = total

                @pl.when(turn == replicas - 1)
                def _():
                    stage_ref[half, :, cols] = total.astype(BF)
                    for peer in range(3):
                        send_grad(half, at, peer).start()

                return inner

            lax.fori_loop(0, 2 * steps, sums, 0)

            @pl.when(turn + 1 < replicas)
            def _():
                if half:
                    wait_block(later)
                else:

                    @pl.when(late | (later % 2 == 0))
                    def _():
                        over(later, even_hbm).wait_recv()
                        relay(later).start()
                        direct(later, even_hbm).wait_recv()
                        relay(later).wait_recv()

                    load_block(later)

                    @pl.when(turn + 3 < replicas)
                    def _():
                        send_block(turn + 3)

                    wait_block(later)

            return carry

        return work

    first = half_pass(0)
    lax.fori_loop(0, replicas - 1, first, 0)
    chain_step(1)
    first(replicas - 1, 0)
    load_block(0)
    wait_block(0)
    second = half_pass(1)
    lax.fori_loop(0, replicas - 1, second, 0)
    if replicas > 2:
        chain_step(2)
    second(replicas - 1, 0)
    load_block(0)
    wait_block(0)
    down_grad_ref[...] = jnp.zeros_like(down_grad_ref)

    def down_work(turn, carry):
        slot = lax.rem(turn, 2)
        later = lax.rem(turn + 1, replicas)

        @pl.when(turn + 1 < replicas)
        def _():
            load_block(later)

        def down_sums(at, inner):
            cols = pl.ds(pl.multiple_of(at * CHUNK, CHUNK), CHUNK)
            down_grad_ref[:, cols] += dot(hidden_ref[:, tokens(turn)], block_ref[slot, :, cols])
            return inner

        lax.fori_loop(0, wide, down_sums, 0)

        @pl.when(turn + 1 < replicas)
        def _():
            wait_block(later)

        return carry

    lax.fori_loop(0, replicas, down_work, 0)
    for peer in range(3):
        gain_copy(peer).wait()
    gain_sum_ref[...] = jnp.sum(gains_land_ref[...], 0)
    own = pl.ds(pl.multiple_of(shard * out_rows, out_rows), out_rows)
    for half in range(2):

        def store_own(at, carry, half=half):
            cols = pl.ds(pl.multiple_of(at * CHUNK, CHUNK), CHUNK)
            target = pl.ds(
                pl.multiple_of(
                    (at // steps) * ff + shard * part + half * half_part + (at % steps) * CHUNK, CHUNK
                ),
                CHUNK,
            )
            gate_up_grad_ref[:, target] = stage_ref[half, own, cols]
            return carry

        lax.fori_loop(0, 2 * steps, store_own, 0)
    for step in range(3, replicas):
        chain_step(step)
    cut = qkv_grad_ref.shape[1]
    for grad_ref, cols in ((qkv_grad_ref, slice(0, cut)), (out_grad_ref, slice(cut, None))):
        grad_ref[...] = terms_ref[replica, :, cols].astype(F32)

        @pl.when(replica > 0)
        def _(grad_ref=grad_ref, cols=cols):
            grad_ref[...] += chain_ref[replica, :, cols].astype(F32)

        @pl.when(replica < replicas - 1)
        def _(grad_ref=grad_ref, cols=cols):
            grad_ref[...] += chain_ref[replicas, :, cols].astype(F32)

    for half in range(2):

        def finish(at, carry, half=half):
            for peer in range(3):
                send_grad(half, at, peer).wait()
            return carry

        lax.fori_loop(0, 2 * steps, finish, 0)
    for turn in range(1, replicas):

        @pl.when(late | (turn % 2 == 0))
        def _(turn=turn):
            over(turn, even_hbm).wait_send()
            direct(turn, even_hbm).wait_send()
            relay(turn).wait_send()

    for block in range(1, replicas):

        @pl.when(replica < block)
        def _(block=block):
            chain_up(block).wait_send()

    for block in range(replicas - 1):

        @pl.when(replica > block)
        def _(block=block):
            chain_down(block).wait_send()


def call_feed_grads(left, hidden, terms, gains, upstream, odd, even, early, gate_up, down, qkv_cols, collective):
    every, width = upstream[0].shape
    sub_rows, attend_cols = terms.shape[1:]
    replicas = odd.shape[0]
    shards = lax.axis_size("shard")
    part = down.shape[0]
    out_rows = left.shape[0] // shards
    vmem, anywhere = pl.BlockSpec(memory_space=pltpu.VMEM), pl.BlockSpec(memory_space=pl.ANY)
    copies = 5 * replicas + 3 * 2 * (part // CHUNK) + 3
    return pl.pallas_call(
        functools.partial(feed_grads_kernel, len(upstream)),
        out_shape=[
            jax.ShapeDtypeStruct((out_rows, 2 * part * shards), BF),
            jax.ShapeDtypeStruct((hidden.shape[0], width), F32),
            jax.ShapeDtypeStruct((sub_rows, qkv_cols), F32),
            jax.ShapeDtypeStruct((sub_rows, attend_cols - qkv_cols), F32),
            jax.ShapeDtypeStruct(gains.shape, F32),
            jax.ShapeDtypeStruct((replicas, every, width), BF),
        ],
        in_specs=[vmem] * 4 + [anywhere] * (5 + len(upstream)),
        out_specs=[vmem] * 5 + [anywhere],
        scratch_shapes=[
            pltpu.VMEM(down.shape, BF),
            pltpu.VMEM((2, every, width), BF),
            pltpu.VMEM((2, 2, every, part // 2), BF),
            pltpu.VMEM((every, part), BF),
            pltpu.VMEM((left.shape[0], part), F32),
            pltpu.VMEM((2, left.shape[0], part), BF),
            pltpu.VMEM((replicas + 1,) + terms.shape[1:], BF),
            pltpu.VMEM((shards,) + gains.shape, F32),
            pltpu.SemaphoreType.DMA((4, 2)),
            pltpu.SemaphoreType.DMA((2, 4)),
            pltpu.SemaphoreType.DMA,
            pltpu.SemaphoreType.DMA((copies,)),
            pltpu.SemaphoreType.DMA((copies,)),
        ],
        compiler_params=pltpu.CompilerParams(
            collective_id=collective, has_side_effects=True, vmem_limit_bytes=VMEM_LIMIT
        ),
        name="feed_grads",
    )(left, hidden, terms, gains, *upstream, odd, even, early, gate_up, down)


def turn_order(replicas):
    return [0] + list(range(1, replicas, 2)) + list(range(2, replicas, 2))


def prepare_kernel(sections, gate_up_hbm, *refs):
    slices, normed_two = refs[:sections], refs[sections : 2 * sections]
    (gathered_hbm, gate_up_all_hbm, hidden_hbm, left_rows_ref,
     normed_two_ref, weight_ref, block_ref, gate_up_ref, hidden_ref, turned_ref,
     load_sems, store_sems, start_sems, send_sems, recv_sems) = refs[2 * sections :]
    shard, beside, across, diagonal = slice_peers()
    peers = (across, diagonal, beside)
    replica, replicas = lax.axis_index("replica"), lax.axis_size("replica")
    shards = lax.axis_size("shard")
    rows, width = normed_two_ref.shape
    every = rows * shards
    part = hidden_ref.shape[1]
    ff_rows = hidden_hbm.shape[0]
    steps = part // CHUNK
    slice_rows = left_rows_ref.shape[0]
    owner = (replica * shards) // replicas
    first_col = lax.rem(replica * shards, replicas) * ff_rows

    def load_weight(side, at):
        place = (slice(None), pl.ds(pl.multiple_of(side * part + at * CHUNK, CHUNK), CHUNK))
        return pltpu.make_async_copy(gate_up_hbm.at[place], weight_ref.at[place], load_sems.at[side, at])

    for at in range(steps):
        for side in range(2):
            load_weight(side, at).start()

    def remote(source, target, at, device):
        return pltpu.make_async_remote_copy(
            source, target, send_sems.at[at], recv_sems.at[at], device_id={"shard": device}, device_id_type=MESH
        )

    def landing(turn, who):
        return gathered_hbm.at[turn, pl.ds(pl.multiple_of(who * rows, rows), rows)]

    def over(turn):
        return remote(landing(turn, shard), landing(turn, shard), 3 * turn, across)

    def direct(turn):
        return remote(landing(turn, shard), landing(turn, shard), 3 * turn + 1, beside)

    def relay(turn):
        return remote(landing(turn, across), landing(turn, across), 3 * turn + 2, beside)

    def from_replica(turn):
        return replica_copy(normed_two_ref, landing(turn, shard), turn, send_sems, recv_sems, 3 * replicas)

    def tokens(turn):
        return pl.ds(pl.multiple_of(lax.rem(replica + turn, replicas) * every, every), every)

    def load_block(turn, slot):
        return pltpu.make_async_copy(gathered_hbm.at[turn], block_ref.at[slot], store_sems.at[0, slot])

    def store_block(turn, slot):
        return pltpu.make_async_copy(gate_up_ref.at[slot], gate_up_all_hbm.at[tokens(turn)], store_sems.at[1, slot])

    def hand_hidden(turn, slot, peer):
        device = peers[peer]
        return remote(
            turned_ref.at[slot, device], hidden_hbm.at[:, tokens(turn)], 4 * replicas + 3 * turn + peer, device
        )

    def keep_hidden(turn, slot):
        return pltpu.make_async_copy(
            turned_ref.at[slot, shard], hidden_hbm.at[:, tokens(turn)], store_sems.at[2, slot]
        )

    loads = [
        [pltpu.make_async_copy(source, target, sem) for source in sources]
        for sources, target, sem in (
            (normed_two, normed_two_ref, start_sems.at[0]),
            (slices, block_ref.at[0], store_sems.at[0, 0]),
        )
    ]
    for copies in loads:
        start_own(copies)
    slice_barrier(peers, range(1, replicas))
    order = turn_order(replicas)
    loads[0][0].wait()
    if replicas > 1:
        from_replica(order[1]).start()

    for at, turn in enumerate(order):
        later = order[at + 1] if at + 1 < replicas else None
        slot = at % 2
        if later is not None:
            from_replica(later).wait_recv()
            over(later).start()
            direct(later).start()
            if at + 2 < replicas:
                from_replica(later).wait_send()
                from_replica(order[at + 2]).start()
        load_block(turn, slot).wait()
        if at > 1:
            store_block(order[at - 2], slot).wait()

        def products(step, carry, at=at, slot=slot):
            cols = pl.ds(pl.multiple_of(step * CHUNK, CHUNK), CHUNK)
            high = pl.ds(pl.multiple_of(part + step * CHUNK, CHUNK), CHUNK)
            if at == 0:
                load_weight(0, step).wait()
                load_weight(1, step).wait()
            gate = dot(block_ref[slot], weight_ref[:, cols])
            up = dot(block_ref[slot], weight_ref[:, high])
            gate_up_ref[slot, :, cols] = gate.astype(BF)
            gate_up_ref[slot, :, high] = up.astype(BF)
            hidden_ref[:, cols] = (gate * jax.nn.sigmoid(gate) * up).astype(BF)
            return carry

        lax.fori_loop(0, steps, products, 0)
        store_block(turn, slot).start()
        if later is not None:
            over(later).wait_recv()
            relay(later).start()

        @pl.when(shard == owner)
        def _(at=at, turn=turn, slot=slot):
            if at > 1:
                keep_hidden(order[at - 2], slot).wait()
                for peer in range(3):
                    hand_hidden(order[at - 2], slot, peer).wait_send()

            def turn_over(device, carry):
                cols = pl.ds(pl.multiple_of(first_col + device * ff_rows, ff_rows), ff_rows)
                turned_ref[slot, device] = hidden_ref[:, cols].T
                return carry

            lax.fori_loop(0, shards, turn_over, 0)
            keep_hidden(turn, slot).start()
            for peer in range(3):
                hand_hidden(turn, slot, peer).start()

        slice_cols = pl.ds(pl.multiple_of(replica * slice_rows, slice_rows), slice_rows)
        left_rows_ref[:, tokens(turn)] = block_ref[slot, :, slice_cols].T
        if later is not None:
            direct(later).wait_recv()
            relay(later).wait_recv()
            load_block(later, 1 - slot).start()

    for at in range(max(0, replicas - 2), replicas):
        store_block(order[at], at % 2).wait()

        @pl.when(shard == owner)
        def _(at=at):
            keep_hidden(order[at], at % 2).wait()
            for peer in range(3):
                hand_hidden(order[at], at % 2, peer).wait_send()

    for turn in range(replicas):
        for peer in range(3):

            @pl.when(peers[peer] == owner)
            def _(turn=turn, peer=peer):
                hand_hidden(turn, 0, peer).wait_recv()

        if turn:
            over(turn).wait_send()
            direct(turn).wait_send()
            relay(turn).wait_send()
        if turn and turn == order[-1]:
            from_replica(turn).wait_send()


def call_prepare(normed_two, gate_up_part, slices, collective):
    rows, width = normed_two[0].shape
    shards, replicas = lax.axis_size("shard"), lax.axis_size("replica")
    part = gate_up_part.shape[1] // 2
    every = rows * shards
    slice_rows = width // replicas
    ff_rows = part // replicas
    vmem, anywhere = pl.BlockSpec(memory_space=pltpu.VMEM), pl.BlockSpec(memory_space=pl.ANY)
    copies = 7 * replicas
    outs = pl.pallas_call(
        functools.partial(prepare_kernel, len(slices)),
        out_shape=[
            jax.ShapeDtypeStruct((replicas, every, width), BF),
            jax.ShapeDtypeStruct((replicas * every, 2 * part), BF),
            jax.ShapeDtypeStruct((ff_rows, replicas * every), BF),
            jax.ShapeDtypeStruct((slice_rows, replicas * every), BF),
        ],
        in_specs=[anywhere] * (1 + 2 * len(slices)),
        out_specs=[anywhere] * 3 + [vmem],
        scratch_shapes=[
            pltpu.VMEM((rows, width), BF),
            pltpu.VMEM(gate_up_part.shape, BF),
            pltpu.VMEM((2, every, width), BF),
            pltpu.VMEM((2, every, 2 * part), BF),
            pltpu.VMEM((every, part), BF),
            pltpu.VMEM((2, shards, ff_rows, every), BF),
            pltpu.SemaphoreType.DMA((2, part // CHUNK)),
            pltpu.SemaphoreType.DMA((3, 2)),
            pltpu.SemaphoreType.DMA((1,)),
            pltpu.SemaphoreType.DMA((copies,)),
            pltpu.SemaphoreType.DMA((copies,)),
        ],
        compiler_params=pltpu.CompilerParams(
            collective_id=collective, has_side_effects=True, vmem_limit_bytes=VMEM_LIMIT
        ),
        name="prepare",
    )(gate_up_part, *slices, *normed_two)
    return outs[1:]


def gather_kernel(mine_ref, gathered_hbm, send_sems, recv_sems):
    shard, beside, across, _ = slice_peers()
    replicas = lax.axis_size("replica")
    rows = mine_ref.shape[0]

    def remote(owner, turn, at, device):
        place = gathered_hbm.at[turn, pl.ds(pl.multiple_of(owner * rows, rows), rows)]
        return pltpu.make_async_remote_copy(
            place, place, send_sems.at[at], recv_sems.at[at], device_id={"shard": device}, device_id_type=MESH
        )

    own_rows = pl.ds(pl.multiple_of(shard * rows, rows), rows)
    slice_barrier((beside, across), range(1, replicas, 2))
    order = list(range(1, replicas, 2))
    spread_copies = [
        replica_copy(mine_ref, gathered_hbm.at[turn, own_rows], turn, send_sems, recv_sems, 3 * replicas)
        for turn in order
    ]
    over = [remote(shard, turn, 3 * turn, across) for turn in order]
    direct = [remote(shard, turn, 3 * turn + 1, beside) for turn in order]
    relays = [remote(across, turn, 3 * turn + 2, beside) for turn in order]
    spread_copies[0].start()
    for at in range(len(order)):
        spread_copies[at].wait_recv()
        over[at].start()
        direct[at].start()
        spread_copies[at].wait_send()
        if at + 1 < len(order):
            spread_copies[at + 1].start()
        if at:
            over[at - 1].wait_recv()
            relays[at - 1].start()
    over[-1].wait_recv()
    relays[-1].start()
    for copy in direct + relays:
        copy.wait_recv()
    for copy in over + direct + relays:
        copy.wait_send()


def call_gather(section, mine, collective):
    replicas, shards = lax.axis_size("replica"), lax.axis_size("shard")
    rows, width = mine.shape
    return pl.pallas_call(
        gated(section, gather_kernel),
        out_shape=jax.ShapeDtypeStruct((replicas, shards * rows, width), BF),
        in_specs=[pl.BlockSpec(memory_space=pltpu.VMEM)],
        out_specs=pl.BlockSpec(memory_space=pl.ANY),
        scratch_shapes=[
            pltpu.SemaphoreType.DMA((4 * replicas,)),
            pltpu.SemaphoreType.DMA((4 * replicas,)),
        ],
        compiler_params=pltpu.CompilerParams(
            collective_id=collective, has_side_effects=True, vmem_limit_bytes=VMEM_LIMIT
        ),
        name="gather",
    )(mine)


def on_device(
    tokens_in,
    positions,
    attn_gain,
    qkv_weight,
    out_weight,
    mlp_gain,
    gate_up_weight,
    down_weight,
    cotangent,
):
    sections = lax.axis_size("section")
    rows, width = tokens_in.shape
    up_steps = [(at, at + 1) for at in range(sections - 1)]
    down_steps = [(at + 1, at) for at in range(sections - 1)]

    cosine, sine = rope_tables(positions)
    allowed = visible(positions)

    tables = (attn_gain, mlp_gain, cosine, sine, allowed)
    qkv_full, out_full, gate_up_part, *attend_first = call_weights(
        qkv_weight[0], out_weight[0], gate_up_weight[0], (tokens_in,) + tables, 3
    )
    down_part = down_weight[0]

    forward = []
    state = tokens_in
    for section in range(sections):
        middle, normed_two, rotated, lefts = (
            call_attend_forward(section, state, *tables, qkv_full, out_full) if section else attend_first
        )
        block_out, normed_two_slice, gate_up = call_feed(
            section, False, (normed_two, middle, gate_up_part, down_part), 8 + section
        )
        forward.append((state, middle, rotated, gate_up, normed_two_slice, normed_two, lefts, block_out))
        if section + 1 < sections:
            state = lax.ppermute(block_out, "section", up_steps)
        if section + 2 == sections:
            held, _ = lax.optimization_barrier((cotangent, block_out))
            early = call_gather(sections - 1, held, 7)
            state, early = lax.optimization_barrier((state, early))

    def pick(values):
        chosen = values[-1]
        for section in range(sections - 1):
            chosen = jnp.where(lax.axis_index("section") == section, values[section], chosen)
        return chosen

    slices, normed_two, lefts, block_out = list(zip(*forward))[4:]
    block_out = pick(block_out)
    backward = []
    upstream = cotangent
    for section in reversed(range(sections)):
        state, middle, rotated, gate_up = forward[section][:4]
        grad_normed_two, upstream_slice, odd = call_feed(
            section, True, (upstream, gate_up, down_part, gate_up_part), 8 + sections + section
        )
        grad_in, grad_low, grad_projected, gains, grad_branch = call_attend_backward(
            section, 8 + 2 * sections + section, grad_normed_two, upstream, middle, state, rotated,
            *tables, qkv_full, out_full,
        )
        backward.insert(0, (upstream, upstream_slice, odd, grad_in, grad_projected, gains, grad_branch))
        if section == sections - 1:
            normed_two, grad_low = lax.optimization_barrier((normed_two, grad_low))
        if section > 0:
            upstream = lax.ppermute(grad_low, "section", down_steps)
        if section == sections - 1:
            gate_up_all, hidden_rows, left_rows = call_prepare(normed_two, gate_up_part, slices, 6)
            upstream, gate_up_all, left_rows, hidden_rows = lax.optimization_barrier(
                (upstream, gate_up_all, left_rows, hidden_rows)
            )

    upstream, upstream_slice, odd, grad_in, grad_projected, gains, grad_branch = zip(*backward)
    grad_in = pick(grad_in)
    terms, gains, even = call_attend_grads(lefts, grad_projected, gains, upstream, grad_branch, 4)
    gate_up_grad, down_grad, qkv_grad, out_grad, gains, _ = call_feed_grads(
        left_rows, hidden_rows, terms, gains, upstream_slice, pick(odd[:-1]), even, early, gate_up_all, down_part,
        grad_projected[0].shape[1], 5,
    )
    gate_up_grad = gate_up_grad.astype(F32)
    return (
        block_out[None],
        grad_in[None],
        gains[0][None],
        qkv_grad[None],
        out_grad[None],
        gains[1][None],
        gate_up_grad[None],
        down_grad[None],
    )


def solution(mesh):
    both = ("replica", "shard")
    return jax.shard_map(
        on_device,
        mesh=mesh,
        in_specs=(
            P(both, None),
            P(both),
            P("section", None),
            P("section", "shard", None),
            P("section", "shard", None),
            P("section", None),
            P("section", "shard", None),
            P("section", "shard", None),
            P(both, None),
        ),
        out_specs=(
            P("section", both, None),
            P("section", both, None),
            P("section", None),
            P("section", both, None),
            P("section", both, None),
            P("section", None),
            P("section", both, None),
            P("section", both, None),
        ),
        check_vma=False,
    )
```

```python
import functools

import jax
import jax.numpy as jnp
from jax import lax
from jax.experimental import pallas as pl
from jax.experimental.pallas import tpu as pltpu
from jax.sharding import PartitionSpec as P

HEADS = 32
KV_HEADS = 8
HEAD = 64
SEQ = 64
EPSILON = 1e-05
ROPE_BASE = 500000.0
BF = jnp.bfloat16
F32 = jnp.float32
CONTRACT_LAST = (((1,), (1,)), ((), ()))
CONTRACT_FIRST = (((0,), (0,)), ((), ()))


MESH = pl.DeviceIdType.MESH
VMEM_LIMIT = 60 * 2**20
TILE = 128


def dot(left, right):
    return jnp.dot(left, right, preferred_element_type=F32)


def dot_rows(left, right):
    return lax.dot_general(left, right, CONTRACT_LAST, preferred_element_type=F32)


def dot_tokens(left, right):
    return lax.dot_general(left, right, CONTRACT_FIRST, preferred_element_type=F32)


def rope_tables(seq_pos):
    half_index = jnp.arange(HEAD // 2, dtype=F32)
    frequency = jnp.power(ROPE_BASE, -2.0 * half_index / HEAD)
    angles = seq_pos.astype(F32)[:, None] * frequency[None, :]
    cosine, sine = jnp.cos(angles), jnp.sin(angles)
    return (
        jnp.concatenate([cosine] * 4, 1),
        jnp.concatenate([-sine, sine, -sine, sine], 1),
    )


def visible(seq_pos):
    rows = seq_pos.shape[0]
    row_index = jnp.arange(rows)[:, None]
    col_index = jnp.arange(rows)[None, :]
    same = row_index // SEQ == col_index // SEQ
    seen = (col_index <= row_index) & (row_index - col_index <= seq_pos[:, None])
    return jnp.where(same & seen, 1.0, 0.0).astype(F32)


def lanes(rows):
    return lax.broadcasted_iota(jnp.int32, (rows, TILE), 1)


def swap_halves(tile, lane):
    return jnp.where(lane % HEAD < HEAD // 2, pltpu.roll(tile, TILE - HEAD // 2, 1), pltpu.roll(tile, HEAD // 2, 1))


def spread(tile, odd, lane):
    turned = pltpu.roll(tile, HEAD, 1)
    lower, upper = (turned, tile) if odd else (tile, turned)
    return jnp.concatenate(
        [jnp.where(lane < HEAD, lower, 0.0), jnp.where(lane < HEAD, 0.0, upper)], 0
    ).astype(BF)


def softmax_pair(queries, spread_keys, allowed):
    scores = dot_rows(queries, spread_keys) * HEAD ** (-0.5)
    halves = []
    for side in range(2):
        masked = jnp.where(allowed > 0.5, scores[:, side * TILE : (side + 1) * TILE], -1e30)
        expon = jnp.exp(masked - jnp.max(masked, -1, keepdims=True))
        halves.append(expon / jnp.sum(expon, -1, keepdims=True))
    return halves


def attend_parts(
    state_ref, gain_one_ref, gain_two_ref, cos_ref, sin_ref, allowed_ref, qkv_hbm, out_hbm,
    middle_ref, normed_two_ref, rotated_ref, lefts_ref,
    qkv_ref, out_ref, normed_ref, attended_ref, sems,
):
    rows, width = state_ref.shape
    cols = qkv_hbm.shape[1]
    step = 512
    rope_cols = (HEADS + KV_HEADS) * HEAD

    def qkv_copy(at):
        return pltpu.make_async_copy(qkv_hbm.at[:, pl.ds(at, step)], qkv_ref.at[:, pl.ds(at, step)], sems.at[at // step])

    def out_copy(at):
        return pltpu.make_async_copy(
            out_hbm.at[:, pl.ds(at, step)], out_ref.at[:, pl.ds(at, step)], sems.at[(cols + at) // step]
        )

    def begin():
        for at in range(0, cols, step):
            qkv_copy(at).start()
        state = state_ref[...].astype(F32)
        inverse = lax.rsqrt(jnp.mean(state * state, -1, keepdims=True) + EPSILON)
        normed_ref[...] = (state * inverse * gain_one_ref[...]).astype(BF)

    def project(at):
        qkv_copy(at).wait()
        lane = lanes(rows)
        projected = dot(normed_ref[...], qkv_ref[:, at : at + step])
        for tile_at in range(0, step, TILE):
            tile = projected[:, tile_at : tile_at + TILE]
            if at + tile_at < rope_cols:
                tile = tile * cos_ref[...] + swap_halves(tile, lane) * sin_ref[...]
            rotated_ref[:, at + tile_at : at + tile_at + TILE] = tile.astype(BF)

    def attend(group):
        lane = lanes(rows)
        key_at = width + group // 2 * TILE
        value_at = rope_cols + group // 2 * TILE
        keys = spread(rotated_ref[:, key_at : key_at + TILE].astype(F32), group % 2, lane)
        values = spread(rotated_ref[:, value_at : value_at + TILE].astype(F32), group % 2, lane)
        for pair in range(2):
            at = (group * 2 + pair) * TILE
            halves = softmax_pair(rotated_ref[:, at : at + TILE], keys, allowed_ref[...])
            probs = jnp.concatenate([half.astype(BF) for half in halves], 1)
            attended_ref[:, at : at + TILE] = dot(probs, values).astype(BF)

    def load_out():
        for at in range(0, width, step):
            out_copy(at).start()

    def leave(at):
        out_copy(at).wait()
        middle = state_ref[:, at : at + step].astype(F32) + dot(attended_ref[...], out_ref[:, at : at + step])
        middle_ref[:, at : at + step] = middle

    def finish():
        middle = middle_ref[...]
        inverse = lax.rsqrt(jnp.mean(middle * middle, -1, keepdims=True) + EPSILON)
        normed_two_ref[...] = (middle * inverse * gain_two_ref[...]).astype(BF)
        lefts_ref[0] = normed_ref[...].T
        lefts_ref[1] = attended_ref[...].T

    first = [begin] + [functools.partial(project, at) for at in range(0, cols, step)]
    first += [functools.partial(attend, group) for group in range(KV_HEADS)]
    second = [functools.partial(leave, at) for at in range(0, width, step)] + [finish]
    return first, load_out, second


def attend_forward(*refs):
    first, load_out, second = attend_parts(*refs)
    first[0]()
    load_out()
    for part in first[1:] + second:
        part()


def attend_backward(
    rounds, grad_ref, upstream_ref, middle_ref, state_ref, rotated_ref,
    gain_one_ref, gain_two_ref, cos_ref, sin_ref, allowed_ref, qkv_hbm, out_hbm,
    grad_state_ref, grad_low_ref, grad_projected_ref, gain_terms_ref, branch_hbm,
    qkv_ref, out_ref, grad_branch_ref, grad_out_ref, middle_grad_ref, sems, keep_sems, send_sems, recv_sems,
):
    rows, width = middle_ref.shape
    cols = qkv_hbm.shape[1]
    step = 512
    steps = width // step
    out_copies = [
        pltpu.make_async_copy(out_hbm.at[pl.ds(at * step, step)], out_ref.at[pl.ds(at * step, step)], sems.at[at])
        for at in range(steps)
    ]
    copies = [
        pltpu.make_async_copy(
            qkv_hbm.at[pl.ds(at * step, step)], qkv_ref.at[pl.ds(at * step, step)], sems.at[steps + at]
        )
        for at in range(steps)
    ]
    for copy in out_copies + copies:
        copy.start()
    shard, beside, across, _ = slice_peers()
    slice_barrier((beside, across))

    def branch_rows(owner, at):
        return branch_hbm.at[at, pl.ds(pl.multiple_of(owner * rows, rows), rows)]

    def remote(source, owner, at, kind, device):
        return pltpu.make_async_remote_copy(
            source, branch_rows(owner, at), send_sems.at[kind, at], recv_sems.at[kind, at],
            device_id={"shard": device}, device_id_type=MESH,
        )

    branch = [grad_branch_ref.at[:, pl.ds(at * step, step)] for at in range(steps)]
    over = [remote(branch[at], shard, at, 0, across) for at in range(steps)]
    direct = [remote(branch[at], shard, at, 1, beside) for at in range(steps)]
    relays = [remote(branch_rows(across, at), across, at, 2, beside) for at in range(steps)]
    keeps = [pltpu.make_async_copy(branch[at], branch_rows(shard, at), keep_sems.at[at]) for at in range(steps)]

    def norm_back(grad, values, gain):
        inverse = lax.rsqrt(jnp.mean(values * values, -1, keepdims=True) + EPSILON)
        normal = values * inverse
        term = jnp.sum(grad * normal, 0, keepdims=True)
        scaled = grad * gain
        return inverse * (scaled - normal * jnp.mean(scaled * normal, -1, keepdims=True)), term

    upstream = upstream_ref[...].astype(F32)
    back, term = norm_back(grad_ref[...], middle_ref[...], gain_two_ref[...])
    gain_terms_ref[1:2, :] = term
    middle_grad_ref[...] = upstream + back
    grad_branch_ref[...] = middle_grad_ref[...].astype(BF)
    for copy in over + direct + keeps:
        copy.start()
    for at in range(steps):
        out_copies[at].wait()
        grad_out_ref[:, at * step : (at + 1) * step] = dot_rows(
            grad_branch_ref[...], out_ref[at * step : (at + 1) * step, :]
        ).astype(BF)
    lane = lanes(rows)
    cosine, sine, allowed = cos_ref[...], sin_ref[...], allowed_ref[...]
    rope_cols = (HEADS + KV_HEADS) * HEAD
    scale = HEAD ** (-0.5)

    def unrotate(tile):
        return tile * cosine - swap_halves(tile, lane) * sine

    def group_step(group_pair, carry):
        key_at = pl.multiple_of(width + group_pair * TILE, TILE)
        value_at = pl.multiple_of(rope_cols + group_pair * TILE, TILE)
        sums = []
        for odd in range(2):
            keys = spread(rotated_ref[:, pl.ds(key_at, TILE)].astype(F32), odd, lane)
            values = spread(rotated_ref[:, pl.ds(value_at, TILE)].astype(F32), odd, lane)
            key_sum = jnp.zeros((rows, TILE), F32)
            value_sum = jnp.zeros((rows, TILE), F32)
            for pair in range(2):
                at = pl.multiple_of(((group_pair * 2 + odd) * 2 + pair) * TILE, TILE)
                queries = rotated_ref[:, pl.ds(at, TILE)]
                grad_out = grad_out_ref[:, pl.ds(at, TILE)]
                halves = softmax_pair(queries, keys, allowed)
                grad_probs = dot_rows(grad_out, values)
                grad_halves = []
                for side in range(2):
                    grad = grad_probs[:, side * TILE : (side + 1) * TILE]
                    row_dot = jnp.sum(halves[side] * grad, -1, keepdims=True)
                    grad_halves.append((halves[side] * (grad - row_dot)).astype(BF))
                grad_scores = jnp.concatenate(grad_halves, 1)
                probs = jnp.concatenate([half.astype(BF) for half in halves], 1)
                grad_projected_ref[:, pl.ds(at, TILE)] = unrotate(dot(grad_scores, keys) * scale).astype(BF)
                key_terms = dot_tokens(grad_scores, queries)
                value_terms = dot_tokens(probs, grad_out)
                key_sum += jnp.where(lane < HEAD, key_terms[:rows], key_terms[rows:])
                value_sum += jnp.where(lane < HEAD, value_terms[:rows], value_terms[rows:])
            sums.append((key_sum + pltpu.roll(key_sum, HEAD, 1), value_sum + pltpu.roll(value_sum, HEAD, 1)))
        keys_grad = jnp.where(lane < HEAD, sums[0][0], sums[1][0]) * scale
        grad_projected_ref[:, pl.ds(key_at, TILE)] = unrotate(keys_grad).astype(BF)
        grad_projected_ref[:, pl.ds(value_at, TILE)] = jnp.where(
            lane < HEAD, sums[0][1], sums[1][1]
        ).astype(BF)
        return carry

    lax.fori_loop(0, KV_HEADS // 2, group_step, 0)
    for at in range(steps):
        over[at].wait_recv()
        relays[at].start()
    for at in range(steps):
        copies[at].wait()
        grad_state_ref[:, at * step : (at + 1) * step] = dot_rows(
            grad_projected_ref[...], qkv_ref[at * step : (at + 1) * step, :]
        )
    state = state_ref[...].astype(F32)
    back, term = norm_back(grad_state_ref[...], state, gain_one_ref[...])
    gain_terms_ref[0:1, :] = term
    grad_state = middle_grad_ref[...] + back
    grad_low = grad_state.astype(BF)
    grad_low_ref[...] = grad_low
    grad_state_ref[...] = grad_low.astype(F32) if rounds else grad_state
    for copy in direct + relays:
        copy.wait()
    for copy in over:
        copy.wait_send()
    for copy in keeps:
        copy.wait()


def gated(section, body):
    def kernel(*refs):
        @pl.when(lax.axis_index("section") == section)
        def _():
            body(*refs)

    return kernel


def attend_shapes(rows, width, cols):
    return [
        jax.ShapeDtypeStruct((rows, width), F32),
        jax.ShapeDtypeStruct((rows, width), BF),
        jax.ShapeDtypeStruct((rows, cols), BF),
        jax.ShapeDtypeStruct((2, width, rows), BF),
    ], [
        pltpu.VMEM((width, cols), BF),
        pltpu.VMEM((width, width), BF),
        pltpu.VMEM((rows, width), BF),
        pltpu.VMEM((rows, width), BF),
        pltpu.SemaphoreType.DMA(((cols + width) // 512,)),
    ]


def call_attend_forward(section, *operands):
    rows, width = operands[0].shape
    out_shape, scratch = attend_shapes(rows, width, operands[6].shape[1])
    specs = [pl.BlockSpec(memory_space=pltpu.VMEM)] * 6 + [pl.BlockSpec(memory_space=pl.ANY)] * 2
    return pl.pallas_call(
        gated(section, attend_forward),
        out_shape=out_shape,
        in_specs=specs,
        out_specs=[pl.BlockSpec(memory_space=pltpu.VMEM)] * 4,
        scratch_shapes=scratch,
        compiler_params=pltpu.CompilerParams(vmem_limit_bytes=VMEM_LIMIT),
        name="attend_forward",
    )(*operands)


def call_attend_backward(section, collective, *operands):
    rows, width = operands[2].shape
    cols = operands[10].shape[1]
    steps = width // 512
    every = lax.axis_size("shard") * rows
    vmem, anywhere = pl.BlockSpec(memory_space=pltpu.VMEM), pl.BlockSpec(memory_space=pl.ANY)
    return pl.pallas_call(
        gated(section, functools.partial(attend_backward, section > 0)),
        out_shape=(
            jax.ShapeDtypeStruct((rows, width), F32),
            jax.ShapeDtypeStruct((rows, width), BF),
            jax.ShapeDtypeStruct((rows, cols), BF),
            jax.ShapeDtypeStruct((2, width), F32),
            jax.ShapeDtypeStruct((steps, every, 512), BF),
        ),
        in_specs=[vmem] * 10 + [anywhere] * 2,
        out_specs=[vmem] * 4 + [anywhere],
        scratch_shapes=[
            pltpu.VMEM((width, cols), BF),
            pltpu.VMEM((width, width), BF),
            pltpu.VMEM((rows, width), BF),
            pltpu.VMEM((rows, width), BF),
            pltpu.VMEM((rows, width), F32),
            pltpu.SemaphoreType.DMA((2 * steps,)),
            pltpu.SemaphoreType.DMA((steps,)),
            pltpu.SemaphoreType.DMA((3, steps)),
            pltpu.SemaphoreType.DMA((3, steps)),
        ],
        compiler_params=pltpu.CompilerParams(
            collective_id=collective, has_side_effects=True, vmem_limit_bytes=VMEM_LIMIT
        ),
        name="attend_backward",
    )(*operands)


def start_own(copies):
    for section, copy in enumerate(copies):

        @pl.when(lax.axis_index("section") == section)
        def _(copy=copy):
            copy.start()


def slice_peers():
    shard = lax.axis_index("shard")
    chip, core = shard // 2, shard % 2
    return shard, chip * 2 + (1 - core), (1 - chip) * 2 + core, (1 - chip) * 2 + (1 - core)


def slice_barrier(devices, turns=(), more=0):
    barrier = pltpu.get_barrier_semaphore()
    replicas = lax.axis_size("replica")
    for device in devices:
        pl.semaphore_signal(barrier, inc=1, device_id={"shard": device}, device_id_type=MESH)
    for turn in turns:
        target = lax.rem(lax.axis_index("replica") + turn, replicas)
        pl.semaphore_signal(barrier, inc=1, device_id={"replica": target}, device_id_type=MESH)
    pl.semaphore_wait(barrier, len(devices) + len(turns) + more)


def replica_copy(source, target, turn, send_sems, recv_sems, base):
    replicas = lax.axis_size("replica")
    device = lax.rem(lax.axis_index("replica") + replicas - turn, replicas)
    return pltpu.make_async_remote_copy(
        source, target, send_sems.at[base + turn], recv_sems.at[base + turn],
        device_id={"replica": device}, device_id_type=MESH,
    )


CHUNK = 512


def feed_kernel(backward, rows, target, *refs):
    if backward:
        (mine_ref, gate_up_hbm, first_hbm, second_hbm, result_ref, all_hbm, others_hbm,
         mid_ref, all_ref, gate_up_ref, first_ref, second_ref, part_ref, take_ref, sent_ref, land_ref, own_ref,
         own_take_ref, load_sems, keep_sems, hold_sems, send_sems, recv_sems) = refs
    else:
        (mine_ref, middle_hbm, first_hbm, second_hbm, result_ref, all_hbm, gate_up_hbm, others_hbm, next_hbm,
         mid_ref, all_ref, gate_up_ref, first_ref, second_ref, part_ref, take_ref, sent_ref, land_ref, own_ref,
         own_take_ref, middle_ref, load_sems, keep_sems, hold_sems, send_sems, recv_sems) = refs
    shard, beside, across, _ = slice_peers()
    chip, core = shard // 2, shard % 2
    half = rows // 2
    parts, spans, _, piece, span_cols = part_ref.shape
    block = 2 * piece
    width = all_ref.shape[1]
    ff = first_ref.shape[0] if backward else second_ref.shape[0]
    first_steps = ff // CHUNK

    def load_first(at):
        if backward:
            place = (pl.ds(pl.multiple_of(at * CHUNK, CHUNK), CHUNK), slice(None))
            return [pltpu.make_async_copy(first_hbm.at[place], first_ref.at[place], load_sems.at[0, at])]
        places = [
            (slice(None), pl.ds(pl.multiple_of(side * ff + at * CHUNK, CHUNK), CHUNK)) for side in range(2)
        ]
        return [
            pltpu.make_async_copy(first_hbm.at[place], first_ref.at[place], load_sems.at[side, at])
            for side, place in enumerate(places)
        ]

    def load_second(at):
        span = pl.ds(pl.multiple_of(at * span_cols, span_cols), span_cols)
        place = (span, slice(None)) if backward else (slice(None), span)
        return pltpu.make_async_copy(second_hbm.at[place], second_ref.at[place], load_sems.at[2, at])

    load_extra = []
    if backward:
        for at in range(2 * lax.axis_size("shard")):
            group, part, owner = at // 4, at // 2 % 2, at % 2
            source = pl.ds(at * half, half)
            place = pl.ds(group * 2 * rows + owner * rows + part * half, half)
            load_extra.append(pltpu.make_async_copy(gate_up_hbm.at[source], gate_up_ref.at[place], hold_sems.at[at]))
    else:
        load_extra.append(pltpu.make_async_copy(middle_hbm, middle_ref, hold_sems.at[0]))
    if backward:
        for copy in load_extra:
            copy.start()
    for at in range(first_steps):
        for copy in load_first(at):
            copy.start()
    for at in range(spans):
        load_second(at).start()
    if not backward:
        load_extra[0].start()

    def remote(source, target, at, device):
        return pltpu.make_async_remote_copy(
            source, target, send_sems.at[at], recv_sems.at[at], device_id={"shard": device}, device_id_type=MESH
        )

    def place_of(owner, part):
        start = part * block + (owner % 2) * piece if parts == 2 else (owner % 2) * piece + part * half
        return pl.ds(pl.multiple_of((owner // 2) * 2 * rows + start, half), half)

    def owned(owner, part):
        return all_ref.at[place_of(owner, part)]

    turns = range(1, lax.axis_size("replica"), 2)
    base = 6 + (2 * parts + 1) * spans
    slice_barrier((beside, across), turns, 0 if target is None else 1)

    def hand_on(part, at):
        place = (pl.ds(part * piece, piece), pl.ds(at * span_cols, span_cols))
        return section_copy(
            result_ref.at[place], next_hbm.at[place], part * spans + at + base + lax.axis_size("replica"),
            send_sems, recv_sems, target,
        )

    def across_copy(part):
        return remote(owned(shard, part), owned(shard, part), part, across)

    def relay(part):
        return remote(owned(across, part), owned(across, part), 4 + part, beside)

    beside_copies = [remote(owned(shard, part), owned(shard, part), 2 + part, beside) for part in range(2)]
    for part in range(2):
        all_ref[place_of(shard, part), :] = mine_ref[part * half : (part + 1) * half, :]
        across_copy(part).start()
    for copy in beside_copies:
        copy.start()
    spread_copies = [
        replica_copy(mine_ref, others_hbm.at[lax.axis_index("replica")], turn, send_sems, recv_sems, base)
        for turn in turns
    ]
    for copy in spread_copies:
        copy.start()

    def first_product(start, count, waits):
        span = pl.ds(pl.multiple_of(start, count), count)

        def step(at, carry):
            cols = pl.ds(pl.multiple_of(at * CHUNK, CHUNK), CHUNK)
            high = pl.ds(pl.multiple_of(ff + at * CHUNK, CHUNK), CHUNK)
            if waits:
                for copy in load_first(at):
                    copy.wait()
            if backward:
                grad_hidden = dot_rows(all_ref[span, :], first_ref[cols, :])
                gate = gate_up_ref[span, cols].astype(F32)
                up = gate_up_ref[span, high].astype(F32)
                sigmoid = jax.nn.sigmoid(gate)
                mid_ref[span, cols] = (grad_hidden * up * sigmoid * (1.0 + gate * (1.0 - sigmoid))).astype(BF)
                mid_ref[span, high] = (grad_hidden * gate * sigmoid).astype(BF)
            else:
                gate = dot(all_ref[span, :], first_ref[:, cols])
                up = dot(all_ref[span, :], first_ref[:, high])
                gate_up_ref[span, cols] = gate.astype(BF)
                gate_up_ref[span, high] = up.astype(BF)
                mid_ref[span, cols] = (gate * jax.nn.sigmoid(gate) * up).astype(BF)
            return carry

        lax.fori_loop(0, first_steps, step, 0)

    def second_product(start, count, at, store):
        span = pl.ds(pl.multiple_of(start, count), count)

        def step(inner, carry):
            cols = pl.ds(pl.multiple_of(at * span_cols + inner * CHUNK, CHUNK), CHUNK)
            if backward:
                partial = dot_rows(mid_ref[span, :], second_ref[cols, :])
            else:
                partial = dot(mid_ref[span, :], second_ref[:, cols])
            store(pl.ds(pl.multiple_of(inner * CHUNK, CHUNK), CHUNK), partial.astype(BF))
            return carry

        lax.fori_loop(0, span_cols // CHUNK, step, 0)

    def give(part, at):
        return remote(part_ref.at[part, at, 1 - core], take_ref.at[part, at], 6 + part * spans + at, beside)

    def cross(part, at):
        return remote(sent_ref.at[part, at], land_ref.at[part, at], 6 + (parts + part) * spans + at, across)

    def give_own(at):
        return remote(own_ref.at[at, 1 - core], own_take_ref.at[at], 6 + 2 * parts * spans + at, beside)

    def pass_on(part, at):
        give(part, at).wait_recv()
        sent_ref[part, at] = (part_ref[part, at, core].astype(F32) + take_ref[part, at].astype(F32)).astype(BF)
        cross(part, at).start()

    own_start = chip * 2 * rows
    other_start = (1 - chip) * 2 * rows
    stores = []
    for copy in beside_copies:
        copy.wait_recv()
    if backward:
        for copy in load_extra:
            copy.wait()
    first_product(own_start, 2 * rows, True)
    if not backward:
        own_place = pl.ds(pl.multiple_of(own_start, 2 * rows), 2 * rows)
        stores.append(pltpu.make_async_copy(gate_up_ref.at[own_place], gate_up_hbm.at[own_place], keep_sems.at[1]))
        stores[-1].start()

    def store_part(part):
        place = pl.ds(pl.multiple_of(other_start + part * block, block), block)
        return pltpu.make_async_copy(gate_up_ref.at[place], gate_up_hbm.at[place], keep_sems.at[2 + part])

    def arrive(part):
        across_copy(part).wait_recv()
        relay(part).start()

    if parts == 1:
        for part in range(2):
            arrive(part)

    def other_part(part, carry):
        if parts == 1:
            for late in range(2):
                relay(late).wait_recv()
        else:
            arrive(part)
            relay(part).wait_recv()
        start = other_start + part * block
        first_product(start, block, False)
        if not backward:
            store_part(part).start()

        def span_step(at, inner):
            @pl.when(part == 0)
            def _():
                load_second(at).wait()

            def store(cols, partial):
                part_ref[part, at, 0, :, cols] = partial[:piece]
                part_ref[part, at, 1, :, cols] = partial[piece:]

            second_product(start, block, at, store)
            give(part, at).start()

            @pl.when(at > 0)
            def _():
                pass_on(part, at - 1)

            return inner

        lax.fori_loop(0, spans, span_step, 0)
        pass_on(part, spans - 1)
        return carry

    lax.fori_loop(0, parts, other_part, 0)
    if not backward:
        stores += [store_part(part) for part in range(parts)]
    for owner in range(lax.axis_size("shard")):
        for part in range(2):
            at = owner * 2 + part
            copy = pltpu.make_async_copy(
                all_ref.at[place_of(owner, part)], all_hbm.at[pl.ds(owner * rows + part * half, half)],
                keep_sems.at[4 + at],
            )
            copy.start()
            stores.append(copy)

    def own_step(at, carry):
        def store(cols, partial):
            for part in range(parts):
                for owner in range(2):
                    first_row = part * block + owner * piece
                    own_ref[at, owner, part * piece : (part + 1) * piece, cols] = partial[first_row : first_row + piece]

        second_product(own_start, 2 * rows, at, store)
        give_own(at).start()
        return carry

    lax.fori_loop(0, spans, own_step, 0)
    if not backward:
        load_extra[0].wait()
    for at in range(spans):
        give_own(at).wait_recv()
        cols = slice(at * span_cols, (at + 1) * span_cols)
        for part in range(parts):
            cross(part, at).wait_recv()
            place = slice(part * piece, (part + 1) * piece)
            total = (
                own_ref[at, core, place].astype(F32)
                + own_take_ref[at, place].astype(F32)
                + land_ref[part, at].astype(F32)
            )
            if backward:
                result_ref[place, cols] = total
            else:
                result_ref[place, cols] = (middle_ref[place, cols] + total).astype(BF)
                if target is not None:
                    hand_on(part, at).start()
    for part in range(2):
        beside_copies[part].wait_send()
        across_copy(part).wait_send()
        relay(part).wait_send()
    for copy in spread_copies + stores:
        copy.wait()
    if target is not None:
        for part in range(parts):
            for at in range(spans):
                hand_on(part, at).wait_send()
    for at in range(spans):
        give_own(at).wait_send()
        for part in range(parts):
            give(part, at).wait_send()
            cross(part, at).wait_send()


def section_copy(source, target, at, send_sems, recv_sems, section):
    return pltpu.make_async_remote_copy(
        source, target, send_sems.at[at], recv_sems.at[at], device_id={"section": section}, device_id_type=MESH
    )


def feed_forward_kernel(section, last, parts, spans, rows, *refs):
    @pl.when(lax.axis_index("section") == section)
    def _():
        feed_kernel(False, rows, None if last else section + 1, *refs)

    if not last:

        @pl.when(lax.axis_index("section") == section + 1)
        def _():
            barrier = pltpu.get_barrier_semaphore()
            pl.semaphore_signal(barrier, inc=1, device_id={"section": section}, device_id_type=MESH)
            next_hbm, send_sems, recv_sems = refs[8], refs[-2], refs[-1]
            base = 6 + (2 * parts + 1) * spans + lax.axis_size("replica")
            high, wide = rows // parts, next_hbm.shape[1] // spans
            for part in range(parts):
                for at in range(spans):
                    place = next_hbm.at[pl.ds(part * high, high), pl.ds(at * wide, wide)]
                    section_copy(place, place, base + part * spans + at, send_sems, recv_sems, section).wait_recv()


def call_feed(section, backward, operands, collective):
    first, second = operands[-2], operands[-1]
    rows, width = operands[0].shape
    shards, replicas = lax.axis_size("shard"), lax.axis_size("replica")
    ff = first.shape[0] if backward else second.shape[0]
    every = shards * rows
    parts, span_cols = (1, CHUNK) if backward else (2, 2 * CHUNK)
    spans, piece_rows = width // span_cols, rows // parts
    vmem, anywhere = pl.BlockSpec(memory_space=pltpu.VMEM), pl.BlockSpec(memory_space=pl.ANY)
    out_shape = [
        jax.ShapeDtypeStruct((rows, width), F32 if backward else BF),
        jax.ShapeDtypeStruct((every, width), BF),
        jax.ShapeDtypeStruct((replicas, rows, width), BF),
    ]
    if not backward:
        out_shape.insert(2, jax.ShapeDtypeStruct((every, 2 * ff), BF))
        out_shape.append(jax.ShapeDtypeStruct((rows, width), BF))
    copies = 6 + (3 * parts + 1) * spans + replicas
    piece = pltpu.VMEM((parts, spans, piece_rows, span_cols), BF)
    scratch = [
        pltpu.VMEM((every, 2 * ff if backward else ff), BF),
        pltpu.VMEM((every, width), BF),
        pltpu.VMEM((every, 2 * ff), BF),
        pltpu.VMEM(first.shape, BF),
        pltpu.VMEM(second.shape, BF),
        pltpu.VMEM((parts, spans, 2, piece_rows, span_cols), BF),
        piece,
        piece,
        piece,
        pltpu.VMEM((spans, 2, rows, span_cols), BF),
        pltpu.VMEM((spans, rows, span_cols), BF),
    ]
    if not backward:
        scratch.append(pltpu.VMEM((rows, width), F32))
    scratch += [
        pltpu.SemaphoreType.DMA((3, max(ff // CHUNK, spans))),
        pltpu.SemaphoreType.DMA((4 + 2 * shards,)),
        pltpu.SemaphoreType.DMA((2 * shards,)),
        pltpu.SemaphoreType.DMA((copies,)),
        pltpu.SemaphoreType.DMA((copies,)),
    ]
    return pl.pallas_call(
        gated(section, functools.partial(feed_kernel, True, rows, None))
        if backward
        else functools.partial(feed_forward_kernel, section, section == lax.axis_size("section") - 1, parts, spans, rows),
        out_shape=out_shape,
        in_specs=[vmem] + [anywhere] * 3,
        out_specs=[vmem] + [anywhere] * (len(out_shape) - 1),
        scratch_shapes=scratch,
        compiler_params=pltpu.CompilerParams(
            collective_id=collective, has_side_effects=True, vmem_limit_bytes=VMEM_LIMIT
        ),
        name="feed_backward" if backward else "feed_forward",
    )(*operands)


def weights_kernel(
    qkv_ref, out_ref, gate_up_ref, state_ref, gain_one_ref, gain_two_ref, cos_ref, sin_ref, allowed_ref,
    qkv_full, out_full, gate_up_part, middle_ref, normed_two_ref, rotated_ref, lefts_ref,
    qkv_hold, out_hold, gate_up_hold, qkv_work, out_work, normed_ref, attended_ref, work_sems,
    local_sems, send_sems, recv_sems,
):
    shard, replica = lax.axis_index("shard"), lax.axis_index("replica")
    chip, core = shard // 2, shard % 2
    beside = {"shard": chip * 2 + (1 - core)}
    across = {"shard": (1 - chip) * 2 + core}
    diagonal = {"shard": (1 - chip) * 2 + (1 - core)}
    mine = replica % 2
    partner = {"replica": replica + 1 - 2 * mine}
    rows = qkv_ref.shape[0]
    half = rows // 2
    ff = gate_up_ref.shape[1] // 2
    part = gate_up_part.shape[1] // 2

    def remote(source, target, at, device):
        return pltpu.make_async_remote_copy(
            source, target, send_sems.at[at], recv_sems.at[at], device_id=device, device_id_type=MESH
        )

    def span(start, count):
        return pl.ds(pl.multiple_of(start, count), count)

    sides = [pl.ds(side * part, part) for side in range(2)]
    loads = [
        pltpu.make_async_copy(qkv_ref, qkv_hold, local_sems.at[0]),
        pltpu.make_async_copy(out_ref, out_hold, local_sems.at[1]),
    ] + [
        pltpu.make_async_copy(
            gate_up_ref.at[:, span(side * ff + shard * part, part)], gate_up_hold.at[side], local_sems.at[2 + side]
        )
        for side in range(2)
    ]
    own_rows = span(shard * rows, rows)
    stores = [
        pltpu.make_async_copy(qkv_hold, qkv_full.at[own_rows], local_sems.at[4]),
        pltpu.make_async_copy(out_hold, out_full.at[own_rows], local_sems.at[5]),
    ] + [
        pltpu.make_async_copy(gate_up_hold.at[side], gate_up_part.at[own_rows, sides[side]], local_sems.at[6 + side])
        for side in range(2)
    ]
    for copy in loads:
        copy.start()

    pieces = []
    for source, whole, count in ((qkv_ref, qkv_full, 64), (out_ref, out_full, 64)):
        for offset in range(0, half, count):

            def place(owner, part_of, whole=whole, offset=offset, count=count):
                return whole.at[span(owner["shard"] * rows + part_of * half + offset, count)]

            own = source.at[span(mine * half + offset, count)]
            pieces.append((own, place, across, True))
    for offset in range(0, half, 128):
        for side in range(2):
            for device in (across, diagonal):

                def place(owner, part_of, offset=offset, side=side):
                    return gate_up_part.at[
                        span(owner["shard"] * rows + part_of * half + offset, 128), pl.ds(side * part, part)
                    ]

                own = gate_up_ref.at[
                    span(mine * half + offset, 128), span(side * ff + device["shard"] * part, part)
                ]
                pieces.append((own, place, device, False))
    count = len(pieces)
    me = {"shard": shard}
    over = [remote(own, place(me, mine), at, device) for at, (own, place, device, _) in enumerate(pieces)]
    passed = [
        remote(place(device, mine), place(device, mine), count + at, partner)
        for at, (_, place, device, _) in enumerate(pieces)
    ]
    relays = [
        [
            remote(place(across, which), place(across, which), (2 + turn) * count + at, beside)
            if relayed
            else None
            for at, (_, place, _, relayed) in enumerate(pieces)
        ]
        for turn, which in enumerate((mine, 1 - mine))
    ]
    direct = [
        remote(qkv_ref, qkv_full.at[span(shard * rows, rows)], 4 * count, beside),
        remote(out_ref, out_full.at[span(shard * rows, rows)], 4 * count + 1, beside),
    ]
    for side in range(2):
        direct.append(
            remote(
                gate_up_ref.at[:, span(side * ff + beside["shard"] * part, part)],
                gate_up_part.at[span(shard * rows, rows), pl.ds(side * part, part)],
                4 * count + 2 + side,
                beside,
            )
        )

    barrier = pltpu.get_barrier_semaphore()
    for device in (beside, across, diagonal, partner):
        pl.semaphore_signal(barrier, inc=1, device_id=device, device_id_type=MESH)
    pl.semaphore_wait(barrier, 4)

    started = []

    def start(copy):
        copy.start()
        started.append(copy)

    ahead = 3
    for copy in over[:ahead]:
        start(copy)
    for copy in direct:
        start(copy)
    for load, store in zip(loads, stores):
        load.wait()
        store.start()
    first, load_out, second = attend_parts(
        state_ref, gain_one_ref, gain_two_ref, cos_ref, sin_ref, allowed_ref, qkv_full, out_full,
        middle_ref, normed_two_ref, rotated_ref, lefts_ref,
        qkv_work, out_work, normed_ref, attended_ref, work_sems,
    )
    qkv_last = half // 64 - 1
    out_last = qkv_last + half // 64
    arrived = [0]

    def wait_relays(last):
        for at in range(arrived[0], last + 1):
            for copies in relays:
                copies[at].wait_recv()
        arrived[0] = last + 1

    def work(parts):
        @pl.when(lax.axis_index("section") == 0)
        def _():
            for part in parts:
                part()

    ready = list(first)
    for at in range(count + 1):
        if at < count:
            over[at].wait_recv()
            start(passed[at])
            if relays[0][at] is not None:
                start(relays[0][at])
            if at + ahead < count:
                over[at].wait_send()
                started[:] = [copy for copy in started if copy is not over[at]]
                start(over[at + ahead])
        if at > 0:
            passed[at - 1].wait_recv()
            if relays[1][at - 1] is not None:
                start(relays[1][at - 1])
        if at == qkv_last + 2:
            wait_relays(qkv_last)
            direct[0].wait_recv()
            stores[0].wait()
        if at == out_last + 2:
            wait_relays(out_last)
            direct[1].wait_recv()
            stores[1].wait()
            work([load_out])
            ready += second
        if at >= qkv_last + 2:
            work(ready[:3])
            ready = ready[3:]
    work(ready)
    for copy in direct[2:]:
        copy.wait_recv()
    for copy in stores[2:]:
        copy.wait()
    for copy in started:
        copy.wait_send()


def call_weights(qkv_weight, out_weight, gate_up_weight, operands, collective):
    shards = lax.axis_size("shard")
    rows = qkv_weight.shape[0]
    count = 2 * (rows // 128) + rows // 64
    out_shape, scratch = attend_shapes(*operands[0].shape, qkv_weight.shape[1])
    vmem = pl.BlockSpec(memory_space=pltpu.VMEM)
    anywhere = pl.BlockSpec(memory_space=pl.ANY)
    return pl.pallas_call(
        weights_kernel,
        out_shape=[
            jax.ShapeDtypeStruct((shards * rows, qkv_weight.shape[1]), BF),
            jax.ShapeDtypeStruct((shards * rows, out_weight.shape[1]), BF),
            jax.ShapeDtypeStruct((shards * rows, gate_up_weight.shape[1] // shards), BF),
        ] + out_shape,
        in_specs=[anywhere] * 3 + [vmem] * len(operands),
        out_specs=[anywhere] * 3 + [vmem] * len(out_shape),
        scratch_shapes=[
            pltpu.VMEM(qkv_weight.shape, BF),
            pltpu.VMEM(out_weight.shape, BF),
            pltpu.VMEM((2, rows, gate_up_weight.shape[1] // (2 * shards)), BF),
            *scratch,
            pltpu.SemaphoreType.DMA((8,)),
            pltpu.SemaphoreType.DMA((4 * count + 4,)),
            pltpu.SemaphoreType.DMA((4 * count + 4,)),
        ],
        compiler_params=pltpu.CompilerParams(
            collective_id=collective, has_side_effects=True, vmem_limit_bytes=VMEM_LIMIT
        ),
        name="weights",
    )(qkv_weight, out_weight, gate_up_weight, *operands)


def repeat(first, last, body):
    def step(at, carry):
        body(at)
        return carry

    if first < last:
        lax.fori_loop(first, last, step, 0)


def by_chunk(count, body):
    repeat(0, count, lambda at: body(pl.ds(pl.multiple_of(at * CHUNK, CHUNK), CHUNK)))


def weight_grads_kernel(sections, left_rows_ref, hidden_ref, *refs):
    sources = [refs[at * sections : (at + 1) * sections] for at in range(7)]
    (gate_up_hbm, down_hbm,
     gate_up_grad_ref, down_grad_ref, qkv_grad_ref, out_grad_ref, gain_sum_ref, gathered_hbm, even_hbm,
     projected_ref, upstream_ref, gains_ref, gains_land_ref, gain_part_ref, gains_last_ref, lefts_ref, left_ref,
     extra_ref, terms_ref, chain_ref, down_ref, block_ref, gate_up_ref, mid_ref, sum_ref, stage_ref,
     start_sems, load_sems, block_sems, keep_sem, send_sems, recv_sems) = refs[7 * sections :]
    shard, beside, across, diagonal = slice_peers()
    peers = (across, diagonal, beside)
    replica, replicas = lax.axis_index("replica"), lax.axis_size("replica")
    here = [lax.axis_index("section") == section for section in range(sections)]
    rows, cols = projected_ref.shape
    every, width = sources[5][0].shape
    pieces, all_pieces = cols // CHUNK, (cols + width) // CHUNK
    staged = stage_ref.shape[2] // CHUNK
    kinds, groups, _, sub_rows, _ = lefts_ref.shape
    part = down_ref.shape[0]
    half_part = part // 2
    ff = gate_up_grad_ref.shape[1] // 2
    steps = half_part // CHUNK
    wide = width // CHUNK
    out_rows = gate_up_grad_ref.shape[0]
    piece_base = 3 * replicas
    spread_base = piece_base + 3 * pieces
    gain_base = spread_base + replicas
    left_base = gain_base + replicas
    chain_base = left_base + kinds * groups * 3
    last_base = chain_base + 2 * replicas
    grad_base = last_base + 3

    def remote(source, target, at, device):
        return pltpu.make_async_remote_copy(
            source, target, send_sems.at[at], recv_sems.at[at], device_id={"shard": device}, device_id_type=MESH
        )

    def owned(owner):
        return pl.ds(pl.multiple_of(owner * rows, rows), rows)

    def piece_place(piece, place=None):
        if piece < 2 * staged:
            place = pl.ds(0, every) if place is None else place
            return stage_ref.at[piece // staged, place, pl.ds(piece % staged * CHUNK, CHUNK)]
        return extra_ref.at[piece - 2 * staged] if place is None else extra_ref.at[piece - 2 * staged, place]

    def piece_copy(owner, piece, kind, device):
        place = piece_place(piece, owned(owner))
        return remote(place, place, piece_base + kind * pieces + piece, device)

    over = [piece_copy(shard, piece, 0, across) for piece in range(pieces)]
    direct = [piece_copy(shard, piece, 1, beside) for piece in range(pieces)]
    relays = [piece_copy(across, piece, 2, beside) for piece in range(pieces)]

    def hand_left(kind, group, peer):
        return remote(
            lefts_ref.at[kind, group, peers[peer]], left_ref.at[kind, group, :, owned(shard)],
            left_base + (kind * groups + group) * 3 + peer, peers[peer],
        )

    lefts = [(kind, group, peer) for kind in reversed(range(kinds)) for group in range(groups) for peer in range(3)]
    loads = []
    for at, target in enumerate((lefts_ref, projected_ref, gains_ref, upstream_ref)):
        loads.append([pltpu.make_async_copy(source, target, start_sems.at[at]) for source in sources[at]])
    load_branch = [
        [
            pltpu.make_async_copy(source.at[piece - pieces], piece_place(piece), start_sems.at[4 + piece - pieces])
            for source in sources[4]
        ]
        for piece in range(pieces, all_pieces)
    ]
    load_own = [pltpu.make_async_copy(source, block_ref.at[0], load_sems.at[2, 0]) for source in sources[5]]
    load_down = pltpu.make_async_copy(down_hbm, down_ref, load_sems.at[3, 0])

    def block_at(turn):
        return lax.rem(replica + turn, replicas)

    def tokens(turn):
        return pl.ds(pl.multiple_of(block_at(turn) * every, every), every)

    def load_gate_up(half, turn, side):
        place = pl.ds(side * part + half * half_part, half_part)
        slot = lax.rem(turn, 2)
        return pltpu.make_async_copy(
            gate_up_hbm.at[tokens(turn), place], gate_up_ref.at[slot, side], load_sems.at[side, slot]
        )

    def block_copies(turn, source):
        slot = lax.rem(turn, 2)
        copies = []
        for at, owner in enumerate(peers + (shard,)):
            own = gathered_hbm.at[turn, owned(owner)] if source is None or at < 3 else source.at[block_at(turn)]
            copies.append(pltpu.make_async_copy(own, block_ref.at[slot, owned(owner)], block_sems.at[slot, at]))
        return copies

    def load_block(turn):
        for copy in block_copies(turn, None)[:3]:
            copy.start()
        cases = [(turn == 0, None), ((turn > 0) & (turn % 2 == 0), even_hbm)]
        for section in range(sections):
            odd_case = here[section] & (turn % 2 == 1)
            cases.append((odd_case, sources[6][section]))
        for case, source in cases:

            @pl.when(case)
            def _(source=source):
                block_copies(turn, source)[3].start()

    def wait_block(turn):
        for copy in block_copies(turn, None):
            copy.wait()

    def landing(turn, owner):
        return gathered_hbm.at[turn, owned(owner)]

    def block_over(turn, source):
        return remote(source.at[block_at(turn)], landing(turn, shard), 3 * turn, across)

    def block_direct(turn, source):
        return remote(source.at[block_at(turn)], landing(turn, shard), 3 * turn + 1, beside)

    def block_relay(turn):
        return remote(landing(turn, across), landing(turn, across), 3 * turn + 2, beside)

    def send_block(turn):
        cases = [(turn % 2 == 0, even_hbm)]
        for section in range(sections):
            odd_case = here[section] & (turn % 2 == 1)
            cases.append((odd_case, sources[6][section]))
        for case, source in cases:

            @pl.when(case)
            def _(source=source):
                block_over(turn, source).start()
                block_direct(turn, source).start()

    def chain_slot(block, at):
        return replicas - (replicas - block) * ((at - block + replicas - 1) // replicas)

    def chain_up(block):
        return pltpu.make_async_remote_copy(
            chain_ref.at[block], chain_ref.at[block], send_sems.at[chain_base + block],
            recv_sems.at[chain_base + block], device_id={"replica": replica + 1}, device_id_type=MESH,
        )

    def chain_down(block):
        return pltpu.make_async_remote_copy(
            chain_ref.at[block], chain_ref.at[chain_slot(block, replica - 1)],
            send_sems.at[chain_base + replicas + block],
            recv_sems.at[chain_base + replicas + block], device_id={"replica": replica - 1}, device_id_type=MESH,
        )

    def add_terms(block):
        def add(place):
            total = chain_ref[block, :, place].astype(F32) + terms_ref[block, :, place].astype(F32)
            chain_ref[block, :, place] = total.astype(BF)

        by_chunk(all_pieces, add)

    def take_terms(block):
        def take(place):
            chain_ref[block, :, place] = terms_ref[block, :, place]

        by_chunk(all_pieces, take)

    def chain_step(step):
        high = replicas - 1 - step + replica

        @pl.when((replica > 0) & (step >= replica))
        def _():
            chain_up(high).wait_recv()

            @pl.when(step < replicas - 1)
            def _():
                add_terms(high)
                chain_up(high).start()

        low = step - (replicas - 1 - replica)

        @pl.when((replica < replicas - 1) & (step >= replicas - 1 - replica))
        def _():
            chain_down(low).wait_recv()

            @pl.when(step < replicas - 1)
            def _():
                add_terms(low)
                chain_down(low).start()

    def gain_copy(peer):
        return remote(gain_part_ref, gains_last_ref.at[shard], last_base + peer, peers[peer])

    def send_grad(half, at, peer):
        device = peers[peer]
        place = pl.ds(pl.multiple_of(at * CHUNK, CHUNK), CHUNK)
        target = pl.ds(
            pl.multiple_of(
                (at // steps) * ff + shard * part + half * half_part + (at % steps) * CHUNK, CHUNK
            ),
            CHUNK,
        )
        return remote(
            stage_ref.at[half, pl.ds(pl.multiple_of(device * out_rows, out_rows), out_rows), place],
            gate_up_grad_ref.at[:, target],
            grad_base + (half * 2 * steps + at) * 3 + peer,
            device,
        )

    def clear_sum():
        def clear(place):
            sum_ref[:, place] = jnp.zeros((sum_ref.shape[0], CHUNK), F32)

        by_chunk(2 * steps, clear)

    def compute(half, turn):
        slot = lax.rem(turn, 2)
        later = lax.rem(turn + 1, replicas)
        for side in range(2):
            load_gate_up(half, turn, side).wait()

        @pl.when(turn + 1 < replicas)
        def _():
            for side in range(2):
                load_gate_up(half, later, side).start()
            if half:
                load_block(later)

        def products(at, inner):
            place = pl.ds(pl.multiple_of(at * CHUNK, CHUNK), CHUNK)
            high = pl.ds(pl.multiple_of(half_part + at * CHUNK, CHUNK), CHUNK)
            down_rows = pl.ds(pl.multiple_of(half * half_part + at * CHUNK, CHUNK), CHUNK)
            grad_hidden = dot_rows(block_ref[slot], down_ref[down_rows, :])
            gate = gate_up_ref[slot, 0, :, place].astype(F32)
            up = gate_up_ref[slot, 1, :, place].astype(F32)
            sigmoid = jax.nn.sigmoid(gate)
            mid_ref[:, place] = (grad_hidden * up * sigmoid * (1.0 + gate * (1.0 - sigmoid))).astype(BF)
            mid_ref[:, high] = (grad_hidden * gate * sigmoid).astype(BF)
            return inner

        lax.fori_loop(0, steps, products, 0)

        def sums(at, inner):
            place = pl.ds(pl.multiple_of(at * CHUNK, CHUNK), CHUNK)
            total = sum_ref[:, place] + dot(left_rows_ref[:, tokens(turn)], mid_ref[:, place])

            @pl.when(turn < replicas - 1)
            def _():
                sum_ref[:, place] = total

            @pl.when(turn == replicas - 1)
            def _():
                stage_ref[half, pl.ds(0, total.shape[0]), place] = total.astype(BF)
                for peer in range(3):
                    send_grad(half, at, peer).start()

            return inner

        lax.fori_loop(0, 2 * steps, sums, 0)

    def first_pass(turn, carry):
        block_over(turn, even_hbm).wait_recv()
        block_relay(turn).start()
        block_direct(turn, even_hbm).wait_recv()
        block_relay(turn).wait_recv()
        load_block(turn)

        @pl.when(turn + 2 < replicas)
        def _():
            send_block(turn + 2)

        wait_block(turn)
        compute(0, turn)
        return carry

    def second_pass(turn, carry):
        compute(1, turn)

        @pl.when(turn + 1 < replicas)
        def _():
            wait_block(lax.rem(turn + 1, replicas))

        return carry

    for copies in loads + load_branch + [load_own]:
        start_own(copies)
    load_down.start()
    for side in range(2):
        load_gate_up(0, 0, side).start()

    barrier = pltpu.get_barrier_semaphore()
    for device in peers:
        pl.semaphore_signal(barrier, inc=1, device_id={"shard": device}, device_id_type=MESH)
    for turn in range(1, replicas):
        target = lax.rem(replica + turn, replicas)
        pl.semaphore_signal(barrier, inc=1, device_id={"replica": target}, device_id_type=MESH)
    pl.semaphore_wait(barrier, 2 + replicas)

    spread_copies = [
        replica_copy(upstream_ref, even_hbm.at[replica], turn, send_sems, recv_sems, spread_base)
        for turn in range(2, replicas, 2)
    ]
    gain_copies = [
        replica_copy(gains_ref, gains_land_ref.at[replica], turn, send_sems, recv_sems, gain_base)
        for turn in range(1, replicas)
    ]
    loads[0][0].wait()
    for place in lefts:
        hand_left(*place).start()
    loads[1][0].wait()
    for piece in range(pieces):
        piece_place(piece, owned(shard))[...] = projected_ref[:, piece * CHUNK : (piece + 1) * CHUNK]
        over[piece].start()
        direct[piece].start()
    loads[2][0].wait()
    gains_land_ref[replica] = gains_ref[...]
    loads[3][0].wait()
    for copy in gain_copies + spread_copies:
        copy.start()
    for kind in range(kinds):
        for group in range(groups):
            left_ref[kind, group, :, owned(shard)] = lefts_ref[kind, group, shard]
    load_own[0].wait()
    keep_own = pltpu.make_async_copy(block_ref.at[0], gathered_hbm.at[0], keep_sem)
    keep_own.start()
    clear_sum()
    load_down.wait()
    compute(0, 0)
    keep_own.wait()

    def product(piece, kind, source):
        left = jnp.concatenate([left_ref[kind, group] for group in range(groups)], 0)
        total = dot(left, source).astype(BF)
        place = pl.ds(pl.multiple_of(piece * CHUNK, CHUNK), CHUNK)
        for group in range(groups):
            terms_ref[group, :, place] = total[group * sub_rows : (group + 1) * sub_rows]

    def staged_product(piece, kind):
        place = pl.ds(pl.multiple_of(piece % staged * CHUNK, CHUNK), CHUNK)
        product(piece, kind, stage_ref[piece // staged, pl.ds(0, every), place])

    for place in lefts:
        hand_left(*place).wait_recv()
    for copies in load_branch:
        copies[0].wait()
    repeat(pieces, min(all_pieces, 2 * staged), lambda piece: staged_product(piece, 1))
    repeat(2 * staged, all_pieces, lambda piece: product(piece, 1, extra_ref[piece - 2 * staged]))
    for piece in range(pieces):
        over[piece].wait_recv()
        relays[piece].start()
    for copy in over:
        copy.wait_send()
    for copy in spread_copies:
        copy.wait()
    for turn in range(1, min(3, replicas)):
        send_block(turn)
    for copy in direct + relays:
        copy.wait()
    repeat(0, pieces, lambda piece: staged_product(piece, 0))
    for block in reversed(range(1, replicas)):

        @pl.when(replica == 0)
        def _(block=block):
            take_terms(block)
            chain_up(block).start()

    for block in range(replicas - 1):

        @pl.when(replica == replicas - 1)
        def _(block=block):
            take_terms(block)
            chain_down(block).start()

    for copy in gain_copies:
        copy.wait()
    gain_part_ref[...] = jnp.sum(gains_land_ref[...], 0)
    gains_last_ref[shard] = gain_part_ref[...]
    for peer in range(3):
        gain_copy(peer).start()
    lax.fori_loop(1, replicas - 1, first_pass, 0)
    chain_step(1)
    first_pass(replicas - 1, 0)
    for side in range(2):
        load_gate_up(1, 0, side).start()
    load_block(0)
    clear_sum()
    wait_block(0)
    lax.fori_loop(0, replicas, second_pass, 0)
    load_block(0)
    if replicas > 2:
        chain_step(2)
    wait_block(0)

    def clear_down(place):
        down_grad_ref[:, place] = jnp.zeros((down_grad_ref.shape[0], CHUNK), F32)

    by_chunk(wide, clear_down)

    def down_pass(turn, carry):
        slot = lax.rem(turn, 2)
        later = lax.rem(turn + 1, replicas)

        @pl.when(turn + 1 < replicas)
        def _():
            load_block(later)

        def down_sums(at, inner):
            place = pl.ds(pl.multiple_of(at * CHUNK, CHUNK), CHUNK)
            down_grad_ref[:, place] += dot(hidden_ref[:, tokens(turn)], block_ref[slot, :, place])
            return inner

        lax.fori_loop(0, wide, down_sums, 0)

        @pl.when(turn + 1 < replicas)
        def _():
            wait_block(later)

        return carry

    lax.fori_loop(0, replicas, down_pass, 0)
    for peer in range(3):
        gain_copy(peer).wait()
    gain_sum_ref[...] = jnp.sum(gains_last_ref[...], 0)
    own = pl.ds(pl.multiple_of(shard * out_rows, out_rows), out_rows)
    for half in range(2):

        def store_own(at, carry, half=half):
            place = pl.ds(pl.multiple_of(at * CHUNK, CHUNK), CHUNK)
            target = pl.ds(
                pl.multiple_of(
                    (at // steps) * ff + shard * part + half * half_part + (at % steps) * CHUNK, CHUNK
                ),
                CHUNK,
            )
            gate_up_grad_ref[:, target] = stage_ref[half, own, place]
            return carry

        lax.fori_loop(0, 2 * steps, store_own, 0)
    for step in range(3, replicas):
        chain_step(step)

    def sum_up(grad_ref, first):
        def add(place):
            source = pl.ds(pl.multiple_of(first + place.start, CHUNK), CHUNK)
            grad_ref[:, place] = terms_ref[replica, :, source].astype(F32)

            @pl.when(replica > 0)
            def _():
                grad_ref[:, place] += chain_ref[replica, :, source].astype(F32)

            @pl.when(replica < replicas - 1)
            def _():
                grad_ref[:, place] += chain_ref[replicas, :, source].astype(F32)

        by_chunk(grad_ref.shape[1] // CHUNK, add)

    sum_up(qkv_grad_ref, 0)
    sum_up(out_grad_ref, cols)
    for half in range(2):

        def finish(at, carry, half=half):
            for peer in range(3):
                send_grad(half, at, peer).wait()
            return carry

        lax.fori_loop(0, 2 * steps, finish, 0)
    for place in lefts:
        hand_left(*place).wait_send()
    for turn in range(1, replicas):
        block_over(turn, even_hbm).wait_send()
        block_direct(turn, even_hbm).wait_send()
        block_relay(turn).wait_send()

    for block in range(1, replicas):

        @pl.when(replica < block)
        def _(block=block):
            chain_up(block).wait_send()

    for block in range(replicas - 1):

        @pl.when(replica > block)
        def _(block=block):
            chain_down(block).wait_send()


def call_weight_grads(left_rows, hidden, lefts, projected, gains, upstream, branch, slices, odd, gate_up, down,
                      collective):
    replicas, shards, sections = lax.axis_size("replica"), lax.axis_size("shard"), len(projected)
    rows, cols = projected[0].shape
    every, width = slices[0].shape
    part = down.shape[0]
    slice_rows = left_rows.shape[0]
    sub_rows = slice_rows // shards
    lefts = [values.reshape(2, replicas, shards, sub_rows, rows) for values in lefts]
    pieces, all_pieces = cols // CHUNK, (cols + width) // CHUNK
    copies = 3 * replicas + 3 * pieces + 2 * replicas + 6 * replicas + 2 * replicas + 3 + 3 * 2 * (part // CHUNK)
    vmem, anywhere = pl.BlockSpec(memory_space=pltpu.VMEM), pl.BlockSpec(memory_space=pl.ANY)
    gain_shape = gains[0].shape
    return pl.pallas_call(
        functools.partial(weight_grads_kernel, sections),
        out_shape=[
            jax.ShapeDtypeStruct((sub_rows, 2 * part * shards), BF),
            jax.ShapeDtypeStruct((hidden.shape[0], width), F32),
            jax.ShapeDtypeStruct((sub_rows, cols), F32),
            jax.ShapeDtypeStruct((sub_rows, width), F32),
            jax.ShapeDtypeStruct(gain_shape, F32),
            jax.ShapeDtypeStruct((replicas, every, width), BF),
            jax.ShapeDtypeStruct((replicas, rows, width), BF),
        ],
        in_specs=[vmem] * 2 + [anywhere] * (7 * sections + 2),
        out_specs=[vmem] * 5 + [anywhere] * 2,
        scratch_shapes=[
            pltpu.VMEM((rows, cols), BF),
            pltpu.VMEM((rows, width), BF),
            pltpu.VMEM(gain_shape, F32),
            pltpu.VMEM((replicas,) + gain_shape, F32),
            pltpu.VMEM(gain_shape, F32),
            pltpu.VMEM((shards,) + gain_shape, F32),
            pltpu.VMEM(lefts[0].shape, BF),
            pltpu.VMEM((2, replicas, sub_rows, every), BF),
            pltpu.VMEM((max(1, all_pieces - 2 * (part // CHUNK)), every, CHUNK), BF),
            pltpu.VMEM((replicas, sub_rows, cols + width), BF),
            pltpu.VMEM((replicas + 1, sub_rows, cols + width), BF),
            pltpu.VMEM(down.shape, BF),
            pltpu.VMEM((2, every, width), BF),
            pltpu.VMEM((2, 2, every, part // 2), BF),
            pltpu.VMEM((every, part), BF),
            pltpu.VMEM((slice_rows, part), F32),
            pltpu.VMEM((2, max(slice_rows, every), part), BF),
            pltpu.SemaphoreType.DMA((4 + all_pieces - pieces,)),
            pltpu.SemaphoreType.DMA((4, 2)),
            pltpu.SemaphoreType.DMA((2, 4)),
            pltpu.SemaphoreType.DMA,
            pltpu.SemaphoreType.DMA((copies,)),
            pltpu.SemaphoreType.DMA((copies,)),
        ],
        compiler_params=pltpu.CompilerParams(
            collective_id=collective, has_side_effects=True, vmem_limit_bytes=VMEM_LIMIT
        ),
        name="weight_grads",
    )(left_rows, hidden, *lefts, *projected, *gains, *upstream, *branch, *slices, *odd, gate_up, down)


def turn_order(replicas):
    return [0] + list(range(1, replicas, 2)) + list(range(2, replicas, 2))


def prepare_kernel(sections, gate_up_hbm, *refs):
    slices, normed_two, odd = [refs[at * sections : (at + 1) * sections] for at in range(3)]
    (gathered_hbm, gate_up_all_hbm, hidden_hbm, left_rows_ref,
     normed_two_ref, weight_ref, block_ref, gate_up_ref, hidden_ref, turned_ref,
     load_sems, store_sems, block_sems, start_sems, send_sems, recv_sems) = refs[3 * sections :]
    shard, beside, across, diagonal = slice_peers()
    peers = (across, diagonal, beside)
    replica, replicas = lax.axis_index("replica"), lax.axis_size("replica")
    shards = lax.axis_size("shard")
    rows, width = normed_two_ref.shape
    every = rows * shards
    part = hidden_ref.shape[1]
    ff_rows = hidden_hbm.shape[0]
    steps = part // CHUNK
    slice_rows = left_rows_ref.shape[0]
    owner = (replica * shards) // replicas
    first_col = lax.rem(replica * shards, replicas) * ff_rows

    def load_weight(side, at):
        place = (slice(None), pl.ds(pl.multiple_of(side * part + at * CHUNK, CHUNK), CHUNK))
        return pltpu.make_async_copy(gate_up_hbm.at[place], weight_ref.at[place], load_sems.at[side, at])

    for at in range(steps):
        for side in range(2):
            load_weight(side, at).start()

    def remote(source, target, at, device):
        return pltpu.make_async_remote_copy(
            source, target, send_sems.at[at], recv_sems.at[at], device_id={"shard": device}, device_id_type=MESH
        )

    def landing(turn, who):
        return gathered_hbm.at[turn, pl.ds(pl.multiple_of(who * rows, rows), rows)]

    def own_sources(turn):
        if turn % 2:
            return [source.at[lax.rem(replica + turn, replicas)] for source in odd]
        return [landing(turn, shard)]

    def over(turn, source=None):
        return remote(landing(turn, shard) if source is None else source, landing(turn, shard), 3 * turn, across)

    def direct(turn, source=None):
        return remote(landing(turn, shard) if source is None else source, landing(turn, shard), 3 * turn + 1, beside)

    def send_block(turn):
        if turn % 2 == 0:
            from_replica(turn).wait_recv()
        copies = [(over(turn, source), direct(turn, source)) for source in own_sources(turn)]
        for section, pair in enumerate(copies):
            if len(copies) == 1:
                for copy in pair:
                    copy.start()
            else:

                @pl.when(lax.axis_index("section") == section)
                def _(pair=pair):
                    for copy in pair:
                        copy.start()

    def relay(turn):
        return remote(landing(turn, across), landing(turn, across), 3 * turn + 2, beside)

    def from_replica(turn):
        return replica_copy(normed_two_ref, landing(turn, shard), turn, send_sems, recv_sems, 3 * replicas)

    def tokens(turn):
        return pl.ds(pl.multiple_of(lax.rem(replica + turn, replicas) * every, every), every)

    def load_block(turn, slot):
        copies = []
        for at, owner in enumerate(peers + (shard,)):
            sources = own_sources(turn) if at == 3 else [landing(turn, owner)]
            place = block_ref.at[slot, pl.ds(pl.multiple_of(owner * rows, rows), rows)]
            copies.append([pltpu.make_async_copy(source, place, block_sems.at[slot, at]) for source in sources])
        return copies

    def start_block(turn, slot):
        for copies in load_block(turn, slot):
            if len(copies) == 1:
                copies[0].start()
            else:
                start_own(copies)

    def store_block(turn, slot):
        return pltpu.make_async_copy(gate_up_ref.at[slot], gate_up_all_hbm.at[tokens(turn)], store_sems.at[1, slot])

    def hand_hidden(turn, slot, peer):
        device = peers[peer]
        return remote(
            turned_ref.at[slot, device], hidden_hbm.at[:, tokens(turn)], 4 * replicas + 3 * turn + peer, device
        )

    def keep_hidden(turn, slot):
        return pltpu.make_async_copy(
            turned_ref.at[slot, shard], hidden_hbm.at[:, tokens(turn)], store_sems.at[2, slot]
        )

    loads = [
        [pltpu.make_async_copy(source, target, sem) for source in sources]
        for sources, target, sem in (
            (normed_two, normed_two_ref, start_sems.at[0]),
            (slices, block_ref.at[0], store_sems.at[0, 0]),
        )
    ]
    for copies in loads:
        start_own(copies)
    slice_barrier(peers, range(2, replicas, 2))
    order = turn_order(replicas)
    loads[0][0].wait()
    evens = [turn for turn in order if turn and turn % 2 == 0]
    for turn in evens[:1]:
        from_replica(turn).start()
    for turn in order[1:3]:
        send_block(turn)

    for at, turn in enumerate(order):
        later = order[at + 1] if at + 1 < replicas else None
        slot = at % 2
        if at and at + 2 < replicas:
            send_block(order[at + 2])
            if order[at + 2] in evens:
                place = evens.index(order[at + 2]) + 1
                if place < len(evens):
                    from_replica(evens[place]).start()
        if at:
            for copies in load_block(turn, slot):
                copies[0].wait()
        else:
            loads[1][0].wait()
        if at > 1:
            store_block(order[at - 2], slot).wait()

        def products(step, carry, at=at, slot=slot):
            cols = pl.ds(pl.multiple_of(step * CHUNK, CHUNK), CHUNK)
            high = pl.ds(pl.multiple_of(part + step * CHUNK, CHUNK), CHUNK)
            if at == 0:
                load_weight(0, step).wait()
                load_weight(1, step).wait()
            gate = dot(block_ref[slot], weight_ref[:, cols])
            up = dot(block_ref[slot], weight_ref[:, high])
            gate_up_ref[slot, :, cols] = gate.astype(BF)
            gate_up_ref[slot, :, high] = up.astype(BF)
            hidden_ref[:, cols] = (gate * jax.nn.sigmoid(gate) * up).astype(BF)
            return carry

        lax.fori_loop(0, steps, products, 0)
        store_block(turn, slot).start()
        if later is not None:
            over(later).wait_recv()
            relay(later).start()

        @pl.when(shard == owner)
        def _(at=at, turn=turn, slot=slot):
            if at > 1:
                keep_hidden(order[at - 2], slot).wait()
                for peer in range(3):
                    hand_hidden(order[at - 2], slot, peer).wait_send()

            def turn_over(device, carry):
                cols = pl.ds(pl.multiple_of(first_col + device * ff_rows, ff_rows), ff_rows)
                turned_ref[slot, device] = hidden_ref[:, cols].T
                return carry

            lax.fori_loop(0, shards, turn_over, 0)
            keep_hidden(turn, slot).start()
            for peer in range(3):
                hand_hidden(turn, slot, peer).start()

        slice_cols = pl.ds(pl.multiple_of(replica * slice_rows, slice_rows), slice_rows)
        left_rows_ref[:, tokens(turn)] = block_ref[slot, :, slice_cols].T
        if later is not None:
            direct(later).wait_recv()
            relay(later).wait_recv()
            start_block(later, 1 - slot)

    for at in range(max(0, replicas - 2), replicas):
        store_block(order[at], at % 2).wait()

        @pl.when(shard == owner)
        def _(at=at):
            keep_hidden(order[at], at % 2).wait()
            for peer in range(3):
                hand_hidden(order[at], at % 2, peer).wait_send()

    for turn in range(replicas):
        for peer in range(3):

            @pl.when(peers[peer] == owner)
            def _(turn=turn, peer=peer):
                hand_hidden(turn, 0, peer).wait_recv()

        if turn:
            over(turn).wait_send()
            direct(turn).wait_send()
            relay(turn).wait_send()
        if turn in evens:
            from_replica(turn).wait_send()


def call_prepare(normed_two, gate_up_part, slices, odd, collective):
    rows, width = normed_two[0].shape
    shards, replicas = lax.axis_size("shard"), lax.axis_size("replica")
    part = gate_up_part.shape[1] // 2
    every = rows * shards
    slice_rows = width // replicas
    ff_rows = part // replicas
    vmem, anywhere = pl.BlockSpec(memory_space=pltpu.VMEM), pl.BlockSpec(memory_space=pl.ANY)
    copies = 7 * replicas
    outs = pl.pallas_call(
        functools.partial(prepare_kernel, len(slices)),
        out_shape=[
            jax.ShapeDtypeStruct((replicas, every, width), BF),
            jax.ShapeDtypeStruct((replicas * every, 2 * part), BF),
            jax.ShapeDtypeStruct((ff_rows, replicas * every), BF),
            jax.ShapeDtypeStruct((slice_rows, replicas * every), BF),
        ],
        in_specs=[anywhere] * (1 + 3 * len(slices)),
        out_specs=[anywhere] * 3 + [vmem],
        scratch_shapes=[
            pltpu.VMEM((rows, width), BF),
            pltpu.VMEM(gate_up_part.shape, BF),
            pltpu.VMEM((2, every, width), BF),
            pltpu.VMEM((2, every, 2 * part), BF),
            pltpu.VMEM((every, part), BF),
            pltpu.VMEM((2, shards, ff_rows, every), BF),
            pltpu.SemaphoreType.DMA((2, part // CHUNK)),
            pltpu.SemaphoreType.DMA((3, 2)),
            pltpu.SemaphoreType.DMA((2, 4)),
            pltpu.SemaphoreType.DMA((1,)),
            pltpu.SemaphoreType.DMA((copies,)),
            pltpu.SemaphoreType.DMA((copies,)),
        ],
        compiler_params=pltpu.CompilerParams(
            collective_id=collective, has_side_effects=True, vmem_limit_bytes=VMEM_LIMIT
        ),
        name="prepare",
    )(gate_up_part, *slices, *normed_two, *odd)
    return outs[1:]


def on_device(
    tokens_in,
    positions,
    attn_gain,
    qkv_weight,
    out_weight,
    mlp_gain,
    gate_up_weight,
    down_weight,
    cotangent,
):
    sections = lax.axis_size("section")
    rows, width = tokens_in.shape
    down_steps = [(at + 1, at) for at in range(sections - 1)]

    cosine, sine = rope_tables(positions)
    allowed = visible(positions)

    tables = (attn_gain, mlp_gain, cosine, sine, allowed)
    qkv_full, out_full, gate_up_part, *attend_first = call_weights(
        qkv_weight[0], out_weight[0], gate_up_weight[0], (tokens_in,) + tables, 3
    )
    down_part = down_weight[0]

    forward = []
    state = tokens_in
    for section in range(sections):
        middle, normed_two, rotated, lefts = (
            call_attend_forward(section, state, *tables, qkv_full, out_full) if section else attend_first
        )
        block_out, normed_two_slice, gate_up, normed_two_odd, state_next = call_feed(
            section, False, (normed_two, middle, gate_up_part, down_part), 8 + section
        )
        forward.append((state, middle, rotated, gate_up, normed_two_slice, normed_two_odd, normed_two, lefts, block_out))
        state = state_next

    def pick(values):
        chosen = values[-1]
        for section in range(sections - 1):
            chosen = jnp.where(lax.axis_index("section") == section, values[section], chosen)
        return chosen

    slices, normed_two_odd, normed_two, lefts, block_out = list(zip(*forward))[4:]
    block_out = pick(block_out)
    backward = []
    upstream = cotangent
    for section in reversed(range(sections)):
        state, middle, rotated, gate_up = forward[section][:4]
        grad_normed_two, upstream_slice, odd = call_feed(
            section, True, (upstream, gate_up, down_part, gate_up_part), 8 + sections + section
        )
        grad_in, grad_low, grad_projected, gains, grad_branch = call_attend_backward(
            section, 8 + 2 * sections + section, grad_normed_two, upstream, middle, state, rotated,
            *tables, qkv_full, out_full,
        )
        backward.insert(0, (upstream, upstream_slice, odd, grad_in, grad_projected, gains, grad_branch))
        if section == sections - 1:
            normed_two, grad_low = lax.optimization_barrier((normed_two, grad_low))
        if section > 0:
            upstream = lax.ppermute(grad_low, "section", down_steps)
        if section == sections - 1:
            gate_up_all, hidden_rows, left_rows = call_prepare(
                normed_two, gate_up_part, slices, normed_two_odd, 6
            )
            upstream, gate_up_all, left_rows, hidden_rows = lax.optimization_barrier(
                (upstream, gate_up_all, left_rows, hidden_rows)
            )

    upstream, upstream_slice, odd, grad_in, grad_projected, gains, grad_branch = zip(*backward)
    grad_in = pick(grad_in)
    gate_up_grad, down_grad, qkv_grad, out_grad, gains, _, _ = call_weight_grads(
        left_rows, hidden_rows, lefts, grad_projected, gains, upstream, grad_branch, upstream_slice, odd,
        gate_up_all, down_part, 5,
    )
    gate_up_grad = gate_up_grad.astype(F32)
    return (
        block_out[None],
        grad_in[None],
        gains[0][None],
        qkv_grad[None],
        out_grad[None],
        gains[1][None],
        gate_up_grad[None],
        down_grad[None],
    )


def solution(mesh):
    both = ("replica", "shard")
    return jax.shard_map(
        on_device,
        mesh=mesh,
        in_specs=(
            P(both, None),
            P(both),
            P("section", None),
            P("section", "shard", None),
            P("section", "shard", None),
            P("section", None),
            P("section", "shard", None),
            P("section", "shard", None),
            P(both, None),
        ),
        out_specs=(
            P("section", both, None),
            P("section", both, None),
            P("section", None),
            P("section", both, None),
            P("section", both, None),
            P("section", None),
            P("section", both, None),
            P("section", both, None),
        ),
        check_vma=False,
    )
```

```python
import functools

import jax
import jax.numpy as jnp
from jax import lax
from jax.experimental import pallas as pl
from jax.experimental.pallas import tpu as pltpu
from jax.sharding import PartitionSpec as P

HEADS = 32
KV_HEADS = 8
HEAD = 64
SEQ = 64
EPSILON = 1e-05
ROPE_BASE = 500000.0
BF = jnp.bfloat16
F32 = jnp.float32
CONTRACT_LAST = (((1,), (1,)), ((), ()))
CONTRACT_FIRST = (((0,), (0,)), ((), ()))


MESH = pl.DeviceIdType.MESH
VMEM_LIMIT = 60 * 2**20
TILE = 128


def dot(left, right):
    return jnp.dot(left, right, preferred_element_type=F32)


def dot_rows(left, right):
    return lax.dot_general(left, right, CONTRACT_LAST, preferred_element_type=F32)


def dot_tokens(left, right):
    return lax.dot_general(left, right, CONTRACT_FIRST, preferred_element_type=F32)


def rope_tables(seq_pos):
    half_index = jnp.arange(HEAD // 2, dtype=F32)
    frequency = jnp.power(ROPE_BASE, -2.0 * half_index / HEAD)
    angles = seq_pos.astype(F32)[:, None] * frequency[None, :]
    cosine, sine = jnp.cos(angles), jnp.sin(angles)
    return (
        jnp.concatenate([cosine] * 4, 1),
        jnp.concatenate([-sine, sine, -sine, sine], 1),
    )


def visible(seq_pos):
    rows = seq_pos.shape[0]
    row_index = jnp.arange(rows)[:, None]
    col_index = jnp.arange(rows)[None, :]
    same = row_index // SEQ == col_index // SEQ
    seen = (col_index <= row_index) & (row_index - col_index <= seq_pos[:, None])
    return jnp.where(same & seen, 1.0, 0.0).astype(F32)


def lanes(rows):
    return lax.broadcasted_iota(jnp.int32, (rows, TILE), 1)


def swap_halves(tile, lane):
    return jnp.where(lane % HEAD < HEAD // 2, pltpu.roll(tile, TILE - HEAD // 2, 1), pltpu.roll(tile, HEAD // 2, 1))


def spread(tile, odd, lane):
    turned = pltpu.roll(tile, HEAD, 1)
    lower, upper = (turned, tile) if odd else (tile, turned)
    return jnp.concatenate(
        [jnp.where(lane < HEAD, lower, 0.0), jnp.where(lane < HEAD, 0.0, upper)], 0
    ).astype(BF)


def softmax_pair(queries, spread_keys, allowed):
    scores = dot_rows(queries, spread_keys) * HEAD ** (-0.5)
    halves = []
    for side in range(2):
        masked = jnp.where(allowed > 0.5, scores[:, side * TILE : (side + 1) * TILE], -1e30)
        expon = jnp.exp(masked - jnp.max(masked, -1, keepdims=True))
        halves.append(expon / jnp.sum(expon, -1, keepdims=True))
    return halves


def attend_parts(
    state_ref, gain_one_ref, gain_two_ref, cos_ref, sin_ref, allowed_ref, qkv_hbm, out_hbm,
    middle_ref, normed_two_ref, rotated_ref, lefts_ref,
    qkv_ref, out_ref, normed_ref, attended_ref, sems,
):
    rows, width = state_ref.shape
    cols = qkv_hbm.shape[1]
    step = 512
    rope_cols = (HEADS + KV_HEADS) * HEAD

    def qkv_copy(at):
        return pltpu.make_async_copy(qkv_hbm.at[:, pl.ds(at, step)], qkv_ref.at[:, pl.ds(at, step)], sems.at[at // step])

    def out_copy(at):
        return pltpu.make_async_copy(
            out_hbm.at[:, pl.ds(at, step)], out_ref.at[:, pl.ds(at, step)], sems.at[(cols + at) // step]
        )

    def begin():
        for at in range(0, cols, step):
            qkv_copy(at).start()
        state = state_ref[...].astype(F32)
        inverse = lax.rsqrt(jnp.mean(state * state, -1, keepdims=True) + EPSILON)
        normed_ref[...] = (state * inverse * gain_one_ref[...]).astype(BF)

    def project(at):
        qkv_copy(at).wait()
        lane = lanes(rows)
        projected = dot(normed_ref[...], qkv_ref[:, at : at + step])
        for tile_at in range(0, step, TILE):
            tile = projected[:, tile_at : tile_at + TILE]
            if at + tile_at < rope_cols:
                tile = tile * cos_ref[...] + swap_halves(tile, lane) * sin_ref[...]
            rotated_ref[:, at + tile_at : at + tile_at + TILE] = tile.astype(BF)

    def attend(group):
        lane = lanes(rows)
        key_at = width + group // 2 * TILE
        value_at = rope_cols + group // 2 * TILE
        keys = spread(rotated_ref[:, key_at : key_at + TILE].astype(F32), group % 2, lane)
        values = spread(rotated_ref[:, value_at : value_at + TILE].astype(F32), group % 2, lane)
        for pair in range(2):
            at = (group * 2 + pair) * TILE
            halves = softmax_pair(rotated_ref[:, at : at + TILE], keys, allowed_ref[...])
            probs = jnp.concatenate([half.astype(BF) for half in halves], 1)
            attended_ref[:, at : at + TILE] = dot(probs, values).astype(BF)

    def load_out():
        for at in range(0, width, step):
            out_copy(at).start()

    def leave(at):
        out_copy(at).wait()
        middle = state_ref[:, at : at + step].astype(F32) + dot(attended_ref[...], out_ref[:, at : at + step])
        middle_ref[:, at : at + step] = middle

    def finish():
        middle = middle_ref[...]
        inverse = lax.rsqrt(jnp.mean(middle * middle, -1, keepdims=True) + EPSILON)
        normed_two_ref[...] = (middle * inverse * gain_two_ref[...]).astype(BF)
        lefts_ref[0] = normed_ref[...].T
        lefts_ref[1] = attended_ref[...].T

    first = [begin] + [functools.partial(project, at) for at in range(0, cols, step)]
    first += [functools.partial(attend, group) for group in range(KV_HEADS)]
    second = [functools.partial(leave, at) for at in range(0, width, step)] + [finish]
    return first, load_out, second


def attend_forward(*refs):
    first, load_out, second = attend_parts(*refs)
    first[0]()
    load_out()
    for part in first[1:] + second:
        part()


def attend_backward(
    rounds, grad_ref, upstream_ref, middle_ref, state_ref, rotated_ref,
    gain_one_ref, gain_two_ref, cos_ref, sin_ref, allowed_ref, qkv_hbm, out_hbm,
    grad_state_ref, grad_low_ref, grad_projected_ref, gain_terms_ref, branch_hbm,
    qkv_ref, out_ref, grad_branch_ref, grad_out_ref, middle_grad_ref, sems, keep_sems, send_sems, recv_sems,
):
    rows, width = middle_ref.shape
    cols = qkv_hbm.shape[1]
    step = 512
    steps = width // step
    out_copies = [
        pltpu.make_async_copy(out_hbm.at[pl.ds(at * step, step)], out_ref.at[pl.ds(at * step, step)], sems.at[at])
        for at in range(steps)
    ]
    copies = [
        pltpu.make_async_copy(
            qkv_hbm.at[pl.ds(at * step, step)], qkv_ref.at[pl.ds(at * step, step)], sems.at[steps + at]
        )
        for at in range(steps)
    ]
    for copy in out_copies + copies:
        copy.start()
    shard, beside, across, _ = slice_peers()
    slice_barrier((beside, across))

    def branch_rows(owner, at):
        return branch_hbm.at[at, pl.ds(pl.multiple_of(owner * rows, rows), rows)]

    def remote(source, owner, at, kind, device):
        return pltpu.make_async_remote_copy(
            source, branch_rows(owner, at), send_sems.at[kind, at], recv_sems.at[kind, at],
            device_id={"shard": device}, device_id_type=MESH,
        )

    branch = [grad_branch_ref.at[:, pl.ds(at * step, step)] for at in range(steps)]
    over = [remote(branch[at], shard, at, 0, across) for at in range(steps)]
    direct = [remote(branch[at], shard, at, 1, beside) for at in range(steps)]
    relays = [remote(branch_rows(across, at), across, at, 2, beside) for at in range(steps)]
    keeps = [pltpu.make_async_copy(branch[at], branch_rows(shard, at), keep_sems.at[at]) for at in range(steps)]

    def norm_back(grad, values, gain):
        inverse = lax.rsqrt(jnp.mean(values * values, -1, keepdims=True) + EPSILON)
        normal = values * inverse
        term = jnp.sum(grad * normal, 0, keepdims=True)
        scaled = grad * gain
        return inverse * (scaled - normal * jnp.mean(scaled * normal, -1, keepdims=True)), term

    upstream = upstream_ref[...].astype(F32)
    back, term = norm_back(grad_ref[...], middle_ref[...], gain_two_ref[...])
    gain_terms_ref[1:2, :] = term
    middle_grad_ref[...] = upstream + back
    grad_branch_ref[...] = middle_grad_ref[...].astype(BF)
    for copy in over + direct + keeps:
        copy.start()
    for at in range(steps):
        out_copies[at].wait()
        grad_out_ref[:, at * step : (at + 1) * step] = dot_rows(
            grad_branch_ref[...], out_ref[at * step : (at + 1) * step, :]
        ).astype(BF)
    lane = lanes(rows)
    cosine, sine, allowed = cos_ref[...], sin_ref[...], allowed_ref[...]
    rope_cols = (HEADS + KV_HEADS) * HEAD
    scale = HEAD ** (-0.5)

    def unrotate(tile):
        return tile * cosine - swap_halves(tile, lane) * sine

    def group_step(group_pair, carry):
        key_at = pl.multiple_of(width + group_pair * TILE, TILE)
        value_at = pl.multiple_of(rope_cols + group_pair * TILE, TILE)
        sums = []
        for odd in range(2):
            keys = spread(rotated_ref[:, pl.ds(key_at, TILE)].astype(F32), odd, lane)
            values = spread(rotated_ref[:, pl.ds(value_at, TILE)].astype(F32), odd, lane)
            key_sum = jnp.zeros((rows, TILE), F32)
            value_sum = jnp.zeros((rows, TILE), F32)
            for pair in range(2):
                at = pl.multiple_of(((group_pair * 2 + odd) * 2 + pair) * TILE, TILE)
                queries = rotated_ref[:, pl.ds(at, TILE)]
                grad_out = grad_out_ref[:, pl.ds(at, TILE)]
                halves = softmax_pair(queries, keys, allowed)
                grad_probs = dot_rows(grad_out, values)
                grad_halves = []
                for side in range(2):
                    grad = grad_probs[:, side * TILE : (side + 1) * TILE]
                    row_dot = jnp.sum(halves[side] * grad, -1, keepdims=True)
                    grad_halves.append((halves[side] * (grad - row_dot)).astype(BF))
                grad_scores = jnp.concatenate(grad_halves, 1)
                probs = jnp.concatenate([half.astype(BF) for half in halves], 1)
                grad_projected_ref[:, pl.ds(at, TILE)] = unrotate(dot(grad_scores, keys) * scale).astype(BF)
                key_terms = dot_tokens(grad_scores, queries)
                value_terms = dot_tokens(probs, grad_out)
                key_sum += jnp.where(lane < HEAD, key_terms[:rows], key_terms[rows:])
                value_sum += jnp.where(lane < HEAD, value_terms[:rows], value_terms[rows:])
            sums.append((key_sum + pltpu.roll(key_sum, HEAD, 1), value_sum + pltpu.roll(value_sum, HEAD, 1)))
        keys_grad = jnp.where(lane < HEAD, sums[0][0], sums[1][0]) * scale
        grad_projected_ref[:, pl.ds(key_at, TILE)] = unrotate(keys_grad).astype(BF)
        grad_projected_ref[:, pl.ds(value_at, TILE)] = jnp.where(
            lane < HEAD, sums[0][1], sums[1][1]
        ).astype(BF)
        return carry

    lax.fori_loop(0, KV_HEADS // 2, group_step, 0)
    for at in range(steps):
        over[at].wait_recv()
        relays[at].start()
    for at in range(steps):
        copies[at].wait()
        grad_state_ref[:, at * step : (at + 1) * step] = dot_rows(
            grad_projected_ref[...], qkv_ref[at * step : (at + 1) * step, :]
        )
    state = state_ref[...].astype(F32)
    back, term = norm_back(grad_state_ref[...], state, gain_one_ref[...])
    gain_terms_ref[0:1, :] = term
    grad_state = middle_grad_ref[...] + back
    grad_low = grad_state.astype(BF)
    grad_low_ref[...] = grad_low
    grad_state_ref[...] = grad_low.astype(F32) if rounds else grad_state
    for copy in direct + relays:
        copy.wait()
    for copy in over:
        copy.wait_send()
    for copy in keeps:
        copy.wait()


def gated(section, body):
    def kernel(*refs):
        @pl.when(lax.axis_index("section") == section)
        def _():
            body(*refs)

    return kernel


def attend_shapes(rows, width, cols):
    return [
        jax.ShapeDtypeStruct((rows, width), F32),
        jax.ShapeDtypeStruct((rows, width), BF),
        jax.ShapeDtypeStruct((rows, cols), BF),
        jax.ShapeDtypeStruct((2, width, rows), BF),
    ], [
        pltpu.VMEM((width, cols), BF),
        pltpu.VMEM((width, width), BF),
        pltpu.VMEM((rows, width), BF),
        pltpu.VMEM((rows, width), BF),
        pltpu.SemaphoreType.DMA(((cols + width) // 512,)),
    ]


def call_attend_forward(section, *operands):
    rows, width = operands[0].shape
    out_shape, scratch = attend_shapes(rows, width, operands[6].shape[1])
    specs = [pl.BlockSpec(memory_space=pltpu.VMEM)] * 6 + [pl.BlockSpec(memory_space=pl.ANY)] * 2
    return pl.pallas_call(
        gated(section, attend_forward),
        out_shape=out_shape,
        in_specs=specs,
        out_specs=[pl.BlockSpec(memory_space=pltpu.VMEM)] * 4,
        scratch_shapes=scratch,
        compiler_params=pltpu.CompilerParams(vmem_limit_bytes=VMEM_LIMIT),
        name="attend_forward",
    )(*operands)


def call_attend_backward(section, collective, *operands):
    rows, width = operands[2].shape
    cols = operands[10].shape[1]
    steps = width // 512
    every = lax.axis_size("shard") * rows
    vmem, anywhere = pl.BlockSpec(memory_space=pltpu.VMEM), pl.BlockSpec(memory_space=pl.ANY)
    return pl.pallas_call(
        gated(section, functools.partial(attend_backward, section > 0)),
        out_shape=(
            jax.ShapeDtypeStruct((rows, width), F32),
            jax.ShapeDtypeStruct((rows, width), BF),
            jax.ShapeDtypeStruct((rows, cols), BF),
            jax.ShapeDtypeStruct((2, width), F32),
            jax.ShapeDtypeStruct((steps, every, 512), BF),
        ),
        in_specs=[vmem] * 10 + [anywhere] * 2,
        out_specs=[vmem] * 4 + [anywhere],
        scratch_shapes=[
            pltpu.VMEM((width, cols), BF),
            pltpu.VMEM((width, width), BF),
            pltpu.VMEM((rows, width), BF),
            pltpu.VMEM((rows, width), BF),
            pltpu.VMEM((rows, width), F32),
            pltpu.SemaphoreType.DMA((2 * steps,)),
            pltpu.SemaphoreType.DMA((steps,)),
            pltpu.SemaphoreType.DMA((3, steps)),
            pltpu.SemaphoreType.DMA((3, steps)),
        ],
        compiler_params=pltpu.CompilerParams(
            collective_id=collective, has_side_effects=True, vmem_limit_bytes=VMEM_LIMIT
        ),
        name="attend_backward",
    )(*operands)


def start_own(copies):
    for section, copy in enumerate(copies):

        @pl.when(lax.axis_index("section") == section)
        def _(copy=copy):
            copy.start()


def slice_peers():
    shard = lax.axis_index("shard")
    chip, core = shard // 2, shard % 2
    return shard, chip * 2 + (1 - core), (1 - chip) * 2 + core, (1 - chip) * 2 + (1 - core)


def slice_barrier(devices, turns=(), more=0):
    barrier = pltpu.get_barrier_semaphore()
    replicas = lax.axis_size("replica")
    for device in devices:
        pl.semaphore_signal(barrier, inc=1, device_id={"shard": device}, device_id_type=MESH)
    for turn in turns:
        target = lax.rem(lax.axis_index("replica") + turn, replicas)
        pl.semaphore_signal(barrier, inc=1, device_id={"replica": target}, device_id_type=MESH)
    pl.semaphore_wait(barrier, len(devices) + len(turns) + more)


def replica_copy(source, target, turn, send_sems, recv_sems, base):
    replicas = lax.axis_size("replica")
    device = lax.rem(lax.axis_index("replica") + replicas - turn, replicas)
    return pltpu.make_async_remote_copy(
        source, target, send_sems.at[base + turn], recv_sems.at[base + turn],
        device_id={"replica": device}, device_id_type=MESH,
    )


CHUNK = 512


def feed_kernel(backward, rows, target, wide, *refs):
    if backward:
        (mine_ref, gate_up_hbm, first_hbm, second_hbm, result_ref, all_hbm, others_hbm,
         mid_ref, all_ref, gate_up_ref, first_ref, second_ref, part_ref, take_ref, sent_ref, land_ref, own_ref,
         own_take_ref, load_sems, keep_sems, hold_sems, send_sems, recv_sems) = refs
    else:
        (mine_ref, middle_hbm, first_hbm, second_hbm, result_ref, all_hbm, gate_up_hbm, others_hbm, next_hbm,
         mid_ref, all_ref, gate_up_ref, first_ref, second_ref, part_ref, take_ref, sent_ref, land_ref, own_ref,
         own_take_ref, middle_ref, load_sems, keep_sems, hold_sems, send_sems, recv_sems) = refs
    shard, beside, across, _ = slice_peers()
    chip, core = shard // 2, shard % 2
    half = rows // 2
    parts, spans, _, piece, span_cols = part_ref.shape
    block = 2 * piece
    width = all_ref.shape[1]
    ff = first_ref.shape[0] if backward else second_ref.shape[0]
    first_steps = ff // CHUNK

    def load_first(at):
        if backward:
            place = (pl.ds(pl.multiple_of(at * CHUNK, CHUNK), CHUNK), slice(None))
            return [pltpu.make_async_copy(first_hbm.at[place], first_ref.at[place], load_sems.at[0, at])]
        places = [
            (slice(None), pl.ds(pl.multiple_of(side * ff + at * CHUNK, CHUNK), CHUNK)) for side in range(2)
        ]
        return [
            pltpu.make_async_copy(first_hbm.at[place], first_ref.at[place], load_sems.at[side, at])
            for side, place in enumerate(places)
        ]

    def load_second(at):
        span = pl.ds(pl.multiple_of(at * span_cols, span_cols), span_cols)
        place = (span, slice(None)) if backward else (slice(None), span)
        return pltpu.make_async_copy(second_hbm.at[place], second_ref.at[place], load_sems.at[2, at])

    load_extra = []
    if backward:
        for at in range(2 * lax.axis_size("shard")):
            group, part, owner = at // 4, at // 2 % 2, at % 2
            source = pl.ds(at * half, half)
            place = pl.ds(group * 2 * rows + owner * rows + part * half, half)
            load_extra.append(pltpu.make_async_copy(gate_up_hbm.at[source], gate_up_ref.at[place], hold_sems.at[at]))
    else:
        load_extra.append(pltpu.make_async_copy(middle_hbm, middle_ref, hold_sems.at[0]))
    if backward:
        for copy in load_extra:
            copy.start()
    for at in range(first_steps):
        for copy in load_first(at):
            copy.start()
    for at in range(spans):
        load_second(at).start()
    if not backward:
        load_extra[0].start()

    def remote(source, target, at, device):
        return pltpu.make_async_remote_copy(
            source, target, send_sems.at[at], recv_sems.at[at], device_id={"shard": device}, device_id_type=MESH
        )

    def place_of(owner, part):
        start = part * block + (owner % 2) * piece if parts == 2 else (owner % 2) * piece + part * half
        return pl.ds(pl.multiple_of((owner // 2) * 2 * rows + start, half), half)

    def owned(owner, part):
        return all_ref.at[place_of(owner, part)]

    turns = spread_turns(wide)
    base = 6 + (2 * parts + 1) * spans
    slice_barrier((beside, across), turns, 0 if target is None else 1)

    def hand_on(part, at):
        place = (pl.ds(part * piece, piece), pl.ds(at * span_cols, span_cols))
        return section_copy(
            result_ref.at[place], next_hbm.at[place], part * spans + at + base + lax.axis_size("replica"),
            send_sems, recv_sems, target,
        )

    def across_copy(part):
        return remote(owned(shard, part), owned(shard, part), part, across)

    def relay(part):
        return remote(owned(across, part), owned(across, part), 4 + part, beside)

    beside_copies = [remote(owned(shard, part), owned(shard, part), 2 + part, beside) for part in range(2)]
    for part in range(2):
        all_ref[place_of(shard, part), :] = mine_ref[part * half : (part + 1) * half, :]
        across_copy(part).start()
    for copy in beside_copies:
        copy.start()
    spread_copies = [
        replica_copy(mine_ref, others_hbm.at[lax.axis_index("replica")], turn, send_sems, recv_sems, base)
        for turn in turns
    ]
    for copy in spread_copies:
        copy.start()

    def first_product(start, count, waits):
        span = pl.ds(pl.multiple_of(start, count), count)

        def step(at, carry):
            cols = pl.ds(pl.multiple_of(at * CHUNK, CHUNK), CHUNK)
            high = pl.ds(pl.multiple_of(ff + at * CHUNK, CHUNK), CHUNK)
            if waits:
                for copy in load_first(at):
                    copy.wait()
            if backward:
                grad_hidden = dot_rows(all_ref[span, :], first_ref[cols, :])
                gate = gate_up_ref[span, cols].astype(F32)
                up = gate_up_ref[span, high].astype(F32)
                sigmoid = jax.nn.sigmoid(gate)
                mid_ref[span, cols] = (grad_hidden * up * sigmoid * (1.0 + gate * (1.0 - sigmoid))).astype(BF)
                mid_ref[span, high] = (grad_hidden * gate * sigmoid).astype(BF)
            else:
                gate = dot(all_ref[span, :], first_ref[:, cols])
                up = dot(all_ref[span, :], first_ref[:, high])
                gate_up_ref[span, cols] = gate.astype(BF)
                gate_up_ref[span, high] = up.astype(BF)
                mid_ref[span, cols] = (gate * jax.nn.sigmoid(gate) * up).astype(BF)
            return carry

        lax.fori_loop(0, first_steps, step, 0)

    def second_product(start, count, at, store):
        span = pl.ds(pl.multiple_of(start, count), count)

        def step(inner, carry):
            cols = pl.ds(pl.multiple_of(at * span_cols + inner * CHUNK, CHUNK), CHUNK)
            if backward:
                partial = dot_rows(mid_ref[span, :], second_ref[cols, :])
            else:
                partial = dot(mid_ref[span, :], second_ref[:, cols])
            store(pl.ds(pl.multiple_of(inner * CHUNK, CHUNK), CHUNK), partial.astype(BF))
            return carry

        lax.fori_loop(0, span_cols // CHUNK, step, 0)

    def give(part, at):
        return remote(part_ref.at[part, at, 1 - core], take_ref.at[part, at], 6 + part * spans + at, beside)

    def cross(part, at):
        return remote(sent_ref.at[part, at], land_ref.at[part, at], 6 + (parts + part) * spans + at, across)

    def give_own(at):
        return remote(own_ref.at[at, 1 - core], own_take_ref.at[at], 6 + 2 * parts * spans + at, beside)

    def pass_on(part, at):
        give(part, at).wait_recv()
        sent_ref[part, at] = (part_ref[part, at, core].astype(F32) + take_ref[part, at].astype(F32)).astype(BF)
        cross(part, at).start()

    own_start = chip * 2 * rows
    other_start = (1 - chip) * 2 * rows
    stores = []
    for copy in beside_copies:
        copy.wait_recv()
    if backward:
        for copy in load_extra:
            copy.wait()
    first_product(own_start, 2 * rows, True)
    if not backward:
        own_place = pl.ds(pl.multiple_of(own_start, 2 * rows), 2 * rows)
        stores.append(pltpu.make_async_copy(gate_up_ref.at[own_place], gate_up_hbm.at[own_place], keep_sems.at[1]))
        stores[-1].start()

    def store_part(part):
        place = pl.ds(pl.multiple_of(other_start + part * block, block), block)
        return pltpu.make_async_copy(gate_up_ref.at[place], gate_up_hbm.at[place], keep_sems.at[2 + part])

    def arrive(part):
        across_copy(part).wait_recv()
        relay(part).start()

    if parts == 1:
        for part in range(2):
            arrive(part)

    def other_part(part, carry):
        if parts == 1:
            for late in range(2):
                relay(late).wait_recv()
        else:
            arrive(part)
            relay(part).wait_recv()
        start = other_start + part * block
        first_product(start, block, False)
        if not backward:
            store_part(part).start()

        def span_step(at, inner):
            @pl.when(part == 0)
            def _():
                load_second(at).wait()

            def store(cols, partial):
                part_ref[part, at, 0, :, cols] = partial[:piece]
                part_ref[part, at, 1, :, cols] = partial[piece:]

            second_product(start, block, at, store)
            give(part, at).start()

            @pl.when(at > 0)
            def _():
                pass_on(part, at - 1)

            return inner

        lax.fori_loop(0, spans, span_step, 0)
        pass_on(part, spans - 1)
        return carry

    lax.fori_loop(0, parts, other_part, 0)
    if not backward:
        stores += [store_part(part) for part in range(parts)]
    for owner in range(lax.axis_size("shard")):
        for part in range(2):
            at = owner * 2 + part
            copy = pltpu.make_async_copy(
                all_ref.at[place_of(owner, part)], all_hbm.at[pl.ds(owner * rows + part * half, half)],
                keep_sems.at[4 + at],
            )
            copy.start()
            stores.append(copy)

    def own_step(at, carry):
        def store(cols, partial):
            for part in range(parts):
                for owner in range(2):
                    first_row = part * block + owner * piece
                    own_ref[at, owner, part * piece : (part + 1) * piece, cols] = partial[first_row : first_row + piece]

        second_product(own_start, 2 * rows, at, store)
        give_own(at).start()
        return carry

    lax.fori_loop(0, spans, own_step, 0)
    if not backward:
        load_extra[0].wait()
    for at in range(spans):
        give_own(at).wait_recv()
    for part in range(parts):
        place = slice(part * piece, (part + 1) * piece)
        for at in range(spans):
            cross(part, at).wait_recv()
            cols = slice(at * span_cols, (at + 1) * span_cols)
            total = (
                own_ref[at, core, place].astype(F32)
                + own_take_ref[at, place].astype(F32)
                + land_ref[part, at].astype(F32)
            )
            if backward:
                result_ref[place, cols] = total
            else:
                result_ref[place, cols] = (middle_ref[place, cols] + total).astype(BF)
                if target is not None:
                    hand_on(part, at).start()
    for part in range(2):
        beside_copies[part].wait_send()
        across_copy(part).wait_send()
        relay(part).wait_send()
    for copy in spread_copies + stores:
        copy.wait()
    if target is not None:
        for part in range(parts):
            for at in range(spans):
                hand_on(part, at).wait_send()
    for at in range(spans):
        give_own(at).wait_send()
        for part in range(parts):
            give(part, at).wait_send()
            cross(part, at).wait_send()


def section_copy(source, target, at, send_sems, recv_sems, section):
    return pltpu.make_async_remote_copy(
        source, target, send_sems.at[at], recv_sems.at[at], device_id={"section": section}, device_id_type=MESH
    )


def spread_turns(wide):
    return range(2, lax.axis_size("replica")) if wide else range(1, lax.axis_size("replica"), 2)


def gather_turns(mine_hbm, gathered_hbm, send_sems, recv_sems):
    shard, beside, across, _ = slice_peers()
    replicas = lax.axis_size("replica")
    rows = mine_hbm.shape[0]

    def remote(owner, turn, at, device):
        place = gathered_hbm.at[turn, pl.ds(pl.multiple_of(owner * rows, rows), rows)]
        return pltpu.make_async_remote_copy(
            place, place, send_sems.at[at], recv_sems.at[at], device_id={"shard": device}, device_id_type=MESH
        )

    own_rows = pl.ds(pl.multiple_of(shard * rows, rows), rows)
    order = [1]
    spread_copies = [
        replica_copy(mine_hbm, gathered_hbm.at[turn, own_rows], turn, send_sems, recv_sems, 3 * replicas)
        for turn in order
    ]
    over = [remote(shard, turn, 3 * turn, across) for turn in order]
    direct = [remote(shard, turn, 3 * turn + 1, beside) for turn in order]
    relays = [remote(across, turn, 3 * turn + 2, beside) for turn in order]
    spread_copies[0].start()
    for at in range(len(order)):
        spread_copies[at].wait_recv()
        over[at].start()
        direct[at].start()
        spread_copies[at].wait_send()
        if at + 1 < len(order):
            spread_copies[at + 1].start()
        if at:
            over[at - 1].wait_recv()
            relays[at - 1].start()
    over[-1].wait_recv()
    relays[-1].start()
    for copy in direct + relays:
        copy.wait_recv()
    for copy in over + direct + relays:
        copy.wait_send()


def feed_forward_kernel(section, last, gathers, parts, spans, rows, *refs):
    if gathers:
        cotangent_hbm, early_hbm, gather_send_sems, gather_recv_sems = refs[4], refs[10], refs[-4], refs[-3]
        refs = refs[:4] + refs[5:10] + refs[11:-4] + refs[-2:]

    @pl.when(lax.axis_index("section") == section)
    def _():
        feed_kernel(False, rows, None if last else section + 1, False, *refs)

    if not last:

        @pl.when(lax.axis_index("section") == section + 1)
        def _():
            barrier = pltpu.get_barrier_semaphore()
            pl.semaphore_signal(barrier, inc=1, device_id={"section": section}, device_id_type=MESH)
            if gathers:
                _, beside, across, _ = slice_peers()
                slice_barrier((beside, across), (1,))
                gather_turns(cotangent_hbm, early_hbm, gather_send_sems, gather_recv_sems)
            next_hbm, send_sems, recv_sems = refs[8], refs[-2], refs[-1]
            base = 6 + (2 * parts + 1) * spans + lax.axis_size("replica")
            high, wide = rows // parts, next_hbm.shape[1] // spans
            for part in range(parts):
                for at in range(spans):
                    place = next_hbm.at[pl.ds(part * high, high), pl.ds(at * wide, wide)]
                    section_copy(place, place, base + part * spans + at, send_sems, recv_sems, section).wait_recv()


def call_feed(section, backward, operands, collective, cotangent=None):
    first, second = operands[-2], operands[-1]
    rows, width = operands[0].shape
    shards, replicas = lax.axis_size("shard"), lax.axis_size("replica")
    ff = first.shape[0] if backward else second.shape[0]
    every = shards * rows
    parts, span_cols = (1, CHUNK) if backward else (2, 2 * CHUNK)
    spans, piece_rows = width // span_cols, rows // parts
    vmem, anywhere = pl.BlockSpec(memory_space=pltpu.VMEM), pl.BlockSpec(memory_space=pl.ANY)
    out_shape = [
        jax.ShapeDtypeStruct((rows, width), F32 if backward else BF),
        jax.ShapeDtypeStruct((every, width), BF),
        jax.ShapeDtypeStruct((replicas, rows, width), BF),
    ]
    if not backward:
        out_shape.insert(2, jax.ShapeDtypeStruct((every, 2 * ff), BF))
        out_shape.append(jax.ShapeDtypeStruct((rows, width), BF))
    copies = 6 + (3 * parts + 1) * spans + replicas
    piece = pltpu.VMEM((parts, spans, piece_rows, span_cols), BF)
    scratch = [
        pltpu.VMEM((every, 2 * ff if backward else ff), BF),
        pltpu.VMEM((every, width), BF),
        pltpu.VMEM((every, 2 * ff), BF),
        pltpu.VMEM(first.shape, BF),
        pltpu.VMEM(second.shape, BF),
        pltpu.VMEM((parts, spans, 2, piece_rows, span_cols), BF),
        piece,
        piece,
        piece,
        pltpu.VMEM((spans, 2, rows, span_cols), BF),
        pltpu.VMEM((spans, rows, span_cols), BF),
    ]
    if not backward:
        scratch.append(pltpu.VMEM((rows, width), F32))
    scratch += [
        pltpu.SemaphoreType.DMA((3, max(ff // CHUNK, spans))),
        pltpu.SemaphoreType.DMA((4 + 2 * shards,)),
        pltpu.SemaphoreType.DMA((2 * shards,)),
        *([pltpu.SemaphoreType.DMA((4 * replicas,))] * (0 if cotangent is None else 2)),
        pltpu.SemaphoreType.DMA((copies,)),
        pltpu.SemaphoreType.DMA((copies,)),
    ]
    if cotangent is not None:
        operands += (cotangent,)
        out_shape.append(jax.ShapeDtypeStruct((replicas, every, width), BF))
    return pl.pallas_call(
        gated(section, functools.partial(feed_kernel, True, rows, None, section == lax.axis_size("section") - 1))
        if backward
        else functools.partial(feed_forward_kernel, section, section == lax.axis_size("section") - 1,
            cotangent is not None, parts, spans, rows),
        out_shape=out_shape,
        in_specs=[vmem] + [anywhere] * (len(operands) - 1),
        out_specs=[vmem] + [anywhere] * (len(out_shape) - 1),
        scratch_shapes=scratch,
        compiler_params=pltpu.CompilerParams(
            collective_id=collective, has_side_effects=True, vmem_limit_bytes=VMEM_LIMIT
        ),
        name="feed_backward" if backward else "feed_forward",
    )(*operands)


def weights_kernel(
    qkv_ref, out_ref, gate_up_ref, state_ref, gain_one_ref, gain_two_ref, cos_ref, sin_ref, allowed_ref,
    qkv_full, out_full, gate_up_part, middle_ref, normed_two_ref, rotated_ref, lefts_ref,
    qkv_hold, out_hold, gate_up_hold, qkv_work, out_work, normed_ref, attended_ref, work_sems,
    local_sems, send_sems, recv_sems,
):
    shard, replica = lax.axis_index("shard"), lax.axis_index("replica")
    chip, core = shard // 2, shard % 2
    beside = {"shard": chip * 2 + (1 - core)}
    across = {"shard": (1 - chip) * 2 + core}
    diagonal = {"shard": (1 - chip) * 2 + (1 - core)}
    mine = replica % 2
    partner = {"replica": replica + 1 - 2 * mine}
    rows = qkv_ref.shape[0]
    half = rows // 2
    ff = gate_up_ref.shape[1] // 2
    part = gate_up_part.shape[1] // 2

    def remote(source, target, at, device):
        return pltpu.make_async_remote_copy(
            source, target, send_sems.at[at], recv_sems.at[at], device_id=device, device_id_type=MESH
        )

    def span(start, count):
        return pl.ds(pl.multiple_of(start, count), count)

    sides = [pl.ds(side * part, part) for side in range(2)]
    loads = [
        pltpu.make_async_copy(qkv_ref, qkv_hold, local_sems.at[0]),
        pltpu.make_async_copy(out_ref, out_hold, local_sems.at[1]),
    ] + [
        pltpu.make_async_copy(
            gate_up_ref.at[:, span(side * ff + shard * part, part)], gate_up_hold.at[side], local_sems.at[2 + side]
        )
        for side in range(2)
    ]
    own_rows = span(shard * rows, rows)
    stores = [
        pltpu.make_async_copy(qkv_hold, qkv_full.at[own_rows], local_sems.at[4]),
        pltpu.make_async_copy(out_hold, out_full.at[own_rows], local_sems.at[5]),
    ] + [
        pltpu.make_async_copy(gate_up_hold.at[side], gate_up_part.at[own_rows, sides[side]], local_sems.at[6 + side])
        for side in range(2)
    ]
    for copy in loads:
        copy.start()

    pieces = []
    for source, whole, count in ((qkv_ref, qkv_full, 64), (out_ref, out_full, 64)):
        for offset in range(0, half, count):

            def place(owner, part_of, whole=whole, offset=offset, count=count):
                return whole.at[span(owner["shard"] * rows + part_of * half + offset, count)]

            own = source.at[span(mine * half + offset, count)]
            pieces.append((own, place, across, True))
    for offset in range(0, half, 64):
        for side in range(2):
            for device in (across, diagonal):

                def place(owner, part_of, offset=offset, side=side):
                    return gate_up_part.at[
                        span(owner["shard"] * rows + part_of * half + offset, 64), pl.ds(side * part, part)
                    ]

                own = gate_up_ref.at[
                    span(mine * half + offset, 64), span(side * ff + device["shard"] * part, part)
                ]
                pieces.append((own, place, device, False))
    count = len(pieces)
    me = {"shard": shard}
    over = [remote(own, place(me, mine), at, device) for at, (own, place, device, _) in enumerate(pieces)]
    passed = [
        remote(place(device, mine), place(device, mine), count + at, partner)
        for at, (_, place, device, _) in enumerate(pieces)
    ]
    relays = [
        [
            remote(place(across, which), place(across, which), (2 + turn) * count + at, beside)
            if relayed
            else None
            for at, (_, place, _, relayed) in enumerate(pieces)
        ]
        for turn, which in enumerate((mine, 1 - mine))
    ]
    direct = [
        remote(qkv_ref, qkv_full.at[span(shard * rows, rows)], 4 * count, beside),
        remote(out_ref, out_full.at[span(shard * rows, rows)], 4 * count + 1, beside),
    ]
    for side in range(2):
        direct.append(
            remote(
                gate_up_ref.at[:, span(side * ff + beside["shard"] * part, part)],
                gate_up_part.at[span(shard * rows, rows), pl.ds(side * part, part)],
                4 * count + 2 + side,
                beside,
            )
        )

    barrier = pltpu.get_barrier_semaphore()
    for device in (beside, across, diagonal, partner):
        pl.semaphore_signal(barrier, inc=1, device_id=device, device_id_type=MESH)
    pl.semaphore_wait(barrier, 4)

    started = []

    def start(copy):
        copy.start()
        started.append(copy)

    ahead = 4
    for copy in over[:ahead]:
        start(copy)
    for copy in direct:
        start(copy)
    for load, store in zip(loads, stores):
        load.wait()
        store.start()
    first, load_out, second = attend_parts(
        state_ref, gain_one_ref, gain_two_ref, cos_ref, sin_ref, allowed_ref, qkv_full, out_full,
        middle_ref, normed_two_ref, rotated_ref, lefts_ref,
        qkv_work, out_work, normed_ref, attended_ref, work_sems,
    )
    qkv_last = half // 64 - 1
    out_last = qkv_last + half // 64
    arrived = [0]

    def wait_relays(last):
        for at in range(arrived[0], last + 1):
            for copies in relays:
                copies[at].wait_recv()
        arrived[0] = last + 1

    def work(parts):
        @pl.when(lax.axis_index("section") == 0)
        def _():
            for part in parts:
                part()

    ready = list(first)
    for at in range(count + 1):
        if at < count:
            over[at].wait_recv()
            start(passed[at])
            if relays[0][at] is not None:
                start(relays[0][at])
            if at + ahead < count:
                over[at].wait_send()
                started[:] = [copy for copy in started if copy is not over[at]]
                start(over[at + ahead])
        if at > 0:
            passed[at - 1].wait_recv()
            if relays[1][at - 1] is not None:
                start(relays[1][at - 1])
        if at == qkv_last + 2:
            wait_relays(qkv_last)
            direct[0].wait_recv()
            stores[0].wait()
        if at == out_last + 2:
            wait_relays(out_last)
            direct[1].wait_recv()
            stores[1].wait()
            work([load_out])
            ready += second
        if at >= qkv_last + 2:
            work(ready[:2])
            ready = ready[2:]
    work(ready)
    for copy in direct[2:]:
        copy.wait_recv()
    for copy in stores[2:]:
        copy.wait()
    for copy in started:
        copy.wait_send()


def call_weights(qkv_weight, out_weight, gate_up_weight, operands, collective):
    shards = lax.axis_size("shard")
    rows = qkv_weight.shape[0]
    count = 2 * (rows // 128) + 4 * (rows // 128)
    out_shape, scratch = attend_shapes(*operands[0].shape, qkv_weight.shape[1])
    vmem = pl.BlockSpec(memory_space=pltpu.VMEM)
    anywhere = pl.BlockSpec(memory_space=pl.ANY)
    return pl.pallas_call(
        weights_kernel,
        out_shape=[
            jax.ShapeDtypeStruct((shards * rows, qkv_weight.shape[1]), BF),
            jax.ShapeDtypeStruct((shards * rows, out_weight.shape[1]), BF),
            jax.ShapeDtypeStruct((shards * rows, gate_up_weight.shape[1] // shards), BF),
        ] + out_shape,
        in_specs=[anywhere] * 3 + [vmem] * len(operands),
        out_specs=[anywhere] * 3 + [vmem] * len(out_shape),
        scratch_shapes=[
            pltpu.VMEM(qkv_weight.shape, BF),
            pltpu.VMEM(out_weight.shape, BF),
            pltpu.VMEM((2, rows, gate_up_weight.shape[1] // (2 * shards)), BF),
            *scratch,
            pltpu.SemaphoreType.DMA((8,)),
            pltpu.SemaphoreType.DMA((4 * count + 4,)),
            pltpu.SemaphoreType.DMA((4 * count + 4,)),
        ],
        compiler_params=pltpu.CompilerParams(
            collective_id=collective, has_side_effects=True, vmem_limit_bytes=VMEM_LIMIT
        ),
        name="weights",
    )(qkv_weight, out_weight, gate_up_weight, *operands)


def repeat(first, last, body):
    def step(at, carry):
        body(at)
        return carry

    if first < last:
        lax.fori_loop(first, last, step, 0)


def by_chunk(count, body):
    repeat(0, count, lambda at: body(pl.ds(pl.multiple_of(at * CHUNK, CHUNK), CHUNK)))


def weight_grads_kernel(sections, left_rows_ref, hidden_ref, *refs):
    sources = [refs[at * sections : (at + 1) * sections] for at in range(7)]
    (early_hbm, gate_up_hbm, down_hbm,
     gate_up_grad_ref, down_grad_ref, qkv_grad_ref, out_grad_ref, gain_sum_ref, gathered_hbm, even_hbm,
     projected_ref, upstream_ref, gains_ref, gains_land_ref, gain_part_ref, gains_last_ref, lefts_ref, left_ref,
     extra_ref, terms_ref, chain_ref, down_ref, block_ref, gate_up_ref, mid_ref, sum_ref, stage_ref,
     start_sems, load_sems, block_sems, keep_sem, send_sems, recv_sems) = refs[7 * sections :]
    shard, beside, across, diagonal = slice_peers()
    peers = (across, diagonal, beside)
    replica, replicas = lax.axis_index("replica"), lax.axis_size("replica")
    early = lax.axis_index("section") == lax.axis_size("section") - 1
    late = lax.axis_index("section") < lax.axis_size("section") - 1
    here = [lax.axis_index("section") == section for section in range(sections)]
    rows, cols = projected_ref.shape
    every, width = sources[5][0].shape
    pieces, all_pieces = cols // CHUNK, (cols + width) // CHUNK
    staged = stage_ref.shape[2] // CHUNK
    kinds, groups, _, sub_rows, _ = lefts_ref.shape
    part = down_ref.shape[0]
    half_part = part // 2
    ff = gate_up_grad_ref.shape[1] // 2
    steps = half_part // CHUNK
    wide = width // CHUNK
    out_rows = gate_up_grad_ref.shape[0]
    piece_base = 3 * replicas
    spread_base = piece_base + 3 * pieces
    gain_base = spread_base + replicas
    left_base = gain_base + replicas
    chain_base = left_base + kinds * groups * 3
    last_base = chain_base + 4 * replicas
    grad_base = last_base + 3

    def remote(source, target, at, device):
        return pltpu.make_async_remote_copy(
            source, target, send_sems.at[at], recv_sems.at[at], device_id={"shard": device}, device_id_type=MESH
        )

    def owned(owner):
        return pl.ds(pl.multiple_of(owner * rows, rows), rows)

    def piece_place(piece, place=None):
        if piece < 2 * staged:
            place = pl.ds(0, every) if place is None else place
            return stage_ref.at[piece // staged, place, pl.ds(piece % staged * CHUNK, CHUNK)]
        return extra_ref.at[piece - 2 * staged] if place is None else extra_ref.at[piece - 2 * staged, place]

    def piece_copy(owner, piece, kind, device):
        place = piece_place(piece, owned(owner))
        return remote(place, place, piece_base + kind * pieces + piece, device)

    over = [piece_copy(shard, piece, 0, across) for piece in range(pieces)]
    direct = [piece_copy(shard, piece, 1, beside) for piece in range(pieces)]
    relays = [piece_copy(across, piece, 2, beside) for piece in range(pieces)]

    def hand_left(kind, group, peer):
        return remote(
            lefts_ref.at[kind, group, peers[peer]], left_ref.at[kind, group, :, owned(shard)],
            left_base + (kind * groups + group) * 3 + peer, peers[peer],
        )

    lefts = [(kind, group, peer) for kind in reversed(range(kinds)) for group in range(groups) for peer in range(3)]
    loads = []
    for at, target in enumerate((lefts_ref, projected_ref, gains_ref, upstream_ref)):
        loads.append([pltpu.make_async_copy(source, target, start_sems.at[at]) for source in sources[at]])
    load_branch = [
        [
            pltpu.make_async_copy(source.at[piece - pieces], piece_place(piece), start_sems.at[4 + piece - pieces])
            for source in sources[4]
        ]
        for piece in range(pieces, all_pieces)
    ]
    load_own = [pltpu.make_async_copy(source, block_ref.at[0], load_sems.at[2, 0]) for source in sources[5]]
    load_down = pltpu.make_async_copy(down_hbm, down_ref, load_sems.at[3, 0])

    def block_at(turn):
        return lax.rem(replica + turn, replicas)

    def tokens(turn):
        return pl.ds(pl.multiple_of(block_at(turn) * every, every), every)

    def load_gate_up(half, turn, side):
        place = pl.ds(side * part + half * half_part, half_part)
        slot = lax.rem(turn, 2)
        return pltpu.make_async_copy(
            gate_up_hbm.at[tokens(turn), place], gate_up_ref.at[slot, side], load_sems.at[side, slot]
        )

    def block_copies(turn, source):
        slot = lax.rem(turn, 2)
        copies = []
        for at, owner in enumerate(peers + (shard,)):
            if source is early_hbm:
                own = early_hbm.at[turn, owned(owner)]
            else:
                own = gathered_hbm.at[turn, owned(owner)] if source is None or at < 3 else source.at[block_at(turn)]
            copies.append(pltpu.make_async_copy(own, block_ref.at[slot, owned(owner)], block_sems.at[slot, at]))
        return copies

    def own_cases(turn):
        cases = [(late & (turn > 0) & (turn % 2 == 0), even_hbm), (early & (turn > 1), sources[6][-1])]
        for section in range(sections - 1):
            cases.append((here[section] & (turn % 2 == 1), sources[6][section]))
        return cases

    def load_block(turn):
        @pl.when(early & (turn == 1))
        def _():
            for copy in block_copies(turn, early_hbm):
                copy.start()

        @pl.when(late | (turn != 1))
        def _():
            for copy in block_copies(turn, None)[:3]:
                copy.start()

        cases = [(turn == 0, None)] + own_cases(turn)
        for case, source in cases:

            @pl.when(case)
            def _(source=source):
                block_copies(turn, source)[3].start()

    def wait_block(turn):
        for copy in block_copies(turn, None):
            copy.wait()

    def landing(turn, owner):
        return gathered_hbm.at[turn, owned(owner)]

    def block_over(turn, source):
        return remote(source.at[block_at(turn)], landing(turn, shard), 3 * turn, across)

    def block_direct(turn, source):
        return remote(source.at[block_at(turn)], landing(turn, shard), 3 * turn + 1, beside)

    def block_relay(turn):
        return remote(landing(turn, across), landing(turn, across), 3 * turn + 2, beside)

    def send_block(turn):
        cases = own_cases(turn)
        for case, source in cases:

            @pl.when(case)
            def _(source=source):
                block_over(turn, source).start()
                block_direct(turn, source).start()

    def chain_slot(block, at):
        return replicas - (replicas - block) * ((at - block + replicas - 1) // replicas)

    spans = ((cols, width), (0, cols))

    def chain_at(phase, slot):
        return chain_ref.at[slot, :, pl.ds(*spans[phase])]

    def chain_up(phase, block):
        at = chain_base + phase * 2 * replicas + block
        return pltpu.make_async_remote_copy(
            chain_at(phase, block), chain_at(phase, block), send_sems.at[at], recv_sems.at[at],
            device_id={"replica": replica + 1}, device_id_type=MESH,
        )

    def chain_down(phase, block):
        at = chain_base + phase * 2 * replicas + replicas + block
        return pltpu.make_async_remote_copy(
            chain_at(phase, block), chain_at(phase, chain_slot(block, replica - 1)), send_sems.at[at], recv_sems.at[at],
            device_id={"replica": replica - 1}, device_id_type=MESH,
        )

    def chain_chunks(phase, body):
        first, count = spans[phase]
        repeat(first // CHUNK, (first + count) // CHUNK, lambda at: body(pl.ds(pl.multiple_of(at * CHUNK, CHUNK), CHUNK)))

    def add_terms(phase, block):
        def add(place):
            total = chain_ref[block, :, place].astype(F32) + terms_ref[block, :, place].astype(F32)
            chain_ref[block, :, place] = total.astype(BF)

        chain_chunks(phase, add)

    def chain_begin(phase):
        def take_terms(block):
            def take(place):
                chain_ref[block, :, place] = terms_ref[block, :, place]

            chain_chunks(phase, take)

        for block in reversed(range(1, replicas)):

            @pl.when(replica == 0)
            def _(block=block):
                take_terms(block)
                chain_up(phase, block).start()

        for block in range(replicas - 1):

            @pl.when(replica == replicas - 1)
            def _(block=block):
                take_terms(block)
                chain_down(phase, block).start()

    def chain_step(phase, step):
        high = replicas - 1 - step + replica

        @pl.when((replica > 0) & (step >= replica))
        def _():
            chain_up(phase, high).wait_recv()

            @pl.when(step < replicas - 1)
            def _():
                add_terms(phase, high)
                chain_up(phase, high).start()

        low = step - (replicas - 1 - replica)

        @pl.when((replica < replicas - 1) & (step >= replicas - 1 - replica))
        def _():
            chain_down(phase, low).wait_recv()

            @pl.when(step < replicas - 1)
            def _():
                add_terms(phase, low)
                chain_down(phase, low).start()

    def gain_copy(peer):
        return remote(gain_part_ref, gains_last_ref.at[shard], last_base + peer, peers[peer])

    def send_grad(half, at, peer):
        device = peers[peer]
        place = pl.ds(pl.multiple_of(at * CHUNK, CHUNK), CHUNK)
        target = pl.ds(
            pl.multiple_of(
                (at // steps) * ff + shard * part + half * half_part + (at % steps) * CHUNK, CHUNK
            ),
            CHUNK,
        )
        return remote(
            stage_ref.at[half, pl.ds(pl.multiple_of(device * out_rows, out_rows), out_rows), place],
            gate_up_grad_ref.at[:, target],
            grad_base + (half * 2 * steps + at) * 3 + peer,
            device,
        )

    def clear_sum():
        def clear(place):
            sum_ref[:, place] = jnp.zeros((sum_ref.shape[0], CHUNK), F32)

        by_chunk(2 * steps, clear)

    def compute(half, turn):
        slot = lax.rem(turn, 2)
        later = lax.rem(turn + 1, replicas)
        for side in range(2):
            load_gate_up(half, turn, side).wait()

        @pl.when(turn + 1 < replicas)
        def _():
            for side in range(2):
                load_gate_up(half, later, side).start()
            if half:
                load_block(later)

        def products(at, inner):
            place = pl.ds(pl.multiple_of(at * CHUNK, CHUNK), CHUNK)
            high = pl.ds(pl.multiple_of(half_part + at * CHUNK, CHUNK), CHUNK)
            down_rows = pl.ds(pl.multiple_of(half * half_part + at * CHUNK, CHUNK), CHUNK)
            grad_hidden = dot_rows(block_ref[slot], down_ref[down_rows, :])
            gate = gate_up_ref[slot, 0, :, place].astype(F32)
            up = gate_up_ref[slot, 1, :, place].astype(F32)
            sigmoid = jax.nn.sigmoid(gate)
            mid_ref[:, place] = (grad_hidden * up * sigmoid * (1.0 + gate * (1.0 - sigmoid))).astype(BF)
            mid_ref[:, high] = (grad_hidden * gate * sigmoid).astype(BF)
            return inner

        lax.fori_loop(0, steps, products, 0)

        def sums(at, inner):
            place = pl.ds(pl.multiple_of(at * CHUNK, CHUNK), CHUNK)
            total = sum_ref[:, place] + dot(left_rows_ref[:, tokens(turn)], mid_ref[:, place])

            @pl.when(turn < replicas - 1)
            def _():
                sum_ref[:, place] = total

            @pl.when(turn == replicas - 1)
            def _():
                stage_ref[half, pl.ds(0, total.shape[0]), place] = total.astype(BF)
                for peer in range(3):
                    send_grad(half, at, peer).start()

            return inner

        lax.fori_loop(0, 2 * steps, sums, 0)

    def first_pass(turn, carry):
        @pl.when(late | (turn != 1))
        def _():
            block_over(turn, even_hbm).wait_recv()
            block_relay(turn).start()
            block_direct(turn, even_hbm).wait_recv()
            block_relay(turn).wait_recv()

        load_block(turn)

        @pl.when(turn + 2 < replicas)
        def _():
            send_block(turn + 2)

        wait_block(turn)
        compute(0, turn)
        return carry

    def second_pass(turn, carry):
        compute(1, turn)

        @pl.when(turn + 1 < replicas)
        def _():
            wait_block(lax.rem(turn + 1, replicas))

        return carry

    for copies in loads + load_branch + [load_own]:
        start_own(copies)
    load_down.start()
    for side in range(2):
        load_gate_up(0, 0, side).start()

    barrier = pltpu.get_barrier_semaphore()
    for device in peers:
        pl.semaphore_signal(barrier, inc=1, device_id={"shard": device}, device_id_type=MESH)
    for turn in range(1, replicas):
        target = lax.rem(replica + turn, replicas)
        pl.semaphore_signal(barrier, inc=1, device_id={"replica": target}, device_id_type=MESH)
    pl.semaphore_wait(barrier, 2 + replicas)

    spread_copies = [
        replica_copy(upstream_ref, even_hbm.at[replica], turn, send_sems, recv_sems, spread_base)
        for turn in range(2, replicas, 2)
    ]
    gain_copies = [
        replica_copy(gains_ref, gains_land_ref.at[replica], turn, send_sems, recv_sems, gain_base)
        for turn in range(1, replicas)
    ]
    loads[0][0].wait()
    for place in lefts:
        hand_left(*place).start()
    loads[1][0].wait()
    for piece in range(pieces):
        piece_place(piece, owned(shard))[...] = projected_ref[:, piece * CHUNK : (piece + 1) * CHUNK]
        over[piece].start()
        direct[piece].start()
    loads[2][0].wait()
    gains_land_ref[replica] = gains_ref[...]
    loads[3][0].wait()
    for copy in gain_copies:
        copy.start()

    @pl.when(late)
    def _():
        for copy in spread_copies:
            copy.start()

    for kind in range(kinds):
        for group in range(groups):
            left_ref[kind, group, :, owned(shard)] = lefts_ref[kind, group, shard]
    load_own[0].wait()
    keep_own = pltpu.make_async_copy(block_ref.at[0], gathered_hbm.at[0], keep_sem)
    keep_own.start()
    clear_sum()

    def product(piece, kind, source):
        left = jnp.concatenate([left_ref[kind, group] for group in range(groups)], 0)
        total = dot(left, source).astype(BF)
        place = pl.ds(pl.multiple_of(piece * CHUNK, CHUNK), CHUNK)
        for group in range(groups):
            terms_ref[group, :, place] = total[group * sub_rows : (group + 1) * sub_rows]

    def staged_product(piece, kind):
        place = pl.ds(pl.multiple_of(piece % staged * CHUNK, CHUNK), CHUNK)
        product(piece, kind, stage_ref[piece // staged, pl.ds(0, every), place])

    for place in lefts[: len(lefts) // kinds]:
        hand_left(*place).wait_recv()
    for copies in load_branch:
        copies[0].wait()
    repeat(pieces, min(all_pieces, 2 * staged), lambda piece: staged_product(piece, 1))
    repeat(2 * staged, all_pieces, lambda piece: product(piece, 1, extra_ref[piece - 2 * staged]))
    chain_begin(0)
    load_down.wait()
    compute(0, 0)
    keep_own.wait()
    if replicas > 2:

        @pl.when(early)
        def _():
            load_block(1)
            wait_block(1)
            compute(0, 1)

    for place in lefts[len(lefts) // kinds :]:
        hand_left(*place).wait_recv()
    for piece in range(pieces):
        over[piece].wait_recv()
        relays[piece].start()
        if piece == pieces // 2:
            chain_step(0, 1)
    for copy in over:
        copy.wait_send()

    @pl.when(late)
    def _():
        for copy in spread_copies:
            copy.wait()

    for turn in range(1, min(3, replicas)):
        send_block(turn)
    for copy in direct + relays:
        copy.wait()
    repeat(0, pieces, lambda piece: staged_product(piece, 0))
    chain_begin(1)
    if replicas > 2:
        chain_step(0, 2)
    for copy in gain_copies:
        copy.wait()
    gain_part_ref[...] = jnp.sum(gains_land_ref[...], 0)
    gains_last_ref[shard] = gain_part_ref[...]
    for peer in range(3):
        gain_copy(peer).start()
    if replicas > 2:

        @pl.when(late)
        def _():
            first_pass(1, 0)

        if replicas > 3:

            @pl.when(early)
            def _():
                send_block(3)

    lax.fori_loop(2, replicas, first_pass, 0)
    for side in range(2):
        load_gate_up(1, 0, side).start()
    load_block(0)
    clear_sum()
    for step in range(3, replicas):
        chain_step(0, step)
    chain_step(1, 1)
    wait_block(0)
    lax.fori_loop(0, 2, second_pass, 0)
    if replicas > 2:
        chain_step(1, 2)
    lax.fori_loop(2, replicas, second_pass, 0)
    load_block(0)
    wait_block(0)

    def clear_down(place):
        down_grad_ref[:, place] = jnp.zeros((down_grad_ref.shape[0], CHUNK), F32)

    by_chunk(wide, clear_down)

    def down_pass(turn, carry):
        slot = lax.rem(turn, 2)
        later = lax.rem(turn + 1, replicas)

        @pl.when(turn + 1 < replicas)
        def _():
            load_block(later)

        def down_sums(at, inner):
            place = pl.ds(pl.multiple_of(at * CHUNK, CHUNK), CHUNK)
            down_grad_ref[:, place] += dot(hidden_ref[:, tokens(turn)], block_ref[slot, :, place])
            return inner

        lax.fori_loop(0, wide, down_sums, 0)

        @pl.when(turn + 1 < replicas)
        def _():
            wait_block(later)

        return carry

    lax.fori_loop(0, replicas, down_pass, 0)
    for peer in range(3):
        gain_copy(peer).wait()
    gain_sum_ref[...] = jnp.sum(gains_last_ref[...], 0)
    own = pl.ds(pl.multiple_of(shard * out_rows, out_rows), out_rows)
    for half in range(2):

        def store_own(at, carry, half=half):
            place = pl.ds(pl.multiple_of(at * CHUNK, CHUNK), CHUNK)
            target = pl.ds(
                pl.multiple_of(
                    (at // steps) * ff + shard * part + half * half_part + (at % steps) * CHUNK, CHUNK
                ),
                CHUNK,
            )
            gate_up_grad_ref[:, target] = stage_ref[half, own, place]
            return carry

        lax.fori_loop(0, 2 * steps, store_own, 0)
    for step in range(3, replicas):
        chain_step(1, step)

    def sum_up(grad_ref, first):
        def add(place):
            source = pl.ds(pl.multiple_of(first + place.start, CHUNK), CHUNK)
            grad_ref[:, place] = terms_ref[replica, :, source].astype(F32)

            @pl.when(replica > 0)
            def _():
                grad_ref[:, place] += chain_ref[replica, :, source].astype(F32)

            @pl.when(replica < replicas - 1)
            def _():
                grad_ref[:, place] += chain_ref[replicas, :, source].astype(F32)

        by_chunk(grad_ref.shape[1] // CHUNK, add)

    sum_up(qkv_grad_ref, 0)
    sum_up(out_grad_ref, cols)
    for half in range(2):

        def finish(at, carry, half=half):
            for peer in range(3):
                send_grad(half, at, peer).wait()
            return carry

        lax.fori_loop(0, 2 * steps, finish, 0)
    for place in lefts:
        hand_left(*place).wait_send()
    for turn in range(1, replicas):

        @pl.when(late | (turn != 1))
        def _(turn=turn):
            block_over(turn, even_hbm).wait_send()
            block_direct(turn, even_hbm).wait_send()
            block_relay(turn).wait_send()


    for phase in range(2):
        for block in range(1, replicas):

            @pl.when(replica < block)
            def _(phase=phase, block=block):
                chain_up(phase, block).wait_send()

        for block in range(replicas - 1):

            @pl.when(replica > block)
            def _(phase=phase, block=block):
                chain_down(phase, block).wait_send()


def call_weight_grads(left_rows, hidden, lefts, projected, gains, upstream, branch, slices, odd, early, gate_up, down,
                      collective):
    replicas, shards, sections = lax.axis_size("replica"), lax.axis_size("shard"), len(projected)
    rows, cols = projected[0].shape
    every, width = slices[0].shape
    part = down.shape[0]
    slice_rows = left_rows.shape[0]
    sub_rows = slice_rows // shards
    lefts = [values.reshape(2, replicas, shards, sub_rows, rows) for values in lefts]
    pieces, all_pieces = cols // CHUNK, (cols + width) // CHUNK
    copies = 3 * replicas + 3 * pieces + 2 * replicas + 6 * replicas + 4 * replicas + 3 + 3 * 2 * (part // CHUNK)
    vmem, anywhere = pl.BlockSpec(memory_space=pltpu.VMEM), pl.BlockSpec(memory_space=pl.ANY)
    gain_shape = gains[0].shape
    return pl.pallas_call(
        functools.partial(weight_grads_kernel, sections),
        out_shape=[
            jax.ShapeDtypeStruct((sub_rows, 2 * part * shards), BF),
            jax.ShapeDtypeStruct((hidden.shape[0], width), F32),
            jax.ShapeDtypeStruct((sub_rows, cols), F32),
            jax.ShapeDtypeStruct((sub_rows, width), F32),
            jax.ShapeDtypeStruct(gain_shape, F32),
            jax.ShapeDtypeStruct((replicas, every, width), BF),
            jax.ShapeDtypeStruct((replicas, rows, width), BF),
        ],
        in_specs=[vmem] * 2 + [anywhere] * (7 * sections + 3),
        out_specs=[vmem] * 5 + [anywhere] * 2,
        scratch_shapes=[
            pltpu.VMEM((rows, cols), BF),
            pltpu.VMEM((rows, width), BF),
            pltpu.VMEM(gain_shape, F32),
            pltpu.VMEM((replicas,) + gain_shape, F32),
            pltpu.VMEM(gain_shape, F32),
            pltpu.VMEM((shards,) + gain_shape, F32),
            pltpu.VMEM(lefts[0].shape, BF),
            pltpu.VMEM((2, replicas, sub_rows, every), BF),
            pltpu.VMEM((max(1, all_pieces - 2 * (part // CHUNK)), every, CHUNK), BF),
            pltpu.VMEM((replicas, sub_rows, cols + width), BF),
            pltpu.VMEM((replicas + 1, sub_rows, cols + width), BF),
            pltpu.VMEM(down.shape, BF),
            pltpu.VMEM((2, every, width), BF),
            pltpu.VMEM((2, 2, every, part // 2), BF),
            pltpu.VMEM((every, part), BF),
            pltpu.VMEM((slice_rows, part), F32),
            pltpu.VMEM((2, max(slice_rows, every), part), BF),
            pltpu.SemaphoreType.DMA((4 + all_pieces - pieces,)),
            pltpu.SemaphoreType.DMA((4, 2)),
            pltpu.SemaphoreType.DMA((2, 4)),
            pltpu.SemaphoreType.DMA,
            pltpu.SemaphoreType.DMA((copies,)),
            pltpu.SemaphoreType.DMA((copies,)),
        ],
        compiler_params=pltpu.CompilerParams(
            collective_id=collective, has_side_effects=True, vmem_limit_bytes=VMEM_LIMIT
        ),
        name="weight_grads",
    )(left_rows, hidden, *lefts, *projected, *gains, *upstream, *branch, *slices, *odd, early, gate_up, down)


def turn_order(replicas):
    return [0] + list(range(1, replicas, 2)) + list(range(2, replicas, 2))


def prepare_kernel(sections, gate_up_hbm, *refs):
    slices, normed_two, odd = [refs[at * sections : (at + 1) * sections] for at in range(3)]
    (gathered_hbm, gate_up_all_hbm, hidden_hbm, left_rows_ref,
     normed_two_ref, weight_ref, block_ref, gate_up_ref, hidden_ref, turned_ref,
     load_sems, store_sems, block_sems, start_sems, send_sems, recv_sems) = refs[3 * sections :]
    shard, beside, across, diagonal = slice_peers()
    peers = (across, diagonal, beside)
    replica, replicas = lax.axis_index("replica"), lax.axis_size("replica")
    shards = lax.axis_size("shard")
    rows, width = normed_two_ref.shape
    every = rows * shards
    part = hidden_ref.shape[1]
    ff_rows = hidden_hbm.shape[0]
    steps = part // CHUNK
    slice_rows = left_rows_ref.shape[0]
    owner = (replica * shards) // replicas
    first_col = lax.rem(replica * shards, replicas) * ff_rows

    def load_weight(side, at):
        place = (slice(None), pl.ds(pl.multiple_of(side * part + at * CHUNK, CHUNK), CHUNK))
        return pltpu.make_async_copy(gate_up_hbm.at[place], weight_ref.at[place], load_sems.at[side, at])

    for at in range(steps):
        for side in range(2):
            load_weight(side, at).start()

    def remote(source, target, at, device):
        return pltpu.make_async_remote_copy(
            source, target, send_sems.at[at], recv_sems.at[at], device_id={"shard": device}, device_id_type=MESH
        )

    def landing(turn, who):
        return gathered_hbm.at[turn, pl.ds(pl.multiple_of(who * rows, rows), rows)]

    def own_sources(turn):
        if turn % 2:
            return [source.at[lax.rem(replica + turn, replicas)] for source in odd]
        return [landing(turn, shard)]

    def over(turn, source=None):
        return remote(landing(turn, shard) if source is None else source, landing(turn, shard), 3 * turn, across)

    def direct(turn, source=None):
        return remote(landing(turn, shard) if source is None else source, landing(turn, shard), 3 * turn + 1, beside)

    def send_block(turn):
        if turn % 2 == 0:
            from_replica(turn).wait_recv()
        copies = [(over(turn, source), direct(turn, source)) for source in own_sources(turn)]
        for section, pair in enumerate(copies):
            if len(copies) == 1:
                for copy in pair:
                    copy.start()
            else:

                @pl.when(lax.axis_index("section") == section)
                def _(pair=pair):
                    for copy in pair:
                        copy.start()

    def relay(turn):
        return remote(landing(turn, across), landing(turn, across), 3 * turn + 2, beside)

    def from_replica(turn):
        return replica_copy(normed_two_ref, landing(turn, shard), turn, send_sems, recv_sems, 3 * replicas)

    def tokens(turn):
        return pl.ds(pl.multiple_of(lax.rem(replica + turn, replicas) * every, every), every)

    def load_block(turn, slot):
        copies = []
        for at, owner in enumerate(peers + (shard,)):
            sources = own_sources(turn) if at == 3 else [landing(turn, owner)]
            place = block_ref.at[slot, pl.ds(pl.multiple_of(owner * rows, rows), rows)]
            copies.append([pltpu.make_async_copy(source, place, block_sems.at[slot, at]) for source in sources])
        return copies

    def start_block(turn, slot):
        for copies in load_block(turn, slot):
            if len(copies) == 1:
                copies[0].start()
            else:
                start_own(copies)

    def store_block(turn, slot):
        return pltpu.make_async_copy(gate_up_ref.at[slot], gate_up_all_hbm.at[tokens(turn)], store_sems.at[1, slot])

    def hand_hidden(turn, slot, peer):
        device = peers[peer]
        return remote(
            turned_ref.at[slot, device], hidden_hbm.at[:, tokens(turn)], 4 * replicas + 3 * turn + peer, device
        )

    def keep_hidden(turn, slot):
        return pltpu.make_async_copy(
            turned_ref.at[slot, shard], hidden_hbm.at[:, tokens(turn)], store_sems.at[2, slot]
        )

    loads = [
        [pltpu.make_async_copy(source, target, sem) for source in sources]
        for sources, target, sem in (
            (normed_two, normed_two_ref, start_sems.at[0]),
            (slices, block_ref.at[0], store_sems.at[0, 0]),
        )
    ]
    for copies in loads:
        start_own(copies)
    slice_barrier(peers, range(2, replicas, 2))
    order = turn_order(replicas)
    loads[0][0].wait()
    evens = [turn for turn in order if turn and turn % 2 == 0]
    for turn in evens[:1]:
        from_replica(turn).start()
    for turn in order[1:3]:
        send_block(turn)

    for at, turn in enumerate(order):
        later = order[at + 1] if at + 1 < replicas else None
        slot = at % 2
        if at and at + 2 < replicas:
            send_block(order[at + 2])
            if order[at + 2] in evens:
                place = evens.index(order[at + 2]) + 1
                if place < len(evens):
                    from_replica(evens[place]).start()
        if at:
            for copies in load_block(turn, slot):
                copies[0].wait()
        else:
            loads[1][0].wait()
        if at > 1:
            store_block(order[at - 2], slot).wait()

        def products(step, carry, at=at, slot=slot):
            cols = pl.ds(pl.multiple_of(step * CHUNK, CHUNK), CHUNK)
            high = pl.ds(pl.multiple_of(part + step * CHUNK, CHUNK), CHUNK)
            if at == 0:
                load_weight(0, step).wait()
                load_weight(1, step).wait()
            gate = dot(block_ref[slot], weight_ref[:, cols])
            up = dot(block_ref[slot], weight_ref[:, high])
            gate_up_ref[slot, :, cols] = gate.astype(BF)
            gate_up_ref[slot, :, high] = up.astype(BF)
            hidden_ref[:, cols] = (gate * jax.nn.sigmoid(gate) * up).astype(BF)
            return carry

        lax.fori_loop(0, steps, products, 0)
        store_block(turn, slot).start()
        if later is not None:
            over(later).wait_recv()
            relay(later).start()

        @pl.when(shard == owner)
        def _(at=at, turn=turn, slot=slot):
            if at > 1:
                keep_hidden(order[at - 2], slot).wait()
                for peer in range(3):
                    hand_hidden(order[at - 2], slot, peer).wait_send()

            def turn_over(device, carry):
                cols = pl.ds(pl.multiple_of(first_col + device * ff_rows, ff_rows), ff_rows)
                turned_ref[slot, device] = hidden_ref[:, cols].T
                return carry

            lax.fori_loop(0, shards, turn_over, 0)
            keep_hidden(turn, slot).start()
            for peer in range(3):
                hand_hidden(turn, slot, peer).start()

        slice_cols = pl.ds(pl.multiple_of(replica * slice_rows, slice_rows), slice_rows)
        left_rows_ref[:, tokens(turn)] = block_ref[slot, :, slice_cols].T
        if later is not None:
            direct(later).wait_recv()
            relay(later).wait_recv()
            start_block(later, 1 - slot)

    for at in range(max(0, replicas - 2), replicas):
        store_block(order[at], at % 2).wait()

        @pl.when(shard == owner)
        def _(at=at):
            keep_hidden(order[at], at % 2).wait()
            for peer in range(3):
                hand_hidden(order[at], at % 2, peer).wait_send()

    for turn in range(replicas):
        for peer in range(3):

            @pl.when(peers[peer] == owner)
            def _(turn=turn, peer=peer):
                hand_hidden(turn, 0, peer).wait_recv()

        if turn:
            over(turn).wait_send()
            direct(turn).wait_send()
            relay(turn).wait_send()
        if turn in evens:
            from_replica(turn).wait_send()


def call_prepare(normed_two, gate_up_part, slices, odd, collective):
    rows, width = normed_two[0].shape
    shards, replicas = lax.axis_size("shard"), lax.axis_size("replica")
    part = gate_up_part.shape[1] // 2
    every = rows * shards
    slice_rows = width // replicas
    ff_rows = part // replicas
    vmem, anywhere = pl.BlockSpec(memory_space=pltpu.VMEM), pl.BlockSpec(memory_space=pl.ANY)
    copies = 7 * replicas
    outs = pl.pallas_call(
        functools.partial(prepare_kernel, len(slices)),
        out_shape=[
            jax.ShapeDtypeStruct((replicas, every, width), BF),
            jax.ShapeDtypeStruct((replicas * every, 2 * part), BF),
            jax.ShapeDtypeStruct((ff_rows, replicas * every), BF),
            jax.ShapeDtypeStruct((slice_rows, replicas * every), BF),
        ],
        in_specs=[anywhere] * (1 + 3 * len(slices)),
        out_specs=[anywhere] * 3 + [vmem],
        scratch_shapes=[
            pltpu.VMEM((rows, width), BF),
            pltpu.VMEM(gate_up_part.shape, BF),
            pltpu.VMEM((2, every, width), BF),
            pltpu.VMEM((2, every, 2 * part), BF),
            pltpu.VMEM((every, part), BF),
            pltpu.VMEM((2, shards, ff_rows, every), BF),
            pltpu.SemaphoreType.DMA((2, part // CHUNK)),
            pltpu.SemaphoreType.DMA((3, 2)),
            pltpu.SemaphoreType.DMA((2, 4)),
            pltpu.SemaphoreType.DMA((1,)),
            pltpu.SemaphoreType.DMA((copies,)),
            pltpu.SemaphoreType.DMA((copies,)),
        ],
        compiler_params=pltpu.CompilerParams(
            collective_id=collective, has_side_effects=True, vmem_limit_bytes=VMEM_LIMIT
        ),
        name="prepare",
    )(gate_up_part, *slices, *normed_two, *odd)
    return outs[1:]


def on_device(
    tokens_in,
    positions,
    attn_gain,
    qkv_weight,
    out_weight,
    mlp_gain,
    gate_up_weight,
    down_weight,
    cotangent,
):
    sections = lax.axis_size("section")
    rows, width = tokens_in.shape
    down_steps = [(at + 1, at) for at in range(sections - 1)]

    cosine, sine = rope_tables(positions)
    allowed = visible(positions)

    tables = (attn_gain, mlp_gain, cosine, sine, allowed)
    qkv_full, out_full, gate_up_part, *attend_first = call_weights(
        qkv_weight[0], out_weight[0], gate_up_weight[0], (tokens_in,) + tables, 3
    )
    down_part = down_weight[0]

    forward = []
    state = tokens_in
    early = None
    for section in range(sections):
        middle, normed_two, rotated, lefts = (
            call_attend_forward(section, state, *tables, qkv_full, out_full) if section else attend_first
        )
        block_out, normed_two_slice, gate_up, normed_two_odd, state_next, *gathered = call_feed(
            section, False, (normed_two, middle, gate_up_part, down_part), 8 + section,
            cotangent if section + 2 == sections else None,
        )
        early = gathered[0] if gathered else early
        forward.append((state, middle, rotated, gate_up, normed_two_slice, normed_two_odd, normed_two, lefts, block_out))
        state = state_next

    def pick(values):
        chosen = values[-1]
        for section in range(sections - 1):
            chosen = jnp.where(lax.axis_index("section") == section, values[section], chosen)
        return chosen

    slices, normed_two_odd, normed_two, lefts, block_out = list(zip(*forward))[4:]
    block_out = pick(block_out)
    backward = []
    upstream = cotangent
    for section in reversed(range(sections)):
        state, middle, rotated, gate_up = forward[section][:4]
        grad_normed_two, upstream_slice, odd = call_feed(
            section, True, (upstream, gate_up, down_part, gate_up_part), 8 + sections + section
        )
        grad_in, grad_low, grad_projected, gains, grad_branch = call_attend_backward(
            section, 8 + 2 * sections + section, grad_normed_two, upstream, middle, state, rotated,
            *tables, qkv_full, out_full,
        )
        backward.insert(0, (upstream, upstream_slice, odd, grad_in, grad_projected, gains, grad_branch))
        if section == sections - 1:
            normed_two, grad_low = lax.optimization_barrier((normed_two, grad_low))
        if section > 0:
            upstream = lax.ppermute(grad_low, "section", down_steps)
        if section == sections - 1:
            gate_up_all, hidden_rows, left_rows = call_prepare(
                normed_two, gate_up_part, slices, normed_two_odd, 6
            )
            upstream, gate_up_all, left_rows, hidden_rows = lax.optimization_barrier(
                (upstream, gate_up_all, left_rows, hidden_rows)
            )

    upstream, upstream_slice, odd, grad_in, grad_projected, gains, grad_branch = zip(*backward)
    grad_in = pick(grad_in)
    gate_up_grad, down_grad, qkv_grad, out_grad, gains, _, _ = call_weight_grads(
        left_rows, hidden_rows, lefts, grad_projected, gains, upstream, grad_branch, upstream_slice, odd,
        early, gate_up_all, down_part, 5,
    )
    gate_up_grad = gate_up_grad.astype(F32)
    return (
        block_out[None],
        grad_in[None],
        gains[0][None],
        qkv_grad[None],
        out_grad[None],
        gains[1][None],
        gate_up_grad[None],
        down_grad[None],
    )


def solution(mesh):
    both = ("replica", "shard")
    return jax.shard_map(
        on_device,
        mesh=mesh,
        in_specs=(
            P(both, None),
            P(both),
            P("section", None),
            P("section", "shard", None),
            P("section", "shard", None),
            P("section", None),
            P("section", "shard", None),
            P("section", "shard", None),
            P(both, None),
        ),
        out_specs=(
            P("section", both, None),
            P("section", both, None),
            P("section", None),
            P("section", both, None),
            P("section", both, None),
            P("section", None),
            P("section", both, None),
            P("section", both, None),
        ),
        check_vma=False,
    )
```

```python
import functools

import jax
import jax.numpy as jnp
from jax import lax
from jax.experimental import pallas as pl
from jax.experimental.pallas import tpu as pltpu
from jax.sharding import PartitionSpec as P

HEADS = 32
KV_HEADS = 8
HEAD = 64
SEQ = 64
EPSILON = 1e-05
ROPE_BASE = 500000.0
BF = jnp.bfloat16
F32 = jnp.float32
CONTRACT_LAST = (((1,), (1,)), ((), ()))
CONTRACT_FIRST = (((0,), (0,)), ((), ()))


MESH = pl.DeviceIdType.MESH
VMEM_LIMIT = 60 * 2**20
TILE = 128


def dot(left, right):
    return jnp.dot(left, right, preferred_element_type=F32)


def dot_rows(left, right):
    return lax.dot_general(left, right, CONTRACT_LAST, preferred_element_type=F32)


def dot_tokens(left, right):
    return lax.dot_general(left, right, CONTRACT_FIRST, preferred_element_type=F32)


def rope_tables(seq_pos):
    half_index = jnp.arange(HEAD // 2, dtype=F32)
    frequency = jnp.power(ROPE_BASE, -2.0 * half_index / HEAD)
    angles = seq_pos.astype(F32)[:, None] * frequency[None, :]
    cosine, sine = jnp.cos(angles), jnp.sin(angles)
    return (
        jnp.concatenate([cosine] * 4, 1),
        jnp.concatenate([-sine, sine, -sine, sine], 1),
    )


def visible(seq_pos):
    rows = seq_pos.shape[0]
    row_index = jnp.arange(rows)[:, None]
    col_index = jnp.arange(rows)[None, :]
    same = row_index // SEQ == col_index // SEQ
    seen = (col_index <= row_index) & (row_index - col_index <= seq_pos[:, None])
    return jnp.where(same & seen, 1.0, 0.0).astype(F32)


def lanes(rows):
    return lax.broadcasted_iota(jnp.int32, (rows, TILE), 1)


def swap_halves(tile, lane):
    return jnp.where(lane % HEAD < HEAD // 2, pltpu.roll(tile, TILE - HEAD // 2, 1), pltpu.roll(tile, HEAD // 2, 1))


def spread(tile, odd, lane):
    turned = pltpu.roll(tile, HEAD, 1)
    lower, upper = (turned, tile) if odd else (tile, turned)
    return jnp.concatenate(
        [jnp.where(lane < HEAD, lower, 0.0), jnp.where(lane < HEAD, 0.0, upper)], 0
    ).astype(BF)


def softmax_pair(queries, spread_keys, allowed):
    scores = dot_rows(queries, spread_keys) * HEAD ** (-0.5)
    halves = []
    for side in range(2):
        masked = jnp.where(allowed > 0.5, scores[:, side * TILE : (side + 1) * TILE], -1e30)
        expon = jnp.exp(masked - jnp.max(masked, -1, keepdims=True))
        halves.append(expon / jnp.sum(expon, -1, keepdims=True))
    return halves


def attend_parts(
    state_ref, gain_one_ref, gain_two_ref, cos_ref, sin_ref, allowed_ref, qkv_hbm, out_hbm,
    middle_ref, normed_two_ref, rotated_ref, lefts_ref,
    qkv_ref, out_ref, normed_ref, attended_ref, sems,
):
    rows, width = state_ref.shape
    cols = qkv_hbm.shape[1]
    step = 512
    rope_cols = (HEADS + KV_HEADS) * HEAD

    def qkv_copy(at):
        return pltpu.make_async_copy(qkv_hbm.at[:, pl.ds(at, step)], qkv_ref.at[:, pl.ds(at, step)], sems.at[at // step])

    def out_copy(at):
        return pltpu.make_async_copy(
            out_hbm.at[:, pl.ds(at, step)], out_ref.at[:, pl.ds(at, step)], sems.at[(cols + at) // step]
        )

    def begin():
        for at in range(0, cols, step):
            qkv_copy(at).start()
        state = state_ref[...].astype(F32)
        inverse = lax.rsqrt(jnp.mean(state * state, -1, keepdims=True) + EPSILON)
        normed_ref[...] = (state * inverse * gain_one_ref[...]).astype(BF)

    def project(at):
        qkv_copy(at).wait()
        lane = lanes(rows)
        projected = dot(normed_ref[...], qkv_ref[:, at : at + step])
        for tile_at in range(0, step, TILE):
            tile = projected[:, tile_at : tile_at + TILE]
            if at + tile_at < rope_cols:
                tile = tile * cos_ref[...] + swap_halves(tile, lane) * sin_ref[...]
            rotated_ref[:, at + tile_at : at + tile_at + TILE] = tile.astype(BF)

    def attend(group):
        lane = lanes(rows)
        key_at = width + group // 2 * TILE
        value_at = rope_cols + group // 2 * TILE
        keys = spread(rotated_ref[:, key_at : key_at + TILE].astype(F32), group % 2, lane)
        values = spread(rotated_ref[:, value_at : value_at + TILE].astype(F32), group % 2, lane)
        for pair in range(2):
            at = (group * 2 + pair) * TILE
            halves = softmax_pair(rotated_ref[:, at : at + TILE], keys, allowed_ref[...])
            probs = jnp.concatenate([half.astype(BF) for half in halves], 1)
            attended_ref[:, at : at + TILE] = dot(probs, values).astype(BF)

    def load_out():
        for at in range(0, width, step):
            out_copy(at).start()

    def leave(at):
        out_copy(at).wait()
        middle = state_ref[:, at : at + step].astype(F32) + dot(attended_ref[...], out_ref[:, at : at + step])
        middle_ref[:, at : at + step] = middle

    def finish():
        middle = middle_ref[...]
        inverse = lax.rsqrt(jnp.mean(middle * middle, -1, keepdims=True) + EPSILON)
        normed_two_ref[...] = (middle * inverse * gain_two_ref[...]).astype(BF)
        lefts_ref[0] = normed_ref[...].T
        lefts_ref[1] = attended_ref[...].T

    first = [begin] + [functools.partial(project, at) for at in range(0, cols, step)]
    first += [functools.partial(attend, group) for group in range(KV_HEADS)]
    second = [functools.partial(leave, at) for at in range(0, width, step)] + [finish]
    return first, load_out, second


def attend_forward(*refs):
    first, load_out, second = attend_parts(*refs)
    first[0]()
    load_out()
    for part in first[1:] + second:
        part()


def attend_backward(
    rounds, grad_ref, upstream_ref, middle_ref, state_ref, rotated_ref,
    gain_one_ref, gain_two_ref, cos_ref, sin_ref, allowed_ref, qkv_hbm, out_hbm,
    grad_state_ref, grad_low_ref, grad_projected_ref, gain_terms_ref, branch_hbm,
    qkv_ref, out_ref, grad_branch_ref, grad_out_ref, middle_grad_ref, sems, keep_sems, send_sems, recv_sems,
):
    rows, width = middle_ref.shape
    cols = qkv_hbm.shape[1]
    step = 512
    steps = width // step
    out_copies = [
        pltpu.make_async_copy(out_hbm.at[pl.ds(at * step, step)], out_ref.at[pl.ds(at * step, step)], sems.at[at])
        for at in range(steps)
    ]
    copies = [
        pltpu.make_async_copy(
            qkv_hbm.at[pl.ds(at * step, step)], qkv_ref.at[pl.ds(at * step, step)], sems.at[steps + at]
        )
        for at in range(steps)
    ]
    for copy in out_copies + copies:
        copy.start()
    shard, beside, across, _ = slice_peers()
    slice_barrier((beside, across))

    def branch_rows(owner, at):
        return branch_hbm.at[at, pl.ds(pl.multiple_of(owner * rows, rows), rows)]

    def remote(source, owner, at, kind, device):
        return pltpu.make_async_remote_copy(
            source, branch_rows(owner, at), send_sems.at[kind, at], recv_sems.at[kind, at],
            device_id={"shard": device}, device_id_type=MESH,
        )

    branch = [grad_branch_ref.at[:, pl.ds(at * step, step)] for at in range(steps)]
    over = [remote(branch[at], shard, at, 0, across) for at in range(steps)]
    direct = [remote(branch[at], shard, at, 1, beside) for at in range(steps)]
    relays = [remote(branch_rows(across, at), across, at, 2, beside) for at in range(steps)]
    keeps = [pltpu.make_async_copy(branch[at], branch_rows(shard, at), keep_sems.at[at]) for at in range(steps)]

    def norm_back(grad, values, gain):
        inverse = lax.rsqrt(jnp.mean(values * values, -1, keepdims=True) + EPSILON)
        normal = values * inverse
        term = jnp.sum(grad * normal, 0, keepdims=True)
        scaled = grad * gain
        return inverse * (scaled - normal * jnp.mean(scaled * normal, -1, keepdims=True)), term

    upstream = upstream_ref[...].astype(F32)
    back, term = norm_back(grad_ref[...], middle_ref[...], gain_two_ref[...])
    gain_terms_ref[1:2, :] = term
    middle_grad_ref[...] = upstream + back
    grad_branch_ref[...] = middle_grad_ref[...].astype(BF)
    for copy in over + direct + keeps:
        copy.start()
    for at in range(steps):
        out_copies[at].wait()
        grad_out_ref[:, at * step : (at + 1) * step] = dot_rows(
            grad_branch_ref[...], out_ref[at * step : (at + 1) * step, :]
        ).astype(BF)
    lane = lanes(rows)
    cosine, sine, allowed = cos_ref[...], sin_ref[...], allowed_ref[...]
    rope_cols = (HEADS + KV_HEADS) * HEAD
    scale = HEAD ** (-0.5)

    def unrotate(tile):
        return tile * cosine - swap_halves(tile, lane) * sine

    def group_step(group_pair, carry):
        key_at = pl.multiple_of(width + group_pair * TILE, TILE)
        value_at = pl.multiple_of(rope_cols + group_pair * TILE, TILE)
        sums = []
        for odd in range(2):
            keys = spread(rotated_ref[:, pl.ds(key_at, TILE)].astype(F32), odd, lane)
            values = spread(rotated_ref[:, pl.ds(value_at, TILE)].astype(F32), odd, lane)
            key_sum = jnp.zeros((rows, TILE), F32)
            value_sum = jnp.zeros((rows, TILE), F32)
            for pair in range(2):
                at = pl.multiple_of(((group_pair * 2 + odd) * 2 + pair) * TILE, TILE)
                queries = rotated_ref[:, pl.ds(at, TILE)]
                grad_out = grad_out_ref[:, pl.ds(at, TILE)]
                halves = softmax_pair(queries, keys, allowed)
                grad_probs = dot_rows(grad_out, values)
                grad_halves = []
                for side in range(2):
                    grad = grad_probs[:, side * TILE : (side + 1) * TILE]
                    row_dot = jnp.sum(halves[side] * grad, -1, keepdims=True)
                    grad_halves.append((halves[side] * (grad - row_dot)).astype(BF))
                grad_scores = jnp.concatenate(grad_halves, 1)
                probs = jnp.concatenate([half.astype(BF) for half in halves], 1)
                grad_projected_ref[:, pl.ds(at, TILE)] = unrotate(dot(grad_scores, keys) * scale).astype(BF)
                key_terms = dot_tokens(grad_scores, queries)
                value_terms = dot_tokens(probs, grad_out)
                key_sum += jnp.where(lane < HEAD, key_terms[:rows], key_terms[rows:])
                value_sum += jnp.where(lane < HEAD, value_terms[:rows], value_terms[rows:])
            sums.append((key_sum + pltpu.roll(key_sum, HEAD, 1), value_sum + pltpu.roll(value_sum, HEAD, 1)))
        keys_grad = jnp.where(lane < HEAD, sums[0][0], sums[1][0]) * scale
        grad_projected_ref[:, pl.ds(key_at, TILE)] = unrotate(keys_grad).astype(BF)
        grad_projected_ref[:, pl.ds(value_at, TILE)] = jnp.where(
            lane < HEAD, sums[0][1], sums[1][1]
        ).astype(BF)
        return carry

    lax.fori_loop(0, KV_HEADS // 2, group_step, 0)
    for at in range(steps):
        over[at].wait_recv()
        relays[at].start()
    for at in range(steps):
        copies[at].wait()
        grad_state_ref[:, at * step : (at + 1) * step] = dot_rows(
            grad_projected_ref[...], qkv_ref[at * step : (at + 1) * step, :]
        )
    state = state_ref[...].astype(F32)
    back, term = norm_back(grad_state_ref[...], state, gain_one_ref[...])
    gain_terms_ref[0:1, :] = term
    grad_state = middle_grad_ref[...] + back
    grad_low = grad_state.astype(BF)
    grad_low_ref[...] = grad_low
    grad_state_ref[...] = grad_low.astype(F32) if rounds else grad_state
    for copy in direct + relays:
        copy.wait()
    for copy in over:
        copy.wait_send()
    for copy in keeps:
        copy.wait()


def gated(section, body):
    def kernel(*refs):
        @pl.when(lax.axis_index("section") == section)
        def _():
            body(*refs)

    return kernel


def attend_shapes(rows, width, cols):
    return [
        jax.ShapeDtypeStruct((rows, width), F32),
        jax.ShapeDtypeStruct((rows, width), BF),
        jax.ShapeDtypeStruct((rows, cols), BF),
        jax.ShapeDtypeStruct((2, width, rows), BF),
    ], [
        pltpu.VMEM((width, cols), BF),
        pltpu.VMEM((width, width), BF),
        pltpu.VMEM((rows, width), BF),
        pltpu.VMEM((rows, width), BF),
        pltpu.SemaphoreType.DMA(((cols + width) // 512,)),
    ]


def call_attend_forward(section, *operands):
    rows, width = operands[0].shape
    out_shape, scratch = attend_shapes(rows, width, operands[6].shape[1])
    specs = [pl.BlockSpec(memory_space=pltpu.VMEM)] * 6 + [pl.BlockSpec(memory_space=pl.ANY)] * 2
    return pl.pallas_call(
        gated(section, attend_forward),
        out_shape=out_shape,
        in_specs=specs,
        out_specs=[pl.BlockSpec(memory_space=pltpu.VMEM)] * 4,
        scratch_shapes=scratch,
        compiler_params=pltpu.CompilerParams(vmem_limit_bytes=VMEM_LIMIT),
        name="attend_forward",
    )(*operands)


def call_attend_backward(section, collective, *operands):
    rows, width = operands[2].shape
    cols = operands[10].shape[1]
    steps = width // 512
    every = lax.axis_size("shard") * rows
    vmem, anywhere = pl.BlockSpec(memory_space=pltpu.VMEM), pl.BlockSpec(memory_space=pl.ANY)
    return pl.pallas_call(
        gated(section, functools.partial(attend_backward, section > 0)),
        out_shape=(
            jax.ShapeDtypeStruct((rows, width), F32),
            jax.ShapeDtypeStruct((rows, width), BF),
            jax.ShapeDtypeStruct((rows, cols), BF),
            jax.ShapeDtypeStruct((2, width), F32),
            jax.ShapeDtypeStruct((steps, every, 512), BF),
        ),
        in_specs=[vmem] * 10 + [anywhere] * 2,
        out_specs=[vmem] * 4 + [anywhere],
        scratch_shapes=[
            pltpu.VMEM((width, cols), BF),
            pltpu.VMEM((width, width), BF),
            pltpu.VMEM((rows, width), BF),
            pltpu.VMEM((rows, width), BF),
            pltpu.VMEM((rows, width), F32),
            pltpu.SemaphoreType.DMA((2 * steps,)),
            pltpu.SemaphoreType.DMA((steps,)),
            pltpu.SemaphoreType.DMA((3, steps)),
            pltpu.SemaphoreType.DMA((3, steps)),
        ],
        compiler_params=pltpu.CompilerParams(
            collective_id=collective, has_side_effects=True, vmem_limit_bytes=VMEM_LIMIT
        ),
        name="attend_backward",
    )(*operands)


def start_own(copies):
    for section, copy in enumerate(copies):

        @pl.when(lax.axis_index("section") == section)
        def _(copy=copy):
            copy.start()


def slice_peers():
    shard = lax.axis_index("shard")
    chip, core = shard // 2, shard % 2
    return shard, chip * 2 + (1 - core), (1 - chip) * 2 + core, (1 - chip) * 2 + (1 - core)


def slice_barrier(devices, turns=(), more=0):
    barrier = pltpu.get_barrier_semaphore()
    replicas = lax.axis_size("replica")
    for device in devices:
        pl.semaphore_signal(barrier, inc=1, device_id={"shard": device}, device_id_type=MESH)
    for turn in turns:
        target = lax.rem(lax.axis_index("replica") + turn, replicas)
        pl.semaphore_signal(barrier, inc=1, device_id={"replica": target}, device_id_type=MESH)
    pl.semaphore_wait(barrier, len(devices) + len(turns) + more)


def replica_copy(source, target, turn, send_sems, recv_sems, base):
    replicas = lax.axis_size("replica")
    device = lax.rem(lax.axis_index("replica") + replicas - turn, replicas)
    return pltpu.make_async_remote_copy(
        source, target, send_sems.at[base + turn], recv_sems.at[base + turn],
        device_id={"replica": device}, device_id_type=MESH,
    )


CHUNK = 512


def feed_kernel(backward, rows, target, wide, *refs):
    if backward:
        (mine_ref, gate_up_hbm, odd_hbm, first_hbm, second_hbm, result_ref, all_hbm, others_hbm, ahead_hbm,
         mid_ref, all_ref, gate_up_ref, first_ref, second_ref, part_ref, take_ref, sent_ref, land_ref, own_ref,
         own_take_ref, load_sems, keep_sems, hold_sems, send_sems, recv_sems) = refs
    else:
        (mine_ref, middle_hbm, first_hbm, second_hbm, result_ref, all_hbm, gate_up_hbm, others_hbm, next_hbm,
         mid_ref, all_ref, gate_up_ref, first_ref, second_ref, part_ref, take_ref, sent_ref, land_ref, own_ref,
         own_take_ref, middle_ref, load_sems, keep_sems, hold_sems, send_sems, recv_sems) = refs
    shard, beside, across, _ = slice_peers()
    chip, core = shard // 2, shard % 2
    half = rows // 2
    parts, spans, _, piece, span_cols = part_ref.shape
    block = 2 * piece
    width = all_ref.shape[1]
    ff = first_ref.shape[0] if backward else second_ref.shape[0]
    first_steps = ff // CHUNK

    def load_first(at):
        if backward:
            place = (pl.ds(pl.multiple_of(at * CHUNK, CHUNK), CHUNK), slice(None))
            return [pltpu.make_async_copy(first_hbm.at[place], first_ref.at[place], load_sems.at[0, at])]
        places = [
            (slice(None), pl.ds(pl.multiple_of(side * ff + at * CHUNK, CHUNK), CHUNK)) for side in range(2)
        ]
        return [
            pltpu.make_async_copy(first_hbm.at[place], first_ref.at[place], load_sems.at[side, at])
            for side, place in enumerate(places)
        ]

    def load_second(at):
        span = pl.ds(pl.multiple_of(at * span_cols, span_cols), span_cols)
        place = (span, slice(None)) if backward else (slice(None), span)
        return pltpu.make_async_copy(second_hbm.at[place], second_ref.at[place], load_sems.at[2, at])

    load_extra = []
    if backward:
        for at in range(2 * lax.axis_size("shard")):
            group, part, owner = at // 4, at // 2 % 2, at % 2
            source = pl.ds(at * half, half)
            place = pl.ds(group * 2 * rows + owner * rows + part * half, half)
            load_extra.append(pltpu.make_async_copy(gate_up_hbm.at[source], gate_up_ref.at[place], hold_sems.at[at]))
    else:
        load_extra.append(pltpu.make_async_copy(middle_hbm, middle_ref, hold_sems.at[0]))
    if backward:
        for copy in load_extra:
            copy.start()
    for at in range(first_steps):
        for copy in load_first(at):
            copy.start()
    for at in range(spans):
        load_second(at).start()
    if not backward:
        load_extra[0].start()

    def remote(source, target, at, device):
        return pltpu.make_async_remote_copy(
            source, target, send_sems.at[at], recv_sems.at[at], device_id={"shard": device}, device_id_type=MESH
        )

    def place_of(owner, part):
        start = part * block + (owner % 2) * piece if parts == 2 else (owner % 2) * piece + part * half
        return pl.ds(pl.multiple_of((owner // 2) * 2 * rows + start, half), half)

    def owned(owner, part):
        return all_ref.at[place_of(owner, part)]

    turns = spread_turns(wide)
    base = 6 + (2 * parts + 1) * spans
    slice_barrier((beside, across), turns, 0 if target is None else 1)

    def hand_on(part, at):
        place = (pl.ds(part * piece, piece), pl.ds(at * span_cols, span_cols))
        return section_copy(
            result_ref.at[place], next_hbm.at[place], part * spans + at + base + lax.axis_size("replica"),
            send_sems, recv_sems, target,
        )

    def across_copy(part):
        return remote(owned(shard, part), owned(shard, part), part, across)

    def relay(part):
        return remote(owned(across, part), owned(across, part), 4 + part, beside)

    beside_copies = [remote(owned(shard, part), owned(shard, part), 2 + part, beside) for part in range(2)]
    for part in range(2):
        all_ref[place_of(shard, part), :] = mine_ref[part * half : (part + 1) * half, :]
        across_copy(part).start()
    for copy in beside_copies:
        copy.start()
    spread_copies = [
        replica_copy(mine_ref, others_hbm.at[lax.axis_index("replica")], turn, send_sems, recv_sems, base)
        for turn in turns
    ]
    for copy in spread_copies:
        copy.start()

    def ahead_rows(owner):
        return ahead_hbm.at[pl.ds(pl.multiple_of(owner * rows, rows), rows)]

    if wide:
        next_rows = odd_hbm.at[lax.rem(lax.axis_index("replica") + 1, lax.axis_size("replica"))]
        ahead_base = base + lax.axis_size("replica")
        ahead_over = remote(next_rows, ahead_rows(shard), ahead_base, across)
        ahead_direct = remote(next_rows, ahead_rows(shard), ahead_base + 1, beside)
        ahead_relay = remote(ahead_rows(across), ahead_rows(across), ahead_base + 2, beside)

    def first_product(start, count, waits):
        span = pl.ds(pl.multiple_of(start, count), count)

        def step(at, carry):
            cols = pl.ds(pl.multiple_of(at * CHUNK, CHUNK), CHUNK)
            high = pl.ds(pl.multiple_of(ff + at * CHUNK, CHUNK), CHUNK)
            if waits:
                for copy in load_first(at):
                    copy.wait()
            if backward:
                grad_hidden = dot_rows(all_ref[span, :], first_ref[cols, :])
                gate = gate_up_ref[span, cols].astype(F32)
                up = gate_up_ref[span, high].astype(F32)
                sigmoid = jax.nn.sigmoid(gate)
                mid_ref[span, cols] = (grad_hidden * up * sigmoid * (1.0 + gate * (1.0 - sigmoid))).astype(BF)
                mid_ref[span, high] = (grad_hidden * gate * sigmoid).astype(BF)
            else:
                gate = dot(all_ref[span, :], first_ref[:, cols])
                up = dot(all_ref[span, :], first_ref[:, high])
                gate_up_ref[span, cols] = gate.astype(BF)
                gate_up_ref[span, high] = up.astype(BF)
                mid_ref[span, cols] = (gate * jax.nn.sigmoid(gate) * up).astype(BF)
            return carry

        lax.fori_loop(0, first_steps, step, 0)

    def second_product(start, count, at, store):
        span = pl.ds(pl.multiple_of(start, count), count)

        def step(inner, carry):
            cols = pl.ds(pl.multiple_of(at * span_cols + inner * CHUNK, CHUNK), CHUNK)
            if backward:
                partial = dot_rows(mid_ref[span, :], second_ref[cols, :])
            else:
                partial = dot(mid_ref[span, :], second_ref[:, cols])
            store(pl.ds(pl.multiple_of(inner * CHUNK, CHUNK), CHUNK), partial.astype(BF))
            return carry

        lax.fori_loop(0, span_cols // CHUNK, step, 0)

    def give(part, at):
        return remote(part_ref.at[part, at, 1 - core], take_ref.at[part, at], 6 + part * spans + at, beside)

    def cross(part, at):
        return remote(sent_ref.at[part, at], land_ref.at[part, at], 6 + (parts + part) * spans + at, across)

    def give_own(at):
        return remote(own_ref.at[at, 1 - core], own_take_ref.at[at], 6 + 2 * parts * spans + at, beside)

    def pass_on(part, at):
        give(part, at).wait_recv()
        sent_ref[part, at] = (part_ref[part, at, core].astype(F32) + take_ref[part, at].astype(F32)).astype(BF)
        cross(part, at).start()

    own_start = chip * 2 * rows
    other_start = (1 - chip) * 2 * rows
    stores = []
    for copy in beside_copies:
        copy.wait_recv()
    if backward:
        for copy in load_extra:
            copy.wait()
    first_product(own_start, 2 * rows, True)
    if not backward:
        own_place = pl.ds(pl.multiple_of(own_start, 2 * rows), 2 * rows)
        stores.append(pltpu.make_async_copy(gate_up_ref.at[own_place], gate_up_hbm.at[own_place], keep_sems.at[1]))
        stores[-1].start()

    def store_part(part):
        place = pl.ds(pl.multiple_of(other_start + part * block, block), block)
        return pltpu.make_async_copy(gate_up_ref.at[place], gate_up_hbm.at[place], keep_sems.at[2 + part])

    def arrive(part):
        across_copy(part).wait_recv()
        relay(part).start()

    if parts == 1:
        for part in range(2):
            arrive(part)

    def other_part(part, carry):
        if parts == 1:
            for late in range(2):
                relay(late).wait_recv()
            if wide:
                ahead_over.start()
                ahead_direct.start()
        else:
            arrive(part)
            relay(part).wait_recv()
        start = other_start + part * block
        first_product(start, block, False)
        if not backward:
            store_part(part).start()

        def span_step(at, inner):
            @pl.when(part == 0)
            def _():
                load_second(at).wait()

            def store(cols, partial):
                part_ref[part, at, 0, :, cols] = partial[:piece]
                part_ref[part, at, 1, :, cols] = partial[piece:]

            second_product(start, block, at, store)
            give(part, at).start()

            @pl.when(at > 0)
            def _():
                pass_on(part, at - 1)

            return inner

        lax.fori_loop(0, spans, span_step, 0)
        pass_on(part, spans - 1)
        return carry

    lax.fori_loop(0, parts, other_part, 0)
    if not backward:
        stores += [store_part(part) for part in range(parts)]
    for owner in range(lax.axis_size("shard")):
        for part in range(2):
            at = owner * 2 + part
            copy = pltpu.make_async_copy(
                all_ref.at[place_of(owner, part)], all_hbm.at[pl.ds(owner * rows + part * half, half)],
                keep_sems.at[4 + at],
            )
            copy.start()
            stores.append(copy)

    def own_step(at, carry):
        def store(cols, partial):
            for part in range(parts):
                for owner in range(2):
                    first_row = part * block + owner * piece
                    own_ref[at, owner, part * piece : (part + 1) * piece, cols] = partial[first_row : first_row + piece]

        second_product(own_start, 2 * rows, at, store)
        give_own(at).start()
        return carry

    lax.fori_loop(0, spans, own_step, 0)
    if wide:
        ahead_over.wait_recv()
        ahead_relay.start()
    if not backward:
        load_extra[0].wait()
    for at in range(spans):
        give_own(at).wait_recv()
    for part in range(parts):
        place = slice(part * piece, (part + 1) * piece)
        for at in range(spans):
            cross(part, at).wait_recv()
            cols = slice(at * span_cols, (at + 1) * span_cols)
            total = (
                own_ref[at, core, place].astype(F32)
                + own_take_ref[at, place].astype(F32)
                + land_ref[part, at].astype(F32)
            )
            if backward:
                result_ref[place, cols] = total
            else:
                result_ref[place, cols] = (middle_ref[place, cols] + total).astype(BF)
                if target is not None:
                    hand_on(part, at).start()
    for part in range(2):
        beside_copies[part].wait_send()
        across_copy(part).wait_send()
        relay(part).wait_send()
    if wide:
        ahead_direct.wait()
        ahead_relay.wait()
        ahead_over.wait_send()
    for copy in spread_copies + stores:
        copy.wait()
    if target is not None:
        for part in range(parts):
            for at in range(spans):
                hand_on(part, at).wait_send()
    for at in range(spans):
        give_own(at).wait_send()
        for part in range(parts):
            give(part, at).wait_send()
            cross(part, at).wait_send()


def section_copy(source, target, at, send_sems, recv_sems, section):
    return pltpu.make_async_remote_copy(
        source, target, send_sems.at[at], recv_sems.at[at], device_id={"section": section}, device_id_type=MESH
    )


def spread_turns(wide):
    return range(2, lax.axis_size("replica")) if wide else range(1, lax.axis_size("replica"), 2)


def gather_turns(mine_hbm, gathered_hbm, send_sems, recv_sems):
    shard, beside, across, _ = slice_peers()
    replicas = lax.axis_size("replica")
    rows = mine_hbm.shape[0]

    def remote(owner, turn, at, device):
        place = gathered_hbm.at[turn, pl.ds(pl.multiple_of(owner * rows, rows), rows)]
        return pltpu.make_async_remote_copy(
            place, place, send_sems.at[at], recv_sems.at[at], device_id={"shard": device}, device_id_type=MESH
        )

    own_rows = pl.ds(pl.multiple_of(shard * rows, rows), rows)
    order = [1]
    spread_copies = [
        replica_copy(mine_hbm, gathered_hbm.at[turn, own_rows], turn, send_sems, recv_sems, 3 * replicas)
        for turn in order
    ]
    over = [remote(shard, turn, 3 * turn, across) for turn in order]
    direct = [remote(shard, turn, 3 * turn + 1, beside) for turn in order]
    relays = [remote(across, turn, 3 * turn + 2, beside) for turn in order]
    spread_copies[0].start()
    for at in range(len(order)):
        spread_copies[at].wait_recv()
        over[at].start()
        direct[at].start()
        spread_copies[at].wait_send()
        if at + 1 < len(order):
            spread_copies[at + 1].start()
        if at:
            over[at - 1].wait_recv()
            relays[at - 1].start()
    over[-1].wait_recv()
    relays[-1].start()
    for copy in direct + relays:
        copy.wait_recv()
    for copy in over + direct + relays:
        copy.wait_send()


def feed_forward_kernel(section, last, gathers, parts, spans, rows, *refs):
    if gathers:
        cotangent_hbm, early_hbm, gather_send_sems, gather_recv_sems = refs[4], refs[10], refs[-4], refs[-3]
        refs = refs[:4] + refs[5:10] + refs[11:-4] + refs[-2:]

    @pl.when(lax.axis_index("section") == section)
    def _():
        feed_kernel(False, rows, None if last else section + 1, False, *refs)

    if not last:

        @pl.when(lax.axis_index("section") == section + 1)
        def _():
            barrier = pltpu.get_barrier_semaphore()
            pl.semaphore_signal(barrier, inc=1, device_id={"section": section}, device_id_type=MESH)
            if gathers:
                _, beside, across, _ = slice_peers()
                slice_barrier((beside, across), (1,))
                gather_turns(cotangent_hbm, early_hbm, gather_send_sems, gather_recv_sems)
            next_hbm, send_sems, recv_sems = refs[8], refs[-2], refs[-1]
            base = 6 + (2 * parts + 1) * spans + lax.axis_size("replica")
            high, wide = rows // parts, next_hbm.shape[1] // spans
            for part in range(parts):
                for at in range(spans):
                    place = next_hbm.at[pl.ds(part * high, high), pl.ds(at * wide, wide)]
                    section_copy(place, place, base + part * spans + at, send_sems, recv_sems, section).wait_recv()


def call_feed(section, backward, operands, collective, cotangent=None):
    first, second = operands[-2], operands[-1]
    rows, width = operands[0].shape
    shards, replicas = lax.axis_size("shard"), lax.axis_size("replica")
    ff = first.shape[0] if backward else second.shape[0]
    every = shards * rows
    parts, span_cols = (1, CHUNK) if backward else (2, 2 * CHUNK)
    spans, piece_rows = width // span_cols, rows // parts
    vmem, anywhere = pl.BlockSpec(memory_space=pltpu.VMEM), pl.BlockSpec(memory_space=pl.ANY)
    out_shape = [
        jax.ShapeDtypeStruct((rows, width), F32 if backward else BF),
        jax.ShapeDtypeStruct((every, width), BF),
        jax.ShapeDtypeStruct((replicas, rows, width), BF),
    ]
    if backward:
        out_shape.append(jax.ShapeDtypeStruct((every, width), BF))
    else:
        out_shape.insert(2, jax.ShapeDtypeStruct((every, 2 * ff), BF))
        out_shape.append(jax.ShapeDtypeStruct((rows, width), BF))
    copies = 6 + (3 * parts + 1) * spans + replicas + 3
    piece = pltpu.VMEM((parts, spans, piece_rows, span_cols), BF)
    scratch = [
        pltpu.VMEM((every, 2 * ff if backward else ff), BF),
        pltpu.VMEM((every, width), BF),
        pltpu.VMEM((every, 2 * ff), BF),
        pltpu.VMEM(first.shape, BF),
        pltpu.VMEM(second.shape, BF),
        pltpu.VMEM((parts, spans, 2, piece_rows, span_cols), BF),
        piece,
        piece,
        piece,
        pltpu.VMEM((spans, 2, rows, span_cols), BF),
        pltpu.VMEM((spans, rows, span_cols), BF),
    ]
    if not backward:
        scratch.append(pltpu.VMEM((rows, width), F32))
    scratch += [
        pltpu.SemaphoreType.DMA((3, max(ff // CHUNK, spans))),
        pltpu.SemaphoreType.DMA((4 + 2 * shards,)),
        pltpu.SemaphoreType.DMA((2 * shards,)),
        *([pltpu.SemaphoreType.DMA((4 * replicas,))] * (0 if cotangent is None else 2)),
        pltpu.SemaphoreType.DMA((copies,)),
        pltpu.SemaphoreType.DMA((copies,)),
    ]
    if cotangent is not None:
        operands += (cotangent,)
        out_shape.append(jax.ShapeDtypeStruct((replicas, every, width), BF))
    return pl.pallas_call(
        gated(section, functools.partial(feed_kernel, True, rows, None, section == lax.axis_size("section") - 1))
        if backward
        else functools.partial(feed_forward_kernel, section, section == lax.axis_size("section") - 1,
            cotangent is not None, parts, spans, rows),
        out_shape=out_shape,
        in_specs=[vmem] + [anywhere] * (len(operands) - 1),
        out_specs=[vmem] + [anywhere] * (len(out_shape) - 1),
        scratch_shapes=scratch,
        compiler_params=pltpu.CompilerParams(
            collective_id=collective, has_side_effects=True, vmem_limit_bytes=VMEM_LIMIT
        ),
        name="feed_backward" if backward else "feed_forward",
    )(*operands)


def weights_kernel(
    qkv_ref, out_ref, gate_up_ref, state_ref, gain_one_ref, gain_two_ref, cos_ref, sin_ref, allowed_ref,
    qkv_full, out_full, gate_up_part, middle_ref, normed_two_ref, rotated_ref, lefts_ref,
    qkv_hold, out_hold, gate_up_hold, qkv_work, out_work, normed_ref, attended_ref, work_sems,
    local_sems, send_sems, recv_sems,
):
    shard, replica = lax.axis_index("shard"), lax.axis_index("replica")
    chip, core = shard // 2, shard % 2
    beside = {"shard": chip * 2 + (1 - core)}
    across = {"shard": (1 - chip) * 2 + core}
    diagonal = {"shard": (1 - chip) * 2 + (1 - core)}
    mine = replica % 2
    partner = {"replica": replica + 1 - 2 * mine}
    rows = qkv_ref.shape[0]
    half = rows // 2
    ff = gate_up_ref.shape[1] // 2
    part = gate_up_part.shape[1] // 2

    def remote(source, target, at, device):
        return pltpu.make_async_remote_copy(
            source, target, send_sems.at[at], recv_sems.at[at], device_id=device, device_id_type=MESH
        )

    def span(start, count):
        return pl.ds(pl.multiple_of(start, count), count)

    sides = [pl.ds(side * part, part) for side in range(2)]
    loads = [
        pltpu.make_async_copy(qkv_ref, qkv_hold, local_sems.at[0]),
        pltpu.make_async_copy(out_ref, out_hold, local_sems.at[1]),
    ] + [
        pltpu.make_async_copy(
            gate_up_ref.at[:, span(side * ff + shard * part, part)], gate_up_hold.at[side], local_sems.at[2 + side]
        )
        for side in range(2)
    ]
    own_rows = span(shard * rows, rows)
    stores = [
        pltpu.make_async_copy(qkv_hold, qkv_full.at[own_rows], local_sems.at[4]),
        pltpu.make_async_copy(out_hold, out_full.at[own_rows], local_sems.at[5]),
    ] + [
        pltpu.make_async_copy(gate_up_hold.at[side], gate_up_part.at[own_rows, sides[side]], local_sems.at[6 + side])
        for side in range(2)
    ]
    for copy in loads:
        copy.start()

    pieces = []
    for source, whole, count in ((qkv_ref, qkv_full, 64), (out_ref, out_full, 64)):
        for offset in range(0, half, count):

            def place(owner, part_of, whole=whole, offset=offset, count=count):
                return whole.at[span(owner["shard"] * rows + part_of * half + offset, count)]

            own = source.at[span(mine * half + offset, count)]
            pieces.append((own, place, across, True))
    for offset in range(0, half, 64):
        for side in range(2):
            for device in (across, diagonal):

                def place(owner, part_of, offset=offset, side=side):
                    return gate_up_part.at[
                        span(owner["shard"] * rows + part_of * half + offset, 64), pl.ds(side * part, part)
                    ]

                own = gate_up_ref.at[
                    span(mine * half + offset, 64), span(side * ff + device["shard"] * part, part)
                ]
                pieces.append((own, place, device, False))
    count = len(pieces)
    me = {"shard": shard}
    over = [remote(own, place(me, mine), at, device) for at, (own, place, device, _) in enumerate(pieces)]
    passed = [
        remote(place(device, mine), place(device, mine), count + at, partner)
        for at, (_, place, device, _) in enumerate(pieces)
    ]
    relays = [
        [
            remote(place(across, which), place(across, which), (2 + turn) * count + at, beside)
            if relayed
            else None
            for at, (_, place, _, relayed) in enumerate(pieces)
        ]
        for turn, which in enumerate((mine, 1 - mine))
    ]
    direct = [
        remote(qkv_ref, qkv_full.at[span(shard * rows, rows)], 4 * count, beside),
        remote(out_ref, out_full.at[span(shard * rows, rows)], 4 * count + 1, beside),
    ]
    for side in range(2):
        direct.append(
            remote(
                gate_up_ref.at[:, span(side * ff + beside["shard"] * part, part)],
                gate_up_part.at[span(shard * rows, rows), pl.ds(side * part, part)],
                4 * count + 2 + side,
                beside,
            )
        )

    barrier = pltpu.get_barrier_semaphore()
    for device in (beside, across, diagonal, partner):
        pl.semaphore_signal(barrier, inc=1, device_id=device, device_id_type=MESH)
    pl.semaphore_wait(barrier, 4)

    started = []

    def start(copy):
        copy.start()
        started.append(copy)

    ahead = 4
    for copy in over[:ahead]:
        start(copy)
    for copy in direct:
        start(copy)
    for load, store in zip(loads, stores):
        load.wait()
        store.start()
    first, load_out, second = attend_parts(
        state_ref, gain_one_ref, gain_two_ref, cos_ref, sin_ref, allowed_ref, qkv_full, out_full,
        middle_ref, normed_two_ref, rotated_ref, lefts_ref,
        qkv_work, out_work, normed_ref, attended_ref, work_sems,
    )
    qkv_last = half // 64 - 1
    out_last = qkv_last + half // 64
    arrived = [0]

    def wait_relays(last):
        for at in range(arrived[0], last + 1):
            for copies in relays:
                copies[at].wait_recv()
        arrived[0] = last + 1

    def work(parts):
        @pl.when(lax.axis_index("section") == 0)
        def _():
            for part in parts:
                part()

    ready = list(first)
    for at in range(count + 1):
        if at < count:
            over[at].wait_recv()
            start(passed[at])
            if relays[0][at] is not None:
                start(relays[0][at])
            if at + ahead < count:
                over[at].wait_send()
                started[:] = [copy for copy in started if copy is not over[at]]
                start(over[at + ahead])
        if at > 0:
            passed[at - 1].wait_recv()
            if relays[1][at - 1] is not None:
                start(relays[1][at - 1])
        if at == qkv_last + 2:
            wait_relays(qkv_last)
            direct[0].wait_recv()
            stores[0].wait()
        if at == out_last + 2:
            wait_relays(out_last)
            direct[1].wait_recv()
            stores[1].wait()
            work([load_out])
            ready += second
        if at >= qkv_last + 2:
            work(ready[:2])
            ready = ready[2:]
    work(ready)
    for copy in direct[2:]:
        copy.wait_recv()
    for copy in stores[2:]:
        copy.wait()
    for copy in started:
        copy.wait_send()


def call_weights(qkv_weight, out_weight, gate_up_weight, operands, collective):
    shards = lax.axis_size("shard")
    rows = qkv_weight.shape[0]
    count = 2 * (rows // 128) + 4 * (rows // 128)
    out_shape, scratch = attend_shapes(*operands[0].shape, qkv_weight.shape[1])
    vmem = pl.BlockSpec(memory_space=pltpu.VMEM)
    anywhere = pl.BlockSpec(memory_space=pl.ANY)
    return pl.pallas_call(
        weights_kernel,
        out_shape=[
            jax.ShapeDtypeStruct((shards * rows, qkv_weight.shape[1]), BF),
            jax.ShapeDtypeStruct((shards * rows, out_weight.shape[1]), BF),
            jax.ShapeDtypeStruct((shards * rows, gate_up_weight.shape[1] // shards), BF),
        ] + out_shape,
        in_specs=[anywhere] * 3 + [vmem] * len(operands),
        out_specs=[anywhere] * 3 + [vmem] * len(out_shape),
        scratch_shapes=[
            pltpu.VMEM(qkv_weight.shape, BF),
            pltpu.VMEM(out_weight.shape, BF),
            pltpu.VMEM((2, rows, gate_up_weight.shape[1] // (2 * shards)), BF),
            *scratch,
            pltpu.SemaphoreType.DMA((8,)),
            pltpu.SemaphoreType.DMA((4 * count + 4,)),
            pltpu.SemaphoreType.DMA((4 * count + 4,)),
        ],
        compiler_params=pltpu.CompilerParams(
            collective_id=collective, has_side_effects=True, vmem_limit_bytes=VMEM_LIMIT
        ),
        name="weights",
    )(qkv_weight, out_weight, gate_up_weight, *operands)


def repeat(first, last, body):
    def step(at, carry):
        body(at)
        return carry

    if first < last:
        lax.fori_loop(first, last, step, 0)


def by_chunk(count, body):
    repeat(0, count, lambda at: body(pl.ds(pl.multiple_of(at * CHUNK, CHUNK), CHUNK)))


def weight_grads_kernel(sections, left_rows_ref, hidden_ref, *refs):
    sources = [refs[at * sections : (at + 1) * sections] for at in range(7)]
    (early_hbm, gate_up_hbm, down_hbm,
     gate_up_grad_ref, down_grad_ref, qkv_grad_ref, out_grad_ref, gain_sum_ref, gathered_hbm, even_hbm,
     projected_ref, upstream_ref, gains_ref, gains_land_ref, gain_part_ref, gains_last_ref, lefts_ref, left_ref,
     extra_ref, terms_ref, chain_ref, down_ref, block_ref, gate_up_ref, mid_ref, sum_ref, stage_ref,
     start_sems, load_sems, block_sems, keep_sem, send_sems, recv_sems) = refs[7 * sections :]
    shard, beside, across, diagonal = slice_peers()
    peers = (across, diagonal, beside)
    replica, replicas = lax.axis_index("replica"), lax.axis_size("replica")
    early = lax.axis_index("section") == lax.axis_size("section") - 1
    late = lax.axis_index("section") < lax.axis_size("section") - 1
    here = [lax.axis_index("section") == section for section in range(sections)]
    rows, cols = projected_ref.shape
    every, width = sources[5][0].shape
    pieces, all_pieces = cols // CHUNK, (cols + width) // CHUNK
    staged = stage_ref.shape[2] // CHUNK
    kinds, groups, _, sub_rows, _ = lefts_ref.shape
    part = down_ref.shape[0]
    half_part = part // 2
    ff = gate_up_grad_ref.shape[1] // 2
    steps = half_part // CHUNK
    wide = width // CHUNK
    out_rows = gate_up_grad_ref.shape[0]
    piece_base = 3 * replicas
    spread_base = piece_base + 3 * pieces
    gain_base = spread_base + replicas
    left_base = gain_base + replicas
    chain_base = left_base + kinds * groups * 3
    last_base = chain_base + 4 * replicas
    grad_base = last_base + 3

    def remote(source, target, at, device):
        return pltpu.make_async_remote_copy(
            source, target, send_sems.at[at], recv_sems.at[at], device_id={"shard": device}, device_id_type=MESH
        )

    def owned(owner):
        return pl.ds(pl.multiple_of(owner * rows, rows), rows)

    def piece_place(piece, place=None):
        if piece < 2 * staged:
            place = pl.ds(0, every) if place is None else place
            return stage_ref.at[piece // staged, place, pl.ds(piece % staged * CHUNK, CHUNK)]
        return extra_ref.at[piece - 2 * staged] if place is None else extra_ref.at[piece - 2 * staged, place]

    def piece_copy(owner, piece, kind, device):
        place = piece_place(piece, owned(owner))
        return remote(place, place, piece_base + kind * pieces + piece, device)

    over = [piece_copy(shard, piece, 0, across) for piece in range(pieces)]
    direct = [piece_copy(shard, piece, 1, beside) for piece in range(pieces)]
    relays = [piece_copy(across, piece, 2, beside) for piece in range(pieces)]

    def hand_left(kind, group, peer):
        return remote(
            lefts_ref.at[kind, group, peers[peer]], left_ref.at[kind, group, :, owned(shard)],
            left_base + (kind * groups + group) * 3 + peer, peers[peer],
        )

    lefts = [(kind, group, peer) for kind in reversed(range(kinds)) for group in range(groups) for peer in range(3)]
    loads = []
    for at, target in enumerate((lefts_ref, projected_ref, gains_ref, upstream_ref)):
        loads.append([pltpu.make_async_copy(source, target, start_sems.at[at]) for source in sources[at]])
    load_branch = [
        [
            pltpu.make_async_copy(source.at[piece - pieces], piece_place(piece), start_sems.at[4 + piece - pieces])
            for source in sources[4]
        ]
        for piece in range(pieces, all_pieces)
    ]
    load_own = [pltpu.make_async_copy(source, block_ref.at[0], load_sems.at[2, 0]) for source in sources[5]]
    load_down = pltpu.make_async_copy(down_hbm, down_ref, load_sems.at[3, 0])

    def block_at(turn):
        return lax.rem(replica + turn, replicas)

    def tokens(turn):
        return pl.ds(pl.multiple_of(block_at(turn) * every, every), every)

    def load_gate_up(half, turn, side):
        place = pl.ds(side * part + half * half_part, half_part)
        slot = lax.rem(turn, 2)
        return pltpu.make_async_copy(
            gate_up_hbm.at[tokens(turn), place], gate_up_ref.at[slot, side], load_sems.at[side, slot]
        )

    def block_copies(turn, source):
        slot = lax.rem(turn, 2)
        copies = []
        for at, owner in enumerate(peers + (shard,)):
            if source is early_hbm:
                own = early_hbm.at[turn, owned(owner)]
            else:
                own = gathered_hbm.at[turn, owned(owner)] if source is None or at < 3 else source.at[block_at(turn)]
            copies.append(pltpu.make_async_copy(own, block_ref.at[slot, owned(owner)], block_sems.at[slot, at]))
        return copies

    def own_cases(turn):
        cases = [(late & (turn > 0) & (turn % 2 == 0), even_hbm), (early & (turn > 1), sources[6][-1])]
        for section in range(sections - 1):
            cases.append((here[section] & (turn % 2 == 1), sources[6][section]))
        return cases

    def load_block(turn):
        @pl.when(early & (turn == 1))
        def _():
            for copy in block_copies(turn, early_hbm):
                copy.start()

        @pl.when(late | (turn != 1))
        def _():
            for copy in block_copies(turn, None)[:3]:
                copy.start()

        cases = [(turn == 0, None)] + own_cases(turn)
        for case, source in cases:

            @pl.when(case)
            def _(source=source):
                block_copies(turn, source)[3].start()

    def wait_block(turn):
        for copy in block_copies(turn, None):
            copy.wait()

    def landing(turn, owner):
        return gathered_hbm.at[turn, owned(owner)]

    def block_over(turn, source):
        return remote(source.at[block_at(turn)], landing(turn, shard), 3 * turn, across)

    def block_direct(turn, source):
        return remote(source.at[block_at(turn)], landing(turn, shard), 3 * turn + 1, beside)

    def block_relay(turn):
        return remote(landing(turn, across), landing(turn, across), 3 * turn + 2, beside)

    def send_block(turn):
        cases = own_cases(turn)
        for case, source in cases:

            @pl.when(case)
            def _(source=source):
                block_over(turn, source).start()
                block_direct(turn, source).start()

    def chain_slot(block, at):
        return replicas - (replicas - block) * ((at - block + replicas - 1) // replicas)

    spans = ((cols, width), (0, cols))

    def chain_at(phase, slot):
        return chain_ref.at[slot, :, pl.ds(*spans[phase])]

    def chain_up(phase, block):
        at = chain_base + phase * 2 * replicas + block
        return pltpu.make_async_remote_copy(
            chain_at(phase, block), chain_at(phase, block), send_sems.at[at], recv_sems.at[at],
            device_id={"replica": replica + 1}, device_id_type=MESH,
        )

    def chain_down(phase, block):
        at = chain_base + phase * 2 * replicas + replicas + block
        return pltpu.make_async_remote_copy(
            chain_at(phase, block), chain_at(phase, chain_slot(block, replica - 1)), send_sems.at[at], recv_sems.at[at],
            device_id={"replica": replica - 1}, device_id_type=MESH,
        )

    def chain_chunks(phase, body):
        first, count = spans[phase]
        repeat(first // CHUNK, (first + count) // CHUNK, lambda at: body(pl.ds(pl.multiple_of(at * CHUNK, CHUNK), CHUNK)))

    def add_terms(phase, block):
        def add(place):
            total = chain_ref[block, :, place].astype(F32) + terms_ref[block, :, place].astype(F32)
            chain_ref[block, :, place] = total.astype(BF)

        chain_chunks(phase, add)

    def chain_begin(phase):
        def take_terms(block):
            def take(place):
                chain_ref[block, :, place] = terms_ref[block, :, place]

            chain_chunks(phase, take)

        for block in reversed(range(1, replicas)):

            @pl.when(replica == 0)
            def _(block=block):
                take_terms(block)
                chain_up(phase, block).start()

        for block in range(replicas - 1):

            @pl.when(replica == replicas - 1)
            def _(block=block):
                take_terms(block)
                chain_down(phase, block).start()

    def chain_step(phase, step):
        high = replicas - 1 - step + replica

        @pl.when((replica > 0) & (step >= replica))
        def _():
            chain_up(phase, high).wait_recv()

            @pl.when(step < replicas - 1)
            def _():
                add_terms(phase, high)
                chain_up(phase, high).start()

        low = step - (replicas - 1 - replica)

        @pl.when((replica < replicas - 1) & (step >= replicas - 1 - replica))
        def _():
            chain_down(phase, low).wait_recv()

            @pl.when(step < replicas - 1)
            def _():
                add_terms(phase, low)
                chain_down(phase, low).start()

    def gain_copy(peer):
        return remote(gain_part_ref, gains_last_ref.at[shard], last_base + peer, peers[peer])

    def send_grad(half, at, peer):
        device = peers[peer]
        place = pl.ds(pl.multiple_of(at * CHUNK, CHUNK), CHUNK)
        target = pl.ds(
            pl.multiple_of(
                (at // steps) * ff + shard * part + half * half_part + (at % steps) * CHUNK, CHUNK
            ),
            CHUNK,
        )
        return remote(
            stage_ref.at[half, pl.ds(pl.multiple_of(device * out_rows, out_rows), out_rows), place],
            gate_up_grad_ref.at[:, target],
            grad_base + (half * 2 * steps + at) * 3 + peer,
            device,
        )

    def clear_sum():
        def clear(place):
            sum_ref[:, place] = jnp.zeros((sum_ref.shape[0], CHUNK), F32)

        by_chunk(2 * steps, clear)

    def compute(half, turn):
        slot = lax.rem(turn, 2)
        later = lax.rem(turn + 1, replicas)
        for side in range(2):
            load_gate_up(half, turn, side).wait()

        @pl.when(turn + 1 < replicas)
        def _():
            for side in range(2):
                load_gate_up(half, later, side).start()
            if half:
                load_block(later)

        def products(at, inner):
            place = pl.ds(pl.multiple_of(at * CHUNK, CHUNK), CHUNK)
            high = pl.ds(pl.multiple_of(half_part + at * CHUNK, CHUNK), CHUNK)
            down_rows = pl.ds(pl.multiple_of(half * half_part + at * CHUNK, CHUNK), CHUNK)
            grad_hidden = dot_rows(block_ref[slot], down_ref[down_rows, :])
            gate = gate_up_ref[slot, 0, :, place].astype(F32)
            up = gate_up_ref[slot, 1, :, place].astype(F32)
            sigmoid = jax.nn.sigmoid(gate)
            mid_ref[:, place] = (grad_hidden * up * sigmoid * (1.0 + gate * (1.0 - sigmoid))).astype(BF)
            mid_ref[:, high] = (grad_hidden * gate * sigmoid).astype(BF)
            return inner

        lax.fori_loop(0, steps, products, 0)

        def sums(at, inner):
            place = pl.ds(pl.multiple_of(at * CHUNK, CHUNK), CHUNK)
            total = sum_ref[:, place] + dot(left_rows_ref[:, tokens(turn)], mid_ref[:, place])

            @pl.when(turn < replicas - 1)
            def _():
                sum_ref[:, place] = total

            @pl.when(turn == replicas - 1)
            def _():
                stage_ref[half, pl.ds(0, total.shape[0]), place] = total.astype(BF)
                for peer in range(3):
                    send_grad(half, at, peer).start()

            return inner

        lax.fori_loop(0, 2 * steps, sums, 0)

    def first_pass(turn, carry):
        @pl.when(late | (turn != 1))
        def _():
            block_over(turn, even_hbm).wait_recv()
            block_relay(turn).start()
            block_direct(turn, even_hbm).wait_recv()
            block_relay(turn).wait_recv()

        load_block(turn)

        @pl.when(turn + 2 < replicas)
        def _():
            send_block(turn + 2)

        wait_block(turn)
        compute(0, turn)
        return carry

    def second_pass(turn, carry):
        compute(1, turn)

        @pl.when(turn + 1 < replicas)
        def _():
            wait_block(lax.rem(turn + 1, replicas))

        return carry

    for copies in loads + load_branch + [load_own]:
        start_own(copies)
    load_down.start()
    for side in range(2):
        load_gate_up(0, 0, side).start()

    barrier = pltpu.get_barrier_semaphore()
    for device in peers:
        pl.semaphore_signal(barrier, inc=1, device_id={"shard": device}, device_id_type=MESH)
    for turn in range(1, replicas):
        target = lax.rem(replica + turn, replicas)
        pl.semaphore_signal(barrier, inc=1, device_id={"replica": target}, device_id_type=MESH)
    pl.semaphore_wait(barrier, 2 + replicas)

    spread_copies = [
        replica_copy(upstream_ref, even_hbm.at[replica], turn, send_sems, recv_sems, spread_base)
        for turn in range(2, replicas, 2)
    ]
    gain_copies = [
        replica_copy(gains_ref, gains_land_ref.at[replica], turn, send_sems, recv_sems, gain_base)
        for turn in range(1, replicas)
    ]
    loads[0][0].wait()
    for place in lefts:
        hand_left(*place).start()
    loads[1][0].wait()
    for piece in range(pieces):
        piece_place(piece, owned(shard))[...] = projected_ref[:, piece * CHUNK : (piece + 1) * CHUNK]
        over[piece].start()
        direct[piece].start()
    loads[2][0].wait()
    gains_land_ref[replica] = gains_ref[...]
    loads[3][0].wait()
    for copy in gain_copies:
        copy.start()

    @pl.when(late)
    def _():
        for copy in spread_copies:
            copy.start()

    for kind in range(kinds):
        for group in range(groups):
            left_ref[kind, group, :, owned(shard)] = lefts_ref[kind, group, shard]
    load_own[0].wait()
    keep_own = pltpu.make_async_copy(block_ref.at[0], gathered_hbm.at[0], keep_sem)
    keep_own.start()
    clear_sum()

    def product(piece, kind, source):
        left = jnp.concatenate([left_ref[kind, group] for group in range(groups)], 0)
        total = dot(left, source).astype(BF)
        place = pl.ds(pl.multiple_of(piece * CHUNK, CHUNK), CHUNK)
        for group in range(groups):
            terms_ref[group, :, place] = total[group * sub_rows : (group + 1) * sub_rows]

    def staged_product(piece, kind):
        place = pl.ds(pl.multiple_of(piece % staged * CHUNK, CHUNK), CHUNK)
        product(piece, kind, stage_ref[piece // staged, pl.ds(0, every), place])

    for place in lefts[: len(lefts) // kinds]:
        hand_left(*place).wait_recv()
    for copies in load_branch:
        copies[0].wait()
    repeat(pieces, min(all_pieces, 2 * staged), lambda piece: staged_product(piece, 1))
    repeat(2 * staged, all_pieces, lambda piece: product(piece, 1, extra_ref[piece - 2 * staged]))
    chain_begin(0)
    load_down.wait()
    compute(0, 0)
    keep_own.wait()
    if replicas > 2:

        @pl.when(early)
        def _():
            load_block(1)
            wait_block(1)
            compute(0, 1)

    for place in lefts[len(lefts) // kinds :]:
        hand_left(*place).wait_recv()
    for piece in range(pieces):
        over[piece].wait_recv()
        relays[piece].start()
        if piece == pieces // 2:
            chain_step(0, 1)
    for copy in over:
        copy.wait_send()

    @pl.when(late)
    def _():
        for copy in spread_copies:
            copy.wait()

    for turn in range(1, min(3, replicas)):
        send_block(turn)
    for copy in direct + relays:
        copy.wait()
    repeat(0, pieces, lambda piece: staged_product(piece, 0))
    chain_begin(1)
    if replicas > 2:
        chain_step(0, 2)
    for copy in gain_copies:
        copy.wait()
    gain_part_ref[...] = jnp.sum(gains_land_ref[...], 0)
    gains_last_ref[shard] = gain_part_ref[...]
    for peer in range(3):
        gain_copy(peer).start()
    if replicas > 2:

        @pl.when(late)
        def _():
            first_pass(1, 0)

        if replicas > 3:

            @pl.when(early)
            def _():
                send_block(3)

    lax.fori_loop(2, replicas, first_pass, 0)
    for side in range(2):
        load_gate_up(1, 0, side).start()
    load_block(0)
    clear_sum()
    for step in range(3, replicas):
        chain_step(0, step)
    chain_step(1, 1)
    wait_block(0)
    lax.fori_loop(0, 2, second_pass, 0)
    if replicas > 2:
        chain_step(1, 2)
    lax.fori_loop(2, replicas, second_pass, 0)
    load_block(0)
    wait_block(0)

    def clear_down(place):
        down_grad_ref[:, place] = jnp.zeros((down_grad_ref.shape[0], CHUNK), F32)

    by_chunk(wide, clear_down)

    def down_pass(turn, carry):
        slot = lax.rem(turn, 2)
        later = lax.rem(turn + 1, replicas)

        @pl.when(turn + 1 < replicas)
        def _():
            load_block(later)

        def down_sums(at, inner):
            place = pl.ds(pl.multiple_of(at * CHUNK, CHUNK), CHUNK)
            down_grad_ref[:, place] += dot(hidden_ref[:, tokens(turn)], block_ref[slot, :, place])
            return inner

        lax.fori_loop(0, wide, down_sums, 0)

        @pl.when(turn + 1 < replicas)
        def _():
            wait_block(later)

        return carry

    lax.fori_loop(0, replicas, down_pass, 0)
    for peer in range(3):
        gain_copy(peer).wait()
    gain_sum_ref[...] = jnp.sum(gains_last_ref[...], 0)
    own = pl.ds(pl.multiple_of(shard * out_rows, out_rows), out_rows)
    for half in range(2):

        def store_own(at, carry, half=half):
            place = pl.ds(pl.multiple_of(at * CHUNK, CHUNK), CHUNK)
            target = pl.ds(
                pl.multiple_of(
                    (at // steps) * ff + shard * part + half * half_part + (at % steps) * CHUNK, CHUNK
                ),
                CHUNK,
            )
            gate_up_grad_ref[:, target] = stage_ref[half, own, place]
            return carry

        lax.fori_loop(0, 2 * steps, store_own, 0)
    for step in range(3, replicas):
        chain_step(1, step)

    def sum_up(grad_ref, first):
        def add(place):
            source = pl.ds(pl.multiple_of(first + place.start, CHUNK), CHUNK)
            grad_ref[:, place] = terms_ref[replica, :, source].astype(F32)

            @pl.when(replica > 0)
            def _():
                grad_ref[:, place] += chain_ref[replica, :, source].astype(F32)

            @pl.when(replica < replicas - 1)
            def _():
                grad_ref[:, place] += chain_ref[replicas, :, source].astype(F32)

        by_chunk(grad_ref.shape[1] // CHUNK, add)

    sum_up(qkv_grad_ref, 0)
    sum_up(out_grad_ref, cols)
    for half in range(2):

        def finish(at, carry, half=half):
            for peer in range(3):
                send_grad(half, at, peer).wait()
            return carry

        lax.fori_loop(0, 2 * steps, finish, 0)
    for place in lefts:
        hand_left(*place).wait_send()
    for turn in range(1, replicas):

        @pl.when(late | (turn != 1))
        def _(turn=turn):
            block_over(turn, even_hbm).wait_send()
            block_direct(turn, even_hbm).wait_send()
            block_relay(turn).wait_send()


    for phase in range(2):
        for block in range(1, replicas):

            @pl.when(replica < block)
            def _(phase=phase, block=block):
                chain_up(phase, block).wait_send()

        for block in range(replicas - 1):

            @pl.when(replica > block)
            def _(phase=phase, block=block):
                chain_down(phase, block).wait_send()


def call_weight_grads(left_rows, hidden, lefts, projected, gains, upstream, branch, slices, odd, early, gate_up, down,
                      collective):
    replicas, shards, sections = lax.axis_size("replica"), lax.axis_size("shard"), len(projected)
    rows, cols = projected[0].shape
    every, width = slices[0].shape
    part = down.shape[0]
    slice_rows = left_rows.shape[0]
    sub_rows = slice_rows // shards
    lefts = [values.reshape(2, replicas, shards, sub_rows, rows) for values in lefts]
    pieces, all_pieces = cols // CHUNK, (cols + width) // CHUNK
    copies = 3 * replicas + 3 * pieces + 2 * replicas + 6 * replicas + 4 * replicas + 3 + 3 * 2 * (part // CHUNK)
    vmem, anywhere = pl.BlockSpec(memory_space=pltpu.VMEM), pl.BlockSpec(memory_space=pl.ANY)
    gain_shape = gains[0].shape
    return pl.pallas_call(
        functools.partial(weight_grads_kernel, sections),
        out_shape=[
            jax.ShapeDtypeStruct((sub_rows, 2 * part * shards), BF),
            jax.ShapeDtypeStruct((hidden.shape[0], width), F32),
            jax.ShapeDtypeStruct((sub_rows, cols), F32),
            jax.ShapeDtypeStruct((sub_rows, width), F32),
            jax.ShapeDtypeStruct(gain_shape, F32),
            jax.ShapeDtypeStruct((replicas, every, width), BF),
            jax.ShapeDtypeStruct((replicas, rows, width), BF),
        ],
        in_specs=[vmem] * 2 + [anywhere] * (7 * sections + 3),
        out_specs=[vmem] * 5 + [anywhere] * 2,
        scratch_shapes=[
            pltpu.VMEM((rows, cols), BF),
            pltpu.VMEM((rows, width), BF),
            pltpu.VMEM(gain_shape, F32),
            pltpu.VMEM((replicas,) + gain_shape, F32),
            pltpu.VMEM(gain_shape, F32),
            pltpu.VMEM((shards,) + gain_shape, F32),
            pltpu.VMEM(lefts[0].shape, BF),
            pltpu.VMEM((2, replicas, sub_rows, every), BF),
            pltpu.VMEM((max(1, all_pieces - 2 * (part // CHUNK)), every, CHUNK), BF),
            pltpu.VMEM((replicas, sub_rows, cols + width), BF),
            pltpu.VMEM((replicas + 1, sub_rows, cols + width), BF),
            pltpu.VMEM(down.shape, BF),
            pltpu.VMEM((2, every, width), BF),
            pltpu.VMEM((2, 2, every, part // 2), BF),
            pltpu.VMEM((every, part), BF),
            pltpu.VMEM((slice_rows, part), F32),
            pltpu.VMEM((2, max(slice_rows, every), part), BF),
            pltpu.SemaphoreType.DMA((4 + all_pieces - pieces,)),
            pltpu.SemaphoreType.DMA((4, 2)),
            pltpu.SemaphoreType.DMA((2, 4)),
            pltpu.SemaphoreType.DMA,
            pltpu.SemaphoreType.DMA((copies,)),
            pltpu.SemaphoreType.DMA((copies,)),
        ],
        compiler_params=pltpu.CompilerParams(
            collective_id=collective, has_side_effects=True, vmem_limit_bytes=VMEM_LIMIT
        ),
        name="weight_grads",
    )(left_rows, hidden, *lefts, *projected, *gains, *upstream, *branch, *slices, *odd, early, gate_up, down)


def turn_order(replicas):
    return [0] + list(range(1, replicas, 2)) + list(range(2, replicas, 2))


def prepare_kernel(sections, gate_up_hbm, ahead_hbm, *refs):
    slices, normed_two, odd = [refs[at * sections : (at + 1) * sections] for at in range(3)]
    (gathered_hbm, gate_up_all_hbm, hidden_hbm, left_rows_ref,
     normed_two_ref, weight_ref, block_ref, gate_up_ref, hidden_ref, turned_ref,
     load_sems, store_sems, block_sems, start_sems, send_sems, recv_sems) = refs[3 * sections :]
    shard, beside, across, diagonal = slice_peers()
    peers = (across, diagonal, beside)
    replica, replicas = lax.axis_index("replica"), lax.axis_size("replica")
    shards = lax.axis_size("shard")
    rows, width = normed_two_ref.shape
    every = rows * shards
    part = hidden_ref.shape[1]
    ff_rows = hidden_hbm.shape[0]
    steps = part // CHUNK
    slice_rows = left_rows_ref.shape[0]
    owner = (replica * shards) // replicas
    first_col = lax.rem(replica * shards, replicas) * ff_rows

    def load_weight(side, at):
        place = (slice(None), pl.ds(pl.multiple_of(side * part + at * CHUNK, CHUNK), CHUNK))
        return pltpu.make_async_copy(gate_up_hbm.at[place], weight_ref.at[place], load_sems.at[side, at])

    for at in range(steps):
        for side in range(2):
            load_weight(side, at).start()

    def remote(source, target, at, device):
        return pltpu.make_async_remote_copy(
            source, target, send_sems.at[at], recv_sems.at[at], device_id={"shard": device}, device_id_type=MESH
        )

    def landing(turn, who):
        return gathered_hbm.at[turn, pl.ds(pl.multiple_of(who * rows, rows), rows)]

    behind = lax.axis_index("section") < sections - 1

    def fetched(turn, body):
        if turn == 1:
            pl.when(behind)(body)
        else:
            body()

    def own_sources(turn):
        if turn % 2:
            return [source.at[lax.rem(replica + turn, replicas)] for source in odd]
        return [landing(turn, shard)]

    def over(turn, source=None):
        return remote(landing(turn, shard) if source is None else source, landing(turn, shard), 3 * turn, across)

    def direct(turn, source=None):
        return remote(landing(turn, shard) if source is None else source, landing(turn, shard), 3 * turn + 1, beside)

    def send_block(turn):
        if turn % 2 == 0:
            from_replica(turn).wait_recv()
        copies = [(over(turn, source), direct(turn, source)) for source in own_sources(turn)]
        for section, pair in enumerate(copies):
            if turn == 1 and section == sections - 1:
                continue
            if len(copies) == 1:
                for copy in pair:
                    copy.start()
            else:

                @pl.when(lax.axis_index("section") == section)
                def _(pair=pair):
                    for copy in pair:
                        copy.start()

    def relay(turn):
        return remote(landing(turn, across), landing(turn, across), 3 * turn + 2, beside)

    def from_replica(turn):
        return replica_copy(normed_two_ref, landing(turn, shard), turn, send_sems, recv_sems, 3 * replicas)

    def tokens(turn):
        return pl.ds(pl.multiple_of(lax.rem(replica + turn, replicas) * every, every), every)

    def load_block(turn, slot):
        copies = []
        for at, owner in enumerate(peers + (shard,)):
            sources = own_sources(turn) if at == 3 else [landing(turn, owner)]
            if turn == 1 and at < 3:
                rows_at = ahead_hbm.at[pl.ds(pl.multiple_of(owner * rows, rows), rows)]
                sources = sources * (sections - 1) + [rows_at]
            place = block_ref.at[slot, pl.ds(pl.multiple_of(owner * rows, rows), rows)]
            copies.append([pltpu.make_async_copy(source, place, block_sems.at[slot, at]) for source in sources])
        return copies

    def start_block(turn, slot):
        for copies in load_block(turn, slot):
            if len(copies) == 1:
                copies[0].start()
            else:
                start_own(copies)

    def store_block(turn, slot):
        return pltpu.make_async_copy(gate_up_ref.at[slot], gate_up_all_hbm.at[tokens(turn)], store_sems.at[1, slot])

    def hand_hidden(turn, slot, peer):
        device = peers[peer]
        return remote(
            turned_ref.at[slot, device], hidden_hbm.at[:, tokens(turn)], 4 * replicas + 3 * turn + peer, device
        )

    def keep_hidden(turn, slot):
        return pltpu.make_async_copy(
            turned_ref.at[slot, shard], hidden_hbm.at[:, tokens(turn)], store_sems.at[2, slot]
        )

    loads = [
        [pltpu.make_async_copy(source, target, sem) for source in sources]
        for sources, target, sem in (
            (normed_two, normed_two_ref, start_sems.at[0]),
            (slices, block_ref.at[0], store_sems.at[0, 0]),
        )
    ]
    for copies in loads:
        start_own(copies)
    slice_barrier(peers, range(2, replicas, 2))
    order = turn_order(replicas)
    loads[0][0].wait()
    evens = [turn for turn in order if turn and turn % 2 == 0]
    for turn in evens[:1]:
        from_replica(turn).start()
    for turn in order[1:3]:
        send_block(turn)

    for at, turn in enumerate(order):
        later = order[at + 1] if at + 1 < replicas else None
        slot = at % 2
        if at and at + 2 < replicas:
            send_block(order[at + 2])
            if order[at + 2] in evens:
                place = evens.index(order[at + 2]) + 1
                if place < len(evens):
                    from_replica(evens[place]).start()
        if at:
            for copies in load_block(turn, slot):
                copies[0].wait()
        else:
            loads[1][0].wait()
        if at > 1:
            store_block(order[at - 2], slot).wait()

        def products(step, carry, at=at, slot=slot):
            cols = pl.ds(pl.multiple_of(step * CHUNK, CHUNK), CHUNK)
            high = pl.ds(pl.multiple_of(part + step * CHUNK, CHUNK), CHUNK)
            if at == 0:
                load_weight(0, step).wait()
                load_weight(1, step).wait()
            gate = dot(block_ref[slot], weight_ref[:, cols])
            up = dot(block_ref[slot], weight_ref[:, high])
            gate_up_ref[slot, :, cols] = gate.astype(BF)
            gate_up_ref[slot, :, high] = up.astype(BF)
            hidden_ref[:, cols] = (gate * jax.nn.sigmoid(gate) * up).astype(BF)
            return carry

        lax.fori_loop(0, steps, products, 0)
        store_block(turn, slot).start()
        if later is not None:

            def pass_on(later=later):
                over(later).wait_recv()
                relay(later).start()

            fetched(later, pass_on)

        @pl.when(shard == owner)
        def _(at=at, turn=turn, slot=slot):
            if at > 1:
                keep_hidden(order[at - 2], slot).wait()
                for peer in range(3):
                    hand_hidden(order[at - 2], slot, peer).wait_send()

            def turn_over(device, carry):
                cols = pl.ds(pl.multiple_of(first_col + device * ff_rows, ff_rows), ff_rows)
                turned_ref[slot, device] = hidden_ref[:, cols].T
                return carry

            lax.fori_loop(0, shards, turn_over, 0)
            keep_hidden(turn, slot).start()
            for peer in range(3):
                hand_hidden(turn, slot, peer).start()

        slice_cols = pl.ds(pl.multiple_of(replica * slice_rows, slice_rows), slice_rows)
        left_rows_ref[:, tokens(turn)] = block_ref[slot, :, slice_cols].T
        if later is not None:

            def arrive(later=later):
                direct(later).wait_recv()
                relay(later).wait_recv()

            fetched(later, arrive)
            start_block(later, 1 - slot)

    for at in range(max(0, replicas - 2), replicas):
        store_block(order[at], at % 2).wait()

        @pl.when(shard == owner)
        def _(at=at):
            keep_hidden(order[at], at % 2).wait()
            for peer in range(3):
                hand_hidden(order[at], at % 2, peer).wait_send()

    for turn in range(replicas):
        for peer in range(3):

            @pl.when(peers[peer] == owner)
            def _(turn=turn, peer=peer):
                hand_hidden(turn, 0, peer).wait_recv()

        if turn:

            def leave(turn=turn):
                over(turn).wait_send()
                direct(turn).wait_send()
                relay(turn).wait_send()

            fetched(turn, leave)
        if turn in evens:
            from_replica(turn).wait_send()


def call_prepare(normed_two, gate_up_part, slices, odd, ahead, collective):
    rows, width = normed_two[0].shape
    shards, replicas = lax.axis_size("shard"), lax.axis_size("replica")
    part = gate_up_part.shape[1] // 2
    every = rows * shards
    slice_rows = width // replicas
    ff_rows = part // replicas
    vmem, anywhere = pl.BlockSpec(memory_space=pltpu.VMEM), pl.BlockSpec(memory_space=pl.ANY)
    copies = 7 * replicas
    outs = pl.pallas_call(
        functools.partial(prepare_kernel, len(slices)),
        out_shape=[
            jax.ShapeDtypeStruct((replicas, every, width), BF),
            jax.ShapeDtypeStruct((replicas * every, 2 * part), BF),
            jax.ShapeDtypeStruct((ff_rows, replicas * every), BF),
            jax.ShapeDtypeStruct((slice_rows, replicas * every), BF),
        ],
        in_specs=[anywhere] * (2 + 3 * len(slices)),
        out_specs=[anywhere] * 3 + [vmem],
        scratch_shapes=[
            pltpu.VMEM((rows, width), BF),
            pltpu.VMEM(gate_up_part.shape, BF),
            pltpu.VMEM((2, every, width), BF),
            pltpu.VMEM((2, every, 2 * part), BF),
            pltpu.VMEM((every, part), BF),
            pltpu.VMEM((2, shards, ff_rows, every), BF),
            pltpu.SemaphoreType.DMA((2, part // CHUNK)),
            pltpu.SemaphoreType.DMA((3, 2)),
            pltpu.SemaphoreType.DMA((2, 4)),
            pltpu.SemaphoreType.DMA((1,)),
            pltpu.SemaphoreType.DMA((copies,)),
            pltpu.SemaphoreType.DMA((copies,)),
        ],
        compiler_params=pltpu.CompilerParams(
            collective_id=collective, has_side_effects=True, vmem_limit_bytes=VMEM_LIMIT
        ),
        name="prepare",
    )(gate_up_part, ahead, *slices, *normed_two, *odd)
    return outs[1:]


def on_device(
    tokens_in,
    positions,
    attn_gain,
    qkv_weight,
    out_weight,
    mlp_gain,
    gate_up_weight,
    down_weight,
    cotangent,
):
    sections = lax.axis_size("section")
    rows, width = tokens_in.shape
    down_steps = [(at + 1, at) for at in range(sections - 1)]

    cosine, sine = rope_tables(positions)
    allowed = visible(positions)

    tables = (attn_gain, mlp_gain, cosine, sine, allowed)
    qkv_full, out_full, gate_up_part, *attend_first = call_weights(
        qkv_weight[0], out_weight[0], gate_up_weight[0], (tokens_in,) + tables, 3
    )
    down_part = down_weight[0]

    forward = []
    state = tokens_in
    early = None
    for section in range(sections):
        middle, normed_two, rotated, lefts = (
            call_attend_forward(section, state, *tables, qkv_full, out_full) if section else attend_first
        )
        block_out, normed_two_slice, gate_up, normed_two_odd, state_next, *gathered = call_feed(
            section, False, (normed_two, middle, gate_up_part, down_part), 8 + section,
            cotangent if section + 2 == sections else None,
        )
        early = gathered[0] if gathered else early
        forward.append((state, middle, rotated, gate_up, normed_two_slice, normed_two_odd, normed_two, lefts, block_out))
        state = state_next

    def pick(values):
        chosen = values[-1]
        for section in range(sections - 1):
            chosen = jnp.where(lax.axis_index("section") == section, values[section], chosen)
        return chosen

    slices, normed_two_odd, normed_two, lefts, block_out = list(zip(*forward))[4:]
    block_out = pick(block_out)
    backward = []
    upstream = cotangent
    for section in reversed(range(sections)):
        state, middle, rotated, gate_up = forward[section][:4]
        grad_normed_two, upstream_slice, odd, ahead = call_feed(
            section, True, (upstream, gate_up, normed_two_odd[section], down_part, gate_up_part), 8 + sections + section
        )
        grad_in, grad_low, grad_projected, gains, grad_branch = call_attend_backward(
            section, 8 + 2 * sections + section, grad_normed_two, upstream, middle, state, rotated,
            *tables, qkv_full, out_full,
        )
        backward.insert(0, (upstream, upstream_slice, odd, grad_in, grad_projected, gains, grad_branch))
        if section == sections - 1:
            normed_two, grad_low = lax.optimization_barrier((normed_two, grad_low))
        if section > 0:
            upstream = lax.ppermute(grad_low, "section", down_steps)
        if section == sections - 1:
            gate_up_all, hidden_rows, left_rows = call_prepare(
                normed_two, gate_up_part, slices, normed_two_odd, ahead, 6
            )
            upstream, gate_up_all, left_rows, hidden_rows = lax.optimization_barrier(
                (upstream, gate_up_all, left_rows, hidden_rows)
            )

    upstream, upstream_slice, odd, grad_in, grad_projected, gains, grad_branch = zip(*backward)
    grad_in = pick(grad_in)
    gate_up_grad, down_grad, qkv_grad, out_grad, gains, _, _ = call_weight_grads(
        left_rows, hidden_rows, lefts, grad_projected, gains, upstream, grad_branch, upstream_slice, odd,
        early, gate_up_all, down_part, 5,
    )
    gate_up_grad = gate_up_grad.astype(F32)
    return (
        block_out[None],
        grad_in[None],
        gains[0][None],
        qkv_grad[None],
        out_grad[None],
        gains[1][None],
        gate_up_grad[None],
        down_grad[None],
    )


def solution(mesh):
    both = ("replica", "shard")
    return jax.shard_map(
        on_device,
        mesh=mesh,
        in_specs=(
            P(both, None),
            P(both),
            P("section", None),
            P("section", "shard", None),
            P("section", "shard", None),
            P("section", None),
            P("section", "shard", None),
            P("section", "shard", None),
            P(both, None),
        ),
        out_specs=(
            P("section", both, None),
            P("section", both, None),
            P("section", None),
            P("section", both, None),
            P("section", both, None),
            P("section", None),
            P("section", both, None),
            P("section", both, None),
        ),
        check_vma=False,
    )
```

```python
import functools

import jax
import jax.numpy as jnp
from jax import lax
from jax.experimental import pallas as pl
from jax.experimental.pallas import tpu as pltpu
from jax.sharding import PartitionSpec as P

HEADS = 32
KV_HEADS = 8
HEAD = 64
SEQ = 64
EPSILON = 1e-05
ROPE_BASE = 500000.0
BF = jnp.bfloat16
F32 = jnp.float32
CONTRACT_LAST = (((1,), (1,)), ((), ()))
CONTRACT_FIRST = (((0,), (0,)), ((), ()))


MESH = pl.DeviceIdType.MESH
VMEM_LIMIT = 60 * 2**20
TILE = 128


def dot(left, right):
    return jnp.dot(left, right, preferred_element_type=F32)


def dot_rows(left, right):
    return lax.dot_general(left, right, CONTRACT_LAST, preferred_element_type=F32)


def dot_tokens(left, right):
    return lax.dot_general(left, right, CONTRACT_FIRST, preferred_element_type=F32)


def rope_tables(seq_pos):
    half_index = jnp.arange(HEAD // 2, dtype=F32)
    frequency = jnp.power(ROPE_BASE, -2.0 * half_index / HEAD)
    angles = seq_pos.astype(F32)[:, None] * frequency[None, :]
    cosine, sine = jnp.cos(angles), jnp.sin(angles)
    return (
        jnp.concatenate([cosine] * 4, 1),
        jnp.concatenate([-sine, sine, -sine, sine], 1),
    )


def visible(seq_pos):
    rows = seq_pos.shape[0]
    row_index = jnp.arange(rows)[:, None]
    col_index = jnp.arange(rows)[None, :]
    same = row_index // SEQ == col_index // SEQ
    seen = (col_index <= row_index) & (row_index - col_index <= seq_pos[:, None])
    return jnp.where(same & seen, 1.0, 0.0).astype(F32)


def lanes(rows):
    return lax.broadcasted_iota(jnp.int32, (rows, TILE), 1)


def swap_halves(tile, lane):
    return jnp.where(lane % HEAD < HEAD // 2, pltpu.roll(tile, TILE - HEAD // 2, 1), pltpu.roll(tile, HEAD // 2, 1))


def spread(tile, odd, lane):
    turned = pltpu.roll(tile, HEAD, 1)
    lower, upper = (turned, tile) if odd else (tile, turned)
    return jnp.concatenate(
        [jnp.where(lane < HEAD, lower, 0.0), jnp.where(lane < HEAD, 0.0, upper)], 0
    ).astype(BF)


def softmax_pair(queries, spread_keys, allowed):
    scores = dot_rows(queries, spread_keys) * HEAD ** (-0.5)
    halves = []
    for side in range(2):
        masked = jnp.where(allowed > 0.5, scores[:, side * TILE : (side + 1) * TILE], -1e30)
        expon = jnp.exp(masked - jnp.max(masked, -1, keepdims=True))
        halves.append(expon / jnp.sum(expon, -1, keepdims=True))
    return halves


def attend_parts(
    state_ref, gain_one_ref, gain_two_ref, cos_ref, sin_ref, allowed_ref, qkv_hbm, out_hbm,
    middle_ref, normed_two_ref, rotated_ref, lefts_ref,
    qkv_ref, out_ref, normed_ref, attended_ref, sems,
):
    rows, width = state_ref.shape
    cols = qkv_hbm.shape[1]
    step = 512
    rope_cols = (HEADS + KV_HEADS) * HEAD

    def qkv_copy(at):
        return pltpu.make_async_copy(qkv_hbm.at[:, pl.ds(at, step)], qkv_ref.at[:, pl.ds(at, step)], sems.at[at // step])

    def out_copy(at):
        return pltpu.make_async_copy(
            out_hbm.at[:, pl.ds(at, step)], out_ref.at[:, pl.ds(at, step)], sems.at[(cols + at) // step]
        )

    def begin():
        for at in range(0, cols, step):
            qkv_copy(at).start()
        state = state_ref[...].astype(F32)
        inverse = lax.rsqrt(jnp.mean(state * state, -1, keepdims=True) + EPSILON)
        normed_ref[...] = (state * inverse * gain_one_ref[...]).astype(BF)

    def project(at):
        qkv_copy(at).wait()
        lane = lanes(rows)
        projected = dot(normed_ref[...], qkv_ref[:, at : at + step])
        for tile_at in range(0, step, TILE):
            tile = projected[:, tile_at : tile_at + TILE]
            if at + tile_at < rope_cols:
                tile = tile * cos_ref[...] + swap_halves(tile, lane) * sin_ref[...]
            rotated_ref[:, at + tile_at : at + tile_at + TILE] = tile.astype(BF)

    def attend(group):
        lane = lanes(rows)
        key_at = width + group // 2 * TILE
        value_at = rope_cols + group // 2 * TILE
        keys = spread(rotated_ref[:, key_at : key_at + TILE].astype(F32), group % 2, lane)
        values = spread(rotated_ref[:, value_at : value_at + TILE].astype(F32), group % 2, lane)
        for pair in range(2):
            at = (group * 2 + pair) * TILE
            halves = softmax_pair(rotated_ref[:, at : at + TILE], keys, allowed_ref[...])
            probs = jnp.concatenate([half.astype(BF) for half in halves], 1)
            attended_ref[:, at : at + TILE] = dot(probs, values).astype(BF)

    def load_out():
        for at in range(0, width, step):
            out_copy(at).start()

    def leave(at):
        out_copy(at).wait()
        middle = state_ref[:, at : at + step].astype(F32) + dot(attended_ref[...], out_ref[:, at : at + step])
        middle_ref[:, at : at + step] = middle

    def finish():
        middle = middle_ref[...]
        inverse = lax.rsqrt(jnp.mean(middle * middle, -1, keepdims=True) + EPSILON)
        normed_two_ref[...] = (middle * inverse * gain_two_ref[...]).astype(BF)
        lefts_ref[0] = normed_ref[...].T
        lefts_ref[1] = attended_ref[...].T

    first = [begin] + [functools.partial(project, at) for at in range(0, cols, step)]
    first += [functools.partial(attend, group) for group in range(KV_HEADS)]
    second = [functools.partial(leave, at) for at in range(0, width, step)] + [finish]
    return first, load_out, second


def attend_forward(*refs):
    first, load_out, second = attend_parts(*refs)
    first[0]()
    load_out()
    for part in first[1:] + second:
        part()


def attend_backward(
    rounds, grad_ref, upstream_ref, middle_ref, state_ref, rotated_ref,
    gain_one_ref, gain_two_ref, cos_ref, sin_ref, allowed_ref, qkv_hbm, out_hbm,
    grad_state_ref, grad_low_ref, grad_projected_ref, gain_terms_ref, branch_hbm,
    qkv_ref, out_ref, grad_branch_ref, grad_out_ref, middle_grad_ref, sems, keep_sems, send_sems, recv_sems,
):
    rows, width = middle_ref.shape
    cols = qkv_hbm.shape[1]
    step = 512
    steps = width // step
    out_copies = [
        pltpu.make_async_copy(out_hbm.at[pl.ds(at * step, step)], out_ref.at[pl.ds(at * step, step)], sems.at[at])
        for at in range(steps)
    ]
    copies = [
        pltpu.make_async_copy(
            qkv_hbm.at[pl.ds(at * step, step)], qkv_ref.at[pl.ds(at * step, step)], sems.at[steps + at]
        )
        for at in range(steps)
    ]
    for copy in out_copies + copies:
        copy.start()
    shard, beside, across, _ = slice_peers()
    slice_barrier((beside, across))

    def branch_rows(owner, at):
        return branch_hbm.at[at, pl.ds(pl.multiple_of(owner * rows, rows), rows)]

    def remote(source, owner, at, kind, device):
        return pltpu.make_async_remote_copy(
            source, branch_rows(owner, at), send_sems.at[kind, at], recv_sems.at[kind, at],
            device_id={"shard": device}, device_id_type=MESH,
        )

    branch = [grad_branch_ref.at[:, pl.ds(at * step, step)] for at in range(steps)]
    over = [remote(branch[at], shard, at, 0, across) for at in range(steps)]
    direct = [remote(branch[at], shard, at, 1, beside) for at in range(steps)]
    relays = [remote(branch_rows(across, at), across, at, 2, beside) for at in range(steps)]
    keeps = [pltpu.make_async_copy(branch[at], branch_rows(shard, at), keep_sems.at[at]) for at in range(steps)]

    def norm_back(grad, values, gain):
        inverse = lax.rsqrt(jnp.mean(values * values, -1, keepdims=True) + EPSILON)
        normal = values * inverse
        term = jnp.sum(grad * normal, 0, keepdims=True)
        scaled = grad * gain
        return inverse * (scaled - normal * jnp.mean(scaled * normal, -1, keepdims=True)), term

    upstream = upstream_ref[...].astype(F32)
    back, term = norm_back(grad_ref[...], middle_ref[...], gain_two_ref[...])
    gain_terms_ref[1:2, :] = term
    middle_grad_ref[...] = upstream + back
    grad_branch_ref[...] = middle_grad_ref[...].astype(BF)
    for copy in over + direct + keeps:
        copy.start()
    for at in range(steps):
        out_copies[at].wait()
        grad_out_ref[:, at * step : (at + 1) * step] = dot_rows(
            grad_branch_ref[...], out_ref[at * step : (at + 1) * step, :]
        ).astype(BF)
    lane = lanes(rows)
    cosine, sine, allowed = cos_ref[...], sin_ref[...], allowed_ref[...]
    rope_cols = (HEADS + KV_HEADS) * HEAD
    scale = HEAD ** (-0.5)

    def unrotate(tile):
        return tile * cosine - swap_halves(tile, lane) * sine

    def group_step(group_pair, carry):
        key_at = pl.multiple_of(width + group_pair * TILE, TILE)
        value_at = pl.multiple_of(rope_cols + group_pair * TILE, TILE)
        sums = []
        for odd in range(2):
            keys = spread(rotated_ref[:, pl.ds(key_at, TILE)].astype(F32), odd, lane)
            values = spread(rotated_ref[:, pl.ds(value_at, TILE)].astype(F32), odd, lane)
            key_sum = jnp.zeros((rows, TILE), F32)
            value_sum = jnp.zeros((rows, TILE), F32)
            for pair in range(2):
                at = pl.multiple_of(((group_pair * 2 + odd) * 2 + pair) * TILE, TILE)
                queries = rotated_ref[:, pl.ds(at, TILE)]
                grad_out = grad_out_ref[:, pl.ds(at, TILE)]
                halves = softmax_pair(queries, keys, allowed)
                grad_probs = dot_rows(grad_out, values)
                grad_halves = []
                for side in range(2):
                    grad = grad_probs[:, side * TILE : (side + 1) * TILE]
                    row_dot = jnp.sum(halves[side] * grad, -1, keepdims=True)
                    grad_halves.append((halves[side] * (grad - row_dot)).astype(BF))
                grad_scores = jnp.concatenate(grad_halves, 1)
                probs = jnp.concatenate([half.astype(BF) for half in halves], 1)
                grad_projected_ref[:, pl.ds(at, TILE)] = unrotate(dot(grad_scores, keys) * scale).astype(BF)
                key_terms = dot_tokens(grad_scores, queries)
                value_terms = dot_tokens(probs, grad_out)
                key_sum += jnp.where(lane < HEAD, key_terms[:rows], key_terms[rows:])
                value_sum += jnp.where(lane < HEAD, value_terms[:rows], value_terms[rows:])
            sums.append((key_sum + pltpu.roll(key_sum, HEAD, 1), value_sum + pltpu.roll(value_sum, HEAD, 1)))
        keys_grad = jnp.where(lane < HEAD, sums[0][0], sums[1][0]) * scale
        grad_projected_ref[:, pl.ds(key_at, TILE)] = unrotate(keys_grad).astype(BF)
        grad_projected_ref[:, pl.ds(value_at, TILE)] = jnp.where(
            lane < HEAD, sums[0][1], sums[1][1]
        ).astype(BF)
        return carry

    lax.fori_loop(0, KV_HEADS // 2, group_step, 0)
    for at in range(steps):
        over[at].wait_recv()
        relays[at].start()
    for at in range(steps):
        copies[at].wait()
        grad_state_ref[:, at * step : (at + 1) * step] = dot_rows(
            grad_projected_ref[...], qkv_ref[at * step : (at + 1) * step, :]
        )
    state = state_ref[...].astype(F32)
    back, term = norm_back(grad_state_ref[...], state, gain_one_ref[...])
    gain_terms_ref[0:1, :] = term
    grad_state = middle_grad_ref[...] + back
    grad_low = grad_state.astype(BF)
    grad_low_ref[...] = grad_low
    grad_state_ref[...] = grad_low.astype(F32) if rounds else grad_state
    for copy in direct + relays:
        copy.wait()
    for copy in over:
        copy.wait_send()
    for copy in keeps:
        copy.wait()


def gated(section, body):
    def kernel(*refs):
        @pl.when(lax.axis_index("section") == section)
        def _():
            body(*refs)

    return kernel


def attend_shapes(rows, width, cols):
    return [
        jax.ShapeDtypeStruct((rows, width), F32),
        jax.ShapeDtypeStruct((rows, width), BF),
        jax.ShapeDtypeStruct((rows, cols), BF),
        jax.ShapeDtypeStruct((2, width, rows), BF),
    ], [
        pltpu.VMEM((width, cols), BF),
        pltpu.VMEM((width, width), BF),
        pltpu.VMEM((rows, width), BF),
        pltpu.VMEM((rows, width), BF),
        pltpu.SemaphoreType.DMA(((cols + width) // 512,)),
    ]


def call_attend_forward(section, *operands):
    rows, width = operands[0].shape
    out_shape, scratch = attend_shapes(rows, width, operands[6].shape[1])
    specs = [pl.BlockSpec(memory_space=pltpu.VMEM)] * 6 + [pl.BlockSpec(memory_space=pl.ANY)] * 2
    return pl.pallas_call(
        gated(section, attend_forward),
        out_shape=out_shape,
        in_specs=specs,
        out_specs=[pl.BlockSpec(memory_space=pltpu.VMEM)] * 4,
        scratch_shapes=scratch,
        compiler_params=pltpu.CompilerParams(vmem_limit_bytes=VMEM_LIMIT),
        name="attend_forward",
    )(*operands)


def call_attend_backward(section, collective, *operands):
    rows, width = operands[2].shape
    cols = operands[10].shape[1]
    steps = width // 512
    every = lax.axis_size("shard") * rows
    vmem, anywhere = pl.BlockSpec(memory_space=pltpu.VMEM), pl.BlockSpec(memory_space=pl.ANY)
    return pl.pallas_call(
        gated(section, functools.partial(attend_backward, section > 0)),
        out_shape=(
            jax.ShapeDtypeStruct((rows, width), F32),
            jax.ShapeDtypeStruct((rows, width), BF),
            jax.ShapeDtypeStruct((rows, cols), BF),
            jax.ShapeDtypeStruct((2, width), F32),
            jax.ShapeDtypeStruct((steps, every, 512), BF),
        ),
        in_specs=[vmem] * 10 + [anywhere] * 2,
        out_specs=[vmem] * 4 + [anywhere],
        scratch_shapes=[
            pltpu.VMEM((width, cols), BF),
            pltpu.VMEM((width, width), BF),
            pltpu.VMEM((rows, width), BF),
            pltpu.VMEM((rows, width), BF),
            pltpu.VMEM((rows, width), F32),
            pltpu.SemaphoreType.DMA((2 * steps,)),
            pltpu.SemaphoreType.DMA((steps,)),
            pltpu.SemaphoreType.DMA((3, steps)),
            pltpu.SemaphoreType.DMA((3, steps)),
        ],
        compiler_params=pltpu.CompilerParams(
            collective_id=collective, has_side_effects=True, vmem_limit_bytes=VMEM_LIMIT
        ),
        name="attend_backward",
    )(*operands)


def start_own(copies):
    for section, copy in enumerate(copies):

        @pl.when(lax.axis_index("section") == section)
        def _(copy=copy):
            copy.start()


def slice_peers():
    shard = lax.axis_index("shard")
    chip, core = shard // 2, shard % 2
    return shard, chip * 2 + (1 - core), (1 - chip) * 2 + core, (1 - chip) * 2 + (1 - core)


def slice_barrier(devices, turns=(), more=0):
    barrier = pltpu.get_barrier_semaphore()
    replicas = lax.axis_size("replica")
    for device in devices:
        pl.semaphore_signal(barrier, inc=1, device_id={"shard": device}, device_id_type=MESH)
    for turn in turns:
        target = lax.rem(lax.axis_index("replica") + turn, replicas)
        pl.semaphore_signal(barrier, inc=1, device_id={"replica": target}, device_id_type=MESH)
    pl.semaphore_wait(barrier, len(devices) + len(turns) + more)


def replica_copy(source, target, turn, send_sems, recv_sems, base):
    replicas = lax.axis_size("replica")
    device = lax.rem(lax.axis_index("replica") + replicas - turn, replicas)
    return pltpu.make_async_remote_copy(
        source, target, send_sems.at[base + turn], recv_sems.at[base + turn],
        device_id={"replica": device}, device_id_type=MESH,
    )


CHUNK = 512


def feed_kernel(backward, rows, target, wide, *refs):
    if backward:
        (mine_ref, gate_up_hbm, odd_hbm, first_hbm, second_hbm, result_ref, all_hbm, others_hbm, ahead_hbm,
         mid_ref, all_ref, gate_up_ref, first_ref, second_ref, part_ref, take_ref, sent_ref, land_ref, own_ref,
         own_take_ref, load_sems, keep_sems, hold_sems, send_sems, recv_sems) = refs
    else:
        (mine_ref, middle_hbm, first_hbm, second_hbm, result_ref, all_hbm, gate_up_hbm, others_hbm, next_hbm,
         mid_ref, all_ref, gate_up_ref, first_ref, second_ref, part_ref, take_ref, sent_ref, land_ref, own_ref,
         own_take_ref, middle_ref, load_sems, keep_sems, hold_sems, send_sems, recv_sems) = refs
    shard, beside, across, _ = slice_peers()
    chip, core = shard // 2, shard % 2
    half = rows // 2
    parts, spans, _, piece, span_cols = part_ref.shape
    block = 2 * piece
    width = all_ref.shape[1]
    ff = first_ref.shape[0] if backward else second_ref.shape[0]
    first_steps = ff // CHUNK

    def load_first(at):
        if backward:
            place = (pl.ds(pl.multiple_of(at * CHUNK, CHUNK), CHUNK), slice(None))
            return [pltpu.make_async_copy(first_hbm.at[place], first_ref.at[place], load_sems.at[0, at])]
        places = [
            (slice(None), pl.ds(pl.multiple_of(side * ff + at * CHUNK, CHUNK), CHUNK)) for side in range(2)
        ]
        return [
            pltpu.make_async_copy(first_hbm.at[place], first_ref.at[place], load_sems.at[side, at])
            for side, place in enumerate(places)
        ]

    def load_second(at):
        span = pl.ds(pl.multiple_of(at * span_cols, span_cols), span_cols)
        place = (span, slice(None)) if backward else (slice(None), span)
        return pltpu.make_async_copy(second_hbm.at[place], second_ref.at[place], load_sems.at[2, at])

    load_extra = []
    if backward:
        for at in range(2 * lax.axis_size("shard")):
            group, part, owner = at // 4, at // 2 % 2, at % 2
            source = pl.ds(at * half, half)
            place = pl.ds(group * 2 * rows + owner * rows + part * half, half)
            load_extra.append(pltpu.make_async_copy(gate_up_hbm.at[source], gate_up_ref.at[place], hold_sems.at[at]))
    else:
        load_extra.append(pltpu.make_async_copy(middle_hbm, middle_ref, hold_sems.at[0]))
    if backward:
        for copy in load_extra:
            copy.start()
    for at in range(first_steps):
        for copy in load_first(at):
            copy.start()
    for at in range(spans):
        load_second(at).start()
    if not backward:
        load_extra[0].start()

    def remote(source, target, at, device):
        return pltpu.make_async_remote_copy(
            source, target, send_sems.at[at], recv_sems.at[at], device_id={"shard": device}, device_id_type=MESH
        )

    def place_of(owner, part):
        start = part * block + (owner % 2) * piece if parts == 2 else (owner % 2) * piece + part * half
        return pl.ds(pl.multiple_of((owner // 2) * 2 * rows + start, half), half)

    def owned(owner, part):
        return all_ref.at[place_of(owner, part)]

    turns = spread_turns(wide)
    base = 6 + (2 * parts + 1) * spans
    slice_barrier((beside, across), turns, 0 if target is None else 1)

    def hand_on(part, at):
        place = (pl.ds(part * piece, piece), pl.ds(at * span_cols, span_cols))
        return section_copy(
            result_ref.at[place], next_hbm.at[place], part * spans + at + base + lax.axis_size("replica"),
            send_sems, recv_sems, target,
        )

    def across_copy(part):
        return remote(owned(shard, part), owned(shard, part), part, across)

    def relay(part):
        return remote(owned(across, part), owned(across, part), 4 + part, beside)

    beside_copies = [remote(owned(shard, part), owned(shard, part), 2 + part, beside) for part in range(2)]
    for part in range(2):
        all_ref[place_of(shard, part), :] = mine_ref[part * half : (part + 1) * half, :]
        across_copy(part).start()
    for copy in beside_copies:
        copy.start()
    spread_copies = [
        replica_copy(mine_ref, others_hbm.at[lax.axis_index("replica")], turn, send_sems, recv_sems, base)
        for turn in turns
    ]
    for copy in spread_copies:
        copy.start()

    def ahead_rows(owner):
        return ahead_hbm.at[pl.ds(pl.multiple_of(owner * rows, rows), rows)]

    if wide:
        next_rows = odd_hbm.at[lax.rem(lax.axis_index("replica") + 1, lax.axis_size("replica"))]
        ahead_base = base + lax.axis_size("replica")
        ahead_over = remote(next_rows, ahead_rows(shard), ahead_base, across)
        ahead_direct = remote(next_rows, ahead_rows(shard), ahead_base + 1, beside)
        ahead_relay = remote(ahead_rows(across), ahead_rows(across), ahead_base + 2, beside)

    def first_product(start, count, waits):
        span = pl.ds(pl.multiple_of(start, count), count)

        def step(at, carry):
            cols = pl.ds(pl.multiple_of(at * CHUNK, CHUNK), CHUNK)
            high = pl.ds(pl.multiple_of(ff + at * CHUNK, CHUNK), CHUNK)
            if waits:
                for copy in load_first(at):
                    copy.wait()
            if backward:
                grad_hidden = dot_rows(all_ref[span, :], first_ref[cols, :])
                gate = gate_up_ref[span, cols].astype(F32)
                up = gate_up_ref[span, high].astype(F32)
                sigmoid = jax.nn.sigmoid(gate)
                mid_ref[span, cols] = (grad_hidden * up * sigmoid * (1.0 + gate * (1.0 - sigmoid))).astype(BF)
                mid_ref[span, high] = (grad_hidden * gate * sigmoid).astype(BF)
            else:
                gate = dot(all_ref[span, :], first_ref[:, cols])
                up = dot(all_ref[span, :], first_ref[:, high])
                gate_up_ref[span, cols] = gate.astype(BF)
                gate_up_ref[span, high] = up.astype(BF)
                mid_ref[span, cols] = (gate * jax.nn.sigmoid(gate) * up).astype(BF)
            return carry

        lax.fori_loop(0, first_steps, step, 0)

    def second_product(start, count, at, store):
        span = pl.ds(pl.multiple_of(start, count), count)

        def step(inner, carry):
            cols = pl.ds(pl.multiple_of(at * span_cols + inner * CHUNK, CHUNK), CHUNK)
            if backward:
                partial = dot_rows(mid_ref[span, :], second_ref[cols, :])
            else:
                partial = dot(mid_ref[span, :], second_ref[:, cols])
            store(pl.ds(pl.multiple_of(inner * CHUNK, CHUNK), CHUNK), partial.astype(BF))
            return carry

        lax.fori_loop(0, span_cols // CHUNK, step, 0)

    def give(part, at):
        return remote(part_ref.at[part, at, 1 - core], take_ref.at[part, at], 6 + part * spans + at, beside)

    def cross(part, at):
        return remote(sent_ref.at[part, at], land_ref.at[part, at], 6 + (parts + part) * spans + at, across)

    def give_own(at):
        return remote(own_ref.at[at, 1 - core], own_take_ref.at[at], 6 + 2 * parts * spans + at, beside)

    def pass_on(part, at):
        give(part, at).wait_recv()
        sent_ref[part, at] = (part_ref[part, at, core].astype(F32) + take_ref[part, at].astype(F32)).astype(BF)
        cross(part, at).start()

    own_start = chip * 2 * rows
    other_start = (1 - chip) * 2 * rows
    stores = []
    for copy in beside_copies:
        copy.wait_recv()
    if backward:
        for copy in load_extra:
            copy.wait()
    first_product(own_start, 2 * rows, True)
    if not backward:
        own_place = pl.ds(pl.multiple_of(own_start, 2 * rows), 2 * rows)
        stores.append(pltpu.make_async_copy(gate_up_ref.at[own_place], gate_up_hbm.at[own_place], keep_sems.at[1]))
        stores[-1].start()

    def store_part(part):
        place = pl.ds(pl.multiple_of(other_start + part * block, block), block)
        return pltpu.make_async_copy(gate_up_ref.at[place], gate_up_hbm.at[place], keep_sems.at[2 + part])

    def arrive(part):
        across_copy(part).wait_recv()
        relay(part).start()

    if parts == 1:
        for part in range(2):
            arrive(part)

    def other_part(part, carry):
        if parts == 1:
            for late in range(2):
                relay(late).wait_recv()
            if wide:
                ahead_over.start()
                ahead_direct.start()
        else:
            arrive(part)
            relay(part).wait_recv()
        start = other_start + part * block
        first_product(start, block, False)
        if not backward:
            store_part(part).start()

        def span_step(at, inner):
            @pl.when(part == 0)
            def _():
                load_second(at).wait()

            def store(cols, partial):
                part_ref[part, at, 0, :, cols] = partial[:piece]
                part_ref[part, at, 1, :, cols] = partial[piece:]

            second_product(start, block, at, store)
            give(part, at).start()

            @pl.when(at > 0)
            def _():
                pass_on(part, at - 1)

            return inner

        lax.fori_loop(0, spans, span_step, 0)
        pass_on(part, spans - 1)
        return carry

    lax.fori_loop(0, parts, other_part, 0)
    if not backward:
        stores += [store_part(part) for part in range(parts)]
    for owner in range(lax.axis_size("shard")):
        for part in range(2):
            at = owner * 2 + part
            copy = pltpu.make_async_copy(
                all_ref.at[place_of(owner, part)], all_hbm.at[pl.ds(owner * rows + part * half, half)],
                keep_sems.at[4 + at],
            )
            copy.start()
            stores.append(copy)

    def own_step(at, carry):
        def store(cols, partial):
            for part in range(parts):
                for owner in range(2):
                    first_row = part * block + owner * piece
                    own_ref[at, owner, part * piece : (part + 1) * piece, cols] = partial[first_row : first_row + piece]

        second_product(own_start, 2 * rows, at, store)
        give_own(at).start()
        return carry

    lax.fori_loop(0, spans, own_step, 0)
    if wide:
        ahead_over.wait_recv()
        ahead_relay.start()
    if not backward:
        load_extra[0].wait()
    for at in range(spans):
        give_own(at).wait_recv()
    for part in range(parts):
        place = slice(part * piece, (part + 1) * piece)
        for at in range(spans):
            cross(part, at).wait_recv()
            cols = slice(at * span_cols, (at + 1) * span_cols)
            total = (
                own_ref[at, core, place].astype(F32)
                + own_take_ref[at, place].astype(F32)
                + land_ref[part, at].astype(F32)
            )
            if backward:
                result_ref[place, cols] = total
            else:
                result_ref[place, cols] = (middle_ref[place, cols] + total).astype(BF)
                if target is not None:
                    hand_on(part, at).start()
    for part in range(2):
        beside_copies[part].wait_send()
        across_copy(part).wait_send()
        relay(part).wait_send()
    if wide:
        ahead_direct.wait()
        ahead_relay.wait()
        ahead_over.wait_send()
    for copy in spread_copies + stores:
        copy.wait()
    if target is not None:
        for part in range(parts):
            for at in range(spans):
                hand_on(part, at).wait_send()
    for at in range(spans):
        give_own(at).wait_send()
        for part in range(parts):
            give(part, at).wait_send()
            cross(part, at).wait_send()


def section_copy(source, target, at, send_sems, recv_sems, section):
    return pltpu.make_async_remote_copy(
        source, target, send_sems.at[at], recv_sems.at[at], device_id={"section": section}, device_id_type=MESH
    )


def spread_turns(wide):
    return range(2, lax.axis_size("replica")) if wide else range(1, lax.axis_size("replica"), 2)


def gather_turns(mine_hbm, gathered_hbm, send_sems, recv_sems):
    shard, beside, across, _ = slice_peers()
    replicas = lax.axis_size("replica")
    rows = mine_hbm.shape[0]

    def remote(owner, turn, at, device):
        place = gathered_hbm.at[turn, pl.ds(pl.multiple_of(owner * rows, rows), rows)]
        return pltpu.make_async_remote_copy(
            place, place, send_sems.at[at], recv_sems.at[at], device_id={"shard": device}, device_id_type=MESH
        )

    own_rows = pl.ds(pl.multiple_of(shard * rows, rows), rows)
    order = [1]
    spread_copies = [
        replica_copy(mine_hbm, gathered_hbm.at[turn, own_rows], turn, send_sems, recv_sems, 3 * replicas)
        for turn in order
    ]
    over = [remote(shard, turn, 3 * turn, across) for turn in order]
    direct = [remote(shard, turn, 3 * turn + 1, beside) for turn in order]
    relays = [remote(across, turn, 3 * turn + 2, beside) for turn in order]
    spread_copies[0].start()
    for at in range(len(order)):
        spread_copies[at].wait_recv()
        over[at].start()
        direct[at].start()
        spread_copies[at].wait_send()
        if at + 1 < len(order):
            spread_copies[at + 1].start()
        if at:
            over[at - 1].wait_recv()
            relays[at - 1].start()
    over[-1].wait_recv()
    relays[-1].start()
    for copy in direct + relays:
        copy.wait_recv()
    for copy in over + direct + relays:
        copy.wait_send()


def feed_forward_kernel(section, last, gathers, parts, spans, rows, *refs):
    if gathers:
        cotangent_hbm, early_hbm, gather_send_sems, gather_recv_sems = refs[4], refs[10], refs[-4], refs[-3]
        refs = refs[:4] + refs[5:10] + refs[11:-4] + refs[-2:]

    @pl.when(lax.axis_index("section") == section)
    def _():
        feed_kernel(False, rows, None if last else section + 1, False, *refs)

    if not last:

        @pl.when(lax.axis_index("section") == section + 1)
        def _():
            barrier = pltpu.get_barrier_semaphore()
            pl.semaphore_signal(barrier, inc=1, device_id={"section": section}, device_id_type=MESH)
            if gathers:
                _, beside, across, _ = slice_peers()
                slice_barrier((beside, across), (1,))
                gather_turns(cotangent_hbm, early_hbm, gather_send_sems, gather_recv_sems)
            next_hbm, send_sems, recv_sems = refs[8], refs[-2], refs[-1]
            base = 6 + (2 * parts + 1) * spans + lax.axis_size("replica")
            high, wide = rows // parts, next_hbm.shape[1] // spans
            for part in range(parts):
                for at in range(spans):
                    place = next_hbm.at[pl.ds(part * high, high), pl.ds(at * wide, wide)]
                    section_copy(place, place, base + part * spans + at, send_sems, recv_sems, section).wait_recv()


def call_feed(section, backward, operands, collective, cotangent=None):
    first, second = operands[-2], operands[-1]
    rows, width = operands[0].shape
    shards, replicas = lax.axis_size("shard"), lax.axis_size("replica")
    ff = first.shape[0] if backward else second.shape[0]
    every = shards * rows
    parts, span_cols = (1, CHUNK) if backward else (2, 2 * CHUNK)
    spans, piece_rows = width // span_cols, rows // parts
    vmem, anywhere = pl.BlockSpec(memory_space=pltpu.VMEM), pl.BlockSpec(memory_space=pl.ANY)
    out_shape = [
        jax.ShapeDtypeStruct((rows, width), F32 if backward else BF),
        jax.ShapeDtypeStruct((every, width), BF),
        jax.ShapeDtypeStruct((replicas, rows, width), BF),
    ]
    if backward:
        out_shape.append(jax.ShapeDtypeStruct((every, width), BF))
    else:
        out_shape.insert(2, jax.ShapeDtypeStruct((every, 2 * ff), BF))
        out_shape.append(jax.ShapeDtypeStruct((rows, width), BF))
    copies = 6 + (3 * parts + 1) * spans + replicas + 3
    piece = pltpu.VMEM((parts, spans, piece_rows, span_cols), BF)
    scratch = [
        pltpu.VMEM((every, 2 * ff if backward else ff), BF),
        pltpu.VMEM((every, width), BF),
        pltpu.VMEM((every, 2 * ff), BF),
        pltpu.VMEM(first.shape, BF),
        pltpu.VMEM(second.shape, BF),
        pltpu.VMEM((parts, spans, 2, piece_rows, span_cols), BF),
        piece,
        piece,
        piece,
        pltpu.VMEM((spans, 2, rows, span_cols), BF),
        pltpu.VMEM((spans, rows, span_cols), BF),
    ]
    if not backward:
        scratch.append(pltpu.VMEM((rows, width), F32))
    scratch += [
        pltpu.SemaphoreType.DMA((3, max(ff // CHUNK, spans))),
        pltpu.SemaphoreType.DMA((4 + 2 * shards,)),
        pltpu.SemaphoreType.DMA((2 * shards,)),
        *([pltpu.SemaphoreType.DMA((4 * replicas,))] * (0 if cotangent is None else 2)),
        pltpu.SemaphoreType.DMA((copies,)),
        pltpu.SemaphoreType.DMA((copies,)),
    ]
    if cotangent is not None:
        operands += (cotangent,)
        out_shape.append(jax.ShapeDtypeStruct((replicas, every, width), BF))
    return pl.pallas_call(
        gated(section, functools.partial(feed_kernel, True, rows, None, section == lax.axis_size("section") - 1))
        if backward
        else functools.partial(feed_forward_kernel, section, section == lax.axis_size("section") - 1,
            cotangent is not None, parts, spans, rows),
        out_shape=out_shape,
        in_specs=[vmem] + [anywhere] * (len(operands) - 1),
        out_specs=[vmem] + [anywhere] * (len(out_shape) - 1),
        scratch_shapes=scratch,
        compiler_params=pltpu.CompilerParams(
            collective_id=collective, has_side_effects=True, vmem_limit_bytes=VMEM_LIMIT
        ),
        name="feed_backward" if backward else "feed_forward",
    )(*operands)


def weights_kernel(
    qkv_ref, out_ref, gate_up_ref, state_ref, gain_one_ref, gain_two_ref, cos_ref, sin_ref, allowed_ref,
    qkv_full, out_full, gate_up_part, middle_ref, normed_two_ref, rotated_ref, lefts_ref,
    qkv_hold, out_hold, gate_up_hold, qkv_work, out_work, normed_ref, attended_ref, work_sems,
    local_sems, send_sems, recv_sems,
):
    shard, replica = lax.axis_index("shard"), lax.axis_index("replica")
    chip, core = shard // 2, shard % 2
    beside = {"shard": chip * 2 + (1 - core)}
    across = {"shard": (1 - chip) * 2 + core}
    diagonal = {"shard": (1 - chip) * 2 + (1 - core)}
    mine = replica % 2
    partner = {"replica": replica + 1 - 2 * mine}
    rows = qkv_ref.shape[0]
    half = rows // 2
    ff = gate_up_ref.shape[1] // 2
    part = gate_up_part.shape[1] // 2

    def remote(source, target, at, device):
        return pltpu.make_async_remote_copy(
            source, target, send_sems.at[at], recv_sems.at[at], device_id=device, device_id_type=MESH
        )

    def span(start, count):
        return pl.ds(pl.multiple_of(start, count), count)

    sides = [pl.ds(side * part, part) for side in range(2)]
    loads = [
        pltpu.make_async_copy(qkv_ref, qkv_hold, local_sems.at[0]),
        pltpu.make_async_copy(out_ref, out_hold, local_sems.at[1]),
    ] + [
        pltpu.make_async_copy(
            gate_up_ref.at[:, span(side * ff + shard * part, part)], gate_up_hold.at[side], local_sems.at[2 + side]
        )
        for side in range(2)
    ]
    own_rows = span(shard * rows, rows)
    stores = [
        pltpu.make_async_copy(qkv_hold, qkv_full.at[own_rows], local_sems.at[4]),
        pltpu.make_async_copy(out_hold, out_full.at[own_rows], local_sems.at[5]),
    ] + [
        pltpu.make_async_copy(gate_up_hold.at[side], gate_up_part.at[own_rows, sides[side]], local_sems.at[6 + side])
        for side in range(2)
    ]
    for copy in loads:
        copy.start()

    pieces = []
    for source, whole, count in ((qkv_ref, qkv_full, 64), (out_ref, out_full, 64)):
        for offset in range(0, half, count):

            def place(owner, part_of, whole=whole, offset=offset, count=count):
                return whole.at[span(owner["shard"] * rows + part_of * half + offset, count)]

            own = source.at[span(mine * half + offset, count)]
            pieces.append((own, place, across, True))
    for offset in range(0, half, 32):
        for side in range(2):
            for device in (across, diagonal):

                def place(owner, part_of, offset=offset, side=side):
                    return gate_up_part.at[
                        span(owner["shard"] * rows + part_of * half + offset, 32), pl.ds(side * part, part)
                    ]

                own = gate_up_ref.at[
                    span(mine * half + offset, 32), span(side * ff + device["shard"] * part, part)
                ]
                pieces.append((own, place, device, False))
    count = len(pieces)
    me = {"shard": shard}
    over = [remote(own, place(me, mine), at, device) for at, (own, place, device, _) in enumerate(pieces)]
    passed = [
        remote(place(device, mine), place(device, mine), count + at, partner)
        for at, (_, place, device, _) in enumerate(pieces)
    ]
    relays = [
        [
            remote(place(across, which), place(across, which), (2 + turn) * count + at, beside)
            if relayed
            else None
            for at, (_, place, _, relayed) in enumerate(pieces)
        ]
        for turn, which in enumerate((mine, 1 - mine))
    ]
    direct = [
        remote(qkv_ref, qkv_full.at[span(shard * rows, rows)], 4 * count, beside),
        remote(out_ref, out_full.at[span(shard * rows, rows)], 4 * count + 1, beside),
    ]
    for side in range(2):
        direct.append(
            remote(
                gate_up_ref.at[:, span(side * ff + beside["shard"] * part, part)],
                gate_up_part.at[span(shard * rows, rows), pl.ds(side * part, part)],
                4 * count + 2 + side,
                beside,
            )
        )

    barrier = pltpu.get_barrier_semaphore()
    for device in (beside, across, diagonal, partner):
        pl.semaphore_signal(barrier, inc=1, device_id=device, device_id_type=MESH)
    pl.semaphore_wait(barrier, 4)

    started = []

    def start(copy):
        copy.start()
        started.append(copy)

    ahead = 6
    for copy in over[:ahead]:
        start(copy)
    for copy in direct:
        start(copy)
    for load, store in zip(loads, stores):
        load.wait()
        store.start()
    first, load_out, second = attend_parts(
        state_ref, gain_one_ref, gain_two_ref, cos_ref, sin_ref, allowed_ref, qkv_full, out_full,
        middle_ref, normed_two_ref, rotated_ref, lefts_ref,
        qkv_work, out_work, normed_ref, attended_ref, work_sems,
    )
    qkv_last = half // 64 - 1
    out_last = qkv_last + half // 64
    arrived = [0]

    def wait_relays(last):
        for at in range(arrived[0], last + 1):
            for copies in relays:
                copies[at].wait_recv()
        arrived[0] = last + 1

    def work(parts):
        @pl.when(lax.axis_index("section") == 0)
        def _():
            for part in parts:
                part()

    ready = list(first)
    for at in range(count + 1):
        if at < count:
            over[at].wait_recv()
            start(passed[at])
            if relays[0][at] is not None:
                start(relays[0][at])
            if at + ahead < count:
                over[at].wait_send()
                started[:] = [copy for copy in started if copy is not over[at]]
                start(over[at + ahead])
        if at > 0:
            passed[at - 1].wait_recv()
            if relays[1][at - 1] is not None:
                start(relays[1][at - 1])
        if at == qkv_last + 2:
            wait_relays(qkv_last)
            direct[0].wait_recv()
            stores[0].wait()
        if at == out_last + 2:
            wait_relays(out_last)
            direct[1].wait_recv()
            stores[1].wait()
            work([load_out])
            ready += second
        if at >= qkv_last + 2:
            work(ready[:2])
            ready = ready[2:]
    work(ready)
    for copy in direct[2:]:
        copy.wait_recv()
    for copy in stores[2:]:
        copy.wait()
    for copy in started:
        copy.wait_send()


def call_weights(qkv_weight, out_weight, gate_up_weight, operands, collective):
    shards = lax.axis_size("shard")
    rows = qkv_weight.shape[0]
    count = 2 * (rows // 128) + 8 * (rows // 128)
    out_shape, scratch = attend_shapes(*operands[0].shape, qkv_weight.shape[1])
    vmem = pl.BlockSpec(memory_space=pltpu.VMEM)
    anywhere = pl.BlockSpec(memory_space=pl.ANY)
    return pl.pallas_call(
        weights_kernel,
        out_shape=[
            jax.ShapeDtypeStruct((shards * rows, qkv_weight.shape[1]), BF),
            jax.ShapeDtypeStruct((shards * rows, out_weight.shape[1]), BF),
            jax.ShapeDtypeStruct((shards * rows, gate_up_weight.shape[1] // shards), BF),
        ] + out_shape,
        in_specs=[anywhere] * 3 + [vmem] * len(operands),
        out_specs=[anywhere] * 3 + [vmem] * len(out_shape),
        scratch_shapes=[
            pltpu.VMEM(qkv_weight.shape, BF),
            pltpu.VMEM(out_weight.shape, BF),
            pltpu.VMEM((2, rows, gate_up_weight.shape[1] // (2 * shards)), BF),
            *scratch,
            pltpu.SemaphoreType.DMA((8,)),
            pltpu.SemaphoreType.DMA((4 * count + 4,)),
            pltpu.SemaphoreType.DMA((4 * count + 4,)),
        ],
        compiler_params=pltpu.CompilerParams(
            collective_id=collective, has_side_effects=True, vmem_limit_bytes=VMEM_LIMIT
        ),
        name="weights",
    )(qkv_weight, out_weight, gate_up_weight, *operands)


def repeat(first, last, body):
    def step(at, carry):
        body(at)
        return carry

    if first < last:
        lax.fori_loop(first, last, step, 0)


def by_chunk(count, body):
    repeat(0, count, lambda at: body(pl.ds(pl.multiple_of(at * CHUNK, CHUNK), CHUNK)))


def weight_grads_kernel(sections, left_rows_ref, hidden_ref, *refs):
    sources = [refs[at * sections : (at + 1) * sections] for at in range(7)]
    (early_hbm, gate_up_hbm, down_hbm,
     gate_up_grad_ref, down_grad_ref, qkv_grad_ref, out_grad_ref, gain_sum_ref, gathered_hbm, even_hbm,
     projected_ref, upstream_ref, gains_ref, gains_land_ref, gain_part_ref, gains_last_ref, lefts_ref, left_ref,
     extra_ref, terms_ref, chain_ref, down_ref, block_ref, gate_up_ref, mid_ref, sum_ref, stage_ref,
     start_sems, load_sems, block_sems, keep_sem, send_sems, recv_sems) = refs[7 * sections :]
    shard, beside, across, diagonal = slice_peers()
    peers = (across, diagonal, beside)
    replica, replicas = lax.axis_index("replica"), lax.axis_size("replica")
    early = lax.axis_index("section") == lax.axis_size("section") - 1
    late = lax.axis_index("section") < lax.axis_size("section") - 1
    here = [lax.axis_index("section") == section for section in range(sections)]
    rows, cols = projected_ref.shape
    every, width = sources[5][0].shape
    pieces, all_pieces = cols // CHUNK, (cols + width) // CHUNK
    staged = stage_ref.shape[2] // CHUNK
    kinds, groups, _, sub_rows, _ = lefts_ref.shape
    part = down_ref.shape[0]
    half_part = part // 2
    ff = gate_up_grad_ref.shape[1] // 2
    steps = half_part // CHUNK
    wide = width // CHUNK
    out_rows = gate_up_grad_ref.shape[0]
    piece_base = 3 * replicas
    spread_base = piece_base + 3 * pieces
    gain_base = spread_base + replicas
    left_base = gain_base + replicas
    chain_base = left_base + kinds * groups * 3
    last_base = chain_base + 4 * replicas
    grad_base = last_base + 3

    def remote(source, target, at, device):
        return pltpu.make_async_remote_copy(
            source, target, send_sems.at[at], recv_sems.at[at], device_id={"shard": device}, device_id_type=MESH
        )

    def owned(owner):
        return pl.ds(pl.multiple_of(owner * rows, rows), rows)

    def piece_place(piece, place=None):
        if piece < 2 * staged:
            place = pl.ds(0, every) if place is None else place
            return stage_ref.at[piece // staged, place, pl.ds(piece % staged * CHUNK, CHUNK)]
        return extra_ref.at[piece - 2 * staged] if place is None else extra_ref.at[piece - 2 * staged, place]

    def piece_copy(owner, piece, kind, device):
        place = piece_place(piece, owned(owner))
        return remote(place, place, piece_base + kind * pieces + piece, device)

    over = [piece_copy(shard, piece, 0, across) for piece in range(pieces)]
    direct = [piece_copy(shard, piece, 1, beside) for piece in range(pieces)]
    relays = [piece_copy(across, piece, 2, beside) for piece in range(pieces)]

    def hand_left(kind, group, peer):
        return remote(
            lefts_ref.at[kind, group, peers[peer]], left_ref.at[kind, group, :, owned(shard)],
            left_base + (kind * groups + group) * 3 + peer, peers[peer],
        )

    lefts = [(kind, group, peer) for kind in reversed(range(kinds)) for group in range(groups) for peer in range(3)]
    loads = []
    for at, target in enumerate((lefts_ref, projected_ref, gains_ref, upstream_ref)):
        loads.append([pltpu.make_async_copy(source, target, start_sems.at[at]) for source in sources[at]])
    load_branch = [
        [
            pltpu.make_async_copy(source.at[piece - pieces], piece_place(piece), start_sems.at[4 + piece - pieces])
            for source in sources[4]
        ]
        for piece in range(pieces, all_pieces)
    ]
    load_own = [pltpu.make_async_copy(source, block_ref.at[0], load_sems.at[2, 0]) for source in sources[5]]
    load_down = pltpu.make_async_copy(down_hbm, down_ref, load_sems.at[3, 0])

    def block_at(turn):
        return lax.rem(replica + turn, replicas)

    def tokens(turn):
        return pl.ds(pl.multiple_of(block_at(turn) * every, every), every)

    def load_gate_up(half, turn, side):
        place = pl.ds(side * part + half * half_part, half_part)
        slot = lax.rem(turn, 2)
        return pltpu.make_async_copy(
            gate_up_hbm.at[tokens(turn), place], gate_up_ref.at[slot, side], load_sems.at[side, slot]
        )

    def block_copies(turn, source):
        slot = lax.rem(turn, 2)
        copies = []
        for at, owner in enumerate(peers + (shard,)):
            if source is early_hbm:
                own = early_hbm.at[turn, owned(owner)]
            else:
                own = gathered_hbm.at[turn, owned(owner)] if source is None or at < 3 else source.at[block_at(turn)]
            copies.append(pltpu.make_async_copy(own, block_ref.at[slot, owned(owner)], block_sems.at[slot, at]))
        return copies

    def own_cases(turn):
        cases = [(late & (turn > 0) & (turn % 2 == 0), even_hbm), (early & (turn > 1), sources[6][-1])]
        for section in range(sections - 1):
            cases.append((here[section] & (turn % 2 == 1), sources[6][section]))
        return cases

    def load_block(turn):
        @pl.when(early & (turn == 1))
        def _():
            for copy in block_copies(turn, early_hbm):
                copy.start()

        @pl.when(late | (turn != 1))
        def _():
            for copy in block_copies(turn, None)[:3]:
                copy.start()

        cases = [(turn == 0, None)] + own_cases(turn)
        for case, source in cases:

            @pl.when(case)
            def _(source=source):
                block_copies(turn, source)[3].start()

    def wait_block(turn):
        for copy in block_copies(turn, None):
            copy.wait()

    def landing(turn, owner):
        return gathered_hbm.at[turn, owned(owner)]

    def block_over(turn, source):
        return remote(source.at[block_at(turn)], landing(turn, shard), 3 * turn, across)

    def block_direct(turn, source):
        return remote(source.at[block_at(turn)], landing(turn, shard), 3 * turn + 1, beside)

    def block_relay(turn):
        return remote(landing(turn, across), landing(turn, across), 3 * turn + 2, beside)

    def send_block(turn):
        cases = own_cases(turn)
        for case, source in cases:

            @pl.when(case)
            def _(source=source):
                block_over(turn, source).start()
                block_direct(turn, source).start()

    def chain_slot(block, at):
        return replicas - (replicas - block) * ((at - block + replicas - 1) // replicas)

    spans = ((cols, width), (0, cols))

    def chain_at(phase, slot):
        return chain_ref.at[slot, :, pl.ds(*spans[phase])]

    def chain_up(phase, block):
        at = chain_base + phase * 2 * replicas + block
        return pltpu.make_async_remote_copy(
            chain_at(phase, block), chain_at(phase, block), send_sems.at[at], recv_sems.at[at],
            device_id={"replica": replica + 1}, device_id_type=MESH,
        )

    def chain_down(phase, block):
        at = chain_base + phase * 2 * replicas + replicas + block
        return pltpu.make_async_remote_copy(
            chain_at(phase, block), chain_at(phase, chain_slot(block, replica - 1)), send_sems.at[at], recv_sems.at[at],
            device_id={"replica": replica - 1}, device_id_type=MESH,
        )

    def chain_chunks(phase, body):
        first, count = spans[phase]
        repeat(first // CHUNK, (first + count) // CHUNK, lambda at: body(pl.ds(pl.multiple_of(at * CHUNK, CHUNK), CHUNK)))

    def add_terms(phase, block):
        def add(place):
            total = chain_ref[block, :, place].astype(F32) + terms_ref[block, :, place].astype(F32)
            chain_ref[block, :, place] = total.astype(BF)

        chain_chunks(phase, add)

    def chain_begin(phase):
        def take_terms(block):
            def take(place):
                chain_ref[block, :, place] = terms_ref[block, :, place]

            chain_chunks(phase, take)

        for block in reversed(range(1, replicas)):

            @pl.when(replica == 0)
            def _(block=block):
                take_terms(block)
                chain_up(phase, block).start()

        for block in range(replicas - 1):

            @pl.when(replica == replicas - 1)
            def _(block=block):
                take_terms(block)
                chain_down(phase, block).start()

    def chain_step(phase, step):
        high = replicas - 1 - step + replica

        @pl.when((replica > 0) & (step >= replica))
        def _():
            chain_up(phase, high).wait_recv()

            @pl.when(step < replicas - 1)
            def _():
                add_terms(phase, high)
                chain_up(phase, high).start()

        low = step - (replicas - 1 - replica)

        @pl.when((replica < replicas - 1) & (step >= replicas - 1 - replica))
        def _():
            chain_down(phase, low).wait_recv()

            @pl.when(step < replicas - 1)
            def _():
                add_terms(phase, low)
                chain_down(phase, low).start()

    def gain_copy(peer):
        return remote(gain_part_ref, gains_last_ref.at[shard], last_base + peer, peers[peer])

    def send_grad(half, at, peer):
        device = peers[peer]
        place = pl.ds(pl.multiple_of(at * CHUNK, CHUNK), CHUNK)
        target = pl.ds(
            pl.multiple_of(
                (at // steps) * ff + shard * part + half * half_part + (at % steps) * CHUNK, CHUNK
            ),
            CHUNK,
        )
        return remote(
            stage_ref.at[half, pl.ds(pl.multiple_of(device * out_rows, out_rows), out_rows), place],
            gate_up_grad_ref.at[:, target],
            grad_base + (half * 2 * steps + at) * 3 + peer,
            device,
        )

    def clear_sum():
        def clear(place):
            sum_ref[:, place] = jnp.zeros((sum_ref.shape[0], CHUNK), F32)

        by_chunk(2 * steps, clear)

    def compute(half, turn):
        slot = lax.rem(turn, 2)
        later = lax.rem(turn + 1, replicas)
        for side in range(2):
            load_gate_up(half, turn, side).wait()

        @pl.when(turn + 1 < replicas)
        def _():
            for side in range(2):
                load_gate_up(half, later, side).start()
            if half:
                load_block(later)

        def products(at, inner):
            place = pl.ds(pl.multiple_of(at * CHUNK, CHUNK), CHUNK)
            high = pl.ds(pl.multiple_of(half_part + at * CHUNK, CHUNK), CHUNK)
            down_rows = pl.ds(pl.multiple_of(half * half_part + at * CHUNK, CHUNK), CHUNK)
            grad_hidden = dot_rows(block_ref[slot], down_ref[down_rows, :])
            gate = gate_up_ref[slot, 0, :, place].astype(F32)
            up = gate_up_ref[slot, 1, :, place].astype(F32)
            sigmoid = jax.nn.sigmoid(gate)
            mid_ref[:, place] = (grad_hidden * up * sigmoid * (1.0 + gate * (1.0 - sigmoid))).astype(BF)
            mid_ref[:, high] = (grad_hidden * gate * sigmoid).astype(BF)
            return inner

        lax.fori_loop(0, steps, products, 0)

        def sums(at, inner):
            place = pl.ds(pl.multiple_of(at * CHUNK, CHUNK), CHUNK)
            total = sum_ref[:, place] + dot(left_rows_ref[:, tokens(turn)], mid_ref[:, place])

            @pl.when(turn < replicas - 1)
            def _():
                sum_ref[:, place] = total

            @pl.when(turn == replicas - 1)
            def _():
                stage_ref[half, pl.ds(0, total.shape[0]), place] = total.astype(BF)
                for peer in range(3):
                    send_grad(half, at, peer).start()

            return inner

        lax.fori_loop(0, 2 * steps, sums, 0)

    def first_pass(turn, carry):
        @pl.when(late | (turn != 1))
        def _():
            block_over(turn, even_hbm).wait_recv()
            block_relay(turn).start()
            block_direct(turn, even_hbm).wait_recv()
            block_relay(turn).wait_recv()

        load_block(turn)

        @pl.when(turn + 2 < replicas)
        def _():
            send_block(turn + 2)

        wait_block(turn)
        compute(0, turn)
        return carry

    def second_pass(turn, carry):
        compute(1, turn)

        @pl.when(turn + 1 < replicas)
        def _():
            wait_block(lax.rem(turn + 1, replicas))

        return carry

    for copies in loads + load_branch + [load_own]:
        start_own(copies)
    load_down.start()
    for side in range(2):
        load_gate_up(0, 0, side).start()

    barrier = pltpu.get_barrier_semaphore()
    for device in peers:
        pl.semaphore_signal(barrier, inc=1, device_id={"shard": device}, device_id_type=MESH)
    for turn in range(1, replicas):
        target = lax.rem(replica + turn, replicas)
        pl.semaphore_signal(barrier, inc=1, device_id={"replica": target}, device_id_type=MESH)
    pl.semaphore_wait(barrier, 2 + replicas)

    spread_copies = [
        replica_copy(upstream_ref, even_hbm.at[replica], turn, send_sems, recv_sems, spread_base)
        for turn in range(2, replicas, 2)
    ]
    gain_copies = [
        replica_copy(gains_ref, gains_land_ref.at[replica], turn, send_sems, recv_sems, gain_base)
        for turn in range(1, replicas)
    ]
    loads[0][0].wait()
    for place in lefts:
        hand_left(*place).start()
    loads[1][0].wait()
    for piece in range(pieces):
        piece_place(piece, owned(shard))[...] = projected_ref[:, piece * CHUNK : (piece + 1) * CHUNK]
        over[piece].start()
        direct[piece].start()
    loads[2][0].wait()
    gains_land_ref[replica] = gains_ref[...]
    loads[3][0].wait()
    for copy in gain_copies:
        copy.start()

    @pl.when(late)
    def _():
        for copy in spread_copies:
            copy.start()

    for kind in range(kinds):
        for group in range(groups):
            left_ref[kind, group, :, owned(shard)] = lefts_ref[kind, group, shard]
    load_own[0].wait()
    keep_own = pltpu.make_async_copy(block_ref.at[0], gathered_hbm.at[0], keep_sem)
    keep_own.start()
    clear_sum()

    def product(piece, kind, source):
        left = jnp.concatenate([left_ref[kind, group] for group in range(groups)], 0)
        total = dot(left, source).astype(BF)
        place = pl.ds(pl.multiple_of(piece * CHUNK, CHUNK), CHUNK)
        for group in range(groups):
            terms_ref[group, :, place] = total[group * sub_rows : (group + 1) * sub_rows]

    def staged_product(piece, kind):
        place = pl.ds(pl.multiple_of(piece % staged * CHUNK, CHUNK), CHUNK)
        product(piece, kind, stage_ref[piece // staged, pl.ds(0, every), place])

    for place in lefts[: len(lefts) // kinds]:
        hand_left(*place).wait_recv()
    for copies in load_branch:
        copies[0].wait()
    repeat(pieces, min(all_pieces, 2 * staged), lambda piece: staged_product(piece, 1))
    repeat(2 * staged, all_pieces, lambda piece: product(piece, 1, extra_ref[piece - 2 * staged]))
    chain_begin(0)
    load_down.wait()
    compute(0, 0)
    keep_own.wait()
    if replicas > 2:

        @pl.when(early)
        def _():
            load_block(1)
            wait_block(1)
            compute(0, 1)

    for place in lefts[len(lefts) // kinds :]:
        hand_left(*place).wait_recv()
    for piece in range(pieces):
        over[piece].wait_recv()
        relays[piece].start()
        if piece == pieces // 2:
            chain_step(0, 1)
    for copy in over:
        copy.wait_send()

    @pl.when(late)
    def _():
        for copy in spread_copies:
            copy.wait()

    for turn in range(1, min(3, replicas)):
        send_block(turn)
    for copy in direct + relays:
        copy.wait()
    repeat(0, pieces, lambda piece: staged_product(piece, 0))
    chain_begin(1)
    if replicas > 2:
        chain_step(0, 2)
    for copy in gain_copies:
        copy.wait()
    gain_part_ref[...] = jnp.sum(gains_land_ref[...], 0)
    gains_last_ref[shard] = gain_part_ref[...]
    for peer in range(3):
        gain_copy(peer).start()
    if replicas > 2:

        @pl.when(late)
        def _():
            first_pass(1, 0)

        if replicas > 3:

            @pl.when(early)
            def _():
                send_block(3)

    lax.fori_loop(2, replicas, first_pass, 0)
    for side in range(2):
        load_gate_up(1, 0, side).start()
    load_block(0)
    clear_sum()
    for step in range(3, replicas):
        chain_step(0, step)
    chain_step(1, 1)
    wait_block(0)
    lax.fori_loop(0, 2, second_pass, 0)
    if replicas > 2:
        chain_step(1, 2)
    lax.fori_loop(2, replicas, second_pass, 0)
    load_block(0)
    wait_block(0)

    def clear_down(place):
        down_grad_ref[:, place] = jnp.zeros((down_grad_ref.shape[0], CHUNK), F32)

    by_chunk(wide, clear_down)

    def down_pass(turn, carry):
        slot = lax.rem(turn, 2)
        later = lax.rem(turn + 1, replicas)

        @pl.when(turn + 1 < replicas)
        def _():
            load_block(later)

        def down_sums(at, inner):
            place = pl.ds(pl.multiple_of(at * CHUNK, CHUNK), CHUNK)
            down_grad_ref[:, place] += dot(hidden_ref[:, tokens(turn)], block_ref[slot, :, place])
            return inner

        lax.fori_loop(0, wide, down_sums, 0)

        @pl.when(turn + 1 < replicas)
        def _():
            wait_block(later)

        return carry

    lax.fori_loop(0, replicas, down_pass, 0)
    for peer in range(3):
        gain_copy(peer).wait()
    gain_sum_ref[...] = jnp.sum(gains_last_ref[...], 0)
    own = pl.ds(pl.multiple_of(shard * out_rows, out_rows), out_rows)
    for half in range(2):

        def store_own(at, carry, half=half):
            place = pl.ds(pl.multiple_of(at * CHUNK, CHUNK), CHUNK)
            target = pl.ds(
                pl.multiple_of(
                    (at // steps) * ff + shard * part + half * half_part + (at % steps) * CHUNK, CHUNK
                ),
                CHUNK,
            )
            gate_up_grad_ref[:, target] = stage_ref[half, own, place]
            return carry

        lax.fori_loop(0, 2 * steps, store_own, 0)
    for step in range(3, replicas):
        chain_step(1, step)

    def sum_up(grad_ref, first):
        def add(place):
            source = pl.ds(pl.multiple_of(first + place.start, CHUNK), CHUNK)
            grad_ref[:, place] = terms_ref[replica, :, source].astype(F32)

            @pl.when(replica > 0)
            def _():
                grad_ref[:, place] += chain_ref[replica, :, source].astype(F32)

            @pl.when(replica < replicas - 1)
            def _():
                grad_ref[:, place] += chain_ref[replicas, :, source].astype(F32)

        by_chunk(grad_ref.shape[1] // CHUNK, add)

    sum_up(qkv_grad_ref, 0)
    sum_up(out_grad_ref, cols)
    for half in range(2):

        def finish(at, carry, half=half):
            for peer in range(3):
                send_grad(half, at, peer).wait()
            return carry

        lax.fori_loop(0, 2 * steps, finish, 0)
    for place in lefts:
        hand_left(*place).wait_send()
    for turn in range(1, replicas):

        @pl.when(late | (turn != 1))
        def _(turn=turn):
            block_over(turn, even_hbm).wait_send()
            block_direct(turn, even_hbm).wait_send()
            block_relay(turn).wait_send()


    for phase in range(2):
        for block in range(1, replicas):

            @pl.when(replica < block)
            def _(phase=phase, block=block):
                chain_up(phase, block).wait_send()

        for block in range(replicas - 1):

            @pl.when(replica > block)
            def _(phase=phase, block=block):
                chain_down(phase, block).wait_send()


def call_weight_grads(left_rows, hidden, lefts, projected, gains, upstream, branch, slices, odd, early, gate_up, down,
                      collective):
    replicas, shards, sections = lax.axis_size("replica"), lax.axis_size("shard"), len(projected)
    rows, cols = projected[0].shape
    every, width = slices[0].shape
    part = down.shape[0]
    slice_rows = left_rows.shape[0]
    sub_rows = slice_rows // shards
    lefts = [values.reshape(2, replicas, shards, sub_rows, rows) for values in lefts]
    pieces, all_pieces = cols // CHUNK, (cols + width) // CHUNK
    copies = 3 * replicas + 3 * pieces + 2 * replicas + 6 * replicas + 4 * replicas + 3 + 3 * 2 * (part // CHUNK)
    vmem, anywhere = pl.BlockSpec(memory_space=pltpu.VMEM), pl.BlockSpec(memory_space=pl.ANY)
    gain_shape = gains[0].shape
    return pl.pallas_call(
        functools.partial(weight_grads_kernel, sections),
        out_shape=[
            jax.ShapeDtypeStruct((sub_rows, 2 * part * shards), BF),
            jax.ShapeDtypeStruct((hidden.shape[0], width), F32),
            jax.ShapeDtypeStruct((sub_rows, cols), F32),
            jax.ShapeDtypeStruct((sub_rows, width), F32),
            jax.ShapeDtypeStruct(gain_shape, F32),
            jax.ShapeDtypeStruct((replicas, every, width), BF),
            jax.ShapeDtypeStruct((replicas, rows, width), BF),
        ],
        in_specs=[vmem] * 2 + [anywhere] * (7 * sections + 3),
        out_specs=[vmem] * 5 + [anywhere] * 2,
        scratch_shapes=[
            pltpu.VMEM((rows, cols), BF),
            pltpu.VMEM((rows, width), BF),
            pltpu.VMEM(gain_shape, F32),
            pltpu.VMEM((replicas,) + gain_shape, F32),
            pltpu.VMEM(gain_shape, F32),
            pltpu.VMEM((shards,) + gain_shape, F32),
            pltpu.VMEM(lefts[0].shape, BF),
            pltpu.VMEM((2, replicas, sub_rows, every), BF),
            pltpu.VMEM((max(1, all_pieces - 2 * (part // CHUNK)), every, CHUNK), BF),
            pltpu.VMEM((replicas, sub_rows, cols + width), BF),
            pltpu.VMEM((replicas + 1, sub_rows, cols + width), BF),
            pltpu.VMEM(down.shape, BF),
            pltpu.VMEM((2, every, width), BF),
            pltpu.VMEM((2, 2, every, part // 2), BF),
            pltpu.VMEM((every, part), BF),
            pltpu.VMEM((slice_rows, part), F32),
            pltpu.VMEM((2, max(slice_rows, every), part), BF),
            pltpu.SemaphoreType.DMA((4 + all_pieces - pieces,)),
            pltpu.SemaphoreType.DMA((4, 2)),
            pltpu.SemaphoreType.DMA((2, 4)),
            pltpu.SemaphoreType.DMA,
            pltpu.SemaphoreType.DMA((copies,)),
            pltpu.SemaphoreType.DMA((copies,)),
        ],
        compiler_params=pltpu.CompilerParams(
            collective_id=collective, has_side_effects=True, vmem_limit_bytes=VMEM_LIMIT
        ),
        name="weight_grads",
    )(left_rows, hidden, *lefts, *projected, *gains, *upstream, *branch, *slices, *odd, early, gate_up, down)


def turn_order(replicas):
    return [0] + list(range(1, replicas, 2)) + list(range(2, replicas, 2))


def prepare_kernel(sections, gate_up_hbm, ahead_hbm, *refs):
    slices, normed_two, odd = [refs[at * sections : (at + 1) * sections] for at in range(3)]
    (gathered_hbm, gate_up_all_hbm, hidden_hbm, left_rows_ref,
     normed_two_ref, weight_ref, block_ref, gate_up_ref, hidden_ref, turned_ref,
     load_sems, store_sems, block_sems, start_sems, send_sems, recv_sems) = refs[3 * sections :]
    shard, beside, across, diagonal = slice_peers()
    peers = (across, diagonal, beside)
    replica, replicas = lax.axis_index("replica"), lax.axis_size("replica")
    shards = lax.axis_size("shard")
    rows, width = normed_two_ref.shape
    every = rows * shards
    part = hidden_ref.shape[1]
    ff_rows = hidden_hbm.shape[0]
    steps = part // CHUNK
    slice_rows = left_rows_ref.shape[0]
    owner = (replica * shards) // replicas
    first_col = lax.rem(replica * shards, replicas) * ff_rows

    def load_weight(side, at):
        place = (slice(None), pl.ds(pl.multiple_of(side * part + at * CHUNK, CHUNK), CHUNK))
        return pltpu.make_async_copy(gate_up_hbm.at[place], weight_ref.at[place], load_sems.at[side, at])

    for at in range(steps):
        for side in range(2):
            load_weight(side, at).start()

    def remote(source, target, at, device):
        return pltpu.make_async_remote_copy(
            source, target, send_sems.at[at], recv_sems.at[at], device_id={"shard": device}, device_id_type=MESH
        )

    def landing(turn, who):
        return gathered_hbm.at[turn, pl.ds(pl.multiple_of(who * rows, rows), rows)]

    behind = lax.axis_index("section") < sections - 1

    def fetched(turn, body):
        if turn == 1:
            pl.when(behind)(body)
        else:
            body()

    def own_sources(turn):
        if turn % 2:
            return [source.at[lax.rem(replica + turn, replicas)] for source in odd]
        return [landing(turn, shard)]

    def over(turn, source=None):
        return remote(landing(turn, shard) if source is None else source, landing(turn, shard), 3 * turn, across)

    def direct(turn, source=None):
        return remote(landing(turn, shard) if source is None else source, landing(turn, shard), 3 * turn + 1, beside)

    def send_block(turn):
        if turn % 2 == 0:
            from_replica(turn).wait_recv()
        copies = [(over(turn, source), direct(turn, source)) for source in own_sources(turn)]
        for section, pair in enumerate(copies):
            if turn == 1 and section == sections - 1:
                continue
            if len(copies) == 1:
                for copy in pair:
                    copy.start()
            else:

                @pl.when(lax.axis_index("section") == section)
                def _(pair=pair):
                    for copy in pair:
                        copy.start()

    def relay(turn):
        return remote(landing(turn, across), landing(turn, across), 3 * turn + 2, beside)

    def from_replica(turn):
        return replica_copy(normed_two_ref, landing(turn, shard), turn, send_sems, recv_sems, 3 * replicas)

    def tokens(turn):
        return pl.ds(pl.multiple_of(lax.rem(replica + turn, replicas) * every, every), every)

    def load_block(turn, slot):
        copies = []
        for at, owner in enumerate(peers + (shard,)):
            sources = own_sources(turn) if at == 3 else [landing(turn, owner)]
            if turn == 1 and at < 3:
                rows_at = ahead_hbm.at[pl.ds(pl.multiple_of(owner * rows, rows), rows)]
                sources = sources * (sections - 1) + [rows_at]
            place = block_ref.at[slot, pl.ds(pl.multiple_of(owner * rows, rows), rows)]
            copies.append([pltpu.make_async_copy(source, place, block_sems.at[slot, at]) for source in sources])
        return copies

    def start_block(turn, slot):
        for copies in load_block(turn, slot):
            if len(copies) == 1:
                copies[0].start()
            else:
                start_own(copies)

    def store_block(turn, slot):
        return pltpu.make_async_copy(gate_up_ref.at[slot], gate_up_all_hbm.at[tokens(turn)], store_sems.at[1, slot])

    def hand_hidden(turn, slot, peer):
        device = peers[peer]
        return remote(
            turned_ref.at[slot, device], hidden_hbm.at[:, tokens(turn)], 4 * replicas + 3 * turn + peer, device
        )

    def keep_hidden(turn, slot):
        return pltpu.make_async_copy(
            turned_ref.at[slot, shard], hidden_hbm.at[:, tokens(turn)], store_sems.at[2, slot]
        )

    loads = [
        [pltpu.make_async_copy(source, target, sem) for source in sources]
        for sources, target, sem in (
            (normed_two, normed_two_ref, start_sems.at[0]),
            (slices, block_ref.at[0], store_sems.at[0, 0]),
        )
    ]
    for copies in loads:
        start_own(copies)
    slice_barrier(peers, range(2, replicas, 2))
    order = turn_order(replicas)
    loads[0][0].wait()
    evens = [turn for turn in order if turn and turn % 2 == 0]
    for turn in evens[:1]:
        from_replica(turn).start()
    for turn in order[1:3]:
        send_block(turn)

    for at, turn in enumerate(order):
        later = order[at + 1] if at + 1 < replicas else None
        slot = at % 2
        if at and at + 2 < replicas:
            send_block(order[at + 2])
            if order[at + 2] in evens:
                place = evens.index(order[at + 2]) + 1
                if place < len(evens):
                    from_replica(evens[place]).start()
        if at:
            for copies in load_block(turn, slot):
                copies[0].wait()
        else:
            loads[1][0].wait()
        if at > 1:
            store_block(order[at - 2], slot).wait()

        def products(step, carry, at=at, slot=slot):
            cols = pl.ds(pl.multiple_of(step * CHUNK, CHUNK), CHUNK)
            high = pl.ds(pl.multiple_of(part + step * CHUNK, CHUNK), CHUNK)
            if at == 0:
                load_weight(0, step).wait()
                load_weight(1, step).wait()
            gate = dot(block_ref[slot], weight_ref[:, cols])
            up = dot(block_ref[slot], weight_ref[:, high])
            gate_up_ref[slot, :, cols] = gate.astype(BF)
            gate_up_ref[slot, :, high] = up.astype(BF)
            hidden_ref[:, cols] = (gate * jax.nn.sigmoid(gate) * up).astype(BF)
            return carry

        lax.fori_loop(0, steps, products, 0)
        store_block(turn, slot).start()
        if later is not None:

            def pass_on(later=later):
                over(later).wait_recv()
                relay(later).start()

            fetched(later, pass_on)

        @pl.when(shard == owner)
        def _(at=at, turn=turn, slot=slot):
            if at > 1:
                keep_hidden(order[at - 2], slot).wait()
                for peer in range(3):
                    hand_hidden(order[at - 2], slot, peer).wait_send()

            def turn_over(device, carry):
                cols = pl.ds(pl.multiple_of(first_col + device * ff_rows, ff_rows), ff_rows)
                turned_ref[slot, device] = hidden_ref[:, cols].T
                return carry

            lax.fori_loop(0, shards, turn_over, 0)
            keep_hidden(turn, slot).start()
            for peer in range(3):
                hand_hidden(turn, slot, peer).start()

        slice_cols = pl.ds(pl.multiple_of(replica * slice_rows, slice_rows), slice_rows)
        left_rows_ref[:, tokens(turn)] = block_ref[slot, :, slice_cols].T
        if later is not None:

            def arrive(later=later):
                direct(later).wait_recv()
                relay(later).wait_recv()

            fetched(later, arrive)
            start_block(later, 1 - slot)

    for at in range(max(0, replicas - 2), replicas):
        store_block(order[at], at % 2).wait()

        @pl.when(shard == owner)
        def _(at=at):
            keep_hidden(order[at], at % 2).wait()
            for peer in range(3):
                hand_hidden(order[at], at % 2, peer).wait_send()

    for turn in range(replicas):
        for peer in range(3):

            @pl.when(peers[peer] == owner)
            def _(turn=turn, peer=peer):
                hand_hidden(turn, 0, peer).wait_recv()

        if turn:

            def leave(turn=turn):
                over(turn).wait_send()
                direct(turn).wait_send()
                relay(turn).wait_send()

            fetched(turn, leave)
        if turn in evens:
            from_replica(turn).wait_send()


def call_prepare(normed_two, gate_up_part, slices, odd, ahead, collective):
    rows, width = normed_two[0].shape
    shards, replicas = lax.axis_size("shard"), lax.axis_size("replica")
    part = gate_up_part.shape[1] // 2
    every = rows * shards
    slice_rows = width // replicas
    ff_rows = part // replicas
    vmem, anywhere = pl.BlockSpec(memory_space=pltpu.VMEM), pl.BlockSpec(memory_space=pl.ANY)
    copies = 7 * replicas
    outs = pl.pallas_call(
        functools.partial(prepare_kernel, len(slices)),
        out_shape=[
            jax.ShapeDtypeStruct((replicas, every, width), BF),
            jax.ShapeDtypeStruct((replicas * every, 2 * part), BF),
            jax.ShapeDtypeStruct((ff_rows, replicas * every), BF),
            jax.ShapeDtypeStruct((slice_rows, replicas * every), BF),
        ],
        in_specs=[anywhere] * (2 + 3 * len(slices)),
        out_specs=[anywhere] * 3 + [vmem],
        scratch_shapes=[
            pltpu.VMEM((rows, width), BF),
            pltpu.VMEM(gate_up_part.shape, BF),
            pltpu.VMEM((2, every, width), BF),
            pltpu.VMEM((2, every, 2 * part), BF),
            pltpu.VMEM((every, part), BF),
            pltpu.VMEM((2, shards, ff_rows, every), BF),
            pltpu.SemaphoreType.DMA((2, part // CHUNK)),
            pltpu.SemaphoreType.DMA((3, 2)),
            pltpu.SemaphoreType.DMA((2, 4)),
            pltpu.SemaphoreType.DMA((1,)),
            pltpu.SemaphoreType.DMA((copies,)),
            pltpu.SemaphoreType.DMA((copies,)),
        ],
        compiler_params=pltpu.CompilerParams(
            collective_id=collective, has_side_effects=True, vmem_limit_bytes=VMEM_LIMIT
        ),
        name="prepare",
    )(gate_up_part, ahead, *slices, *normed_two, *odd)
    return outs[1:]


def on_device(
    tokens_in,
    positions,
    attn_gain,
    qkv_weight,
    out_weight,
    mlp_gain,
    gate_up_weight,
    down_weight,
    cotangent,
):
    sections = lax.axis_size("section")
    rows, width = tokens_in.shape
    down_steps = [(at + 1, at) for at in range(sections - 1)]

    cosine, sine = rope_tables(positions)
    allowed = visible(positions)

    tables = (attn_gain, mlp_gain, cosine, sine, allowed)
    qkv_full, out_full, gate_up_part, *attend_first = call_weights(
        qkv_weight[0], out_weight[0], gate_up_weight[0], (tokens_in,) + tables, 3
    )
    down_part = down_weight[0]

    forward = []
    state = tokens_in
    early = None
    for section in range(sections):
        middle, normed_two, rotated, lefts = (
            call_attend_forward(section, state, *tables, qkv_full, out_full) if section else attend_first
        )
        block_out, normed_two_slice, gate_up, normed_two_odd, state_next, *gathered = call_feed(
            section, False, (normed_two, middle, gate_up_part, down_part), 8 + section,
            cotangent if section + 2 == sections else None,
        )
        early = gathered[0] if gathered else early
        forward.append((state, middle, rotated, gate_up, normed_two_slice, normed_two_odd, normed_two, lefts, block_out))
        state = state_next

    def pick(values):
        chosen = values[-1]
        for section in range(sections - 1):
            chosen = jnp.where(lax.axis_index("section") == section, values[section], chosen)
        return chosen

    slices, normed_two_odd, normed_two, lefts, block_out = list(zip(*forward))[4:]
    block_out = pick(block_out)
    backward = []
    upstream = cotangent
    for section in reversed(range(sections)):
        state, middle, rotated, gate_up = forward[section][:4]
        grad_normed_two, upstream_slice, odd, ahead = call_feed(
            section, True, (upstream, gate_up, normed_two_odd[section], down_part, gate_up_part), 8 + sections + section
        )
        grad_in, grad_low, grad_projected, gains, grad_branch = call_attend_backward(
            section, 8 + 2 * sections + section, grad_normed_two, upstream, middle, state, rotated,
            *tables, qkv_full, out_full,
        )
        backward.insert(0, (upstream, upstream_slice, odd, grad_in, grad_projected, gains, grad_branch))
        if section == sections - 1:
            normed_two, grad_low = lax.optimization_barrier((normed_two, grad_low))
        if section > 0:
            upstream = lax.ppermute(grad_low, "section", down_steps)
        if section == sections - 1:
            gate_up_all, hidden_rows, left_rows = call_prepare(
                normed_two, gate_up_part, slices, normed_two_odd, ahead, 6
            )
            upstream, gate_up_all, left_rows, hidden_rows = lax.optimization_barrier(
                (upstream, gate_up_all, left_rows, hidden_rows)
            )

    upstream, upstream_slice, odd, grad_in, grad_projected, gains, grad_branch = zip(*backward)
    grad_in = pick(grad_in)
    gate_up_grad, down_grad, qkv_grad, out_grad, gains, _, _ = call_weight_grads(
        left_rows, hidden_rows, lefts, grad_projected, gains, upstream, grad_branch, upstream_slice, odd,
        early, gate_up_all, down_part, 5,
    )
    gate_up_grad = gate_up_grad.astype(F32)
    return (
        block_out[None],
        grad_in[None],
        gains[0][None],
        qkv_grad[None],
        out_grad[None],
        gains[1][None],
        gate_up_grad[None],
        down_grad[None],
    )


def solution(mesh):
    both = ("replica", "shard")
    return jax.shard_map(
        on_device,
        mesh=mesh,
        in_specs=(
            P(both, None),
            P(both),
            P("section", None),
            P("section", "shard", None),
            P("section", "shard", None),
            P("section", None),
            P("section", "shard", None),
            P("section", "shard", None),
            P(both, None),
        ),
        out_specs=(
            P("section", both, None),
            P("section", both, None),
            P("section", None),
            P("section", both, None),
            P("section", both, None),
            P("section", None),
            P("section", both, None),
            P("section", both, None),
        ),
        check_vma=False,
    )
```
